32 devices in a mesh: dp: 16 (over z, y, core), fsdp: 2 (over x).
Axes of the slice: x: 2, y: 2, z: 4, core: 2. Of those that a mesh axis runs over, the one named last changes fastest.
Arguments:
- inputs: bfloat16 [32, 512, 768], P('dp', 'fsdp'), may hold values from -6 to 6
- box_coords: int32 [32, 512, 4], P('dp'), may hold values from 0 to 999
- mlm_mask: int32 [32, 512], P('dp', 'fsdp'), may hold values from 0 to 1, as said below
- cotangent: bfloat16 [32, 512, 768], P('dp', 'fsdp'), may hold values from -6 to 6
- params: float32 [7208960], P('fsdp')
- first_moment: float32 [7208960], P('fsdp'), may hold values from -0.15625 to 0.15625
- second_moment: float32 [7208960], P('fsdp'), may hold values from 1e-06 to 0.001
Outputs:
- layer_out: bfloat16 [32, 512, 768], P('dp', 'fsdp')
- input_grad: bfloat16 [32, 512, 768], P('dp', 'fsdp')
- weight_grad: float32 [7208960], P('fsdp')
- grad_norm: float32 [], replicated
- param_update: float32 [7208960], P('fsdp')
- new_first: float32 [7208960], P('fsdp')
The draws below stay inside these ranges and needn't reach their ends.
Inputs may be any that keep to these rules, and one draw needn't show every extreme that they name: `mlm_mask`: the first token of every document is masked.
All inputs are finite; a program needn't handle non-finite values.
Results may differ from the reference program's by a relative error of at most 0.015.
The reference program's roundings to bfloat16 on the way count: a program that leaves them out, or rounds other values in their place, can miss the bound.
Values may be sent and summed in bfloat16 or wider, within the bound.
A program may use at most 256 MiB of HBM per device.

```python
import functools
import math
import jax
import jax.numpy as jnp
from jax import lax

D = 768
HEADS = 12
HDIM = 64
FF = 3072
BUCKETS = 32
FEAT = 128
QMAX = 1000
LEN = 512
DOCS = 2
ALL_DOCS = 32
PADDED = 7208960


def param_laws():
    return (((D, 3 * D), D ** (-0.5), 0.0), ((2 * D,), 0.3, 0.0), ((D, D), 4.0 * D ** (-0.5), 0.0), ((D,), 0.1, 0.0), ((D,), 0.1, 1.0), ((D,), 0.1, 0.0), ((D, FF), D ** (-0.5), 0.0), ((FF,), 0.3, 0.0), ((FF, D), FF ** (-0.5), 0.0), ((D,), 0.1, 0.0), ((D,), 0.1, 1.0), ((D,), 0.1, 0.0), ((FEAT, D), FEAT ** (-0.5), 0.0), ((3, BUCKETS, HEADS), 1.0, 0.0))


def draw_params(key, part):
    key = jax.random.fold_in(key, 11)
    pieces = []
    used_count = 0
    for number, law_entry in enumerate(param_laws()):
        length = 1
        for extent in law_entry[0]:
            length = length * extent
        subkey = jax.random.fold_in(key, number)
        sample = jax.random.normal(subkey, (length,), jnp.float32)
        pieces.append(law_entry[2] + law_entry[1] * sample)
        used_count = used_count + length
    pieces.append(0.01 * jax.random.normal(jax.random.fold_in(key, 97), (PADDED - used_count,), jnp.float32))
    return jnp.concatenate(pieces)


def draw_mlm_mask(key, part):
    key = jax.random.fold_in(key, 5)
    draws_int = jax.random.randint(key, (ALL_DOCS, LEN), 0, 4000)
    doc_index = jnp.arange(ALL_DOCS, dtype=jnp.int32)[:, None]
    token_index = jnp.arange(LEN, dtype=jnp.int32)[None, :]
    limits = 300 + 600 * doc_index // ALL_DOCS
    return ((draws_int < limits) | (token_index == 0)).astype(jnp.int32)


def place_ends(values, key, least, high):
    longest = values.shape.index(max(values.shape))
    spots = []
    for shift in (0, 1):
        where = [jax.random.randint(jax.random.fold_in(key, axis), (), 0, length) for axis, length in enumerate(values.shape)]
        where[longest] = (where[longest] + shift) % values.shape[longest]
        spots.append(tuple(where))
    return values.at[spots[0]].set(least).at[spots[1]].set(high)


def level_of(key, dims, cuts, low, high):
    factor_of = 1.0
    for position, blocks in cuts:
        steps = jax.random.uniform(jax.random.fold_in(jax.random.fold_in(key, 6), position), (blocks,), jnp.float32, low / len(cuts), high / len(cuts))
        factor_of = factor_of * jnp.repeat(jnp.exp(steps), dims[position] // blocks).reshape((-1,) + (1,) * (len(dims) - 1 - position))
    return factor_of


def scatter_about(own_key, dims, scale, limit, cuts=(), held_as=jnp.bfloat16):
    level = level_of(own_key, dims, cuts, -0.22, 0.18) if cuts else 1.0
    values = jax.random.normal(own_key, dims, jnp.float32) * scale * level
    return jnp.minimum(jnp.maximum(values, -limit), limit).astype(held_as)


def setup_inputs(seed: int = 0) -> dict:
    streams_of = jax.random.split(jax.random.key(seed), 8)
    return {
        "inputs": scatter_about(streams_of[0], (ALL_DOCS, LEN, D), 1.0, 6.0, ((0, 16), (1, 2))),
        "box_coords": place_ends(jax.random.randint(streams_of[1], (ALL_DOCS, LEN, 4), 0, QMAX), jax.random.fold_in(streams_of[1], 1), 0, QMAX - 1).astype(jnp.int32),
        "mlm_mask": draw_mlm_mask(jax.random.fold_in(streams_of[7], 71), 0),
        "cotangent": scatter_about(streams_of[3], (ALL_DOCS, LEN, D), 1.0, 6.0, ((0, 16), (1, 2))),
        "params": draw_params(jax.random.fold_in(streams_of[7], 71), 0),
        "first_moment": scatter_about(streams_of[5], (PADDED,), 0.01, 0.15625, ((0, 2),), jnp.float32),
        "second_moment": jnp.clip(jnp.exp(math.log(0.001) - 6.9077553 * jax.random.uniform(streams_of[6], (PADDED,), jnp.float32) ** level_of(streams_of[6], (PADDED,), ((0, 2),), -0.2, 0.2)), 9.999999974752427e-07, 0.001),
    }


@jax.custom_vjp
def low(v):
    return lax.optimization_barrier(v.astype(jnp.bfloat16)).astype(jnp.float32)

@jax.custom_vjp
def low_back(v):
    return v

def low_keep(v):
    return (low(v), None)

def low_pass(kept, grad):
    return (grad,)

def back_keep(v):
    return (v, None)

def back_low(kept, grad):
    return (low(grad),)
low.defvjp(low_keep, low_pass)
low_back.defvjp(back_keep, back_low)
highest = lax.Precision.HIGHEST
norm_eps = 1e-05
adam_one = 0.9
adam_two = 0.999
adam_eps = 1e-08
adam_steps = 100.0
decay_rate = 0.01
table_factor = 5.0

def layout_plan():
    return (('w_qkv', (D, 3 * D)), ('qv_bias', (2 * D,)), ('w_out', (D, D)), ('out_bias', (D,)), ('gain_one', (D,)), ('shift_one', (D,)), ('w_up', (D, FF)), ('up_bias', (FF,)), ('w_down', (FF, D)), ('down_bias', (D,)), ('gain_two', (D,)), ('shift_two', (D,)), ('w_layout', (FEAT, D)), ('tables', (3, BUCKETS, HEADS)))

def element_count(entry_shape):
    return functools.reduce(lambda running, extent: running * extent, entry_shape, 1)

def unpack(flat_vector):
    segments = {}
    offset = 0
    for entry_name, entry_shape in layout_plan():
        length = element_count(entry_shape)
        segments[entry_name] = flat_vector[offset:offset + length].reshape(entry_shape)
        offset = offset + length
    return segments

def special_start():
    offset = 0
    for entry_name, entry_shape in layout_plan():
        if entry_name == 'w_layout':
            return offset
        offset = offset + element_count(entry_shape)
    return offset

def bucket_of(offsets):
    half_count = BUCKETS // 2
    quarter_count = half_count // 2
    spread = jnp.abs(offsets)
    result = half_count * (offsets > 0).astype(jnp.int32)
    for level_index in range(1, half_count):
        threshold = level_index if level_index <= quarter_count else quarter_count * 2 ** (level_index - quarter_count)
        result = result + (spread >= threshold).astype(jnp.int32)
    return result

def layout_features(coords):
    freq_count = FEAT // 8
    factors = (jnp.arange(freq_count, dtype=jnp.int32) + 1) ** 2
    phases = coords[..., :, None] * factors % 4096
    angles = phases.astype(jnp.float32) * (2.0 * math.pi / 4096.0)
    wave_parts = jnp.concatenate([jnp.sin(angles), jnp.cos(angles)], axis=-1)
    return wave_parts.reshape(coords.shape[:-1] + (FEAT,))

def product(operand, matrix):
    return jnp.einsum('...d,de->...e', operand, matrix, precision=highest)

def layer_norm(values, gain_row, shift_row):
    centered = values - lax.optimization_barrier(jnp.mean(values, -1, keepdims=True))
    inverse = lax.rsqrt(lax.optimization_barrier(jnp.mean(centered * centered, -1, keepdims=True)) + norm_eps)
    return centered * inverse * gain_row + shift_row

def attend(query_rows, key_rows, value_rows, x_centres, y_centres, tables):
    positions = jnp.arange(LEN, dtype=jnp.int32)
    heads_query = query_rows.reshape(LEN, HEADS, HDIM)
    heads_key = key_rows.reshape(LEN, HEADS, HDIM)
    heads_value = value_rows.reshape(LEN, HEADS, HDIM)
    scores = jnp.einsum('qhd,khd->hqk', heads_query, heads_key, precision=highest) * HDIM ** (-0.5)
    levels = jnp.arange(BUCKETS, dtype=jnp.int32)
    for table_index, centres in enumerate((positions, x_centres, y_centres)):
        bucket_ids = bucket_of(centres[None, :] - centres[:, None])
        one_hot = (bucket_ids[None] == levels[:, None, None]).astype(jnp.float32)
        scores = scores + jnp.einsum('nqk,nh->hqk', one_hot, tables[table_index], precision=highest)
    scores = low_back(scores)
    soft_weights = jax.nn.softmax(scores, axis=-1)
    mixed_rows = jnp.einsum('hqk,khd->qhd', low(soft_weights), heads_value, precision=highest)
    return mixed_rows.reshape(LEN, D)

def forward(inputs_in, features, x_centres, y_centres, params_in):
    weights = unpack(low(params_in))
    start_rows = low_back(inputs_in + product(low(features), weights['w_layout']))
    rounded = low(start_rows)
    qkv_weight = weights['w_qkv']
    bias_pair = weights['qv_bias']
    query_rows = low(low_back(product(rounded, qkv_weight[:, :D]) + bias_pair[:D]))
    key_rows = low(low_back(product(rounded, qkv_weight[:, D:2 * D])))
    value_rows = low(low_back(product(rounded, qkv_weight[:, 2 * D:]) + bias_pair[D:]))
    tables = weights['tables']

    def one_doc(doc_args):
        return attend(doc_args[0], doc_args[1], doc_args[2], doc_args[3], doc_args[4], tables)
    mixed_rows = lax.map(jax.checkpoint(one_doc), (query_rows, key_rows, value_rows, x_centres, y_centres))
    mixed_rows = low(low_back(mixed_rows))
    branch_one = low_back(product(mixed_rows, weights['w_out']) + weights['out_bias'])
    first_rows = layer_norm(start_rows + branch_one, weights['gain_one'], weights['shift_one'])
    up_rows = low_back(product(low(first_rows), weights['w_up']) + weights['up_bias'])
    hidden = low(jax.nn.gelu(up_rows, approximate=False))
    branch_two = low_back(product(hidden, weights['w_down']) + weights['down_bias'])
    return layer_norm(first_rows + branch_two, weights['gain_two'], weights['shift_two'])

def adamw(weights_in, grads_in, first_in, second_in, positions):
    rate_scale = jnp.where(positions >= special_start(), table_factor, 1.0)
    first_new = adam_one * first_in + (1.0 - adam_one) * grads_in
    second_new = adam_two * second_in + (1.0 - adam_two) * grads_in * grads_in
    corrected = first_new / (1.0 - adam_one ** adam_steps) / (jnp.sqrt(second_new / (1.0 - adam_two ** adam_steps)) + adam_eps)
    return (rate_scale * (corrected + decay_rate * weights_in), first_new)

def reference(inputs, box_coords, mlm_mask, cotangent, params, first_moment, second_moment):
    mask_values = mlm_mask.astype(jnp.float32)
    total_masked = jnp.sum(mask_values)
    features = layout_features(box_coords)
    x_centres = box_coords[..., 0] + box_coords[..., 2]
    y_centres = box_coords[..., 1] + box_coords[..., 3]
    scaled = cotangent.astype(jnp.float32) * mask_values[..., None] / total_masked
    group_count = ALL_DOCS // DOCS

    def regroup(array):
        return array.reshape((group_count, DOCS) + array.shape[1:])
    stacked = (regroup(inputs.astype(jnp.float32)), regroup(features), regroup(x_centres), regroup(y_centres), regroup(scaled))

    def one_group(running, group_args):
        group_in, group_feat, group_x, group_y, group_cot = group_args

        def closed(values_in, weights_in):
            return forward(values_in, group_feat, group_x, group_y, weights_in)
        result, backward = jax.vjp(closed, group_in, params)
        grad_in, grad_weights = backward(group_cot)
        return (running + grad_weights, (result.astype(jnp.bfloat16), grad_in.astype(jnp.bfloat16)))
    grads, (outputs, input_grads) = lax.scan(one_group, jnp.zeros((PADDED,), jnp.float32), stacked)
    norm_value = jnp.sqrt(jnp.sum(grads * grads))
    update, new_first = adamw(params, grads, first_moment, second_moment, jnp.arange(PADDED, dtype=jnp.int32))
    return (outputs.reshape(ALL_DOCS, LEN, D), input_grads.reshape(ALL_DOCS, LEN, D), grads, norm_value, update, new_first)
```

```python
import functools
import math

import jax
import jax.numpy as jnp
import numpy as np
from jax import lax
from jax.experimental import pallas as pl
from jax.experimental.pallas import tpu as pltpu
from jax.sharding import PartitionSpec as P

D = 768
HEADS = 12
HDIM = 64
FF = 3072
BUCKETS = 32
FEAT = 128
LEN = 512
PADDED = 7208960
SHARD = PADDED // 2
FLAT = SHARD // 128
PAIRS = HEADS // 2
QROWS = 128

norm_eps = 1e-05
adam_one = 0.9
adam_two = 0.999
adam_eps = 1e-08
adam_steps = 100.0
decay_rate = 0.01
table_factor = 5.0

MESH = pl.DeviceIdType.MESH
F32 = jnp.float32
BF16 = jnp.bfloat16
VMEM = pl.BlockSpec(memory_space=pltpu.VMEM)
ANY = pl.BlockSpec(memory_space=pl.ANY)

ROWS = 28672
CHUNK = 2048
CHUNKS = ROWS // CHUNK
CUT = 404
UP_A, UP_B = 416, 368
OUT0 = 18 * D
UP0 = OUT0 + 6 * D
SM0 = UP0 + 24 * UP_A
UP1 = 0
DOWN1 = 24 * UP_B
LAY1 = DOWN1 + 6 * FF
SM1 = LAY1 + 6 * FEAT
F_OUT = 13836
F_UP = 18462
F_UPB1 = 8734
F_DOWN1 = 8758
F_SM1 = 27190
F_LAY1 = 27208
F_TAB1 = 27976
LEAD = 104


def nt(a, b):
    return lax.dot_general(a, b, (((1,), (1,)), ((), ())), preferred_element_type=F32)


def nn(a, b):
    return lax.dot_general(a, b, (((1,), (0,)), ((), ())), preferred_element_type=F32)


def tn(a, b):
    return lax.dot_general(a, b, (((0,), (0,)), ((), ())), preferred_element_type=F32)


def radices(replicas):
    stages, stride, left = [], 2, replicas // 2
    if left % 2 == 0:
        stages.append((2, stride))
        stride, left = stride * 2, left // 2
    while left > 1:
        radix = left if left <= 8 else 4
        stages.append((radix, stride))
        stride, left = stride * radix, left // radix
    return stages


def place():
    return lax.axis_index("dp"), lax.axis_index("fsdp")


def member(dp, radix, stride, digit):
    return dp + (digit - (dp // stride) % radix) * stride


def peers(stages):
    dp, fs = place()
    found = [(dp + 1 - 2 * (dp % 2), fs), (dp, 1 - fs)]
    for radix, stride in stages:
        mine = (dp // stride) % radix
        for step in range(1, radix):
            found.append((member(dp, radix, stride, (mine + step) % radix), fs))
    return found


def greet(stages):
    barrier = pltpu.get_barrier_semaphore()
    all_peers = peers(stages)
    for peer in all_peers:
        pl.semaphore_signal(barrier, inc=1, device_id=peer, device_id_type=MESH)
    pl.semaphore_wait(barrier, len(all_peers))


def remote(src, dst, send, recv, peer):
    return pltpu.make_async_remote_copy(
        src_ref=src, dst_ref=dst, send_sem=send, recv_sem=recv, device_id=peer, device_id_type=MESH
    )


def rows_at(start, size):
    return pl.ds(pl.multiple_of(start, 16), size)


def offsets(dp, stages, extent):
    size = extent // 2
    start = (dp % 2) * size
    found = [(start, size)]
    for radix, stride in stages:
        size = size // radix
        start = start + ((dp // stride) % radix) * size
        found.append((start, size))
    return found


def row_of(ref_rows, start, count):
    return jnp.concatenate([ref_rows[start + i : start + i + 1, :] for i in range(count)], axis=1)


def relayout_tasks(plane, flat, out):
    tasks = []

    def block(dst, src, count, stride):
        def run():
            out[plane, pl.ds(dst, count), :] = flat[pl.ds(LEAD + src, count, stride=stride), :].astype(BF16)

        tasks.append((dst + count, run))

    def window(dst, src, count):
        def run():
            out[plane, pl.ds(dst, count), :] = flat[pl.ds(LEAD + src, count), :].astype(BF16)

        tasks.append((dst + count, run))

    if plane == 0:
        for pos in range(18):
            block(pos * D, (pos % 3) * 6 + pos // 3, D, 18)
        for c in range(6):
            block(OUT0 + c * D, F_OUT + c, D, 6)
        for c in range(24):
            block(UP0 + c * UP_A, F_UP + c, UP_A, 24)
        window(SM0, 13824, 16)
        window(SM0 + 16, 18440, 32)
        used = SM0 + 48
    else:
        for c in range(24):
            block(UP1 + c * UP_B, c - 98, UP_B, 24)
        for c in range(6):
            block(DOWN1 + c * FF, F_DOWN1 + c, FF, 6)
        for c in range(6):
            block(LAY1 + c * FEAT, F_LAY1 + c, FEAT, 6)
        window(SM1, 8728, 32)
        window(SM1 + 32, 27184, 32)
        window(SM1 + 64, 27976, 16)
        used = SM1 + 80

    def clear():
        out[plane, pl.ds(used, ROWS - used), :] = jnp.zeros((ROWS - used, 128), BF16)

    tasks.append((ROWS, clear))
    return tasks


def direct_type(position):
    return position % 4 == 1


def gather_kernel(
    stages, p_hbm, xin, cot, cnt, wall, xdoc, cdoc, total,
    flat, zall, xs, cs, cnt_slots, in_sem, x_send, x_recv, c_send, c_recv, act_send, act_recv,
    n_send, n_recv, out_sem, *stage_sems,
):
    dp, fs = place()
    other = 1 - fs
    pieces = 8
    span = FLAT // pieces
    loads = [
        pltpu.make_async_copy(
            p_hbm.at[pl.ds(i * span, span)], flat.at[pl.ds(LEAD + i * span, span)], in_sem.at[i]
        )
        for i in range(pieces)
    ]
    for load in loads:
        load.start()
    flat[pl.ds(0, LEAD), :] = jnp.zeros((LEAD, 128), F32)
    flat[pl.ds(LEAD + FLAT, 288), :] = jnp.zeros((288, 128), F32)
    greet(stages)
    x_peer = (dp, other)
    core_peer = (dp + 1 - 2 * (dp % 2), fs)
    half = LEN // 2

    def act_copies(send):
        where = rows_at((fs if send else other) * half, half)
        return [
            remote(xin.at[other], xs.at[where], act_send.at[0], act_recv.at[0], x_peer),
            remote(cot.at[other], cs.at[where], act_send.at[1], act_recv.at[1], x_peer),
        ]

    for copy in act_copies(True):
        copy.start()
    for load in loads:
        load.wait()

    order = [(CHUNKS - 1 + i) % CHUNKS for i in range(CHUNKS)]
    parts = offsets(dp, stages, CHUNK)

    def x_copy(position, plane):
        start, size = parts[0] if direct_type(position) else parts[-1]
        where = zall.at[plane, rows_at(order[position] * CHUNK + start, size)]
        return remote(where, where, x_send.at[position], x_recv.at[position], x_peer)

    def stage_copies(level, position, receive):
        radix, stride = stages[level]
        start, size = parts[level + 1]
        mine = (dp // stride) % radix
        send_sem, recv_sem = stage_sems[2 * level], stage_sems[2 * level + 1]
        copies = []
        for step in range(1, radix):
            peer = (member(dp, radix, stride, (mine + step) % radix), fs)
            shift = ((mine - step + radix) % radix - mine) * size if receive else 0
            where = zall.at[other, rows_at(order[position] * CHUNK + start + shift, size)]
            copies.append(
                remote(where, where, send_sem.at[position, step - 1], recv_sem.at[position, step - 1], peer)
            )
        return copies

    def core_copy(position, receive):
        size = CHUNK // 2
        start = (1 - dp % 2 if receive else dp % 2) * size
        where = zall.at[other, rows_at(order[position] * CHUNK + start, size)]
        return remote(where, where, c_send.at[position], c_recv.at[position], core_peer)

    levels = len(stages)

    def advance(position, stage):
        if direct_type(position):
            if stage == 0:
                x_copy(position, other).wait_recv()
                core_copy(position, False).start()
            return
        if stage == 0:
            x_copy(position, other).wait_recv()
        else:
            for copy in stage_copies(levels - stage, position, True):
                copy.wait_recv()
        if stage < levels:
            for copy in stage_copies(levels - 1 - stage, position, False):
                copy.start()
        else:
            core_copy(position, False).start()

    rounds = [[core_peer], [x_peer]] + [
        [
            (member(dp, radix, stride, ((dp // stride) % radix + step) % radix), fs)
            for step in range(1, radix)
        ]
        for radix, stride in stages
    ]

    def count_copies(number):
        base = sum(len(r) for r in rounds[:number])
        return [
            remote(total.at[...], cnt_slots.at[base + i], n_send.at[base + i], n_recv.at[base + i], peer)
            for i, peer in enumerate(rounds[number])
        ]

    def count_round(number):
        if number > 0:
            for copy in count_copies(number - 1):
                copy.wait()
            base = sum(len(r) for r in rounds[: number - 1])
            gathered = total[...]
            for i in range(len(rounds[number - 1])):
                gathered = gathered + cnt_slots[base + i]
            total[...] = gathered
        if number < len(rounds):
            for copy in count_copies(number):
                copy.start()

    total[...] = cnt[...]
    count_round(0)

    tasks = [relayout_tasks(0, flat, zall), relayout_tasks(1, flat, zall)]
    done = [set(), set()]
    for position in range(CHUNKS + levels + 1):
        if position < CHUNKS:
            low, high = order[position] * CHUNK, (order[position] + 1) * CHUNK
            for plane in range(2):
                run, start = [], 0
                for number, (end, task) in enumerate(tasks[plane]):
                    if start < high and end > low and number not in done[plane]:
                        done[plane].add(number)
                        run.append(task)
                    start = end

                @pl.when(fs == plane)
                def _(run=run):
                    for task in run:
                        task()

            x_copy(position, fs).start()
        for stage in range(levels + 1):
            if 0 <= position - 1 - stage < CHUNKS:
                advance(position - 1 - stage, stage)
        if 2 <= position and (position - 2) % 2 == 0 and (position - 2) // 2 + 1 <= len(rounds):
            count_round((position - 2) // 2 + 1)
    xdoc[pl.ds(fs * half, half), :] = xin[fs]
    cdoc[pl.ds(fs * half, half), :] = cot[fs]
    outs = [
        pltpu.make_async_copy(zall.at[fs], wall.at[fs], out_sem.at[0]),
    ]
    outs[0].start()
    for copy in act_copies(False):
        copy.wait_recv()
    xdoc[pl.ds(other * half, half), :] = xs[pl.ds(other * half, half), :]
    cdoc[pl.ds(other * half, half), :] = cs[pl.ds(other * half, half), :]
    for copy in act_copies(True):
        copy.wait_send()
    for position in range(CHUNKS):
        core_copy(position, True).wait_recv()
        core_copy(position, False).wait_send()
        x_copy(position, fs).wait_send()
        if not direct_type(position):
            for level in range(levels):
                for copy in stage_copies(level, position, False):
                    copy.wait_send()
    outs.append(pltpu.make_async_copy(zall.at[other], wall.at[other], out_sem.at[1]))
    outs[1].start()
    for copy in outs:
        copy.wait()


def gather_weights(stages, p2, xin, cot, cnt):
    count_peers = 2 + sum(radix - 1 for radix, _ in stages)
    sems = []
    for radix, _ in stages:
        sems += [pltpu.SemaphoreType.DMA((CHUNKS, radix - 1))] * 2
    half = LEN // 2
    return pl.pallas_call(
        functools.partial(gather_kernel, stages),
        name="gather_weights",
        out_shape=(
            jax.ShapeDtypeStruct((2, ROWS, 128), BF16),
            jax.ShapeDtypeStruct((LEN, D), BF16),
            jax.ShapeDtypeStruct((LEN, D), BF16),
            jax.ShapeDtypeStruct((8, 128), F32),
        ),
        in_specs=[ANY, VMEM, VMEM, VMEM],
        out_specs=(ANY, VMEM, VMEM, VMEM),
        scratch_shapes=[
            pltpu.VMEM((LEAD + FLAT + 288, 128), F32),
            pltpu.VMEM((2, ROWS, 128), BF16),
            pltpu.VMEM((LEN, D), BF16),
            pltpu.VMEM((LEN, D), BF16),
            pltpu.VMEM((count_peers, 8, 128), F32),
            pltpu.SemaphoreType.DMA((8,)),
            pltpu.SemaphoreType.DMA((CHUNKS,)),
            pltpu.SemaphoreType.DMA((CHUNKS,)),
            pltpu.SemaphoreType.DMA((CHUNKS,)),
            pltpu.SemaphoreType.DMA((CHUNKS,)),
            pltpu.SemaphoreType.DMA((2,)),
            pltpu.SemaphoreType.DMA((2,)),
            pltpu.SemaphoreType.DMA((count_peers,)),
            pltpu.SemaphoreType.DMA((count_peers,)),
            pltpu.SemaphoreType.DMA((2,)),
        ]
        + sems,
        compiler_params=pltpu.CompilerParams(
            collective_id=1, has_side_effects=True, vmem_limit_bytes=60 * 2**20
        ),
    )(p2, xin, cot, cnt)


def table_constants():
    width = BUCKETS * HEADS
    lane = np.arange(width)
    pick = np.zeros((3, width, 128), np.float32)
    for table in range(3):
        pick[table, lane, 32 * table + lane // HEADS] = 1.0
    keep = (lane[None, :] % HEADS == np.arange(16)[:, None]).astype(np.float32)
    return pick.astype(jnp.bfloat16), keep


def bucket_of(offset):
    spread = jnp.abs(offset)
    result = jnp.minimum(spread, 8) + jnp.where(offset > 0, 16, 0)
    for level in range(9, 16):
        result = result + jnp.where(spread >= 8 * 2 ** (level - 8), 1, 0)
    return result


def up_block(wall, j):
    columns = []
    for c in (2 * j, 2 * j + 1):
        first = wall[0, rows_at(UP0 + c * UP_A, UP_A), :]
        second = wall[1, rows_at(UP1 + c * UP_B + 16, UP_B - 16), :]
        columns.append(jnp.concatenate([first, second], axis=0))
    return jnp.concatenate(columns, axis=1)


def down_rows(wall, j):
    return jnp.concatenate(
        [wall[1, rows_at(DOWN1 + c * FF + j * 256, 256), :] for c in range(6)], axis=1
    )


def merge_up(wall):
    row = lax.broadcasted_iota(jnp.int32, (16, 128), 0)

    def one(c, carry):
        low_at = rows_at(UP0 + c * UP_A + UP_A - 16, 16)
        low = wall[0, low_at, :].astype(F32)
        high = wall[1, rows_at(UP1 + c * UP_B, 16), :].astype(F32)
        cut = jnp.where(c < 2, CUT + 1 - 400, CUT - 400)
        wall[0, low_at, :] = jnp.where(row < cut, low, high).astype(BF16)
        return carry

    lax.fori_loop(0, 24, one, 0)


def stats(values):
    mean = jnp.mean(values, axis=1, keepdims=True)
    centered = values - mean
    inverse = lax.rsqrt(jnp.mean(centered * centered, axis=1, keepdims=True) + norm_eps)
    return centered * inverse, inverse


def forward_kernel(
    wall_hbm, xdoc, features, coord_row, coord_col, pick, keep,
    layer_out, rounded, qkv, probs, mixed, normed_one, inverse_one, first_low, hidden, slope,
    normed_two, inverse_two,
    wall, start, up_bias, acc, bias, sem,
):
    load = pltpu.make_async_copy(wall_hbm, wall, sem.at[0])
    load.start()
    load.wait()
    merge_up(wall)
    small0 = wall[0, pl.ds(SM0, 48), :].astype(F32)
    small1 = wall[1, pl.ds(SM1, 80), :].astype(F32)
    qv_bias = row_of(small0, 0, 12)
    out_bias, gain_one, shift_one = (row_of(small0, 20 + 6 * i, 6) for i in range(3))
    down_bias, gain_two, shift_two = (row_of(small1, 38 + 6 * i, 6) for i in range(3))

    w_layout = jnp.concatenate([wall[1, pl.ds(LAY1 + c * FEAT, FEAT), :] for c in range(6)], axis=1)
    start[...] = xdoc[...].astype(F32) + nn(features[...], w_layout)
    rounded[...] = start[...].astype(BF16)

    heads_by_lane = jnp.zeros((16, 128), F32)
    for table in range(3):
        flat_row = row_of(small1, 64 + 3 * table, 3)
        spread = (jnp.broadcast_to(flat_row, (16, 384)) * keep[...]).astype(BF16)
        heads_by_lane = heads_by_lane + nn(spread, pick[table])
    rows_by_head = [jnp.broadcast_to(heads_by_lane[h : h + 1, :], (8, 128)) for h in range(HEADS)]

    def bias_rows(a, carry):
        at = pl.ds(pl.multiple_of(a * 8, 8), 8)
        for j in range(4):
            lanes = pl.ds(j * 128, 128)
            sums = [None] * HEADS
            for table in range(3):
                far = coord_row[table : table + 1, j * 128 : (j + 1) * 128]
                near = coord_col[at, table : table + 1]
                index = bucket_of(jnp.broadcast_to(far, (8, 128)) - near) + 32 * table
                for h in range(HEADS):
                    found = jnp.take_along_axis(rows_by_head[h], index, axis=1)
                    sums[h] = found if sums[h] is None else sums[h] + found
            for h in range(HEADS):
                bias[h, at, lanes] = sums[h]
        return carry

    lax.fori_loop(0, LEN // 8, bias_rows, 0)

    left = lax.broadcasted_iota(jnp.int32, (LEN, 128), 1) < HDIM
    for pair in range(PAIRS):
        weight = jnp.concatenate(
            [wall[0, pl.ds((3 * pair + i) * D, D), :] for i in range(3)], axis=1
        )
        part = nn(rounded[...], weight)
        lanes = slice(pair * 128, (pair + 1) * 128)
        query = (part[:, :128] + qv_bias[:, lanes]).astype(BF16)
        qkv[3 * pair] = query * HDIM**-0.5
        qkv[3 * pair + 1] = part[:, 128:256].astype(BF16)
        value_bias = qv_bias[:, D + pair * 128 : D + (pair + 1) * 128]
        qkv[3 * pair + 2] = (part[:, 256:] + value_bias).astype(BF16)

    def attend(pair, carry):
        query, key, value = qkv[3 * pair], qkv[3 * pair + 1], qkv[3 * pair + 2]
        found = []
        for side in range(2):
            head = 2 * pair + side
            mine = left if side == 0 else jnp.logical_not(left)
            for at in (slice(r, r + QROWS) for r in range(0, LEN, QROWS)):
                part = query[at]
                scores = nt(jnp.where(mine[at], part, jnp.zeros_like(part)), key) + bias[head, at, :]
                scores = jnp.exp(scores - jnp.max(scores, axis=1, keepdims=True))
                soft = scores * (1.0 / jnp.sum(scores, axis=1, keepdims=True))
                probs[head, at, :] = soft.astype(BF16)
            found.append(nn(probs[head], value))
        mixed[:, pl.ds(pl.multiple_of(pair * 128, 128), 128)] = jnp.where(left, found[0], found[1]).astype(BF16)
        return carry

    lax.fori_loop(0, PAIRS, attend, 0)

    w_out = jnp.concatenate([wall[0, pl.ds(OUT0 + c * D, D), :] for c in range(6)], axis=1)

    def first_rows(r, carry):
        at = pl.ds(pl.multiple_of(r * QROWS, QROWS), QROWS)
        normed, inverse = stats(start[at, :] + nn(mixed[at, :], w_out) + out_bias)
        normed_one[at, :] = normed
        inverse_one[at, :] = inverse
        result = normed * gain_one + shift_one
        first_low[at, :] = result.astype(BF16)
        acc[at, :] = result + down_bias
        return carry

    lax.fori_loop(0, LEN // QROWS, first_rows, 0)
    for j in range(12):
        up_bias[:, j * 256 : (j + 1) * 256] = row_of(small1, 6 + 2 * j, 2)

    def feed_step(j, carry):
        lanes = pl.ds(pl.multiple_of(j * 256, 256), 256)
        up = nn(first_low[...], up_block(wall, j)) + up_bias[:, lanes]
        half_up = 0.5 + 0.5 * lax.erf(up * math.sqrt(0.5))
        bell = jnp.exp(-0.5 * up * up) * (1.0 / math.sqrt(2.0 * math.pi))
        slope[:, lanes] = (half_up + up * bell).astype(BF16)
        part = (up * half_up).astype(BF16)
        hidden[:, lanes] = part
        acc[...] += nn(part, down_rows(wall, j))
        return carry

    lax.fori_loop(0, 12, feed_step, 0)

    def second_rows(r, carry):
        at = pl.ds(pl.multiple_of(r * QROWS, QROWS), QROWS)
        normed, inverse = stats(acc[at, :])
        normed_two[at, :] = normed
        inverse_two[at, :] = inverse
        layer_out[at, :] = (normed * gain_two + shift_two).astype(BF16)
        return carry

    lax.fori_loop(0, LEN // QROWS, second_rows, 0)


def forward_pass(wall, xdoc, features, coord_row, coord_col):
    pick, keep = table_constants()
    sds = jax.ShapeDtypeStruct
    return pl.pallas_call(
        forward_kernel,
        name="forward",
        out_shape=(
            sds((LEN, D), BF16),
            sds((LEN, D), BF16),
            sds((18, LEN, 128), BF16),
            sds((HEADS, LEN, LEN), BF16),
            sds((LEN, D), BF16),
            sds((LEN, D), F32),
            sds((LEN, 1), F32),
            sds((LEN, D), BF16),
            sds((LEN, FF), BF16),
            sds((LEN, FF), BF16),
            sds((LEN, D), F32),
            sds((LEN, 1), F32),
        ),
        in_specs=[ANY] + [VMEM] * 6,
        out_specs=(VMEM,) * 12,
        scratch_shapes=[
            pltpu.VMEM((2, ROWS, 128), BF16),
            pltpu.VMEM((LEN, D), F32),
            pltpu.VMEM((1, FF), F32),
            pltpu.VMEM((LEN, D), F32),
            pltpu.VMEM((HEADS, LEN, LEN), F32),
            pltpu.SemaphoreType.DMA((1,)),
        ],
        compiler_params=pltpu.CompilerParams(vmem_limit_bytes=62 * 2**20),
    )(wall, xdoc, features, coord_row, coord_col, jnp.asarray(pick), jnp.asarray(keep))


G_SMALL = (("qv_bias", 0, 0, 12), ("out_bias", 0, 12, 6), ("gain_one", 0, 18, 6), ("shift_one", 0, 24, 6),
           ("up_bias", 1, 0, 24), ("down_bias", 1, 24, 6), ("gain_two", 1, 30, 6), ("shift_two", 1, 36, 6),
           ("tables", 1, 42, 9))


def spread_norm(normed, inverse, gain, grad):
    scaled = grad * gain
    return inverse * (
        scaled
        - jnp.mean(scaled, axis=1, keepdims=True)
        - normed * jnp.mean(scaled * normed, axis=1, keepdims=True)
    )


def total_rows(values):
    return jnp.sum(values.astype(F32), axis=0, keepdims=True)


def backward_kernel(
    wall_hbm, cdoc, total, rounded, qkv, probs_hbm, mixed, normed_one, inverse_one, first_low, hidden_hbm,
    slope_hbm, normed_two, inverse_two, features, coord_row, coord_col, pick, keep,
    input_grad, grads,
    wall, gstack, acc, branch, hidden, d_up, probs, d_mixed, d_scores, less, prefix, small, lut, places,
    sem, out_sem, probs_sem,
):
    loads = [
        pltpu.make_async_copy(wall_hbm, wall, sem.at[0]),
        pltpu.make_async_copy(hidden_hbm, hidden, sem.at[1]),
        pltpu.make_async_copy(slope_hbm, d_up, sem.at[2]),
    ]
    for load in loads:
        load.start()

    def probs_copy(pair, slot):
        return pltpu.make_async_copy(
            probs_hbm.at[pl.ds(2 * pair, 2)], probs.at[pl.ds(2 * slot, 2)], probs_sem.at[slot]
        )

    probs_copy(0, 0).start()
    for load in loads:
        load.wait()
    merge_up(wall)
    small0 = wall[0, pl.ds(SM0, 48), :].astype(F32)
    small1 = wall[1, pl.ds(SM1, 80), :].astype(F32)
    gain_one = row_of(small0, 26, 6)
    gain_two = row_of(small1, 44, 6)
    small[...] = jnp.zeros_like(small)
    spots = {name: (plane, first_row) for name, plane, first_row, _ in G_SMALL}

    def keep_small(name, vector):
        plane, at = spots[name]
        for i in range(vector.shape[1] // 128):
            small[plane, at + i : at + i + 1, :] = vector[:, i * 128 : (i + 1) * 128]

    count = total[0:1, 0:1]
    none = jnp.zeros((1, D), F32)

    def second_rows(r, sums):
        at = pl.ds(pl.multiple_of(r * QROWS, QROWS), QROWS)
        grad_out = cdoc[at, :].astype(F32) / count
        normed = normed_two[at, :]
        result = spread_norm(normed, inverse_two[at, :], gain_two, grad_out)
        acc[at, :] = result
        low = result.astype(BF16)
        branch[at, :] = low
        return sums[0] + total_rows(grad_out * normed), sums[1] + total_rows(grad_out), sums[2] + total_rows(low)

    sums = lax.fori_loop(0, LEN // QROWS, second_rows, (none, none, none))
    for name, vector in zip(("gain_two", "shift_two", "down_bias"), sums):
        keep_small(name, vector)
    plane_up, at_up = spots["up_bias"]

    def down_step(j, carry):
        lanes = pl.ds(pl.multiple_of(j * 256, 256), 256)
        grad = nt(branch[...], down_rows(wall, j))
        part = (grad * d_up[:, lanes].astype(F32)).astype(BF16)
        d_up[:, lanes] = part
        sums = total_rows(part)
        small[plane_up, pl.ds(at_up + 2 * j, 1), :] = sums[:, :128]
        small[plane_up, pl.ds(at_up + 2 * j + 1, 1), :] = sums[:, 128:]
        down = tn(hidden[:, lanes], branch[...]).astype(BF16)
        for c in range(6):
            gstack[1, rows_at(DOWN1 + c * FF + j * 256, 256), :] = down[:, c * 128 : (c + 1) * 128]
        return carry

    lax.fori_loop(0, 12, down_step, 0)

    def up_step(j, carry):
        lanes = pl.ds(pl.multiple_of(j * 256, 256), 256)
        part = d_up[:, lanes]
        up = tn(first_low[...], part).astype(BF16)
        for i in range(2):
            c = 2 * j + i
            gstack[0, rows_at(UP0 + c * UP_A, UP_A), :] = up[:UP_A, i * 128 : (i + 1) * 128]
            gstack[1, rows_at(UP1 + c * UP_B, UP_B), :] = up[D - UP_B :, i * 128 : (i + 1) * 128]
        acc[...] += nt(part, up_block(wall, j))
        return carry

    lax.fori_loop(0, 12, up_step, 0)

    w_out = jnp.concatenate([wall[0, pl.ds(OUT0 + c * D, D), :] for c in range(6)], axis=1)

    def first_rows(r, sums):
        at = pl.ds(pl.multiple_of(r * QROWS, QROWS), QROWS)
        grad, normed = acc[at, :], normed_one[at, :]
        result = spread_norm(normed, inverse_one[at, :], gain_one, grad)
        acc[at, :] = result
        low = result.astype(BF16)
        branch[at, :] = low
        d_mixed[at, :] = nt(low, w_out).astype(BF16)
        return sums[0] + total_rows(grad * normed), sums[1] + total_rows(grad), sums[2] + total_rows(low)

    sums = lax.fori_loop(0, LEN // QROWS, first_rows, (none, none, none))
    for name, vector in zip(("gain_one", "shift_one", "out_bias"), sums):
        keep_small(name, vector)

    def out_step(j, carry):
        lanes = pl.ds(pl.multiple_of(j * 256, 256), 256)
        part = tn(mixed[...], branch[:, lanes]).astype(BF16)
        for i in range(2):
            gstack[0, rows_at(OUT0 + (2 * j + i) * D, D), :] = part[:, i * 128 : (i + 1) * 128]
        return carry

    lax.fori_loop(0, 3, out_step, 0)

    left = lax.broadcasted_iota(jnp.int32, (LEN, 128), 1) < HDIM

    def attend(pair, carry):
        query, key, value = qkv[3 * pair], qkv[3 * pair + 1], qkv[3 * pair + 2]
        slot = pair % 2

        @pl.when(pair + 1 < PAIRS)
        def _():
            probs_copy(pair + 1, 1 - slot).start()

        probs_copy(pair, slot).wait()
        grad = d_mixed[:, pl.ds(pl.multiple_of(pair * 128, 128), 128)]
        found = []
        for side in range(2):
            head = 2 * pair + side
            mine = left if side == 0 else jnp.logical_not(left)
            for at in (slice(r, r + QROWS) for r in range(0, LEN, QROWS)):
                part = grad[at]
                d_probs = nt(jnp.where(mine[at], part, jnp.zeros_like(part)), value)
                soft = probs[2 * slot + side, at, :].astype(F32)
                inner = jnp.sum(soft * d_probs, axis=1, keepdims=True)
                d_scores[head, at, :] = (soft * (d_probs - inner)).astype(BF16)
            scores = d_scores[head]
            found.append((nn(scores, key), tn(scores, query), tn(probs[2 * slot + side], grad)))
        d_query = (jnp.where(left, found[0][0], found[1][0]) * HDIM**-0.5).astype(BF16)
        d_key = jnp.where(left, found[0][1], found[1][1]).astype(BF16)
        d_value = jnp.where(left, found[0][2], found[1][2]).astype(BF16)
        both = jnp.concatenate([d_query, d_key, d_value], axis=1)
        plane, spot = spots["qv_bias"]
        small[plane, pl.ds(spot + pair, 1), :] = total_rows(d_query)
        small[plane, pl.ds(spot + 6 + pair, 1), :] = total_rows(d_value)
        at = pl.multiple_of(3 * pair * D, 16)
        weight = jnp.concatenate([wall[0, rows_at(at + i * D, D), :] for i in range(3)], axis=1)
        acc[...] += nt(both, weight)
        part = tn(rounded[...], both).astype(BF16)
        for i in range(3):
            gstack[0, rows_at(at + i * D, D), :] = part[:, i * 128 : (i + 1) * 128]
        return carry

    lax.fori_loop(0, PAIRS, attend, 0)
    result = acc[...].astype(BF16)
    input_grad[...] = result
    layout = tn(features[...], result).astype(BF16)
    for c in range(6):
        gstack[1, pl.ds(LAY1 + c * FEAT, FEAT), :] = layout[:, c * 128 : (c + 1) * 128]

    table_grads(d_scores, coord_row, coord_col, pick, keep, less, prefix, small, lut, places, spots)

    gstack[0, pl.ds(SM0, ROWS - SM0), :] = jnp.zeros((ROWS - SM0, 128), BF16)
    gstack[1, pl.ds(SM1, ROWS - SM1), :] = jnp.zeros((ROWS - SM1, 128), BF16)
    gstack[0, pl.ds(SM0, 64), :] = small[0].astype(BF16)
    gstack[1, pl.ds(SM1, 64), :] = small[1].astype(BF16)
    store = pltpu.make_async_copy(gstack, grads, out_sem.at[0])
    store.start()
    store.wait()


def table_grads(d_scores, coord_row, coord_col, pick, keep, less, prefix, small, lut, places, spots):
    lane = lax.broadcasted_iota(jnp.int32, (8, 128), 1)
    step = lane % 16
    level = jnp.where(step <= 8, step, lax.shift_left(jnp.full_like(step, 8), jnp.maximum(step - 8, 0)))
    edge = jnp.where(lane < 16, 1 - level, jnp.where(lane == 16, 1 << 12, level))
    rows = []
    for table in range(3):
        key_row = coord_row[table : table + 1, :]
        key_col = coord_col[:, table : table + 1]
        less[...] = jnp.where(
            jnp.broadcast_to(key_col, (LEN, LEN)) <= jnp.broadcast_to(key_row, (LEN, LEN)), 1.0, 0.0
        ).astype(BF16)
        code = key_col * LEN + lax.broadcasted_iota(jnp.int32, (LEN, 1), 0)
        for group in range(16):
            value = lax.broadcasted_iota(jnp.int32, (LEN, 128), 1) + group * 128
            best = jnp.max(
                jnp.where(jnp.broadcast_to(key_col, (LEN, 128)) < value, jnp.broadcast_to(code, (LEN, 128)), -1),
                axis=0, keepdims=True,
            )
            lut[group : group + 1, :] = jnp.where(best < 0, LEN, best & (LEN - 1))

        def find(a, carry):
            at = pl.ds(pl.multiple_of(a * 8, 8), 8)
            value = jnp.clip(coord_col[at, table : table + 1] + edge, 0, 2047)
            low, high = value & 127, value >> 7
            found = jnp.full((8, 128), LEN, jnp.int32)
            for group in range(16):
                row = jnp.broadcast_to(lut[group : group + 1, :], (8, 128))
                found = jnp.where(high == group, jnp.take_along_axis(row, low, axis=1), found)
            places[at, :] = found
            return carry

        lax.fori_loop(0, LEN // 8, find, 0)

        sums = []
        for batch in range(3):
            for h in range(4):
                prefix[h] = nn(d_scores[batch * 4 + h], less[...])

            def pick_up(a, carry):
                at = pl.ds(pl.multiple_of(a * 8, 8), 8)
                place_of = places[at, :]
                low, high = place_of & 127, place_of >> 7
                result = []
                for h in range(4):
                    value = jnp.zeros((8, 128), F32)
                    for j in range(4):
                        part = jnp.take_along_axis(prefix[h, at, j * 128 : (j + 1) * 128], low, axis=1)
                        value = jnp.where(high == j, part, value)
                    result.append(carry[h] + value)
                return tuple(result)

            sums += lax.fori_loop(
                0, LEN // 8, pick_up, tuple(jnp.zeros((8, 128), F32) for _ in range(4)), unroll=4
            )
        heads = jnp.concatenate(
            [jnp.sum(s, axis=0, keepdims=True) for s in sums] + [jnp.zeros((4, 128), F32)], axis=0
        )
        after = pltpu.roll(heads, 127, 1)
        whole = pltpu.roll(heads, 15, 1)
        lanes = lax.broadcasted_iota(jnp.int32, (16, 128), 1)
        buckets = jnp.where(lanes < 16, heads - after, after - heads)
        buckets = jnp.where(lanes == 15, heads, buckets)
        buckets = jnp.where(lanes == 16, 0.0, buckets)
        buckets = jnp.where(lanes == 31, whole - heads, buckets)
        buckets = jnp.where(lanes < 32, buckets, 0.0)
        placed = buckets if table == 0 else pltpu.roll(buckets, 32 * table, 1)
        flat_row = jnp.sum(nt(placed.astype(BF16), pick[table]) * keep[...], axis=0, keepdims=True)
        plane, at = spots["tables"]
        for i in range(3):
            row_at = at + 3 * table + i
            small[plane, row_at : row_at + 1, :] = flat_row[:, i * 128 : (i + 1) * 128]


def backward_pass(wall, cdoc, total, saved, features, coord_row, coord_col):
    pick, keep = table_constants()
    sds = jax.ShapeDtypeStruct
    return pl.pallas_call(
        backward_kernel,
        name="backward",
        out_shape=(sds((LEN, D), BF16), sds((2, ROWS, 128), BF16)),
        in_specs=[ANY] + [VMEM] * 4 + [ANY] + [VMEM] * 4 + [ANY] * 2 + [VMEM] * 7,
        out_specs=(VMEM, ANY),
        scratch_shapes=[
            pltpu.VMEM((2, ROWS, 128), BF16),
            pltpu.VMEM((2, ROWS, 128), BF16),
            pltpu.VMEM((LEN, D), F32),
            pltpu.VMEM((LEN, D), BF16),
            pltpu.VMEM((LEN, FF), BF16),
            pltpu.VMEM((LEN, FF), BF16),
            pltpu.VMEM((4, LEN, LEN), BF16),
            pltpu.VMEM((LEN, D), BF16),
            pltpu.VMEM((HEADS, LEN, LEN), BF16),
            pltpu.VMEM((LEN, LEN), BF16),
            pltpu.VMEM((4, LEN, LEN), F32),
            pltpu.VMEM((2, 64, 128), F32),
            pltpu.VMEM((16, 128), jnp.int32),
            pltpu.VMEM((LEN, 128), jnp.int32),
            pltpu.SemaphoreType.DMA((3,)),
            pltpu.SemaphoreType.DMA((1,)),
            pltpu.SemaphoreType.DMA((2,)),
        ],
        compiler_params=pltpu.CompilerParams(vmem_limit_bytes=64 * 2**20 - 2**18),
    )(wall, cdoc, total, *saved, features, coord_row, coord_col, jnp.asarray(pick), jnp.asarray(keep))


def reduce_kernel(stages, grads, pair_grad, out, pair_out, gstack, core_slots, x_slots, final, in_sem, fin_sem,
                  act_send, act_recv, c_send, c_recv, x_send, x_recv, b_send, b_recv, *rest):
    levels = len(stages)
    slots, sems = rest[:levels], rest[levels:]
    dp, fs = place()
    other = 1 - fs
    x_peer = (dp, other)
    core_peer = (dp + 1 - 2 * (dp % 2), fs)
    half = LEN // 2
    loads = [
        pltpu.make_async_copy(
            grads.at[:, pl.ds(i * CHUNK, CHUNK)], gstack.at[:, pl.ds(i * CHUNK, CHUNK)], in_sem.at[i]
        )
        for i in range(CHUNKS)
    ]
    order = [(2 * CHUNKS - 2 - i) % CHUNKS for i in range(CHUNKS)]
    for i in order:
        loads[i].start()
    greet(stages)

    sent = remote(pair_grad.at[rows_at(other * half, half)], pair_out, act_send.at[0], act_recv.at[0], x_peer)
    sent.start()

    parts = offsets(dp, stages, CHUNK)
    core_size = CHUNK // 2

    def core_copy(position, plane):
        base = order[position] * CHUNK
        return remote(
            gstack.at[plane, rows_at(base + (1 - dp % 2) * core_size, core_size)],
            core_slots.at[plane, position], c_send.at[position, plane], c_recv.at[position, plane], core_peer,
        )

    def x_copy(position):
        where = rows_at(order[position] * CHUNK + parts[0][0], core_size)
        return remote(gstack.at[other, where], x_slots.at[position], x_send.at[position], x_recv.at[position], x_peer)

    def scatter_copies(level, position):
        radix, stride = stages[level]
        start, size = parts[level]
        size = size // radix
        mine = (dp // stride) % radix
        copies = []
        for step in range(1, radix):
            target = (mine + step) % radix
            where = rows_at(order[position] * CHUNK + start + target * size, size)
            copies.append(
                remote(
                    gstack.at[fs, where], slots[level].at[position, step - 1],
                    sems[4 * level].at[position, step - 1], sems[4 * level + 1].at[position, step - 1],
                    (member(dp, radix, stride, target), fs),
                )
            )
        return copies

    def spread_copies(level, position, receive):
        radix, stride = stages[level]
        start, size = parts[level + 1]
        mine = (dp // stride) % radix
        copies = []
        for step in range(1, radix):
            shift = ((mine - step + radix) % radix - mine) * size if receive else 0
            where = final.at[rows_at(order[position] * CHUNK + start + shift, size)]
            copies.append(
                remote(
                    where, where, sems[4 * level + 2].at[position, step - 1], sems[4 * level + 3].at[position, step - 1],
                    (member(dp, radix, stride, (mine + step) % radix), fs),
                )
            )
        return copies

    def back_copy(position, receive):
        start = (1 - dp % 2 if receive else dp % 2) * core_size
        where = final.at[rows_at(order[position] * CHUNK + start, core_size)]
        return remote(where, where, b_send.at[position], b_recv.at[position], core_peer)

    def write_copy(position):
        where = pl.ds(order[position] * CHUNK, CHUNK)
        return pltpu.make_async_copy(final.at[where], out.at[where], fin_sem.at[position])

    def add_rows(plane, start, size, terms, target=None):
        where = rows_at(start, size)
        value = gstack[plane, where, :].astype(F32)
        for term in terms:
            value = value + term.astype(F32)
        if target is None:
            gstack[plane, where, :] = value.astype(BF16)
        else:
            target[where, :] = value.astype(BF16)

    def step_of(position, stage):
        base = order[position] * CHUNK
        if stage == 0:
            loads[order[position]].wait()
            for plane in range(2):
                core_copy(position, plane).start()
        elif stage == 1:
            for plane in range(2):
                core_copy(position, plane).wait_recv()
            add_rows(other, base + parts[0][0], core_size, [core_slots[other, position]])
            x_copy(position).start()
        elif stage <= levels + 2:
            level = stage - 2
            start, size = parts[level]
            if level == 0:
                x_copy(position).wait_recv()
                terms = [core_slots[fs, position], x_slots[position]]
            else:
                for copy in scatter_copies(level - 1, position):
                    copy.wait_recv()
                radix = stages[level - 1][0]
                terms = [slots[level - 1][position, i] for i in range(radix - 1)]
            if level < levels:
                add_rows(fs, base + start, size, terms)
                for copy in scatter_copies(level, position):
                    copy.start()
            else:
                add_rows(fs, base + start, size, terms, final)
                for copy in spread_copies(levels - 1, position, False):
                    copy.start()
        elif stage <= 2 * levels + 2:
            level = 2 * levels + 2 - stage
            for copy in spread_copies(level, position, True):
                copy.wait_recv()
            if level > 0:
                for copy in spread_copies(level - 1, position, False):
                    copy.start()
            else:
                back_copy(position, False).start()
        else:
            back_copy(position, True).wait_recv()
            write_copy(position).start()

    last = 2 * levels + 3
    for step in range(CHUNKS + last):
        for stage in range(last + 1):
            if 0 <= step - stage < CHUNKS:
                step_of(step - stage, stage)
    sent.wait()
    for position in range(CHUNKS):
        write_copy(position).wait()
        back_copy(position, False).wait_send()
        x_copy(position).wait_send()
        for plane in range(2):
            core_copy(position, plane).wait_send()
        for level in range(levels):
            for copy in scatter_copies(level, position) + spread_copies(level, position, False):
                copy.wait_send()


def reduce_grads(stages, grads, pair_grad):
    slots, sems = [], []
    size = CHUNK // 2
    for radix, _ in stages:
        size = size // radix
        slots.append(pltpu.VMEM((CHUNKS, radix - 1, size, 128), BF16))
        sems += [pltpu.SemaphoreType.DMA((CHUNKS, radix - 1))] * 4
    dma = pltpu.SemaphoreType.DMA
    return pl.pallas_call(
        functools.partial(reduce_kernel, stages),
        name="reduce_grads",
        out_shape=(jax.ShapeDtypeStruct((ROWS, 128), BF16), jax.ShapeDtypeStruct((LEN // 2, D), BF16)),
        in_specs=[ANY, VMEM],
        out_specs=(ANY, VMEM),
        scratch_shapes=[
            pltpu.VMEM((2, ROWS, 128), BF16),
            pltpu.VMEM((2, CHUNKS, CHUNK // 2, 128), BF16),
            pltpu.VMEM((CHUNKS, CHUNK // 2, 128), BF16),
            pltpu.VMEM((ROWS, 128), BF16),
            dma((CHUNKS,)), dma((CHUNKS,)), dma((1,)), dma((1,)),
            dma((CHUNKS, 2)), dma((CHUNKS, 2)), dma((CHUNKS,)), dma((CHUNKS,)), dma((CHUNKS,)), dma((CHUNKS,)),
        ]
        + slots
        + sems,
        compiler_params=pltpu.CompilerParams(
            collective_id=2, has_side_effects=True, vmem_limit_bytes=60 * 2**20
        ),
    )(grads, pair_grad)


BLOCK = 1760


def flatten_rows(plane, source, flat):
    def block(src, dst, count, stride):
        flat[pl.ds(LEAD + dst, count, stride=stride), :] = source[pl.ds(src, count), :].astype(F32)

    if plane == 0:
        for c in range(24):
            block(UP0 + c * UP_A, F_UP + c, UP_A, 24)
        for pos in range(18):
            block(pos * D, (pos % 3) * 6 + pos // 3, D, 18)
        for c in range(6):
            block(OUT0 + c * D, F_OUT + c, D, 6)
        small = source[pl.ds(SM0, 64), :].astype(F32)
        flat[pl.ds(LEAD + 13824, 12), :] = small[0:12]
        flat[pl.ds(LEAD + 18444, 18), :] = small[12:30]
    else:
        for c in range(24):
            block(UP1 + c * UP_B, c - 98, UP_B, 24)
        for c in range(6):
            block(DOWN1 + c * FF, F_DOWN1 + c, FF, 6)
        for c in range(6):
            block(LAY1 + c * FEAT, F_LAY1 + c, FEAT, 6)
        small = source[pl.ds(SM1, 64), :].astype(F32)
        flat[pl.ds(LEAD + F_UPB1, 24), :] = small[0:24]
        flat[pl.ds(LEAD + F_SM1, 18), :] = small[24:42]
        flat[pl.ds(LEAD + F_TAB1, 9), :] = small[42:51]
        rest = FLAT - F_TAB1 - 9
        flat[pl.ds(LEAD + F_TAB1 + 9, rest), :] = jnp.zeros((rest, 128), F32)


def adam_kernel(source, weights, first, second, grad_out, update_out, first_out, square, flat):
    step = pl.program_id(0)
    fs = lax.axis_index("fsdp")

    @pl.when(step == 0)
    def _():
        square[...] = jnp.zeros_like(square)

        @pl.when(fs == 0)
        def _():
            flatten_rows(0, source, flat)

        @pl.when(fs == 1)
        def _():
            flatten_rows(1, source, flat)

    part = 160
    row = lax.broadcasted_iota(jnp.int32, (part, 128), 0)

    def some(i, carry):
        at = pl.ds(pl.multiple_of(i * part, 8), part)
        begin = pl.multiple_of(step * BLOCK + i * part, 8)
        grad = flat[pl.ds(LEAD + begin, part), :]
        grad_out[at, :] = grad
        new_first = adam_one * first[at, :] + (1.0 - adam_one) * grad
        new_second = adam_two * second[at, :] + (1.0 - adam_two) * grad * grad
        corrected = (
            new_first
            / (1.0 - adam_one**adam_steps)
            / (jnp.sqrt(new_second / (1.0 - adam_two**adam_steps)) + adam_eps)
        )
        rate = jnp.where((fs == 1) & (row + begin >= F_LAY1), table_factor, 1.0)
        update_out[at, :] = rate * (corrected + decay_rate * weights[at, :])
        first_out[at, :] = new_first
        squares = grad * grad
        return carry + jnp.sum(squares.reshape(part // 8, 8, 128), axis=0)

    square[...] += lax.fori_loop(0, BLOCK // part, some, jnp.zeros((8, 128), F32))


def adam(source, weights, first, second):
    block = pl.BlockSpec((BLOCK, 128), lambda i: (i, 0))
    vector = jax.ShapeDtypeStruct((FLAT, 128), F32)
    return pl.pallas_call(
        adam_kernel,
        name="adamw",
        grid=(FLAT // BLOCK,),
        out_shape=(vector, vector, vector, jax.ShapeDtypeStruct((8, 128), F32)),
        in_specs=[VMEM, block, block, block],
        out_specs=(block, block, block, pl.BlockSpec((8, 128), lambda i: (0, 0))),
        scratch_shapes=[pltpu.VMEM((LEAD + FLAT + 288, 128), F32)],
        compiler_params=pltpu.CompilerParams(vmem_limit_bytes=60 * 2**20),
    )(source, weights, first, second)


def layout_features(coords):
    freq_count = FEAT // 8
    factors = (jnp.arange(freq_count, dtype=jnp.int32) + 1) ** 2
    phases = coords[..., :, None] * factors % 4096
    angles = phases.astype(F32) * (2.0 * math.pi / 4096.0)
    wave_parts = jnp.concatenate([jnp.sin(angles), jnp.cos(angles)], axis=-1)
    return wave_parts.reshape(coords.shape[:-1] + (FEAT,))


def local(stages, inputs, box_coords, mlm_mask, cotangent, params, first_moment, second_moment):
    fs = lax.axis_index("fsdp")
    half = LEN // 2
    masked = cotangent * mlm_mask.astype(BF16)[..., None]
    count = jnp.full((8, 128), jnp.sum(mlm_mask.astype(F32)))
    boxes = lax.dynamic_index_in_dim(box_coords, fs, 0, keepdims=False)
    features = layout_features(boxes).astype(BF16)
    coord_col = jnp.stack(
        [jnp.arange(LEN, dtype=jnp.int32), boxes[:, 0] + boxes[:, 2], boxes[:, 1] + boxes[:, 3]], axis=1
    )
    coord_row = coord_col.T
    flat = [v.reshape(FLAT, 128) for v in (params, first_moment, second_moment)]
    wall, xdoc, cdoc, total = gather_weights(stages, flat[0], inputs, masked, count)
    out_doc, *saved = forward_pass(wall, xdoc, features, coord_row, coord_col)
    grad_doc, grads = backward_pass(wall, cdoc, total, saved, features, coord_row, coord_col)
    reduced, grad_other = reduce_grads(stages, grads, grad_doc)
    out_other = lax.ppermute(
        lax.dynamic_slice_in_dim(out_doc, (1 - fs) * half, half, 0), "fsdp", [(0, 1), (1, 0)]
    )

    def owned(doc, moved):
        mine = lax.dynamic_slice_in_dim(doc, fs * half, half, 0)
        return jnp.where(fs == 0, jnp.stack([mine, moved]), jnp.stack([moved, mine]))

    grad, update, new_first, square = adam(reduced, *flat)
    norm = jnp.sqrt(lax.psum(jnp.sum(square), "fsdp"))
    return (
        owned(out_doc, out_other),
        owned(grad_doc, grad_other),
        grad.reshape(-1),
        norm,
        update.reshape(-1),
        new_first.reshape(-1),
    )


def solution(mesh):
    in_specs = (
        P("dp", "fsdp", None),
        P("dp", None, None),
        P("dp", "fsdp"),
        P("dp", "fsdp", None),
        P("fsdp"),
        P("fsdp"),
        P("fsdp"),
    )
    out_specs = (P("dp", "fsdp", None), P("dp", "fsdp", None), P("fsdp"), P(), P("fsdp"), P("fsdp"))
    stages = radices(mesh.shape["dp"])
    return jax.shard_map(
        functools.partial(local, stages), mesh=mesh, in_specs=in_specs, out_specs=out_specs, check_vma=False
    )
```

```python
import functools
import math

import jax
import jax.numpy as jnp
import numpy as np
from jax import lax
from jax.experimental import pallas as pl
from jax.experimental.pallas import tpu as pltpu
from jax.sharding import PartitionSpec as P

D = 768
HEADS = 12
HDIM = 64
FF = 3072
BUCKETS = 32
FEAT = 128
LEN = 512
PADDED = 7208960
SHARD = PADDED // 2
FLAT = SHARD // 128
PAIRS = HEADS // 2
QROWS = 128

norm_eps = 1e-05
adam_one = 0.9
adam_two = 0.999
adam_eps = 1e-08
adam_steps = 100.0
decay_rate = 0.01
table_factor = 5.0

MESH = pl.DeviceIdType.MESH
F32 = jnp.float32
BF16 = jnp.bfloat16
VMEM = pl.BlockSpec(memory_space=pltpu.VMEM)
ANY = pl.BlockSpec(memory_space=pl.ANY)

ROWS = 28672
CHUNK = 2048
CHUNKS = ROWS // CHUNK
CUT = 404
UP_A, UP_B = 416, 368
OUT0 = 18 * D
UP0 = OUT0 + 6 * D
SM0 = UP0 + 24 * UP_A
UP1 = 0
DOWN1 = 24 * UP_B
DOWN_END = DOWN1 + 6 * FF
LAY1 = 27648
SM1 = LAY1 + 6 * FEAT
F_OUT = 13836
F_UP = 18462
F_UPB1 = 8734
F_DOWN1 = 8758
F_SM1 = 27190
F_LAY1 = 27208
F_TAB1 = 27976
LEAD = 104


def nt(a, b):
    return lax.dot_general(a, b, (((1,), (1,)), ((), ())), preferred_element_type=F32)


def nn(a, b):
    return lax.dot_general(a, b, (((1,), (0,)), ((), ())), preferred_element_type=F32)


def tn(a, b):
    return lax.dot_general(a, b, (((0,), (0,)), ((), ())), preferred_element_type=F32)


def radices(replicas):
    stages, stride, left = [], 2, replicas // 2
    if left % 2 == 0:
        stages.append((2, stride))
        stride, left = stride * 2, left // 2
    while left > 1:
        radix = left if left <= 8 else 4
        stages.append((radix, stride))
        stride, left = stride * radix, left // radix
    return stages


def place():
    return lax.axis_index("dp"), lax.axis_index("fsdp")


def member(dp, radix, stride, digit):
    return dp + (digit - (dp // stride) % radix) * stride


def peers(stages):
    dp, fs = place()
    found = [(dp + 1 - 2 * (dp % 2), fs), (dp, 1 - fs)]
    for radix, stride in stages:
        mine = (dp // stride) % radix
        for step in range(1, radix):
            found.append((member(dp, radix, stride, (mine + step) % radix), fs))
    return found


def greet(stages):
    barrier = pltpu.get_barrier_semaphore()
    all_peers = peers(stages)
    for peer in all_peers:
        pl.semaphore_signal(barrier, inc=1, device_id=peer, device_id_type=MESH)
    pl.semaphore_wait(barrier, len(all_peers))


def remote(src, dst, send, recv, peer):
    return pltpu.make_async_remote_copy(
        src_ref=src, dst_ref=dst, send_sem=send, recv_sem=recv, device_id=peer, device_id_type=MESH
    )


def rows_at(start, size):
    return pl.ds(pl.multiple_of(start, 16), size)


def offsets(dp, stages, extent):
    size = extent // 2
    start = (dp % 2) * size
    found = [(start, size)]
    for radix, stride in stages:
        size = size // radix
        start = start + ((dp // stride) % radix) * size
        found.append((start, size))
    return found


def row_of(ref_rows, start, count):
    return jnp.concatenate([ref_rows[start + i : start + i + 1, :] for i in range(count)], axis=1)


def relayout_tasks(plane, flat, out):
    tasks = []

    def block(dst, src, count, stride):
        def run():
            out[plane, pl.ds(dst, count), :] = flat[pl.ds(LEAD + src, count, stride=stride), :].astype(BF16)

        tasks.append((dst + count, run))

    def window(dst, src, count):
        def run():
            out[plane, pl.ds(dst, count), :] = flat[pl.ds(LEAD + src, count), :].astype(BF16)

        tasks.append((dst + count, run))

    def clear(low, high):
        def run():
            out[plane, pl.ds(low, high - low), :] = jnp.zeros((high - low, 128), BF16)

        tasks.append((high, run))

    if plane == 0:
        for pos in range(18):
            block(pos * D, (pos % 3) * 6 + pos // 3, D, 18)
        for c in range(6):
            block(OUT0 + c * D, F_OUT + c, D, 6)
        for c in range(24):
            block(UP0 + c * UP_A, F_UP + c, UP_A, 24)
        window(SM0, 13824, 16)
        window(SM0 + 16, 18440, 32)
        used = SM0 + 48
    else:
        for c in range(24):
            block(UP1 + c * UP_B, c - 98, UP_B, 24)
        for j in range(12):
            for c in range(6):
                block(DOWN1 + j * 1536 + c * 256, F_DOWN1 + j * 1536 + c, 256, 6)
        clear(DOWN_END, LAY1)
        for c in range(6):
            block(LAY1 + c * FEAT, F_LAY1 + c, FEAT, 6)
        window(SM1, 8728, 32)
        window(SM1 + 32, 27184, 32)
        window(SM1 + 64, 27976, 16)
        used = SM1 + 80

    clear(used, ROWS)
    return tasks


def direct_type(position):
    return position % 4 == 1


def gather_kernel(
    stages, p_hbm, xin, cot, cnt, wall, xdoc, cdoc, total,
    flat, zall, xs, cs, cnt_slots, in_sem, x_send, x_recv, c_send, c_recv, act_send, act_recv,
    n_send, n_recv, out_sem, *stage_sems,
):
    dp, fs = place()
    other = 1 - fs
    pieces = 8
    span = FLAT // pieces
    loads = [
        pltpu.make_async_copy(
            p_hbm.at[pl.ds(i * span, span)], flat.at[pl.ds(LEAD + i * span, span)], in_sem.at[i]
        )
        for i in range(pieces)
    ]
    for load in loads:
        load.start()
    flat[pl.ds(0, LEAD), :] = jnp.zeros((LEAD, 128), F32)
    flat[pl.ds(LEAD + FLAT, 288), :] = jnp.zeros((288, 128), F32)
    greet(stages)
    x_peer = (dp, other)
    core_peer = (dp + 1 - 2 * (dp % 2), fs)
    half = LEN // 2

    def act_copies(send):
        where = rows_at((fs if send else other) * half, half)
        return [
            remote(xin.at[other], xs.at[where], act_send.at[0], act_recv.at[0], x_peer),
            remote(cot.at[other], cs.at[where], act_send.at[1], act_recv.at[1], x_peer),
        ]

    for copy in act_copies(True):
        copy.start()
    for load in loads:
        load.wait()

    order = [(CHUNKS - 1 + i) % CHUNKS for i in range(CHUNKS)]
    parts = offsets(dp, stages, CHUNK)

    def x_copy(position, plane):
        start, size = parts[0] if direct_type(position) else parts[-1]
        where = zall.at[plane, rows_at(order[position] * CHUNK + start, size)]
        return remote(where, where, x_send.at[position], x_recv.at[position], x_peer)

    def stage_copies(level, position, receive):
        radix, stride = stages[level]
        start, size = parts[level + 1]
        mine = (dp // stride) % radix
        send_sem, recv_sem = stage_sems[2 * level], stage_sems[2 * level + 1]
        copies = []
        for step in range(1, radix):
            peer = (member(dp, radix, stride, (mine + step) % radix), fs)
            shift = ((mine - step + radix) % radix - mine) * size if receive else 0
            where = zall.at[other, rows_at(order[position] * CHUNK + start + shift, size)]
            copies.append(
                remote(where, where, send_sem.at[position, step - 1], recv_sem.at[position, step - 1], peer)
            )
        return copies

    def core_copy(position, receive):
        size = CHUNK // 2
        start = (1 - dp % 2 if receive else dp % 2) * size
        where = zall.at[other, rows_at(order[position] * CHUNK + start, size)]
        return remote(where, where, c_send.at[position], c_recv.at[position], core_peer)

    levels = len(stages)

    def advance(position, stage):
        if direct_type(position):
            if stage == 0:
                x_copy(position, other).wait_recv()
                core_copy(position, False).start()
            return
        if stage == 0:
            x_copy(position, other).wait_recv()
        else:
            for copy in stage_copies(levels - stage, position, True):
                copy.wait_recv()
        if stage < levels:
            for copy in stage_copies(levels - 1 - stage, position, False):
                copy.start()
        else:
            core_copy(position, False).start()

    rounds = [[core_peer], [x_peer]] + [
        [
            (member(dp, radix, stride, ((dp // stride) % radix + step) % radix), fs)
            for step in range(1, radix)
        ]
        for radix, stride in stages
    ]

    def count_copies(number):
        base = sum(len(r) for r in rounds[:number])
        return [
            remote(total.at[...], cnt_slots.at[base + i], n_send.at[base + i], n_recv.at[base + i], peer)
            for i, peer in enumerate(rounds[number])
        ]

    def count_round(number):
        if number > 0:
            for copy in count_copies(number - 1):
                copy.wait()
            base = sum(len(r) for r in rounds[: number - 1])
            gathered = total[...]
            for i in range(len(rounds[number - 1])):
                gathered = gathered + cnt_slots[base + i]
            total[...] = gathered
        if number < len(rounds):
            for copy in count_copies(number):
                copy.start()

    total[...] = cnt[...]
    count_round(0)

    tasks = [relayout_tasks(0, flat, zall), relayout_tasks(1, flat, zall)]
    done = [set(), set()]
    for position in range(CHUNKS + levels + 1):
        if position < CHUNKS:
            low, high = order[position] * CHUNK, (order[position] + 1) * CHUNK
            for plane in range(2):
                run, start = [], 0
                for number, (end, task) in enumerate(tasks[plane]):
                    if start < high and end > low and number not in done[plane]:
                        done[plane].add(number)
                        run.append(task)
                    start = end

                @pl.when(fs == plane)
                def _(run=run):
                    for task in run:
                        task()

            x_copy(position, fs).start()
        for stage in range(levels + 1):
            if 0 <= position - 1 - stage < CHUNKS:
                advance(position - 1 - stage, stage)
        if 2 <= position and (position - 2) % 2 == 0 and (position - 2) // 2 + 1 <= len(rounds):
            count_round((position - 2) // 2 + 1)
    xdoc[pl.ds(fs * half, half), :] = xin[fs]
    cdoc[pl.ds(fs * half, half), :] = cot[fs]
    outs = [
        pltpu.make_async_copy(zall.at[fs], wall.at[fs], out_sem.at[0]),
    ]
    outs[0].start()
    for copy in act_copies(False):
        copy.wait_recv()
    xdoc[pl.ds(other * half, half), :] = xs[pl.ds(other * half, half), :]
    cdoc[pl.ds(other * half, half), :] = cs[pl.ds(other * half, half), :]
    for copy in act_copies(True):
        copy.wait_send()
    for position in range(CHUNKS):
        core_copy(position, True).wait_recv()
        core_copy(position, False).wait_send()
        x_copy(position, fs).wait_send()
        if not direct_type(position):
            for level in range(levels):
                for copy in stage_copies(level, position, False):
                    copy.wait_send()
    outs.append(pltpu.make_async_copy(zall.at[other], wall.at[other], out_sem.at[1]))
    outs[1].start()
    for copy in outs:
        copy.wait()


def gather_weights(stages, p2, xin, cot, cnt):
    count_peers = 2 + sum(radix - 1 for radix, _ in stages)
    sems = []
    for radix, _ in stages:
        sems += [pltpu.SemaphoreType.DMA((CHUNKS, radix - 1))] * 2
    half = LEN // 2
    return pl.pallas_call(
        functools.partial(gather_kernel, stages),
        name="gather_weights",
        out_shape=(
            jax.ShapeDtypeStruct((2, ROWS, 128), BF16),
            jax.ShapeDtypeStruct((LEN, D), BF16),
            jax.ShapeDtypeStruct((LEN, D), BF16),
            jax.ShapeDtypeStruct((8, 128), F32),
        ),
        in_specs=[ANY, VMEM, VMEM, VMEM],
        out_specs=(ANY, VMEM, VMEM, VMEM),
        scratch_shapes=[
            pltpu.VMEM((LEAD + FLAT + 288, 128), F32),
            pltpu.VMEM((2, ROWS, 128), BF16),
            pltpu.VMEM((LEN, D), BF16),
            pltpu.VMEM((LEN, D), BF16),
            pltpu.VMEM((count_peers, 8, 128), F32),
            pltpu.SemaphoreType.DMA((8,)),
            pltpu.SemaphoreType.DMA((CHUNKS,)),
            pltpu.SemaphoreType.DMA((CHUNKS,)),
            pltpu.SemaphoreType.DMA((CHUNKS,)),
            pltpu.SemaphoreType.DMA((CHUNKS,)),
            pltpu.SemaphoreType.DMA((2,)),
            pltpu.SemaphoreType.DMA((2,)),
            pltpu.SemaphoreType.DMA((count_peers,)),
            pltpu.SemaphoreType.DMA((count_peers,)),
            pltpu.SemaphoreType.DMA((2,)),
        ]
        + sems,
        compiler_params=pltpu.CompilerParams(
            collective_id=1, has_side_effects=True, vmem_limit_bytes=60 * 2**20
        ),
    )(p2, xin, cot, cnt)


def table_constants():
    width = BUCKETS * HEADS
    lane = np.arange(width)
    pick = np.zeros((3, width, 128), np.float32)
    for table in range(3):
        pick[table, lane, 32 * table + lane // HEADS] = 1.0
    keep = (lane[None, :] % HEADS == np.arange(16)[:, None]).astype(np.float32)
    return pick.astype(jnp.bfloat16), keep


def bucket_of(offset):
    spread = jnp.abs(offset)
    result = jnp.minimum(spread, 8) + jnp.where(offset > 0, 16, 0)
    for level in range(9, 16):
        result = result + jnp.where(spread >= 8 * 2 ** (level - 8), 1, 0)
    return result


def up_block(wall, j):
    columns = []
    for c in (2 * j, 2 * j + 1):
        first = wall[0, rows_at(UP0 + c * UP_A, UP_A), :]
        second = wall[1, rows_at(UP1 + c * UP_B + 16, UP_B - 16), :]
        columns.append(jnp.concatenate([first, second], axis=0))
    return jnp.concatenate(columns, axis=1)


def down_rows(wall, j):
    return jnp.concatenate(
        [wall[1, rows_at(DOWN1 + j * 1536 + c * 256, 256), :] for c in range(6)], axis=1
    )


def merge_up(wall):
    row = lax.broadcasted_iota(jnp.int32, (16, 128), 0)

    def one(c, carry):
        low_at = rows_at(UP0 + c * UP_A + UP_A - 16, 16)
        low = wall[0, low_at, :].astype(F32)
        high = wall[1, rows_at(UP1 + c * UP_B, 16), :].astype(F32)
        cut = jnp.where(c < 2, CUT + 1 - 400, CUT - 400)
        wall[0, low_at, :] = jnp.where(row < cut, low, high).astype(BF16)
        return carry

    lax.fori_loop(0, 24, one, 0)


def stats(values):
    mean = jnp.mean(values, axis=1, keepdims=True)
    centered = values - mean
    inverse = lax.rsqrt(jnp.mean(centered * centered, axis=1, keepdims=True) + norm_eps)
    return centered * inverse, inverse


def find_places(coord_col, lut, places):
    lane = lax.broadcasted_iota(jnp.int32, (8, 128), 1)
    step = lane % 16
    level = jnp.where(step <= 8, step, lax.shift_left(jnp.full_like(step, 8), jnp.maximum(step - 8, 0)))
    edge = jnp.where(lane < 16, 1 - level, jnp.where(lane == 16, 1 << 12, level))

    def line_rows(a, carry):
        at = pl.ds(pl.multiple_of(a * 8, 8), 8)
        value = coord_col[at, 0:1] + edge
        places[0, at, :] = jnp.where(value <= 0, LEN, jnp.minimum(value, LEN) - 1)
        return carry

    lax.fori_loop(0, LEN // 8, line_rows, 0, unroll=4)
    for table in (1, 2):
        def look(a, best):
            at = pl.ds(pl.multiple_of(a * 8, 8), 8)
            near = jnp.broadcast_to(coord_col[at, table : table + 1], (8, 128))
            code = near * LEN + (lax.broadcasted_iota(jnp.int32, (8, 128), 0) + a * 8)
            return tuple(
                jnp.maximum(best[g], jnp.where(near < lane + 128 * g, code, -1)) for g in range(16)
            )

        best = lax.fori_loop(
            0, LEN // 8, look, tuple(jnp.full((8, 128), -1, jnp.int32) for _ in range(16)), unroll=2
        )
        for g in range(16):
            most = jnp.max(best[g], axis=0, keepdims=True)
            lut[g : g + 1, :] = jnp.where(most < 0, LEN, most & (LEN - 1))
        luts = [jnp.broadcast_to(lut[g : g + 1, :], (8, 128)) for g in range(16)]

        def find(a, carry):
            at = pl.ds(pl.multiple_of(a * 8, 8), 8)
            value = jnp.clip(coord_col[at, table : table + 1] + edge, 0, 2047)
            low, high = value & 127, value >> 7
            found = jnp.full((8, 128), LEN, jnp.int32)
            for g in range(16):
                found = jnp.where(high == g, jnp.take_along_axis(luts[g], low, axis=1), found)
            places[table, at, :] = found
            return carry

        lax.fori_loop(0, LEN // 8, find, 0, unroll=4)


def forward_kernel(
    wall_hbm, xdoc, features, coord_row, coord_col, pick, keep,
    layer_out, rounded, qkv, probs, mixed, normed_one, inverse_one, first_low, hidden, slope,
    normed_two, inverse_two, places, wall_out,
    wall, start, up_bias, acc, bias, indices, lut, sem,
):
    load = pltpu.make_async_copy(wall_hbm, wall, sem.at[0])
    load.start()
    load.wait()
    merge_up(wall)
    store = pltpu.make_async_copy(wall, wall_out, sem.at[0])
    store.start()
    small0 = wall[0, pl.ds(SM0, 48), :].astype(F32)
    small1 = wall[1, pl.ds(SM1, 80), :].astype(F32)
    qv_bias = row_of(small0, 0, 12)
    out_bias, gain_one, shift_one = (row_of(small0, 20 + 6 * i, 6) for i in range(3))
    down_bias, gain_two, shift_two = (row_of(small1, 38 + 6 * i, 6) for i in range(3))

    w_layout = jnp.concatenate([wall[1, pl.ds(LAY1 + c * FEAT, FEAT), :] for c in range(6)], axis=1)
    start[...] = xdoc[...].astype(F32) + nn(features[...], w_layout)
    rounded[...] = start[...].astype(BF16)

    heads_by_lane = jnp.zeros((16, 128), F32)
    for table in range(3):
        flat_row = row_of(small1, 64 + 3 * table, 3)
        spread = (jnp.broadcast_to(flat_row, (16, 384)) * keep[...]).astype(BF16)
        heads_by_lane = heads_by_lane + nn(spread, pick[table])
    rows_by_head = [jnp.broadcast_to(heads_by_lane[h : h + 1, :], (8, 128)) for h in range(HEADS)]

    def index_rows(a, carry):
        at = pl.ds(pl.multiple_of(a * 8, 8), 8)
        for table in range(3):
            near = jnp.broadcast_to(coord_col[at, table : table + 1], (8, 128))
            for j in range(4):
                far = coord_row[table : table + 1, j * 128 : (j + 1) * 128]
                indices[table, at, j * 128 : (j + 1) * 128] = (
                    bucket_of(jnp.broadcast_to(far, (8, 128)) - near) + 32 * table
                )
        return carry

    lax.fori_loop(0, LEN // 8, index_rows, 0, unroll=4)

    def bias_rows(a, carry):
        at = pl.ds(pl.multiple_of(a * 8, 8), 8)
        for j in range(4):
            lanes = pl.ds(j * 128, 128)
            sums = [None] * HEADS
            for table in range(3):
                index = indices[table, at, lanes]
                for h in range(HEADS):
                    found = jnp.take_along_axis(rows_by_head[h], index, axis=1)
                    sums[h] = found if sums[h] is None else sums[h] + found
            for h in range(HEADS):
                bias[h, at, lanes] = sums[h]
        return carry

    lax.fori_loop(0, LEN // 8, bias_rows, 0, unroll=4)
    find_places(coord_col, lut, places)

    left = lax.broadcasted_iota(jnp.int32, (LEN, 128), 1) < HDIM
    for pair in range(PAIRS):
        weight = jnp.concatenate(
            [wall[0, pl.ds((3 * pair + i) * D, D), :] for i in range(3)], axis=1
        )
        part = nn(rounded[...], weight)
        lanes = slice(pair * 128, (pair + 1) * 128)
        query = (part[:, :128] + qv_bias[:, lanes]).astype(BF16)
        qkv[3 * pair] = query * HDIM**-0.5
        qkv[3 * pair + 1] = part[:, 128:256].astype(BF16)
        value_bias = qv_bias[:, D + pair * 128 : D + (pair + 1) * 128]
        qkv[3 * pair + 2] = (part[:, 256:] + value_bias).astype(BF16)

    def attend(pair, carry):
        query, key, value = qkv[3 * pair], qkv[3 * pair + 1], qkv[3 * pair + 2]
        found = [[], []]
        for side in range(2):
            head = 2 * pair + side
            mine = left if side == 0 else jnp.logical_not(left)
            for r in range(0, LEN, QROWS):
                at = slice(r, r + QROWS)
                part = query[at]
                scores = nt(jnp.where(mine[at], part, jnp.zeros_like(part)), key) + bias[head, at, :]
                scores = jnp.exp(scores - jnp.max(scores, axis=1, keepdims=True))
                soft = (scores * (1.0 / jnp.sum(scores, axis=1, keepdims=True))).astype(BF16)
                for j in range(4):
                    probs[rows_at((4 * head + j) * LEN + r, QROWS), :] = soft[:, j * 128 : (j + 1) * 128]
                found[side].append(nn(soft, value))
        mixed[:, pl.ds(pl.multiple_of(pair * 128, 128), 128)] = jnp.where(
            left, jnp.concatenate(found[0], axis=0), jnp.concatenate(found[1], axis=0)
        ).astype(BF16)
        return carry

    lax.fori_loop(0, PAIRS, attend, 0)

    w_out = jnp.concatenate([wall[0, pl.ds(OUT0 + c * D, D), :] for c in range(6)], axis=1)

    def first_rows(r, carry):
        at = pl.ds(pl.multiple_of(r * QROWS, QROWS), QROWS)
        normed, inverse = stats(start[at, :] + nn(mixed[at, :], w_out) + out_bias)
        normed_one[at, :] = normed
        inverse_one[at, :] = inverse
        result = normed * gain_one + shift_one
        first_low[at, :] = result.astype(BF16)
        acc[at, :] = result + down_bias
        return carry

    lax.fori_loop(0, LEN // QROWS, first_rows, 0)
    for j in range(12):
        up_bias[:, j * 256 : (j + 1) * 256] = row_of(small1, 6 + 2 * j, 2)

    def feed_step(j, carry):
        lanes = pl.ds(pl.multiple_of(j * 256, 256), 256)
        up = nn(first_low[...], up_block(wall, j)) + up_bias[:, lanes]
        half_up = 0.5 + 0.5 * lax.erf(up * math.sqrt(0.5))
        bell = jnp.exp(-0.5 * up * up) * (1.0 / math.sqrt(2.0 * math.pi))
        slope[:, lanes] = (half_up + up * bell).astype(BF16)
        part = (up * half_up).astype(BF16)
        hidden[:, lanes] = part
        acc[...] += nn(part, down_rows(wall, j))
        return carry

    lax.fori_loop(0, 12, feed_step, 0)

    def second_rows(r, carry):
        at = pl.ds(pl.multiple_of(r * QROWS, QROWS), QROWS)
        normed, inverse = stats(acc[at, :])
        normed_two[at, :] = normed
        inverse_two[at, :] = inverse
        layer_out[at, :] = (normed * gain_two + shift_two).astype(BF16)
        return carry

    lax.fori_loop(0, LEN // QROWS, second_rows, 0)
    store.wait()


def forward_pass(wall, xdoc, features, coord_row, coord_col):
    pick, keep = table_constants()
    sds = jax.ShapeDtypeStruct
    return pl.pallas_call(
        forward_kernel,
        name="forward",
        out_shape=(
            sds((LEN, D), BF16),
            sds((LEN, D), BF16),
            sds((18, LEN, 128), BF16),
            sds((HEADS * 4 * LEN, 128), BF16),
            sds((LEN, D), BF16),
            sds((LEN, D), F32),
            sds((LEN, 1), F32),
            sds((LEN, D), BF16),
            sds((LEN, FF), BF16),
            sds((LEN, FF), BF16),
            sds((LEN, D), F32),
            sds((LEN, 1), F32),
            sds((3, LEN, 128), jnp.int32),
            sds((2, ROWS, 128), BF16),
        ),
        in_specs=[ANY] + [VMEM] * 6,
        out_specs=(VMEM,) * 13 + (ANY,),
        scratch_shapes=[
            pltpu.VMEM((2, ROWS, 128), BF16),
            pltpu.VMEM((LEN, D), F32),
            pltpu.VMEM((1, FF), F32),
            pltpu.VMEM((LEN, D), F32),
            pltpu.VMEM((HEADS, LEN, LEN), F32),
            pltpu.VMEM((3, LEN, LEN), jnp.int32),
            pltpu.VMEM((16, 128), jnp.int32),
            pltpu.SemaphoreType.DMA((1,)),
        ],
        compiler_params=pltpu.CompilerParams(vmem_limit_bytes=62 * 2**20),
    )(wall, xdoc, features, coord_row, coord_col, jnp.asarray(pick), jnp.asarray(keep))


G_SMALL = (("qv_bias", 0, 0, 12), ("out_bias", 0, 12, 6), ("gain_one", 0, 18, 6), ("shift_one", 0, 24, 6),
           ("up_bias", 1, 0, 24), ("down_bias", 1, 24, 6), ("gain_two", 1, 30, 6), ("shift_two", 1, 36, 6),
           ("tables", 1, 42, 9))


def spread_norm(normed, inverse, gain, grad):
    scaled = grad * gain
    return inverse * (
        scaled
        - jnp.mean(scaled, axis=1, keepdims=True)
        - normed * jnp.mean(scaled * normed, axis=1, keepdims=True)
    )


def total_rows(values):
    return jnp.sum(values.astype(F32), axis=0, keepdims=True)


def reduce_chunk(stages):
    replicas = 2
    for radix, _ in stages:
        replicas *= radix
    return max(1024, 16 * replicas)


SKEW = 2


class Reduction:
    def __init__(self, stages, gstack, out, core_slots, x_slots, pieces, slots, sems):
        self.stages, self.gstack, self.out = stages, gstack, out
        self.core_slots, self.x_slots, self.pieces, self.slots = core_slots, x_slots, pieces, slots
        (self.c_send, self.c_recv, self.x_send, self.x_recv, self.b_send, self.b_recv, self.own_sem) = sems[:7]
        self.sems = sems[7:]
        self.dp, self.fs = place()
        self.other = 1 - self.fs
        self.size = reduce_chunk(stages)
        self.count = ROWS // self.size
        self.levels = len(stages)
        self.parts = offsets(self.dp, stages, self.size)
        self.half = self.size // 2
        self.x_peer = (self.dp, self.other)
        self.core_peer = (self.dp + 1 - 2 * (self.dp % 2), self.fs)

    def base(self, position):
        return lax.rem(2 * self.count - 2 - position, self.count) * self.size

    def ready(self, row):
        return jnp.maximum(self.count - 1 - (row + self.size - 1) // self.size, 0)

    def core_copy(self, position, plane):
        where = rows_at(self.base(position) + (1 - self.dp % 2) * self.half, self.half)
        return remote(
            self.gstack.at[plane, where], self.core_slots.at[plane, position],
            self.c_send.at[plane, position], self.c_recv.at[plane, position], self.core_peer,
        )

    def x_copy(self, position):
        where = rows_at(self.base(position) + self.parts[0][0], self.half)
        return remote(
            self.gstack.at[self.other, where], self.x_slots.at[position],
            self.x_send.at[position], self.x_recv.at[position], self.x_peer,
        )

    def scatter_copies(self, level, position):
        radix, stride = self.stages[level]
        start, size = self.parts[level]
        size = size // radix
        mine = (self.dp // stride) % radix
        copies = []
        for step in range(1, radix):
            target = (mine + step) % radix
            where = rows_at(self.base(position) + start + target * size, size)
            copies.append(
                remote(
                    self.gstack.at[self.fs, where], self.slots[level].at[position, step - 1],
                    self.sems[4 * level].at[position, step - 1], self.sems[4 * level + 1].at[position, step - 1],
                    (member(self.dp, radix, stride, target), self.fs),
                )
            )
        return copies

    def spread_copies(self, level, position, receive):
        radix, stride = self.stages[level]
        start, size = self.parts[level + 1]
        mine = (self.dp // stride) % radix
        copies = []
        for step in range(1, radix):
            shift = ((mine - step + radix) % radix - mine) * size if receive else 0
            where = self.out.at[rows_at(self.base(position) + start + shift, size)]
            source = self.pieces.at[position] if level == self.levels - 1 and not receive else where
            copies.append(
                remote(
                    source, where,
                    self.sems[4 * level + 2].at[position, step - 1], self.sems[4 * level + 3].at[position, step - 1],
                    (member(self.dp, radix, stride, (mine + step) % radix), self.fs),
                )
            )
        return copies

    def own_copy(self, position):
        start, size = self.parts[-1]
        return pltpu.make_async_copy(
            self.pieces.at[position], self.out.at[rows_at(self.base(position) + start, size)],
            self.own_sem.at[position],
        )

    def back_copy(self, position, receive):
        start = (1 - self.dp % 2 if receive else self.dp % 2) * self.half
        where = self.out.at[rows_at(self.base(position) + start, self.half)]
        return remote(where, where, self.b_send.at[position], self.b_recv.at[position], self.core_peer)

    def feed(self, plane, low, high):
        def one(position, carry):
            self.core_copy(position, plane).start()
            return carry

        lax.fori_loop(low, high, one, 0)

    def push(self, low, high):
        def one(position, carry):
            self.core_copy(position, self.other).wait_recv()
            where = rows_at(self.base(position) + self.parts[0][0], self.half)
            value = self.gstack[self.other, where, :].astype(F32) + self.core_slots[self.other, position].astype(F32)
            self.gstack[self.other, where, :] = value.astype(BF16)
            self.x_copy(position).start()
            return carry

        lax.fori_loop(low, high, one, 0)

    def work(self, position, step):
        levels = self.levels
        base = self.base(position)
        if step <= levels:
            start, size = self.parts[step]
            where = rows_at(base + start, size)
            if step == 0:
                self.core_copy(position, self.fs).wait_recv()
                self.x_copy(position).wait_recv()
                terms = [self.core_slots[self.fs, position], self.x_slots[position]]
            else:
                for copy in self.scatter_copies(step - 1, position):
                    copy.wait()
                terms = [self.slots[step - 1][position, i] for i in range(self.stages[step - 1][0] - 1)]
            value = self.gstack[self.fs, where, :].astype(F32)
            for term in terms:
                value = value + term.astype(F32)
            if step < levels:
                self.gstack[self.fs, where, :] = value.astype(BF16)
                for copy in self.scatter_copies(step, position):
                    copy.start()
            else:
                self.pieces[position] = value.astype(BF16)
                self.own_copy(position).start()
                for copy in self.spread_copies(levels - 1, position, False):
                    copy.start()
        else:
            level = 2 * levels - step
            for copy in self.spread_copies(level, position, True):
                copy.wait_recv()
            for copy in self.spread_copies(level, position, False):
                copy.wait_send()
            if level == levels - 1:
                self.own_copy(position).wait()
                self.x_copy(position).wait_send()
                for plane in range(2):
                    self.core_copy(position, plane).wait_send()
            if level > 0:
                for copy in self.spread_copies(level - 1, position, False):
                    copy.start()
            else:
                self.back_copy(position, False).start()

    def tick(self, number):
        for step in range(2 * self.levels, -1, -1):
            position = number - SKEW * step

            @pl.when((position >= 0) & (position < self.count))
            def _(position=position, step=step):
                self.work(position, step)

    def ticks(self):
        return self.count + 2 * SKEW * self.levels

    def finish(self):
        def one(position, carry):
            self.back_copy(position, True).wait_recv()
            self.back_copy(position, False).wait_send()
            return carry

        lax.fori_loop(0, self.count, one, 0)


def reduction_scratch(stages):
    size = reduce_chunk(stages)
    count, half = ROWS // size, size // 2
    dma = pltpu.SemaphoreType.DMA
    slots, sems = [], []
    for radix, _ in stages:
        half = half // radix
        slots.append(pltpu.VMEM((count, radix - 1, half, 128), BF16))
        sems += [dma((count, radix - 1))] * 4
    return (
        [
            pltpu.VMEM((2, count, size // 2, 128), BF16),
            pltpu.VMEM((count, size // 2, 128), BF16),
            pltpu.VMEM((count, half, 128), BF16),
        ]
        + slots,
        [dma((2, count)), dma((2, count))] + [dma((count,))] * 5 + sems,
    )


def backward_kernel(
    stages,
    wall_hbm, cdoc_hbm, total, rounded_hbm, qkv_hbm, probs_hbm, mixed_hbm, one_hbm, inverse_one, low_hbm, hidden_hbm,
    slope_hbm, two_hbm, inverse_two, places_hbm, features, coord_row, coord_col, pick, keep,
    input_grad, reduced, norm,
    wall, gstack, acc, branch, hidden, d_up, low, rounded, qkv, mixed, normed_one, less, places, prefix, small,
    square_slots, load_sem, step_sem, probs_sem, act_send, act_recv, act_sem, n_send, n_recv, *rest,
):
    levels = len(stages)
    parts_vmem, sems = rest[: 3 + levels], rest[3 + levels :]
    red = Reduction(stages, gstack, reduced, parts_vmem[0], parts_vmem[1], parts_vmem[2], parts_vmem[3:], sems)
    dp, fs, other = red.dp, red.fs, red.other
    half = LEN // 2

    early = [
        pltpu.make_async_copy(wall_hbm.at[:, pl.ds(SM0, 256)], wall.at[:, pl.ds(SM0, 256)], load_sem.at[0]),
        pltpu.make_async_copy(cdoc_hbm, branch, load_sem.at[1]),
        pltpu.make_async_copy(two_hbm, acc, load_sem.at[2]),
    ]
    lows = [pltpu.make_async_copy(low_hbm, low, load_sem.at[3])]
    rest_loads = [
        pltpu.make_async_copy(one_hbm, normed_one, load_sem.at[4]),
        pltpu.make_async_copy(wall_hbm.at[0, pl.ds(0, UP0)], wall.at[0, pl.ds(0, UP0)], load_sem.at[5]),
        pltpu.make_async_copy(mixed_hbm, mixed, load_sem.at[6]),
        pltpu.make_async_copy(qkv_hbm, qkv, load_sem.at[7]),
        pltpu.make_async_copy(rounded_hbm, rounded, load_sem.at[8]),
        pltpu.make_async_copy(places_hbm, places, load_sem.at[9]),
    ]

    def step_loads(j):
        lanes = pl.ds(pl.multiple_of(j * 256, 256), 256)
        areas = [(1, DOWN1 + 1536 * j, 1536), (0, UP0 + 2 * UP_A * j, 2 * UP_A), (1, UP1 + 2 * UP_B * j, 2 * UP_B)]
        copies = [
            pltpu.make_async_copy(
                wall_hbm.at[plane, rows_at(start, size)], wall.at[plane, rows_at(start, size)], step_sem.at[i, j]
            )
            for i, (plane, start, size) in enumerate(areas)
        ]
        copies.append(pltpu.make_async_copy(hidden_hbm.at[:, lanes], hidden.at[:, lanes], step_sem.at[3, j]))
        copies.append(pltpu.make_async_copy(slope_hbm.at[:, lanes], d_up.at[:, lanes], step_sem.at[4, j]))
        return copies

    for load in early + lows:
        load.start()

    def start_loads(it, carry):
        for load in step_loads(11 - it):
            load.start()
        return carry

    lax.fori_loop(0, 12, start_loads, 0)
    for load in rest_loads:
        load.start()
    greet(stages)
    small[...] = jnp.zeros_like(small)
    gstack[1, pl.ds(DOWN_END, LAY1 - DOWN_END), :] = jnp.zeros((LAY1 - DOWN_END, 128), BF16)
    for load in early:
        load.wait()

    small0 = wall[0, pl.ds(SM0, 48), :].astype(F32)
    small1 = wall[1, pl.ds(SM1, 80), :].astype(F32)
    gain_one = row_of(small0, 26, 6)
    gain_two = row_of(small1, 44, 6)
    spots = {name: (plane, first_row) for name, plane, first_row, _ in G_SMALL}

    def keep_small(name, vector):
        plane, at = spots[name]
        for i in range(vector.shape[1] // 128):
            small[plane, at + i : at + i + 1, :] = vector[:, i * 128 : (i + 1) * 128]

    count = total[0:1, 0:1]
    none = jnp.zeros((1, D), F32)

    def second_rows(r, sums):
        at = pl.ds(pl.multiple_of(r * QROWS, QROWS), QROWS)
        grad_out = branch[at, :].astype(F32) / count
        normed = acc[at, :]
        result = spread_norm(normed, inverse_two[at, :], gain_two, grad_out)
        acc[at, :] = result
        lower = result.astype(BF16)
        branch[at, :] = lower
        return sums[0] + total_rows(grad_out * normed), sums[1] + total_rows(grad_out), sums[2] + total_rows(lower)

    sums = lax.fori_loop(0, LEN // QROWS, second_rows, (none, none, none))
    for name, vector in zip(("gain_two", "shift_two", "down_bias"), sums):
        keep_small(name, vector)
    plane_up, at_up = spots["up_bias"]
    lows[0].wait()

    def fed(plane, it):
        row = UP0 + 2 * UP_A * (11 - it) if plane == 0 else DOWN1 + 1536 * (11 - it)
        return red.ready(row)

    def of_other(values):
        return jnp.where(other == 0, values[0], values[1])

    fine = red.count >= 28
    tile_row = lax.broadcasted_iota(jnp.int32, (16, 128), 0)

    def feed_step(it, carry):
        j = 11 - it
        for load in step_loads(j):
            load.wait()
        for plane in range(2):
            red.feed(plane, fed(plane, it - 2), fed(plane, it - 1))
        red.push(of_other([fed(p, it - 3) for p in range(2)]), of_other([fed(p, it - 2) for p in range(2)]))
        lanes = pl.ds(pl.multiple_of(j * 256, 256), 256)
        grad = nt(branch[...], down_rows(wall, j))
        part = (grad * d_up[:, lanes].astype(F32)).astype(BF16)
        d_up[:, lanes] = part
        sums = total_rows(part)
        small[plane_up, pl.ds(at_up + 2 * j, 1), :] = sums[:, :128]
        small[plane_up, pl.ds(at_up + 2 * j + 1, 1), :] = sums[:, 128:]
        down = tn(hidden[:, lanes], branch[...]).astype(BF16)
        for c in range(6):
            gstack[1, rows_at(DOWN1 + j * 1536 + c * 256, 256), :] = down[:, c * 128 : (c + 1) * 128]
        up = tn(low[...], part)
        for i in range(2):
            c = 2 * j + i
            cut = jnp.where(c < 2, CUT + 1 - 400, CUT - 400)
            columns = up[:, i * 128 : (i + 1) * 128]
            tile = columns[400:416]
            gstack[0, rows_at(UP0 + c * UP_A, 400), :] = columns[:400].astype(BF16)
            gstack[0, rows_at(UP0 + c * UP_A + 400, 16), :] = jnp.where(tile_row < cut, tile, 0.0).astype(BF16)
            gstack[1, rows_at(UP1 + c * UP_B, 16), :] = jnp.where(tile_row < cut, 0.0, tile).astype(BF16)
            gstack[1, rows_at(UP1 + c * UP_B + 16, UP_B - 16), :] = columns[416:].astype(BF16)
        acc[...] += nt(part, up_block(wall, j))
        return carry

    lax.fori_loop(0, 12, feed_step, 0)

    def probs_copy(pair, slot):
        size = 8 * LEN
        return pltpu.make_async_copy(
            probs_hbm.at[rows_at(pair * size, size)], wall.at[0, rows_at(UP0 + slot * size, size)], probs_sem.at[slot]
        )

    probs_copy(PAIRS - 1, 0).start()
    last = red.count - 1
    red.feed(0, fed(0, 10), fed(0, 11))
    red.feed(1, fed(1, 10), last)
    red.push(of_other([fed(p, 9) for p in range(2)]), of_other([fed(p, 10) for p in range(2)]))
    for load in rest_loads:
        load.wait()

    w_out = jnp.concatenate([wall[0, pl.ds(OUT0 + c * D, D), :] for c in range(6)], axis=1)

    def first_rows(r, sums):
        at = pl.ds(pl.multiple_of(r * QROWS, QROWS), QROWS)
        grad, normed = acc[at, :], normed_one[at, :]
        result = spread_norm(normed, inverse_one[at, :], gain_one, grad)
        acc[at, :] = result
        lower = result.astype(BF16)
        branch[at, :] = lower
        low[at, :] = nt(lower, w_out).astype(BF16)
        return sums[0] + total_rows(grad * normed), sums[1] + total_rows(grad), sums[2] + total_rows(lower)

    sums = lax.fori_loop(0, LEN // QROWS, first_rows, (none, none, none))
    for name, vector in zip(("gain_one", "shift_one", "out_bias"), sums):
        keep_small(name, vector)
    red.push(of_other([fed(p, 10) for p in range(2)]), jnp.where(other == 0, fed(0, 11), last))

    def drain(number, carry):
        red.tick(number)
        return carry

    per_pair = 2 if fine else 1

    def out_step(j, carry):
        lanes = pl.ds(pl.multiple_of(j * 256, 256), 256)
        part = tn(mixed[...], branch[:, lanes]).astype(BF16)
        for i in range(2):
            gstack[0, rows_at(OUT0 + (2 * j + i) * D, D), :] = part[:, i * 128 : (i + 1) * 128]
        return carry

    lax.fori_loop(0, 3, out_step, 0)
    drain(0, 0)
    drain(1, 0)

    left = lax.broadcasted_iota(jnp.int32, (LEN, 128), 1) < HDIM

    def sent(it):
        return red.ready(jnp.where(it <= -2, UP0, 2304 * (5 - it)))

    def score_rows(head, j, start, size):
        return rows_at((4 * head + j) * LEN + start, size)

    def attend(it, carry):
        pair = PAIRS - 1 - it
        slot = lax.rem(it, 2)

        @pl.when(it + 1 < PAIRS)
        def _():
            probs_copy(pair - 1, 1 - slot).start()

        red.feed(0, sent(it - 2), sent(it - 1))

        @pl.when(other == 0)
        def _():
            red.push(sent(it - 3), sent(it - 2))

        lax.fori_loop(2 + per_pair * it, 2 + per_pair * (it + 1), drain, 0)
        probs_copy(pair, slot).wait()
        query, key, value = qkv[3 * pair], qkv[3 * pair + 1], qkv[3 * pair + 2]
        grad = low[:, pl.ds(pl.multiple_of(pair * 128, 128), 128)]
        found = []
        for side in range(2):
            head = 2 * pair + side
            mine = left if side == 0 else jnp.logical_not(left)
            base = UP0 + slot * 8 * LEN + side * 4 * LEN
            for r in range(0, LEN, QROWS):
                part = grad[r : r + QROWS]
                d_probs = nt(jnp.where(mine[r : r + QROWS], part, jnp.zeros_like(part)), value)
                soft = jnp.concatenate(
                    [wall[0, rows_at(base + j * LEN + r, QROWS), :] for j in range(4)], axis=1
                ).astype(F32)
                inner = jnp.sum(soft * d_probs, axis=1, keepdims=True)
                scores = (soft * (d_probs - inner)).astype(BF16)
                for j in range(4):
                    wall[1, score_rows(head, j, r, QROWS), :] = scores[:, j * 128 : (j + 1) * 128]
            scores = jnp.concatenate([wall[1, score_rows(head, j, 0, LEN), :] for j in range(4)], axis=1)
            chances = jnp.concatenate([wall[0, rows_at(base + j * LEN, LEN), :] for j in range(4)], axis=1)
            found.append((nn(scores, key), tn(scores, query), tn(chances, grad)))
        d_query = (jnp.where(left, found[0][0], found[1][0]) * HDIM**-0.5).astype(BF16)
        d_key = jnp.where(left, found[0][1], found[1][1]).astype(BF16)
        d_value = jnp.where(left, found[0][2], found[1][2]).astype(BF16)
        both = jnp.concatenate([d_query, d_key, d_value], axis=1)
        plane, spot = spots["qv_bias"]
        small[plane, pl.ds(spot + pair, 1), :] = total_rows(d_query)
        small[plane, pl.ds(spot + 6 + pair, 1), :] = total_rows(d_value)
        at = pl.multiple_of(3 * pair * D, 16)
        weight = jnp.concatenate([wall[0, rows_at(at + i * D, D), :] for i in range(3)], axis=1)
        acc[...] += nt(both, weight)
        part = tn(rounded[...], both).astype(BF16)
        for i in range(3):
            gstack[0, rows_at(at + i * D, D), :] = part[:, i * 128 : (i + 1) * 128]
        return carry

    lax.fori_loop(0, PAIRS, attend, 0)
    red.feed(0, sent(4), sent(5))

    @pl.when(other == 0)
    def _():
        red.push(sent(3), sent(4))

    branch[...] = acc[...].astype(BF16)
    act_out = remote(branch.at[rows_at(other * half, half)], input_grad.at[fs], act_send.at[0], act_recv.at[0], red.x_peer)
    act_in = remote(branch.at[rows_at(other * half, half)], input_grad.at[other], act_send.at[0], act_recv.at[0], red.x_peer)
    act_own = pltpu.make_async_copy(branch.at[rows_at(fs * half, half)], input_grad.at[fs], act_sem.at[0])
    act_out.start()
    act_own.start()
    layout = tn(features[...], branch[...]).astype(BF16)
    for c in range(6):
        gstack[1, pl.ds(LAY1 + c * FEAT, FEAT), :] = layout[:, c * 128 : (c + 1) * 128]

    @pl.when(other == 0)
    def _():
        red.push(sent(4), sent(5))

    late = 2 + per_pair * PAIRS
    pace = 2 if fine else 5
    table_grads(wall, coord_row, coord_col, pick, keep, less, places, prefix, small, spots, red, late, pace)
    late += (23 + pace) // pace

    for plane in range(2):
        gstack[plane, pl.ds(SM0, 64), :] = small[plane].astype(BF16)
        gstack[plane, pl.ds(SM0 + 64, ROWS - SM0 - 64), :] = jnp.zeros((ROWS - SM0 - 64, 128), BF16)
        red.feed(plane, last, last + 1)
    red.push(last, last + 1)

    summed = red.count + SKEW * levels
    lax.fori_loop(late, summed, drain, 0)

    def squares(position, carry):
        piece = red.pieces[position].astype(F32)
        return carry + jnp.sum((piece * piece).reshape(-1, 8, 128), axis=0)

    value = lax.fori_loop(0, red.count, squares, jnp.zeros((8, 128), F32))
    value = jnp.sum(jnp.sum(value, axis=0, keepdims=True), axis=1, keepdims=True)
    norm[...] = jnp.broadcast_to(value, (8, 128))
    rounds = [
        [
            (member(dp, radix, stride, ((dp // stride) % radix + step) % radix), fs)
            for step in range(1, radix)
        ]
        for radix, stride in stages
    ] + [[red.core_peer], [red.x_peer]]

    def square_copies(number):
        base = sum(len(r) for r in rounds[:number])
        return [
            remote(norm.at[...], square_slots.at[base + i], n_send.at[base + i], n_recv.at[base + i], peer)
            for i, peer in enumerate(rounds[number])
        ]

    for number in range(max(red.ticks() - summed, len(rounds)) + 1):
        if number < len(rounds):
            for copy in square_copies(number):
                copy.start()
        if summed + number < red.ticks():
            red.tick(summed + number)
        if number < len(rounds):
            gathered = norm[...]
            base = sum(len(r) for r in rounds[:number])
            for i, copy in enumerate(square_copies(number)):
                copy.wait()
                gathered = gathered + square_slots[base + i]
            norm[...] = gathered
    norm[...] = jnp.sqrt(norm[...])

    red.finish()
    act_own.wait()
    act_out.wait_send()
    act_in.wait_recv()


def table_grads(wall, coord_row, coord_col, pick, keep, less, places, prefix, small, spots, red, late, pace):
    block = 64
    for table in range(3):
        key_row = jnp.broadcast_to(coord_row[table : table + 1, :], (16, LEN))

        def less_rows(a, carry):
            at = pl.ds(pl.multiple_of(a * 16, 16), 16)
            near = jnp.broadcast_to(coord_col[at, table : table + 1], (16, LEN))
            less[at, :] = jnp.where(near <= key_row, 1.0, 0.0).astype(BF16)
            return carry

        lax.fori_loop(0, LEN // 16, less_rows, 0, unroll=4)

        def query_rows(b, sums):
            @pl.when(lax.rem(table * 8 + b, pace) == 0)
            def _():
                red.tick(late + (table * 8 + b) // pace)

            start = b * block
            scores = jnp.concatenate(
                [
                    jnp.concatenate(
                        [wall[1, rows_at((4 * h + j) * LEN + start, block), :] for j in range(4)], axis=1
                    )
                    for h in range(HEADS)
                ],
                axis=0,
            )
            prefix[...] = nn(scores, less[...]).reshape(HEADS, block, LEN)

            def pick_up(a, carry):
                at = pl.ds(pl.multiple_of(a * 8, 8), 8)
                place_of = places[table, pl.ds(pl.multiple_of(start + a * 8, 8), 8), :]
                low, high = place_of & 127, place_of >> 7
                result = []
                for h in range(HEADS):
                    value = jnp.zeros((8, 128), F32)
                    for j in range(4):
                        part = jnp.take_along_axis(prefix[h, at, j * 128 : (j + 1) * 128], low, axis=1)
                        value = jnp.where(high == j, part, value)
                    result.append(carry[h] + value)
                return tuple(result)

            return lax.fori_loop(0, block // 8, pick_up, sums, unroll=4)

        sums = lax.fori_loop(
            0, LEN // block, query_rows, tuple(jnp.zeros((8, 128), F32) for _ in range(HEADS))
        )
        heads = jnp.concatenate(
            [jnp.sum(s, axis=0, keepdims=True) for s in sums] + [jnp.zeros((4, 128), F32)], axis=0
        )
        after = pltpu.roll(heads, 127, 1)
        whole = pltpu.roll(heads, 15, 1)
        lanes = lax.broadcasted_iota(jnp.int32, (16, 128), 1)
        buckets = jnp.where(lanes < 16, heads - after, after - heads)
        buckets = jnp.where(lanes == 15, heads, buckets)
        buckets = jnp.where(lanes == 16, 0.0, buckets)
        buckets = jnp.where(lanes == 31, whole - heads, buckets)
        buckets = jnp.where(lanes < 32, buckets, 0.0)
        placed = buckets if table == 0 else pltpu.roll(buckets, 32 * table, 1)
        flat_row = jnp.sum(nt(placed.astype(BF16), pick[table]) * keep[...], axis=0, keepdims=True)
        plane, at = spots["tables"]
        for i in range(3):
            row_at = at + 3 * table + i
            small[plane, row_at : row_at + 1, :] = flat_row[:, i * 128 : (i + 1) * 128]


def backward_pass(stages, wall, cdoc, total, saved, features, coord_row, coord_col):
    pick, keep = table_constants()
    sds = jax.ShapeDtypeStruct
    count_peers = 2 + sum(radix - 1 for radix, _ in stages)
    dma = pltpu.SemaphoreType.DMA
    buffers, sems = reduction_scratch(stages)
    return pl.pallas_call(
        functools.partial(backward_kernel, stages),
        name="backward_reduce",
        out_shape=(sds((2, LEN // 2, D), BF16), sds((ROWS, 128), BF16), sds((8, 128), F32)),
        in_specs=[ANY, ANY, VMEM, ANY, ANY, ANY, ANY, ANY, VMEM, ANY, ANY, ANY, ANY, VMEM, ANY] + [VMEM] * 5,
        out_specs=(ANY, ANY, VMEM),
        scratch_shapes=[
            pltpu.VMEM((2, ROWS, 128), BF16),
            pltpu.VMEM((2, ROWS, 128), BF16),
            pltpu.VMEM((LEN, D), F32),
            pltpu.VMEM((LEN, D), BF16),
            pltpu.VMEM((LEN, FF), BF16),
            pltpu.VMEM((LEN, FF), BF16),
            pltpu.VMEM((LEN, D), BF16),
            pltpu.VMEM((LEN, D), BF16),
            pltpu.VMEM((18, LEN, 128), BF16),
            pltpu.VMEM((LEN, D), BF16),
            pltpu.VMEM((LEN, D), F32),
            pltpu.VMEM((LEN, LEN), BF16),
            pltpu.VMEM((3, LEN, 128), jnp.int32),
            pltpu.VMEM((HEADS, 64, LEN), F32),
            pltpu.VMEM((2, 64, 128), F32),
            pltpu.VMEM((count_peers, 8, 128), F32),
            dma((10,)), dma((5, 12)), dma((2,)), dma((1,)), dma((1,)), dma((1,)), dma((count_peers,)), dma((count_peers,)),
        ]
        + buffers
        + sems,
        compiler_params=pltpu.CompilerParams(
            collective_id=2, has_side_effects=True, vmem_limit_bytes=64 * 2**20 - 2**16
        ),
    )(wall, cdoc, total, *saved, features, coord_row, coord_col, jnp.asarray(pick), jnp.asarray(keep))


BLOCK = 1760


def flatten_rows(plane, source, flat):
    def block(src, dst, count, stride):
        flat[pl.ds(LEAD + dst, count, stride=stride), :] = source[pl.ds(src, count), :].astype(F32)

    if plane == 0:
        for c in range(24):
            block(UP0 + c * UP_A, F_UP + c, UP_A, 24)
        for pos in range(18):
            block(pos * D, (pos % 3) * 6 + pos // 3, D, 18)
        for c in range(6):
            block(OUT0 + c * D, F_OUT + c, D, 6)
        small = source[pl.ds(SM0, 64), :].astype(F32)
        flat[pl.ds(LEAD + 13824, 12), :] = small[0:12]
        flat[pl.ds(LEAD + 18444, 18), :] = small[12:30]
    else:
        for c in range(24):
            block(UP1 + c * UP_B, c - 98, UP_B, 24)
        for j in range(12):
            for c in range(6):
                block(DOWN1 + j * 1536 + c * 256, F_DOWN1 + j * 1536 + c, 256, 6)
        for c in range(6):
            block(LAY1 + c * FEAT, F_LAY1 + c, FEAT, 6)
        small = source[pl.ds(SM1, 64), :].astype(F32)
        flat[pl.ds(LEAD + F_UPB1, 24), :] = small[0:24]
        flat[pl.ds(LEAD + F_SM1, 18), :] = small[24:42]
        flat[pl.ds(LEAD + F_TAB1, 9), :] = small[42:51]
        rest = FLAT - F_TAB1 - 9
        flat[pl.ds(LEAD + F_TAB1 + 9, rest), :] = jnp.zeros((rest, 128), F32)


def adam_kernel(source, weights, first, second, grad_out, update_out, first_out, flat):
    step = pl.program_id(0)
    fs = lax.axis_index("fsdp")

    @pl.when(step == 0)
    def _():
        @pl.when(fs == 0)
        def _():
            flatten_rows(0, source, flat)

        @pl.when(fs == 1)
        def _():
            flatten_rows(1, source, flat)

    part = 160
    row = lax.broadcasted_iota(jnp.int32, (part, 128), 0)

    def some(i, carry):
        at = pl.ds(pl.multiple_of(i * part, 8), part)
        begin = pl.multiple_of(step * BLOCK + i * part, 8)
        grad = flat[pl.ds(LEAD + begin, part), :]
        grad_out[at, :] = grad
        new_first = adam_one * first[at, :] + (1.0 - adam_one) * grad
        new_second = adam_two * second[at, :] + (1.0 - adam_two) * grad * grad
        corrected = (
            new_first
            / (1.0 - adam_one**adam_steps)
            / (jnp.sqrt(new_second / (1.0 - adam_two**adam_steps)) + adam_eps)
        )
        rate = jnp.where((fs == 1) & (row + begin >= F_LAY1), table_factor, 1.0)
        update_out[at, :] = rate * (corrected + decay_rate * weights[at, :])
        first_out[at, :] = new_first
        return carry

    lax.fori_loop(0, BLOCK // part, some, 0)


def adam(source, weights, first, second):
    block = pl.BlockSpec((BLOCK, 128), lambda i: (i, 0))
    vector = jax.ShapeDtypeStruct((FLAT, 128), F32)
    return pl.pallas_call(
        adam_kernel,
        name="adamw",
        grid=(FLAT // BLOCK,),
        out_shape=(vector, vector, vector),
        in_specs=[VMEM, block, block, block],
        out_specs=(block, block, block),
        scratch_shapes=[pltpu.VMEM((LEAD + FLAT + 288, 128), F32)],
        compiler_params=pltpu.CompilerParams(vmem_limit_bytes=60 * 2**20),
    )(source, weights, first, second)


def layout_features(coords):
    freq_count = FEAT // 8
    factors = (jnp.arange(freq_count, dtype=jnp.int32) + 1) ** 2
    phases = coords[..., :, None] * factors % 4096
    angles = phases.astype(F32) * (2.0 * math.pi / 4096.0)
    wave_parts = jnp.concatenate([jnp.sin(angles), jnp.cos(angles)], axis=-1)
    return wave_parts.reshape(coords.shape[:-1] + (FEAT,))


def local(stages, inputs, box_coords, mlm_mask, cotangent, params, first_moment, second_moment):
    fs = lax.axis_index("fsdp")
    half = LEN // 2
    masked = cotangent * mlm_mask.astype(BF16)[..., None]
    count = jnp.full((8, 128), jnp.sum(mlm_mask.astype(F32)))
    boxes = lax.dynamic_index_in_dim(box_coords, fs, 0, keepdims=False)
    features = layout_features(boxes).astype(BF16)
    coord_col = jnp.stack(
        [jnp.arange(LEN, dtype=jnp.int32), boxes[:, 0] + boxes[:, 2], boxes[:, 1] + boxes[:, 3]], axis=1
    )
    coord_row = coord_col.T
    flat = [v.reshape(FLAT, 128) for v in (params, first_moment, second_moment)]
    wall, xdoc, cdoc, total = gather_weights(stages, flat[0], inputs, masked, count)
    out_doc, *saved, wall = forward_pass(wall, xdoc, features, coord_row, coord_col)
    input_grad, reduced, norm = backward_pass(stages, wall, cdoc, total, saved, features, coord_row, coord_col)
    out_other = lax.ppermute(
        lax.dynamic_slice_in_dim(out_doc, (1 - fs) * half, half, 0), "fsdp", [(0, 1), (1, 0)]
    )
    out_mine = lax.dynamic_slice_in_dim(out_doc, fs * half, half, 0)
    layer_out = jnp.where(fs == 0, jnp.stack([out_mine, out_other]), jnp.stack([out_other, out_mine]))
    grad, update, new_first = adam(reduced, *flat)
    return (layer_out, input_grad, grad.reshape(-1), norm[0, 0], update.reshape(-1), new_first.reshape(-1))


def solution(mesh):
    in_specs = (
        P("dp", "fsdp", None),
        P("dp", None, None),
        P("dp", "fsdp"),
        P("dp", "fsdp", None),
        P("fsdp"),
        P("fsdp"),
        P("fsdp"),
    )
    out_specs = (P("dp", "fsdp", None), P("dp", "fsdp", None), P("fsdp"), P(), P("fsdp"), P("fsdp"))
    stages = radices(mesh.shape["dp"])
    return jax.shard_map(
        functools.partial(local, stages), mesh=mesh, in_specs=in_specs, out_specs=out_specs, check_vma=False
    )
```

```python
import functools
import math

import jax
import jax.numpy as jnp
import numpy as np
from jax import lax
from jax.experimental import pallas as pl
from jax.experimental.pallas import tpu as pltpu
from jax.sharding import PartitionSpec as P

D = 768
HEADS = 12
HDIM = 64
FF = 3072
BUCKETS = 32
FEAT = 128
LEN = 512
PADDED = 7208960
SHARD = PADDED // 2
FLAT = SHARD // 128
PAIRS = HEADS // 2
QROWS = 256
AROWS = 512
BROWS = 256
SKEW = 2

norm_eps = 1e-05
adam_one = 0.9
adam_two = 0.999
adam_eps = 1e-08
adam_steps = 100.0
decay_rate = 0.01
table_factor = 5.0

MESH = pl.DeviceIdType.MESH
F32 = jnp.float32
BF16 = jnp.bfloat16
VMEM = pl.BlockSpec(memory_space=pltpu.VMEM)
ANY = pl.BlockSpec(memory_space=pl.ANY)

ROWS = 28672
CHUNK = 2048
CHUNKS = ROWS // CHUNK
CUT = 404
UP_A, UP_B = 416, 368
OUT0 = 18 * D
UP0 = OUT0 + 6 * D
SM0 = UP0 + 24 * UP_A
UP1 = 0
DOWN1 = 24 * UP_B
DOWN_END = DOWN1 + 6 * FF
LAY1 = 27648
SM1 = LAY1 + 6 * FEAT
F_OUT = 13836
F_UP = 18462
F_UPB1 = 8734
F_DOWN1 = 8758
F_SM1 = 27190
F_LAY1 = 27208
F_TAB1 = 27976
LEAD = 104


def nt(a, b):
    return lax.dot_general(a, b, (((1,), (1,)), ((), ())), preferred_element_type=F32)


def nn(a, b):
    return lax.dot_general(a, b, (((1,), (0,)), ((), ())), preferred_element_type=F32)


def tn(a, b):
    return lax.dot_general(a, b, (((0,), (0,)), ((), ())), preferred_element_type=F32)


def radices(replicas):
    stages, stride, left = [], 2, replicas // 2
    if left % 2 == 0:
        stages.append((2, stride))
        stride, left = stride * 2, left // 2
    while left > 1:
        radix = left if left <= 8 else 4
        stages.append((radix, stride))
        stride, left = stride * radix, left // radix
    return stages


def place():
    return lax.axis_index("dp"), lax.axis_index("fsdp")


def member(dp, radix, stride, digit):
    return dp + (digit - (dp // stride) % radix) * stride


def peers(stages):
    dp, fs = place()
    found = [(dp + 1 - 2 * (dp % 2), fs), (dp, 1 - fs)]
    for radix, stride in stages:
        mine = (dp // stride) % radix
        for step in range(1, radix):
            found.append((member(dp, radix, stride, (mine + step) % radix), fs))
    return found


def greet(stages):
    barrier = pltpu.get_barrier_semaphore()
    all_peers = peers(stages)
    for peer in all_peers:
        pl.semaphore_signal(barrier, inc=1, device_id=peer, device_id_type=MESH)
    pl.semaphore_wait(barrier, len(all_peers))


def remote(src, dst, send, recv, peer):
    return pltpu.make_async_remote_copy(
        src_ref=src, dst_ref=dst, send_sem=send, recv_sem=recv, device_id=peer, device_id_type=MESH
    )


def rows_at(start, size):
    return pl.ds(pl.multiple_of(start, 16), size)


def offsets(dp, stages, extent):
    size = extent // 2
    start = (dp % 2) * size
    found = [(start, size)]
    for radix, stride in stages:
        size = size // radix
        start = start + ((dp // stride) % radix) * size
        found.append((start, size))
    return found


def row_of(ref_rows, start, count):
    return jnp.concatenate([ref_rows[start + i : start + i + 1, :] for i in range(count)], axis=1)


def table_constants():
    width = BUCKETS * HEADS
    lane = np.arange(width)
    pick = np.zeros((3, width, 128), np.float32)
    for table in range(3):
        pick[table, lane, 32 * table + lane // HEADS] = 1.0
    keep = (lane[None, :] % HEADS == np.arange(16)[:, None]).astype(np.float32)
    return pick.astype(jnp.bfloat16), keep


def bucket_of(offset):
    spread = jnp.abs(offset)
    result = jnp.minimum(spread, 8) + jnp.where(offset > 0, 16, 0)
    for level in range(9, 16):
        result = result + jnp.where(spread >= 8 * 2 ** (level - 8), 1, 0)
    return result


def up_block(wall, j):
    columns = []
    for c in (2 * j, 2 * j + 1):
        first = wall[0, rows_at(UP0 + c * UP_A, UP_A), :]
        second = wall[1, rows_at(UP1 + c * UP_B + 16, UP_B - 16), :]
        columns.append(jnp.concatenate([first, second], axis=0))
    return jnp.concatenate(columns, axis=1)


def down_rows(wall, j):
    return jnp.concatenate(
        [wall[1, rows_at(DOWN1 + j * 1536 + c * 256, 256), :] for c in range(6)], axis=1
    )


def merge_up(wall):
    row = lax.broadcasted_iota(jnp.int32, (16, 128), 0)

    def one(c, carry):
        low_at = rows_at(UP0 + c * UP_A + UP_A - 16, 16)
        low = wall[0, low_at, :].astype(F32)
        high = wall[1, rows_at(UP1 + c * UP_B, 16), :].astype(F32)
        cut = jnp.where(c < 2, CUT + 1 - 400, CUT - 400)
        wall[0, low_at, :] = jnp.where(row < cut, low, high).astype(BF16)
        return carry

    lax.fori_loop(0, 24, one, 0)


def stats(values):
    mean = jnp.mean(values, axis=1, keepdims=True)
    centered = values - mean
    inverse = lax.rsqrt(jnp.mean(centered * centered, axis=1, keepdims=True) + norm_eps)
    return centered * inverse, inverse


def find_places(coord_col, lut, places, tick):
    lane = lax.broadcasted_iota(jnp.int32, (8, 128), 1)
    step = lane % 16
    level = jnp.where(step <= 8, step, lax.shift_left(jnp.full_like(step, 8), jnp.maximum(step - 8, 0)))
    edge = jnp.where(lane < 16, 1 - level, jnp.where(lane == 16, 1 << 12, level))

    def line_rows(a, carry):
        at = pl.ds(pl.multiple_of(a * 8, 8), 8)
        value = coord_col[at, 0:1] + edge
        places[0, at, :] = jnp.where(value <= 0, LEN, jnp.minimum(value, LEN) - 1)
        return carry

    lax.fori_loop(0, LEN // 8, line_rows, 0, unroll=4)
    for table in (1, 2):
        def look(a, best):
            at = pl.ds(pl.multiple_of(a * 8, 8), 8)
            near = jnp.broadcast_to(coord_col[at, table : table + 1], (8, 128))
            code = near * LEN + (lax.broadcasted_iota(jnp.int32, (8, 128), 0) + a * 8)
            return tuple(
                jnp.maximum(best[g], jnp.where(near < lane + 128 * g, code, -1)) for g in range(16)
            )

        best = lax.fori_loop(
            0, LEN // 8, look, tuple(jnp.full((8, 128), -1, jnp.int32) for _ in range(16)), unroll=2
        )
        tick()
        for g in range(16):
            most = jnp.max(best[g], axis=0, keepdims=True)
            lut[g : g + 1, :] = jnp.where(most < 0, LEN, most & (LEN - 1))
        luts = [jnp.broadcast_to(lut[g : g + 1, :], (8, 128)) for g in range(16)]

        def find(a, carry):
            at = pl.ds(pl.multiple_of(a * 8, 8), 8)
            value = jnp.clip(coord_col[at, table : table + 1] + edge, 0, 2047)
            low, high = value & 127, value >> 7
            found = jnp.full((8, 128), LEN, jnp.int32)
            for g in range(16):
                found = jnp.where(high == g, jnp.take_along_axis(luts[g], low, axis=1), found)
            places[table, at, :] = found
            return carry

        for part in range(2):
            lax.fori_loop(part * 32, part * 32 + 32, find, 0, unroll=4)
            tick()


def relayout(plane, flat, out, group):
    def blocks(count, dst, src, rows, stride):
        def one(i, carry):
            out[plane, rows_at(dst(i), rows), :] = flat[pl.ds(LEAD + src(i), rows, stride=stride), :].astype(BF16)
            return carry

        lax.fori_loop(0, count, one, 0)

    def window(dst, src, count):
        out[plane, pl.ds(dst, count), :] = flat[pl.ds(LEAD + src, count), :].astype(BF16)

    def clear(low, high):
        out[plane, pl.ds(low, high - low), :] = jnp.zeros((high - low, 128), BF16)

    if plane == 0 and group == 0:
        blocks(24, lambda c: UP0 + c * UP_A, lambda c: F_UP + c, UP_A, 24)
        window(SM0, 13824, 16)
        window(SM0 + 16, 18440, 32)
        clear(SM0 + 48, ROWS)
    elif plane == 0 and group == 1:
        blocks(18, lambda pos: pos * D, lambda pos: lax.rem(pos, 3) * 6 + pos // 3, D, 18)
    elif plane == 0:
        blocks(6, lambda c: OUT0 + c * D, lambda c: F_OUT + c, D, 6)
    elif group == 0:
        for c in range(6):
            blocks(12, lambda j: DOWN1 + j * 1536 + c * 256, lambda j: F_DOWN1 + j * 1536 + c, 256, 6)
        clear(DOWN_END, LAY1)
        blocks(6, lambda c: LAY1 + c * FEAT, lambda c: F_LAY1 + c, FEAT, 6)
        window(SM1, 8728, 32)
        window(SM1 + 32, 27184, 32)
        window(SM1 + 64, 27976, 16)
        clear(SM1 + 80, ROWS)
    elif group == 1:
        blocks(24, lambda c: UP1 + c * UP_B, lambda c: c - 98, UP_B, 24)


class Gather:
    def __init__(self, stages, zall, x_send, x_recv, c_send, c_recv, sems):
        self.stages, self.zall, self.sems = stages, zall, sems
        self.x_send, self.x_recv, self.c_send, self.c_recv = x_send, x_recv, c_send, c_recv
        self.dp, self.fs = place()
        self.other = 1 - self.fs
        self.levels = len(stages)
        self.parts = offsets(self.dp, stages, CHUNK)
        self.x_peer = (self.dp, self.other)
        self.core_peer = (self.dp + 1 - 2 * (self.dp % 2), self.fs)

    def base(self, position):
        return lax.rem(CHUNKS - 1 + position, CHUNKS) * CHUNK

    def direct(self, position):
        return (position == 4) | (position == 9) | (position == 12)

    def x_copy(self, position, plane, direct):
        start, size = self.parts[0] if direct else self.parts[-1]
        where = self.zall.at[plane, rows_at(self.base(position) + start, size)]
        return remote(where, where, self.x_send.at[position], self.x_recv.at[position], self.x_peer)

    def send(self, low, high):
        def one(position, carry):
            direct = self.direct(position)

            @pl.when(direct)
            def _():
                self.x_copy(position, self.fs, True).start()

            @pl.when(jnp.logical_not(direct))
            def _():
                self.x_copy(position, self.fs, False).start()

            return carry

        lax.fori_loop(low, high, one, 0)

    def stage_copies(self, level, position, receive):
        radix, stride = self.stages[level]
        start, size = self.parts[level + 1]
        mine = (self.dp // stride) % radix
        copies = []
        for step in range(1, radix):
            peer = (member(self.dp, radix, stride, (mine + step) % radix), self.fs)
            shift = ((mine - step + radix) % radix - mine) * size if receive else 0
            where = self.zall.at[self.other, rows_at(self.base(position) + start + shift, size)]
            copies.append(
                remote(
                    where, where, self.sems[2 * level].at[position, step - 1],
                    self.sems[2 * level + 1].at[position, step - 1], peer,
                )
            )
        return copies

    def core_copy(self, position, receive):
        size = CHUNK // 2
        start = (1 - self.dp % 2 if receive else self.dp % 2) * size
        where = self.zall.at[self.other, rows_at(self.base(position) + start, size)]
        return remote(where, where, self.c_send.at[position], self.c_recv.at[position], self.core_peer)

    def work(self, position, step):
        direct = self.direct(position)
        levels = self.levels
        if step == levels + 1:
            self.core_copy(position, True).wait_recv()
            self.core_copy(position, False).wait_send()

            @pl.when(direct)
            def _():
                self.x_copy(position, self.fs, True).wait_send()

            @pl.when(jnp.logical_not(direct))
            def _():
                self.x_copy(position, self.fs, False).wait_send()
                for level in range(levels):
                    for copy in self.stage_copies(level, position, False):
                        copy.wait_send()

            return
        if step == 0:

            @pl.when(direct)
            def _():
                self.x_copy(position, self.other, True).wait_recv()
                self.core_copy(position, False).start()

        @pl.when(jnp.logical_not(direct))
        def _():
            if step == 0:
                self.x_copy(position, self.other, False).wait_recv()
            else:
                for copy in self.stage_copies(levels - step, position, True):
                    copy.wait_recv()
            if step < levels:
                for copy in self.stage_copies(levels - 1 - step, position, False):
                    copy.start()
            else:
                self.core_copy(position, False).start()

    def tick(self, number):
        for step in range(self.levels + 1, -1, -1):
            position = number - SKEW * step

            @pl.when((position >= 0) & (position < CHUNKS))
            def _(position=position, step=step):
                self.work(position, step)

    def ticks(self):
        return CHUNKS + SKEW * (self.levels + 1)


def forward_kernel(
    stages, p_hbm, xin, cot, cnt, features, coord_row, coord_col, pick, keep,
    wall_out, cdoc_out, total, rounded_out, qkv_out, probs_out, mixed_out, one_out, inverse_one, low_out, hidden_out,
    slope_out, two_out, inverse_two, places_out, layer_out,
    flat, wall, xs, cs, cnt_slots, start, up_bias, acc, indices, lut, rounded, qkv, probs, mixed, normed, low, hidden,
    slope, places, layer,
    in_sem, x_send, x_recv, c_send, c_recv, act_send, act_recv, n_send, n_recv, out_sem, probs_sem, feed_sem, *stage_sems,
):
    net = Gather(stages, wall, x_send, x_recv, c_send, c_recv, stage_sems)
    dp, fs, other = net.dp, net.fs, net.other
    half = LEN // 2
    pieces = 8
    span = FLAT // pieces
    loads = [
        pltpu.make_async_copy(
            p_hbm.at[pl.ds(i * span, span)], flat.at[pl.ds(LEAD + i * span, span)], in_sem.at[i]
        )
        for i in range(pieces)
    ]
    for load in loads:
        load.start()
    flat[pl.ds(0, LEAD), :] = jnp.zeros((LEAD, 128), F32)
    flat[pl.ds(LEAD + FLAT, 288), :] = jnp.zeros((288, 128), F32)
    greet(stages)

    def act_copy(number, source, target, receive):
        where = rows_at((other if receive else fs) * half, half)
        return remote(source.at[other], target.at[where], act_send.at[number], act_recv.at[number], net.x_peer)

    rounds = [
        [
            (member(dp, radix, stride, ((dp // stride) % radix + step) % radix), fs)
            for step in range(1, radix)
        ]
        for radix, stride in stages
    ] + [[net.core_peer], [net.x_peer]]

    def count_copies(number):
        base = sum(len(r) for r in rounds[:number])
        return [
            remote(total.at[...], cnt_slots.at[base + i], n_send.at[base + i], n_recv.at[base + i], peer)
            for i, peer in enumerate(rounds[number])
        ]

    def count_round(number):
        if 0 < number <= len(rounds):
            gathered = total[...]
            base = sum(len(r) for r in rounds[: number - 1])
            for i, copy in enumerate(count_copies(number - 1)):
                copy.wait()
                gathered = gathered + cnt_slots[base + i]
            total[...] = gathered
        if number < len(rounds):
            for copy in count_copies(number):
                copy.start()

    total[...] = cnt[...]
    count_round(0)
    for load in loads:
        load.wait()
    for group, (low_at, high_at) in enumerate(((0, 1), (1, 7), (7, CHUNKS))):
        for plane in range(2):

            @pl.when(fs == plane)
            def _(plane=plane, group=group):
                relayout(plane, flat, wall, group)

        net.send(low_at, high_at)
        if group == 1:
            act_copy(0, xin, xs, False).start()
    xs[pl.ds(fs * half, half), :] = xin[fs]
    cs[pl.ds(fs * half, half), :] = cot[fs]

    def index_rows(a, carry):
        at = pl.ds(pl.multiple_of(a * 8, 8), 8)
        for table in range(3):
            near = jnp.broadcast_to(coord_col[at, table : table + 1], (8, 128))
            for j in range(4):
                far = coord_row[table : table + 1, j * 128 : (j + 1) * 128]
                indices[table, at, j * 128 : (j + 1) * 128] = (
                    bucket_of(jnp.broadcast_to(far, (8, 128)) - near) + 32 * table
                )
        return carry

    lax.fori_loop(0, LEN // 8, index_rows, 0, unroll=4)
    passed = [0]

    def tick():
        net.tick(passed[0])
        if passed[0] % 2 == 0:
            count_round(passed[0] // 2 + 1)
        passed[0] += 1

    find_places(coord_col, lut, places, tick)
    outs = []

    def put(source, target):
        copy = pltpu.make_async_copy(source, target, out_sem.at[len(outs)])
        copy.start()
        outs.append(copy)

    put(places, places_out)
    while passed[0] < 1 + SKEW * (net.levels + 1):
        tick()

    small1 = wall[1, pl.ds(SM1, 80), :].astype(F32)
    heads_by_lane = jnp.zeros((16, 128), F32)
    for table in range(3):
        flat_row = row_of(small1, 64 + 3 * table, 3)
        spread = (jnp.broadcast_to(flat_row, (16, 384)) * keep[...]).astype(BF16)
        heads_by_lane = heads_by_lane + nn(spread, pick[table])
    rows_by_head = [jnp.broadcast_to(heads_by_lane[h : h + 1, :], (8, 128)) for h in range(HEADS)]
    begun = passed[0]

    def bias_rows(a, carry):
        @pl.when(lax.rem(a, 2) == 1)
        def _():
            net.tick(begun + a // 2)

        for b in range(4):
            row = a * 32 + b * 8
            at = pl.ds(pl.multiple_of(row, 8), 8)
            for j in range(4):
                sums = [None] * HEADS
                for table in range(3):
                    index = indices[table, at, j * 128 : (j + 1) * 128]
                    for h in range(HEADS):
                        found = jnp.take_along_axis(rows_by_head[h], index, axis=1)
                        sums[h] = found if sums[h] is None else sums[h] + found
                for h in range(HEADS):
                    flat[pl.ds(pl.multiple_of((4 * h + j) * LEN + row, 8), 8), :] = sums[h]
        return carry

    lax.fori_loop(0, LEN // 32, bias_rows, 0)

    act_copy(1, cot, cs, False).start()
    small0 = wall[0, pl.ds(SM0, 48), :].astype(F32)
    qv_bias = row_of(small0, 0, 12)
    out_bias, gain_one, shift_one = (row_of(small0, 20 + 6 * i, 6) for i in range(3))
    down_bias, gain_two, shift_two = (row_of(small1, 38 + 6 * i, 6) for i in range(3))
    act_copy(0, xin, xs, True).wait_recv()

    w_layout = jnp.concatenate([wall[1, pl.ds(LAY1 + c * FEAT, FEAT), :] for c in range(6)], axis=1)

    def start_rows(r, carry):
        at = pl.ds(pl.multiple_of(r * QROWS, QROWS), QROWS)
        rows = xs[at, :].astype(F32) + nn(features[at, :], w_layout)
        start[at, :] = rows
        rounded[at, :] = rows.astype(BF16)
        return carry

    lax.fori_loop(0, LEN // QROWS, start_rows, 0)
    put(rounded, rounded_out)
    for i in range(18):
        up_bias[:, i * 128 : (i + 1) * 128] = (
            jnp.zeros((1, 128), F32)
            if i % 3 == 1
            else qv_bias[:, (i // 3 + 3 * (i % 3)) * 128 : (i // 3 + 3 * (i % 3) + 1) * 128]
        )
    left = lax.broadcasted_iota(jnp.int32, (LEN, 128), 1) < HDIM

    def probs_copy(pair):
        where = rows_at(pair * 8 * LEN, 8 * LEN)
        return pltpu.make_async_copy(probs.at[where], probs_out.at[where], probs_sem.at[pair])

    begun += LEN // 64
    assert net.ticks() - begun <= PAIRS

    def attend(pair, carry):
        @pl.when(begun + pair < net.ticks())
        def _():
            net.tick(begun + pair)

        at = pl.multiple_of(3 * pair * D, 16)
        weight = jnp.concatenate([wall[0, rows_at(at + i * D, D), :] for i in range(3)], axis=1)
        part = nn(rounded[...], weight) + up_bias[:, pl.ds(pl.multiple_of(pair * 384, 128), 384)]
        query = part[:, :128].astype(BF16) * HDIM**-0.5
        key = part[:, 128:256].astype(BF16)
        value = part[:, 256:].astype(BF16)
        qkv[3 * pair] = query
        qkv[3 * pair + 1] = key
        qkv[3 * pair + 2] = value
        found = [[], []]
        for side in range(2):
            head = 2 * pair + side
            mine = left if side == 0 else jnp.logical_not(left)
            for r in range(0, LEN, AROWS):
                some = query[r : r + AROWS]
                extra = jnp.concatenate(
                    [flat[rows_at((4 * head + j) * LEN + r, AROWS), :] for j in range(4)], axis=1
                )
                scores = nt(jnp.where(mine[r : r + AROWS], some, jnp.zeros_like(some)), key) + extra
                scores = jnp.exp(scores - jnp.max(scores, axis=1, keepdims=True))
                soft = (scores * (1.0 / jnp.sum(scores, axis=1, keepdims=True))).astype(BF16)
                for j in range(4):
                    probs[rows_at((4 * head + j) * LEN + r, AROWS), :] = soft[:, j * 128 : (j + 1) * 128]
                found[side].append(nn(soft, value))
        mixed[:, pl.ds(pl.multiple_of(pair * 128, 128), 128)] = jnp.where(
            left, jnp.concatenate(found[0], axis=0), jnp.concatenate(found[1], axis=0)
        ).astype(BF16)
        probs_copy(pair).start()
        return carry

    lax.fori_loop(0, PAIRS, attend, 0)
    merge_up(wall)
    put(wall, wall_out)
    put(qkv, qkv_out)
    put(mixed, mixed_out)

    w_out = jnp.concatenate([wall[0, pl.ds(OUT0 + c * D, D), :] for c in range(6)], axis=1)

    def first_rows(r, carry):
        at = pl.ds(pl.multiple_of(r * QROWS, QROWS), QROWS)
        unit, inverse = stats(start[at, :] + nn(mixed[at, :], w_out) + out_bias)
        normed[at, :] = unit
        inverse_one[at, :] = inverse
        result = unit * gain_one + shift_one
        low[at, :] = result.astype(BF16)
        acc[at, :] = result + down_bias
        return carry

    lax.fori_loop(0, LEN // QROWS, first_rows, 0)
    put(normed, one_out)
    put(low, low_out)
    for j in range(12):
        up_bias[:, j * 256 : (j + 1) * 256] = row_of(small1, 6 + 2 * j, 2)

    def feed_copies(j):
        lanes = pl.ds(pl.multiple_of(j * 256, 256), 256)
        return [
            pltpu.make_async_copy(hidden.at[:, lanes], hidden_out.at[:, lanes], feed_sem.at[0, j]),
            pltpu.make_async_copy(slope.at[:, lanes], slope_out.at[:, lanes], feed_sem.at[1, j]),
        ]

    def feed_step(j, carry):
        lanes = pl.ds(pl.multiple_of(j * 256, 256), 256)
        up = nn(low[...], up_block(wall, j)) + up_bias[:, lanes]
        half_up = 0.5 + 0.5 * lax.erf(up * math.sqrt(0.5))
        bell = jnp.exp(-0.5 * up * up) * (1.0 / math.sqrt(2.0 * math.pi))
        slope[:, lanes] = (half_up + up * bell).astype(BF16)
        part = (up * half_up).astype(BF16)
        hidden[:, lanes] = part
        acc[...] += nn(part, down_rows(wall, j))
        for copy in feed_copies(j):
            copy.start()
        return carry

    lax.fori_loop(0, 12, feed_step, 0, unroll=3)

    def second_rows(r, carry):
        at = pl.ds(pl.multiple_of(r * QROWS, QROWS), QROWS)
        unit, inverse = stats(acc[at, :])
        acc[at, :] = unit
        inverse_two[at, :] = inverse
        layer[at, :] = (unit * gain_two + shift_two).astype(BF16)
        return carry

    lax.fori_loop(0, LEN // QROWS, second_rows, 0)
    put(acc, two_out)
    put(layer, layer_out)
    act_copy(1, cot, cs, True).wait_recv()
    put(cs, cdoc_out)
    for number in range(2):
        act_copy(number, (xin, cot)[number], (xs, cs)[number], False).wait_send()
    for pair in range(PAIRS):
        probs_copy(pair).wait()
    for copy in outs:
        copy.wait()

    def feed_wait(j, carry):
        for copy in feed_copies(j):
            copy.wait()
        return carry

    lax.fori_loop(0, 12, feed_wait, 0)


def forward_pass(stages, p2, xin, cot, cnt, features, coord_row, coord_col):
    pick, keep = table_constants()
    sds = jax.ShapeDtypeStruct
    dma = pltpu.SemaphoreType.DMA
    count_peers = 2 + sum(radix - 1 for radix, _ in stages)
    sems = []
    for radix, _ in stages:
        sems += [dma((CHUNKS, radix - 1))] * 2
    return pl.pallas_call(
        functools.partial(forward_kernel, stages),
        name="gather_forward",
        out_shape=(
            sds((2, ROWS, 128), BF16),
            sds((LEN, D), BF16),
            sds((8, 128), F32),
            sds((LEN, D), BF16),
            sds((18, LEN, 128), BF16),
            sds((HEADS * 4 * LEN, 128), BF16),
            sds((LEN, D), BF16),
            sds((LEN, D), F32),
            sds((LEN, 1), F32),
            sds((LEN, D), BF16),
            sds((LEN, FF), BF16),
            sds((LEN, FF), BF16),
            sds((LEN, D), F32),
            sds((LEN, 1), F32),
            sds((3, LEN, 128), jnp.int32),
            sds((LEN, D), BF16),
        ),
        in_specs=[ANY] + [VMEM] * 8,
        out_specs=(ANY, ANY, VMEM, ANY, ANY, ANY, ANY, ANY, VMEM, ANY, ANY, ANY, ANY, VMEM, ANY, ANY),
        scratch_shapes=[
            pltpu.VMEM((LEAD + FLAT + 288, 128), F32),
            pltpu.VMEM((2, ROWS, 128), BF16),
            pltpu.VMEM((LEN, D), BF16),
            pltpu.VMEM((LEN, D), BF16),
            pltpu.VMEM((count_peers, 8, 128), F32),
            pltpu.VMEM((LEN, D), F32),
            pltpu.VMEM((1, FF), F32),
            pltpu.VMEM((LEN, D), F32),
            pltpu.VMEM((3, LEN, LEN), jnp.int32),
            pltpu.VMEM((16, 128), jnp.int32),
            pltpu.VMEM((LEN, D), BF16),
            pltpu.VMEM((18, LEN, 128), BF16),
            pltpu.VMEM((HEADS * 4 * LEN, 128), BF16),
            pltpu.VMEM((LEN, D), BF16),
            pltpu.VMEM((LEN, D), F32),
            pltpu.VMEM((LEN, D), BF16),
            pltpu.VMEM((LEN, FF), BF16),
            pltpu.VMEM((LEN, FF), BF16),
            pltpu.VMEM((3, LEN, 128), jnp.int32),
            pltpu.VMEM((LEN, D), BF16),
            dma((8,)), dma((CHUNKS,)), dma((CHUNKS,)), dma((CHUNKS,)), dma((CHUNKS,)), dma((2,)), dma((2,)),
            dma((count_peers,)), dma((count_peers,)), dma((16,)), dma((PAIRS,)), dma((2, 12)),
        ]
        + sems,
        compiler_params=pltpu.CompilerParams(
            collective_id=1, has_side_effects=True, vmem_limit_bytes=64 * 2**20 - 2**16
        ),
    )(p2, xin, cot, cnt, features, coord_row, coord_col, jnp.asarray(pick), jnp.asarray(keep))


G_SMALL = (("qv_bias", 0, 0, 12), ("out_bias", 0, 12, 6), ("gain_one", 0, 18, 6), ("shift_one", 0, 24, 6),
           ("up_bias", 1, 0, 24), ("down_bias", 1, 24, 6), ("gain_two", 1, 30, 6), ("shift_two", 1, 36, 6),
           ("tables", 1, 42, 9))


def spread_norm(normed, inverse, gain, grad):
    scaled = grad * gain
    return inverse * (
        scaled
        - jnp.mean(scaled, axis=1, keepdims=True)
        - normed * jnp.mean(scaled * normed, axis=1, keepdims=True)
    )


def total_rows(values):
    return jnp.sum(values.astype(F32), axis=0, keepdims=True)


def reduce_chunk(stages):
    replicas = 2
    for radix, _ in stages:
        replicas *= radix
    return max(1024, 16 * replicas)


class Reduction:
    def __init__(self, stages, gstack, out, core_slots, x_slots, pieces, slots, sems):
        self.stages, self.gstack, self.out = stages, gstack, out
        self.core_slots, self.x_slots, self.pieces, self.slots = core_slots, x_slots, pieces, slots
        (self.c_send, self.c_recv, self.x_send, self.x_recv, self.b_send, self.b_recv, self.own_sem) = sems[:7]
        self.sems = sems[7:]
        self.dp, self.fs = place()
        self.other = 1 - self.fs
        self.size = reduce_chunk(stages)
        self.count = ROWS // self.size
        self.levels = len(stages)
        self.parts = offsets(self.dp, stages, self.size)
        self.half = self.size // 2
        self.x_peer = (self.dp, self.other)
        self.core_peer = (self.dp + 1 - 2 * (self.dp % 2), self.fs)

    def base(self, position):
        return lax.rem(2 * self.count - 2 - position, self.count) * self.size

    def ready(self, row):
        return jnp.maximum(self.count - 1 - (row + self.size - 1) // self.size, 0)

    def core_copy(self, position, plane):
        where = rows_at(self.base(position) + (1 - self.dp % 2) * self.half, self.half)
        return remote(
            self.gstack.at[plane, where], self.core_slots.at[plane, position],
            self.c_send.at[plane, position], self.c_recv.at[plane, position], self.core_peer,
        )

    def x_copy(self, position):
        where = rows_at(self.base(position) + self.parts[0][0], self.half)
        return remote(
            self.gstack.at[self.other, where], self.x_slots.at[position],
            self.x_send.at[position], self.x_recv.at[position], self.x_peer,
        )

    def scatter_copies(self, level, position):
        radix, stride = self.stages[level]
        start, size = self.parts[level]
        size = size // radix
        mine = (self.dp // stride) % radix
        copies = []
        for step in range(1, radix):
            target = (mine + step) % radix
            where = rows_at(self.base(position) + start + target * size, size)
            copies.append(
                remote(
                    self.gstack.at[self.fs, where], self.slots[level].at[position, step - 1],
                    self.sems[4 * level].at[position, step - 1], self.sems[4 * level + 1].at[position, step - 1],
                    (member(self.dp, radix, stride, target), self.fs),
                )
            )
        return copies

    def spread_copies(self, level, position, receive):
        radix, stride = self.stages[level]
        start, size = self.parts[level + 1]
        mine = (self.dp // stride) % radix
        copies = []
        for step in range(1, radix):
            shift = ((mine - step + radix) % radix - mine) * size if receive else 0
            where = self.out.at[rows_at(self.base(position) + start + shift, size)]
            source = self.pieces.at[position] if level == self.levels - 1 and not receive else where
            copies.append(
                remote(
                    source, where,
                    self.sems[4 * level + 2].at[position, step - 1], self.sems[4 * level + 3].at[position, step - 1],
                    (member(self.dp, radix, stride, (mine + step) % radix), self.fs),
                )
            )
        return copies

    def own_copy(self, position):
        start, size = self.parts[-1]
        return pltpu.make_async_copy(
            self.pieces.at[position], self.out.at[rows_at(self.base(position) + start, size)],
            self.own_sem.at[position],
        )

    def back_copy(self, position, receive):
        start = (1 - self.dp % 2 if receive else self.dp % 2) * self.half
        where = self.out.at[rows_at(self.base(position) + start, self.half)]
        return remote(where, where, self.b_send.at[position], self.b_recv.at[position], self.core_peer)

    def feed(self, plane, low, high):
        def one(position, carry):
            self.core_copy(position, plane).start()
            return carry

        lax.fori_loop(low, high, one, 0)

    def push(self, low, high):
        def one(position, carry):
            self.core_copy(position, self.other).wait_recv()
            where = rows_at(self.base(position) + self.parts[0][0], self.half)
            value = self.gstack[self.other, where, :].astype(F32) + self.core_slots[self.other, position].astype(F32)
            self.gstack[self.other, where, :] = value.astype(BF16)
            self.x_copy(position).start()
            return carry

        lax.fori_loop(low, high, one, 0)

    def work(self, position, step):
        levels = self.levels
        base = self.base(position)
        if step <= levels:
            start, size = self.parts[step]
            where = rows_at(base + start, size)
            if step == 0:
                self.core_copy(position, self.fs).wait_recv()
                self.x_copy(position).wait_recv()
                terms = [self.core_slots[self.fs, position], self.x_slots[position]]
            else:
                for copy in self.scatter_copies(step - 1, position):
                    copy.wait()
                terms = [self.slots[step - 1][position, i] for i in range(self.stages[step - 1][0] - 1)]
            value = self.gstack[self.fs, where, :].astype(F32)
            for term in terms:
                value = value + term.astype(F32)
            if step < levels:
                self.gstack[self.fs, where, :] = value.astype(BF16)
                for copy in self.scatter_copies(step, position):
                    copy.start()
            else:
                self.pieces[position] = value.astype(BF16)
                self.own_copy(position).start()
                for copy in self.spread_copies(levels - 1, position, False):
                    copy.start()
        else:
            level = 2 * levels - step
            for copy in self.spread_copies(level, position, True):
                copy.wait_recv()
            for copy in self.spread_copies(level, position, False):
                copy.wait_send()
            if level == levels - 1:
                self.own_copy(position).wait()
                self.x_copy(position).wait_send()
                for plane in range(2):
                    self.core_copy(position, plane).wait_send()
            if level > 0:
                for copy in self.spread_copies(level - 1, position, False):
                    copy.start()
            else:
                self.back_copy(position, False).start()

    def tick(self, number):
        for step in range(2 * self.levels, -1, -1):
            position = number - SKEW * step

            @pl.when((position >= 0) & (position < self.count))
            def _(position=position, step=step):
                self.work(position, step)

    def ticks(self):
        return self.count + 2 * SKEW * self.levels

    def finish(self):
        def one(position, carry):
            self.back_copy(position, True).wait_recv()
            self.back_copy(position, False).wait_send()
            return carry

        lax.fori_loop(0, self.count, one, 0)


def reduction_scratch(stages):
    size = reduce_chunk(stages)
    count, half = ROWS // size, size // 2
    dma = pltpu.SemaphoreType.DMA
    slots, sems = [], []
    for radix, _ in stages:
        half = half // radix
        slots.append(pltpu.VMEM((count, radix - 1, half, 128), BF16))
        sems += [dma((count, radix - 1))] * 4
    return (
        [
            pltpu.VMEM((2, count, size // 2, 128), BF16),
            pltpu.VMEM((count, size // 2, 128), BF16),
            pltpu.VMEM((count, half, 128), BF16),
        ]
        + slots,
        [dma((2, count)), dma((2, count))] + [dma((count,))] * 5 + sems,
    )


def backward_kernel(
    stages,
    wall_hbm, cdoc_hbm, total, layer_hbm, rounded_hbm, qkv_hbm, probs_hbm, mixed_hbm, one_hbm, inverse_one, low_hbm, hidden_hbm,
    slope_hbm, two_hbm, inverse_two, places_hbm, features, coord_row, coord_col, pick, keep,
    layer_out, input_grad, reduced, norm,
    wall, gstack, acc, branch, hidden, d_up, low, rounded, qkv, mixed, normed_one, less, places, prefix, small,
    square_slots, load_sem, step_sem, probs_sem, act_send, act_recv, act_sem, n_send, n_recv, *rest,
):
    levels = len(stages)
    parts_vmem, sems = rest[: 3 + levels], rest[3 + levels :]
    red = Reduction(stages, gstack, reduced, parts_vmem[0], parts_vmem[1], parts_vmem[2], parts_vmem[3:], sems)
    dp, fs, other = red.dp, red.fs, red.other
    half = LEN // 2

    early = [
        pltpu.make_async_copy(wall_hbm.at[:, pl.ds(SM0, 256)], wall.at[:, pl.ds(SM0, 256)], load_sem.at[0]),
        pltpu.make_async_copy(cdoc_hbm, branch, load_sem.at[1]),
        pltpu.make_async_copy(two_hbm, acc, load_sem.at[2]),
    ]
    lows = [pltpu.make_async_copy(low_hbm, low, load_sem.at[3])]
    rest_loads = [
        pltpu.make_async_copy(one_hbm, normed_one, load_sem.at[4]),
        pltpu.make_async_copy(wall_hbm.at[0, pl.ds(0, UP0)], wall.at[0, pl.ds(0, UP0)], load_sem.at[5]),
        pltpu.make_async_copy(mixed_hbm, mixed, load_sem.at[6]),
        pltpu.make_async_copy(qkv_hbm, qkv, load_sem.at[7]),
        pltpu.make_async_copy(rounded_hbm, rounded, load_sem.at[8]),
        pltpu.make_async_copy(places_hbm, places, load_sem.at[9]),
    ]

    def step_loads(j):
        lanes = pl.ds(pl.multiple_of(j * 256, 256), 256)
        areas = [(1, DOWN1 + 1536 * j, 1536), (0, UP0 + 2 * UP_A * j, 2 * UP_A), (1, UP1 + 2 * UP_B * j, 2 * UP_B)]
        copies = [
            pltpu.make_async_copy(
                wall_hbm.at[plane, rows_at(start, size)], wall.at[plane, rows_at(start, size)], step_sem.at[i, j]
            )
            for i, (plane, start, size) in enumerate(areas)
        ]
        copies.append(pltpu.make_async_copy(hidden_hbm.at[:, lanes], hidden.at[:, lanes], step_sem.at[3, j]))
        copies.append(pltpu.make_async_copy(slope_hbm.at[:, lanes], d_up.at[:, lanes], step_sem.at[4, j]))
        return copies

    for load in early + lows:
        load.start()

    def start_loads(it, carry):
        for load in step_loads(11 - it):
            load.start()
        return carry

    lax.fori_loop(0, 12, start_loads, 0)
    for load in rest_loads:
        load.start()
    greet(stages)

    def layer_copy(receive):
        return remote(
            layer_hbm.at[rows_at(other * half, half)], layer_out.at[other if receive else fs],
            act_send.at[1], act_recv.at[1], red.x_peer,
        )

    layer_copy(False).start()
    layer_own = pltpu.make_async_copy(layer_hbm.at[rows_at(fs * half, half)], layer_out.at[fs], act_sem.at[1])
    layer_own.start()
    small[...] = jnp.zeros_like(small)
    gstack[1, pl.ds(DOWN_END, LAY1 - DOWN_END), :] = jnp.zeros((LAY1 - DOWN_END, 128), BF16)
    for load in early:
        load.wait()

    small0 = wall[0, pl.ds(SM0, 48), :].astype(F32)
    small1 = wall[1, pl.ds(SM1, 80), :].astype(F32)
    gain_one = row_of(small0, 26, 6)
    gain_two = row_of(small1, 44, 6)
    spots = {name: (plane, first_row) for name, plane, first_row, _ in G_SMALL}

    def keep_small(name, vector):
        plane, at = spots[name]
        for i in range(vector.shape[1] // 128):
            small[plane, at + i : at + i + 1, :] = vector[:, i * 128 : (i + 1) * 128]

    count = total[0:1, 0:1]
    none = jnp.zeros((1, D), F32)

    def second_rows(r, sums):
        at = pl.ds(pl.multiple_of(r * QROWS, QROWS), QROWS)
        grad_out = branch[at, :].astype(F32) / count
        normed = acc[at, :]
        result = spread_norm(normed, inverse_two[at, :], gain_two, grad_out)
        acc[at, :] = result
        lower = result.astype(BF16)
        branch[at, :] = lower
        return sums[0] + total_rows(grad_out * normed), sums[1] + total_rows(grad_out), sums[2] + total_rows(lower)

    sums = lax.fori_loop(0, LEN // QROWS, second_rows, (none, none, none))
    for name, vector in zip(("gain_two", "shift_two", "down_bias"), sums):
        keep_small(name, vector)
    plane_up, at_up = spots["up_bias"]
    lows[0].wait()

    def fed(plane, it):
        row = UP0 + 2 * UP_A * (11 - it) if plane == 0 else DOWN1 + 1536 * (11 - it)
        return red.ready(row)

    def of_other(values):
        return jnp.where(other == 0, values[0], values[1])

    fine = red.count >= 28
    tile_row = lax.broadcasted_iota(jnp.int32, (16, 128), 0)

    def feed_step(it, carry):
        j = 11 - it
        for load in step_loads(j):
            load.wait()
        for plane in range(2):
            red.feed(plane, fed(plane, it - 2), fed(plane, it - 1))
        red.push(of_other([fed(p, it - 3) for p in range(2)]), of_other([fed(p, it - 2) for p in range(2)]))
        lanes = pl.ds(pl.multiple_of(j * 256, 256), 256)
        grad = nt(branch[...], down_rows(wall, j))
        part = (grad * d_up[:, lanes].astype(F32)).astype(BF16)
        d_up[:, lanes] = part
        sums = total_rows(part)
        small[plane_up, pl.ds(at_up + 2 * j, 1), :] = sums[:, :128]
        small[plane_up, pl.ds(at_up + 2 * j + 1, 1), :] = sums[:, 128:]
        down = tn(hidden[:, lanes], branch[...]).astype(BF16)
        for c in range(6):
            gstack[1, rows_at(DOWN1 + j * 1536 + c * 256, 256), :] = down[:, c * 128 : (c + 1) * 128]
        up = tn(low[...], part)
        for i in range(2):
            c = 2 * j + i
            cut = jnp.where(c < 2, CUT + 1 - 400, CUT - 400)
            columns = up[:, i * 128 : (i + 1) * 128]
            tile = columns[400:416]
            gstack[0, rows_at(UP0 + c * UP_A, 400), :] = columns[:400].astype(BF16)
            gstack[0, rows_at(UP0 + c * UP_A + 400, 16), :] = jnp.where(tile_row < cut, tile, 0.0).astype(BF16)
            gstack[1, rows_at(UP1 + c * UP_B, 16), :] = jnp.where(tile_row < cut, 0.0, tile).astype(BF16)
            gstack[1, rows_at(UP1 + c * UP_B + 16, UP_B - 16), :] = columns[416:].astype(BF16)
        acc[...] += nt(part, up_block(wall, j))
        return carry

    lax.fori_loop(0, 12, feed_step, 0)

    def probs_copy(pair, slot):
        size = 8 * LEN
        return pltpu.make_async_copy(
            probs_hbm.at[rows_at(pair * size, size)], wall.at[0, rows_at(UP0 + slot * size, size)], probs_sem.at[slot]
        )

    probs_copy(PAIRS - 1, 0).start()
    last = red.count - 1
    red.feed(0, fed(0, 10), fed(0, 11))
    red.feed(1, fed(1, 10), last)
    red.push(of_other([fed(p, 9) for p in range(2)]), of_other([fed(p, 10) for p in range(2)]))
    for load in rest_loads:
        load.wait()

    w_out = jnp.concatenate([wall[0, pl.ds(OUT0 + c * D, D), :] for c in range(6)], axis=1)

    def first_rows(r, sums):
        at = pl.ds(pl.multiple_of(r * QROWS, QROWS), QROWS)
        grad, normed = acc[at, :], normed_one[at, :]
        result = spread_norm(normed, inverse_one[at, :], gain_one, grad)
        acc[at, :] = result
        lower = result.astype(BF16)
        branch[at, :] = lower
        low[at, :] = nt(lower, w_out).astype(BF16)
        return sums[0] + total_rows(grad * normed), sums[1] + total_rows(grad), sums[2] + total_rows(lower)

    sums = lax.fori_loop(0, LEN // QROWS, first_rows, (none, none, none))
    for name, vector in zip(("gain_one", "shift_one", "out_bias"), sums):
        keep_small(name, vector)
    red.push(of_other([fed(p, 10) for p in range(2)]), jnp.where(other == 0, fed(0, 11), last))

    def drain(number, carry):
        red.tick(number)
        return carry

    per_pair = 2 if fine else 1

    def out_step(j, carry):
        lanes = pl.ds(pl.multiple_of(j * 256, 256), 256)
        part = tn(mixed[...], branch[:, lanes]).astype(BF16)
        for i in range(2):
            gstack[0, rows_at(OUT0 + (2 * j + i) * D, D), :] = part[:, i * 128 : (i + 1) * 128]
        return carry

    lax.fori_loop(0, 3, out_step, 0)
    drain(0, 0)
    drain(1, 0)

    left = lax.broadcasted_iota(jnp.int32, (LEN, 128), 1) < HDIM

    def sent(it):
        return red.ready(jnp.where(it <= -2, UP0, 2304 * (5 - it)))

    def score_rows(head, j, start, size):
        return rows_at((4 * head + j) * LEN + start, size)

    def attend(it, carry):
        pair = PAIRS - 1 - it
        slot = lax.rem(it, 2)

        @pl.when(it + 1 < PAIRS)
        def _():
            probs_copy(pair - 1, 1 - slot).start()

        red.feed(0, sent(it - 2), sent(it - 1))

        @pl.when(other == 0)
        def _():
            red.push(sent(it - 3), sent(it - 2))

        lax.fori_loop(2 + per_pair * it, 2 + per_pair * (it + 1), drain, 0)
        probs_copy(pair, slot).wait()
        query, key, value = qkv[3 * pair], qkv[3 * pair + 1], qkv[3 * pair + 2]
        grad = low[:, pl.ds(pl.multiple_of(pair * 128, 128), 128)]
        found = []
        for side in range(2):
            head = 2 * pair + side
            mine = left if side == 0 else jnp.logical_not(left)
            base = UP0 + slot * 8 * LEN + side * 4 * LEN
            for r in range(0, LEN, BROWS):
                part = grad[r : r + BROWS]
                d_probs = nt(jnp.where(mine[r : r + BROWS], part, jnp.zeros_like(part)), value)
                soft = jnp.concatenate(
                    [wall[0, rows_at(base + j * LEN + r, BROWS), :] for j in range(4)], axis=1
                ).astype(F32)
                inner = jnp.sum(soft * d_probs, axis=1, keepdims=True)
                scores = (soft * (d_probs - inner)).astype(BF16)
                for j in range(4):
                    wall[1, score_rows(head, j, r, BROWS), :] = scores[:, j * 128 : (j + 1) * 128]
            scores = jnp.concatenate([wall[1, score_rows(head, j, 0, LEN), :] for j in range(4)], axis=1)
            chances = jnp.concatenate([wall[0, rows_at(base + j * LEN, LEN), :] for j in range(4)], axis=1)
            found.append((nn(scores, key), tn(scores, query), tn(chances, grad)))
        d_query = (jnp.where(left, found[0][0], found[1][0]) * HDIM**-0.5).astype(BF16)
        d_key = jnp.where(left, found[0][1], found[1][1]).astype(BF16)
        d_value = jnp.where(left, found[0][2], found[1][2]).astype(BF16)
        both = jnp.concatenate([d_query, d_key, d_value], axis=1)
        plane, spot = spots["qv_bias"]
        small[plane, pl.ds(spot + pair, 1), :] = total_rows(d_query)
        small[plane, pl.ds(spot + 6 + pair, 1), :] = total_rows(d_value)
        at = pl.multiple_of(3 * pair * D, 16)
        weight = jnp.concatenate([wall[0, rows_at(at + i * D, D), :] for i in range(3)], axis=1)
        acc[...] += nt(both, weight)
        part = tn(rounded[...], both).astype(BF16)
        for i in range(3):
            gstack[0, rows_at(at + i * D, D), :] = part[:, i * 128 : (i + 1) * 128]
        return carry

    lax.fori_loop(0, PAIRS, attend, 0)
    red.feed(0, sent(4), sent(5))

    @pl.when(other == 0)
    def _():
        red.push(sent(3), sent(4))

    branch[...] = acc[...].astype(BF16)
    act_out = remote(branch.at[rows_at(other * half, half)], input_grad.at[fs], act_send.at[0], act_recv.at[0], red.x_peer)
    act_in = remote(branch.at[rows_at(other * half, half)], input_grad.at[other], act_send.at[0], act_recv.at[0], red.x_peer)
    act_own = pltpu.make_async_copy(branch.at[rows_at(fs * half, half)], input_grad.at[fs], act_sem.at[0])
    act_out.start()
    act_own.start()
    layout = tn(features[...], branch[...]).astype(BF16)
    for c in range(6):
        gstack[1, pl.ds(LAY1 + c * FEAT, FEAT), :] = layout[:, c * 128 : (c + 1) * 128]

    @pl.when(other == 0)
    def _():
        red.push(sent(4), sent(5))

    late = 2 + per_pair * PAIRS
    pace = 2 if fine else 5
    table_grads(wall, coord_row, coord_col, pick, keep, less, places, prefix, small, spots, red, late, pace)
    late += (23 + pace) // pace

    for plane in range(2):
        gstack[plane, pl.ds(SM0, 64), :] = small[plane].astype(BF16)
        gstack[plane, pl.ds(SM0 + 64, ROWS - SM0 - 64), :] = jnp.zeros((ROWS - SM0 - 64, 128), BF16)
        red.feed(plane, last, last + 1)
    red.push(last, last + 1)

    summed = red.count + SKEW * levels
    lax.fori_loop(late, summed, drain, 0)

    def squares(position, carry):
        piece = red.pieces[position].astype(F32)
        return carry + jnp.sum((piece * piece).reshape(-1, 8, 128), axis=0)

    value = lax.fori_loop(0, red.count, squares, jnp.zeros((8, 128), F32))
    value = jnp.sum(jnp.sum(value, axis=0, keepdims=True), axis=1, keepdims=True)
    norm[...] = jnp.broadcast_to(value, (8, 128))
    rounds = [
        [
            (member(dp, radix, stride, ((dp // stride) % radix + step) % radix), fs)
            for step in range(1, radix)
        ]
        for radix, stride in stages
    ] + [[red.core_peer], [red.x_peer]]

    def square_copies(number):
        base = sum(len(r) for r in rounds[:number])
        return [
            remote(norm.at[...], square_slots.at[base + i], n_send.at[base + i], n_recv.at[base + i], peer)
            for i, peer in enumerate(rounds[number])
        ]

    for number in range(max(red.ticks() - summed, len(rounds)) + 1):
        if number < len(rounds):
            for copy in square_copies(number):
                copy.start()
        if summed + number < red.ticks():
            red.tick(summed + number)
        if number < len(rounds):
            gathered = norm[...]
            base = sum(len(r) for r in rounds[:number])
            for i, copy in enumerate(square_copies(number)):
                copy.wait()
                gathered = gathered + square_slots[base + i]
            norm[...] = gathered
    norm[...] = jnp.sqrt(norm[...])

    red.finish()
    act_own.wait()
    act_out.wait_send()
    act_in.wait_recv()
    layer_own.wait()
    layer_copy(False).wait_send()
    layer_copy(True).wait_recv()


def table_grads(wall, coord_row, coord_col, pick, keep, less, places, prefix, small, spots, red, late, pace):
    block = 64
    for table in range(3):
        key_row = jnp.broadcast_to(coord_row[table : table + 1, :], (16, LEN))

        def less_rows(a, carry):
            at = pl.ds(pl.multiple_of(a * 16, 16), 16)
            near = jnp.broadcast_to(coord_col[at, table : table + 1], (16, LEN))
            less[at, :] = jnp.where(near <= key_row, 1.0, 0.0).astype(BF16)
            return carry

        lax.fori_loop(0, LEN // 16, less_rows, 0, unroll=4)

        def query_rows(b, sums):
            @pl.when(lax.rem(table * 8 + b, pace) == 0)
            def _():
                red.tick(late + (table * 8 + b) // pace)

            start = b * block
            scores = jnp.concatenate(
                [
                    jnp.concatenate(
                        [wall[1, rows_at((4 * h + j) * LEN + start, block), :] for j in range(4)], axis=1
                    )
                    for h in range(HEADS)
                ],
                axis=0,
            )
            prefix[...] = nn(scores, less[...]).reshape(HEADS, block, LEN)

            def pick_up(a, carry):
                at = pl.ds(pl.multiple_of(a * 8, 8), 8)
                place_of = places[table, pl.ds(pl.multiple_of(start + a * 8, 8), 8), :]
                low, high = place_of & 127, place_of >> 7
                result = []
                for h in range(HEADS):
                    value = jnp.zeros((8, 128), F32)
                    for j in range(4):
                        part = jnp.take_along_axis(prefix[h, at, j * 128 : (j + 1) * 128], low, axis=1)
                        value = jnp.where(high == j, part, value)
                    result.append(carry[h] + value)
                return tuple(result)

            return lax.fori_loop(0, block // 8, pick_up, sums, unroll=4)

        sums = lax.fori_loop(
            0, LEN // block, query_rows, tuple(jnp.zeros((8, 128), F32) for _ in range(HEADS))
        )
        heads = jnp.concatenate(
            [jnp.sum(s, axis=0, keepdims=True) for s in sums] + [jnp.zeros((4, 128), F32)], axis=0
        )
        after = pltpu.roll(heads, 127, 1)
        whole = pltpu.roll(heads, 15, 1)
        lanes = lax.broadcasted_iota(jnp.int32, (16, 128), 1)
        buckets = jnp.where(lanes < 16, heads - after, after - heads)
        buckets = jnp.where(lanes == 15, heads, buckets)
        buckets = jnp.where(lanes == 16, 0.0, buckets)
        buckets = jnp.where(lanes == 31, whole - heads, buckets)
        buckets = jnp.where(lanes < 32, buckets, 0.0)
        placed = buckets if table == 0 else pltpu.roll(buckets, 32 * table, 1)
        flat_row = jnp.sum(nt(placed.astype(BF16), pick[table]) * keep[...], axis=0, keepdims=True)
        plane, at = spots["tables"]
        for i in range(3):
            row_at = at + 3 * table + i
            small[plane, row_at : row_at + 1, :] = flat_row[:, i * 128 : (i + 1) * 128]


def backward_pass(stages, wall, cdoc, total, out_doc, saved, features, coord_row, coord_col):
    pick, keep = table_constants()
    sds = jax.ShapeDtypeStruct
    count_peers = 2 + sum(radix - 1 for radix, _ in stages)
    dma = pltpu.SemaphoreType.DMA
    buffers, sems = reduction_scratch(stages)
    return pl.pallas_call(
        functools.partial(backward_kernel, stages),
        name="backward_reduce",
        out_shape=(sds((2, LEN // 2, D), BF16), sds((2, LEN // 2, D), BF16), sds((ROWS, 128), BF16), sds((8, 128), F32)),
        in_specs=[ANY, ANY, VMEM, ANY, ANY, ANY, ANY, ANY, ANY, VMEM, ANY, ANY, ANY, ANY, VMEM, ANY] + [VMEM] * 5,
        out_specs=(ANY, ANY, ANY, VMEM),
        scratch_shapes=[
            pltpu.VMEM((2, ROWS, 128), BF16),
            pltpu.VMEM((2, ROWS, 128), BF16),
            pltpu.VMEM((LEN, D), F32),
            pltpu.VMEM((LEN, D), BF16),
            pltpu.VMEM((LEN, FF), BF16),
            pltpu.VMEM((LEN, FF), BF16),
            pltpu.VMEM((LEN, D), BF16),
            pltpu.VMEM((LEN, D), BF16),
            pltpu.VMEM((18, LEN, 128), BF16),
            pltpu.VMEM((LEN, D), BF16),
            pltpu.VMEM((LEN, D), F32),
            pltpu.VMEM((LEN, LEN), BF16),
            pltpu.VMEM((3, LEN, 128), jnp.int32),
            pltpu.VMEM((HEADS, 64, LEN), F32),
            pltpu.VMEM((2, 64, 128), F32),
            pltpu.VMEM((count_peers, 8, 128), F32),
            dma((10,)), dma((5, 12)), dma((2,)), dma((2,)), dma((2,)), dma((2,)), dma((count_peers,)), dma((count_peers,)),
        ]
        + buffers
        + sems,
        compiler_params=pltpu.CompilerParams(
            collective_id=2, has_side_effects=True, vmem_limit_bytes=64 * 2**20 - 2**16
        ),
    )(wall, cdoc, total, out_doc, *saved, features, coord_row, coord_col, jnp.asarray(pick), jnp.asarray(keep))


BLOCK = 1760


def flatten_rows(plane, source, flat):
    def block(src, dst, count, stride):
        flat[pl.ds(LEAD + dst, count, stride=stride), :] = source[pl.ds(src, count), :].astype(F32)

    if plane == 0:
        for c in range(24):
            block(UP0 + c * UP_A, F_UP + c, UP_A, 24)
        for pos in range(18):
            block(pos * D, (pos % 3) * 6 + pos // 3, D, 18)
        for c in range(6):
            block(OUT0 + c * D, F_OUT + c, D, 6)
        small = source[pl.ds(SM0, 64), :].astype(F32)
        flat[pl.ds(LEAD + 13824, 12), :] = small[0:12]
        flat[pl.ds(LEAD + 18444, 18), :] = small[12:30]
    else:
        for c in range(24):
            block(UP1 + c * UP_B, c - 98, UP_B, 24)
        for j in range(12):
            for c in range(6):
                block(DOWN1 + j * 1536 + c * 256, F_DOWN1 + j * 1536 + c, 256, 6)
        for c in range(6):
            block(LAY1 + c * FEAT, F_LAY1 + c, FEAT, 6)
        small = source[pl.ds(SM1, 64), :].astype(F32)
        flat[pl.ds(LEAD + F_UPB1, 24), :] = small[0:24]
        flat[pl.ds(LEAD + F_SM1, 18), :] = small[24:42]
        flat[pl.ds(LEAD + F_TAB1, 9), :] = small[42:51]
        rest = FLAT - F_TAB1 - 9
        flat[pl.ds(LEAD + F_TAB1 + 9, rest), :] = jnp.zeros((rest, 128), F32)


def adam_kernel(source, weights, first, second, grad_out, update_out, first_out, flat):
    step = pl.program_id(0)
    fs = lax.axis_index("fsdp")

    @pl.when(step == 0)
    def _():
        @pl.when(fs == 0)
        def _():
            flatten_rows(0, source, flat)

        @pl.when(fs == 1)
        def _():
            flatten_rows(1, source, flat)

    part = 160
    row = lax.broadcasted_iota(jnp.int32, (part, 128), 0)

    def some(i, carry):
        at = pl.ds(pl.multiple_of(i * part, 8), part)
        begin = pl.multiple_of(step * BLOCK + i * part, 8)
        grad = flat[pl.ds(LEAD + begin, part), :]
        grad_out[at, :] = grad
        new_first = adam_one * first[at, :] + (1.0 - adam_one) * grad
        new_second = adam_two * second[at, :] + (1.0 - adam_two) * grad * grad
        corrected = (
            new_first
            / (1.0 - adam_one**adam_steps)
            / (jnp.sqrt(new_second / (1.0 - adam_two**adam_steps)) + adam_eps)
        )
        rate = jnp.where((fs == 1) & (row + begin >= F_LAY1), table_factor, 1.0)
        update_out[at, :] = rate * (corrected + decay_rate * weights[at, :])
        first_out[at, :] = new_first
        return carry

    lax.fori_loop(0, BLOCK // part, some, 0)


def adam(source, weights, first, second):
    block = pl.BlockSpec((BLOCK, 128), lambda i: (i, 0))
    vector = jax.ShapeDtypeStruct((FLAT, 128), F32)
    return pl.pallas_call(
        adam_kernel,
        name="adamw",
        grid=(FLAT // BLOCK,),
        out_shape=(vector, vector, vector),
        in_specs=[VMEM, block, block, block],
        out_specs=(block, block, block),
        scratch_shapes=[pltpu.VMEM((LEAD + FLAT + 288, 128), F32)],
        compiler_params=pltpu.CompilerParams(vmem_limit_bytes=60 * 2**20),
    )(source, weights, first, second)


def layout_features(coords):
    freq_count = FEAT // 8
    factors = (jnp.arange(freq_count, dtype=jnp.int32) + 1) ** 2
    phases = coords[..., :, None] * factors % 4096
    angles = phases.astype(F32) * (2.0 * math.pi / 4096.0)
    wave_parts = jnp.concatenate([jnp.sin(angles), jnp.cos(angles)], axis=-1)
    return wave_parts.reshape(coords.shape[:-1] + (FEAT,))


def local(stages, inputs, box_coords, mlm_mask, cotangent, params, first_moment, second_moment):
    fs = lax.axis_index("fsdp")
    masked = cotangent * mlm_mask.astype(BF16)[..., None]
    count = jnp.full((8, 128), jnp.sum(mlm_mask.astype(F32)))
    boxes = lax.dynamic_index_in_dim(box_coords, fs, 0, keepdims=False)
    features = layout_features(boxes).astype(BF16)
    coord_col = jnp.stack(
        [jnp.arange(LEN, dtype=jnp.int32), boxes[:, 0] + boxes[:, 2], boxes[:, 1] + boxes[:, 3]], axis=1
    )
    coord_row = coord_col.T
    flat = [v.reshape(FLAT, 128) for v in (params, first_moment, second_moment)]
    wall, cdoc, total, *saved, out_doc = forward_pass(
        stages, flat[0], inputs, masked, count, features, coord_row, coord_col
    )
    layer_out, input_grad, reduced, norm = backward_pass(
        stages, wall, cdoc, total, out_doc, saved, features, coord_row, coord_col
    )
    grad, update, new_first = adam(reduced, *flat)
    return (layer_out, input_grad, grad.reshape(-1), norm[0, 0], update.reshape(-1), new_first.reshape(-1))


def solution(mesh):
    in_specs = (
        P("dp", "fsdp", None),
        P("dp", None, None),
        P("dp", "fsdp"),
        P("dp", "fsdp", None),
        P("fsdp"),
        P("fsdp"),
        P("fsdp"),
    )
    out_specs = (P("dp", "fsdp", None), P("dp", "fsdp", None), P("fsdp"), P(), P("fsdp"), P("fsdp"))
    stages = radices(mesh.shape["dp"])
    return jax.shard_map(
        functools.partial(local, stages), mesh=mesh, in_specs=in_specs, out_specs=out_specs, check_vma=False
    )
```

```python
import functools
import math

import jax
import jax.numpy as jnp
import numpy as np
from jax import lax
from jax.experimental import pallas as pl
from jax.experimental.pallas import tpu as pltpu
from jax.sharding import PartitionSpec as P

D = 768
HEADS = 12
HDIM = 64
FF = 3072
BUCKETS = 32
FEAT = 128
LEN = 512
PADDED = 7208960
SHARD = PADDED // 2
FLAT = SHARD // 128
PAIRS = HEADS // 2
QROWS = 256
AROWS = 512
BROWS = 256
SKEW = 2

norm_eps = 1e-05
adam_one = 0.9
adam_two = 0.999
adam_eps = 1e-08
adam_steps = 100.0
decay_rate = 0.01
table_factor = 5.0

MESH = pl.DeviceIdType.MESH
F32 = jnp.float32
BF16 = jnp.bfloat16
VMEM = pl.BlockSpec(memory_space=pltpu.VMEM)
ANY = pl.BlockSpec(memory_space=pl.ANY)

ROWS = 28672
CHUNK = 2048
CHUNKS = ROWS // CHUNK
CUT = 404
UP_A, UP_B = 416, 368
OUT0 = 18 * D
UP0 = OUT0 + 6 * D
SM0 = UP0 + 24 * UP_A
UP1 = 0
DOWN1 = 24 * UP_B
DOWN_END = DOWN1 + 6 * FF
LAY1 = 27648
SM1 = LAY1 + 6 * FEAT
F_OUT = 13836
F_UP = 18462
F_UPB1 = 8734
F_DOWN1 = 8758
F_SM1 = 27190
F_LAY1 = 27208
F_TAB1 = 27976
LEAD = 104


def nt(a, b):
    return lax.dot_general(a, b, (((1,), (1,)), ((), ())), preferred_element_type=F32)


def nn(a, b):
    return lax.dot_general(a, b, (((1,), (0,)), ((), ())), preferred_element_type=F32)


def tn(a, b):
    return lax.dot_general(a, b, (((0,), (0,)), ((), ())), preferred_element_type=F32)


def radices(replicas):
    stages, stride, left = [], 2, replicas // 2
    if left % 2 == 0:
        stages.append((2, stride))
        stride, left = stride * 2, left // 2
    while left > 1:
        radix = left if left <= 8 else 4
        stages.append((radix, stride))
        stride, left = stride * radix, left // radix
    return stages


def place():
    return lax.axis_index("dp"), lax.axis_index("fsdp")


def member(dp, radix, stride, digit):
    return dp + (digit - (dp // stride) % radix) * stride


def peers(stages):
    dp, fs = place()
    found = [(dp + 1 - 2 * (dp % 2), fs), (dp, 1 - fs)]
    for radix, stride in stages:
        mine = (dp // stride) % radix
        for step in range(1, radix):
            found.append((member(dp, radix, stride, (mine + step) % radix), fs))
    return found


def greet_signal(stages):
    barrier = pltpu.get_barrier_semaphore()
    for peer in peers(stages):
        pl.semaphore_signal(barrier, inc=1, device_id=peer, device_id_type=MESH)


def greet_wait(stages):
    pl.semaphore_wait(pltpu.get_barrier_semaphore(), len(peers(stages)))


def remote(src, dst, send, recv, peer):
    return pltpu.make_async_remote_copy(
        src_ref=src, dst_ref=dst, send_sem=send, recv_sem=recv, device_id=peer, device_id_type=MESH
    )


def rows_at(start, size):
    return pl.ds(pl.multiple_of(start, 16), size)


def offsets(dp, stages, extent):
    size = extent // 2
    start = (dp % 2) * size
    found = [(start, size)]
    for radix, stride in stages:
        size = size // radix
        start = start + ((dp // stride) % radix) * size
        found.append((start, size))
    return found


def row_of(ref_rows, start, count):
    return jnp.concatenate([ref_rows[start + i : start + i + 1, :] for i in range(count)], axis=1)


def table_constants():
    width = BUCKETS * HEADS
    lane = np.arange(width)
    pick = np.zeros((3, width, 128), np.float32)
    for table in range(3):
        pick[table, lane, 32 * table + lane // HEADS] = 1.0
    keep = (lane[None, :] % HEADS == np.arange(16)[:, None]).astype(np.float32)
    return pick.astype(jnp.bfloat16), keep


def bucket_of(offset):
    spread = jnp.abs(offset)
    result = jnp.minimum(spread, 8) + jnp.where(offset > 0, 16, 0)
    for level in range(9, 16):
        result = result + jnp.where(spread >= 8 * 2 ** (level - 8), 1, 0)
    return result


def up_block(wall, j):
    columns = []
    for c in (2 * j, 2 * j + 1):
        first = wall[0, rows_at(UP0 + c * UP_A, UP_A), :]
        second = wall[1, rows_at(UP1 + c * UP_B + 16, UP_B - 16), :]
        columns.append(jnp.concatenate([first, second], axis=0))
    return jnp.concatenate(columns, axis=1)


def down_rows(wall, j):
    return jnp.concatenate(
        [wall[1, rows_at(DOWN1 + j * 1536 + c * 256, 256), :] for c in range(6)], axis=1
    )


def merge_up(wall):
    row = lax.broadcasted_iota(jnp.int32, (16, 128), 0)

    def one(c, carry):
        low_at = rows_at(UP0 + c * UP_A + UP_A - 16, 16)
        low = wall[0, low_at, :].astype(F32)
        high = wall[1, rows_at(UP1 + c * UP_B, 16), :].astype(F32)
        cut = jnp.where(c < 2, CUT + 1 - 400, CUT - 400)
        wall[0, low_at, :] = jnp.where(row < cut, low, high).astype(BF16)
        return carry

    lax.fori_loop(0, 24, one, 0)


def stats(values):
    mean = jnp.mean(values, axis=1, keepdims=True)
    centered = values - mean
    inverse = lax.rsqrt(jnp.mean(centered * centered, axis=1, keepdims=True) + norm_eps)
    return centered * inverse, inverse


def find_places(coord_col, lut, ranks, places):
    lane = lax.broadcasted_iota(jnp.int32, (8, 128), 1)
    step = lane % 16
    level = jnp.where(step <= 8, step, lax.shift_left(jnp.full_like(step, 8), jnp.maximum(step - 8, 0)))
    edge = jnp.where(lane < 16, 1 - level, jnp.where(lane == 16, 1 << 12, level))

    def line_rows(a, carry):
        at = pl.ds(pl.multiple_of(a * 8, 8), 8)
        value = coord_col[at, 0:1] + edge
        places[0, at, :] = jnp.where(value <= 0, LEN, jnp.minimum(value, LEN) - 1)
        return carry

    lax.fori_loop(0, LEN // 8, line_rows, 0, unroll=4)
    lanes = lax.broadcasted_iota(jnp.int32, (LEN, 128), 1)
    ones = jnp.ones((LEN, 128), BF16)

    def flags(condition):
        return jnp.where(condition, 1.0, 0.0).astype(BF16)

    for table in (1, 2):
        near = jnp.broadcast_to(coord_col[:, table : table + 1], (LEN, 128))
        group = near >> 7
        below = tn(flags(group == lanes), flags((near & 127) < lanes)) + tn(flags(group < lanes), ones)
        lut[...] = below[:16].astype(jnp.int32)
        luts = [jnp.broadcast_to(lut[g : g + 1, :], (8, 128)) for g in range(16)]

        def find(a, carry):
            at = pl.ds(pl.multiple_of(a * 8, 8), 8)
            value = jnp.clip(coord_col[at, table : table + 1] + edge, 0, 2047)
            low, high = value & 127, value >> 7
            found = jnp.zeros((8, 128), jnp.int32)
            for g in range(16):
                found = jnp.where(high == g, jnp.take_along_axis(luts[g], low, axis=1), found)
            places[table, at, :] = jnp.where(found == 0, LEN, found - 1)
            return carry

        lax.fori_loop(0, LEN // 8, find, 0, unroll=8)


def relayout(plane, flat, out, group):
    def blocks(count, dst, src, rows, stride):
        def one(i, carry):
            out[plane, rows_at(dst(i), rows), :] = flat[pl.ds(LEAD + src(i), rows, stride=stride), :].astype(BF16)
            return carry

        lax.fori_loop(0, count, one, 0)

    def window(dst, src, count):
        out[plane, pl.ds(dst, count), :] = flat[pl.ds(LEAD + src, count), :].astype(BF16)

    def clear(low, high):
        out[plane, pl.ds(low, high - low), :] = jnp.zeros((high - low, 128), BF16)

    if plane == 0 and group == 0:
        blocks(24, lambda c: UP0 + c * UP_A, lambda c: F_UP + c, UP_A, 24)
        window(SM0, 13824, 16)
        window(SM0 + 16, 18440, 32)
        clear(SM0 + 48, ROWS)
    elif plane == 0 and group == 1:
        blocks(18, lambda pos: pos * D, lambda pos: lax.rem(pos, 3) * 6 + pos // 3, D, 18)
    elif plane == 0:
        blocks(6, lambda c: OUT0 + c * D, lambda c: F_OUT + c, D, 6)
    elif group == 0:
        for c in range(6):
            blocks(12, lambda j: DOWN1 + j * 1536 + c * 256, lambda j: F_DOWN1 + j * 1536 + c, 256, 6)
        clear(DOWN_END, LAY1)
        blocks(6, lambda c: LAY1 + c * FEAT, lambda c: F_LAY1 + c, FEAT, 6)
        window(SM1, 8728, 32)
        window(SM1 + 32, 27184, 32)
        window(SM1 + 64, 27976, 16)
        clear(SM1 + 80, ROWS)
    elif group == 1:
        blocks(24, lambda c: UP1 + c * UP_B, lambda c: c - 98, UP_B, 24)


class Gather:
    def __init__(self, stages, zall, x_send, x_recv, c_send, c_recv, sems):
        self.stages, self.zall, self.sems = stages, zall, sems
        self.x_send, self.x_recv, self.c_send, self.c_recv = x_send, x_recv, c_send, c_recv
        self.dp, self.fs = place()
        self.other = 1 - self.fs
        self.levels = len(stages)
        self.parts = offsets(self.dp, stages, CHUNK)
        self.x_peer = (self.dp, self.other)
        self.core_peer = (self.dp + 1 - 2 * (self.dp % 2), self.fs)

    def base(self, position):
        return lax.rem(CHUNKS - 1 + position, CHUNKS) * CHUNK

    def direct(self, position):
        return (position == 2) | (position == 6) | (position == 10)

    def x_copy(self, position, plane, direct):
        start, size = self.parts[0] if direct else self.parts[-1]
        where = self.zall.at[plane, rows_at(self.base(position) + start, size)]
        return remote(where, where, self.x_send.at[0], self.x_recv.at[position], self.x_peer)

    def send(self, low, high):
        def one(position, carry):
            direct = self.direct(position)

            @pl.when(direct)
            def _():
                self.x_copy(position, self.fs, True).start()

            @pl.when(jnp.logical_not(direct))
            def _():
                self.x_copy(position, self.fs, False).start()

            return carry

        lax.fori_loop(low, high, one, 0)

    def stage_copies(self, level, position):
        radix, stride = self.stages[level]
        start, size = self.parts[level + 1]
        mine = (self.dp // stride) % radix
        copies = []
        for step in range(1, radix):
            peer = (member(self.dp, radix, stride, (mine + step) % radix), self.fs)
            where = self.zall.at[self.other, rows_at(self.base(position) + start, size)]
            copies.append(
                remote(where, where, self.sems[2 * level].at[0], self.sems[2 * level + 1].at[position], peer)
            )
        return copies

    def stage_wait(self, level, position):
        size = (self.stages[level][0] - 1) * self.parts[level + 1][1]
        where = self.zall.at[self.other, rows_at(self.base(position) + self.parts[level][0], size)]
        remote(
            where, where, self.sems[2 * level].at[0], self.sems[2 * level + 1].at[position], self.x_peer
        ).wait_recv()

    def core_copy(self, position, receive):
        size = CHUNK // 2
        start = (1 - self.dp % 2 if receive else self.dp % 2) * size
        where = self.zall.at[self.other, rows_at(self.base(position) + start, size)]
        return remote(where, where, self.c_send.at[0], self.c_recv.at[position], self.core_peer)

    def work(self, position, step):
        direct = self.direct(position)
        levels = self.levels
        if step == levels + 1:
            self.core_copy(position, True).wait_recv()
            return
        if step == 0:

            @pl.when(direct)
            def _():
                self.x_copy(position, self.other, True).wait_recv()
                self.core_copy(position, False).start()

        @pl.when(jnp.logical_not(direct))
        def _():
            if step == 0:
                self.x_copy(position, self.other, False).wait_recv()
            else:
                self.stage_wait(levels - step, position)
            if step < levels:
                for copy in self.stage_copies(levels - 1 - step, position):
                    copy.start()
            else:
                self.core_copy(position, False).start()

    def tick(self, number):
        for step in range(self.levels + 1, -1, -1):
            position = number - SKEW * step

            @pl.when((position >= 0) & (position < CHUNKS))
            def _(position=position, step=step):
                self.work(position, step)

    def ticks(self):
        return CHUNKS + SKEW * (self.levels + 1)

    def finish(self):
        staged = CHUNKS - 3
        sent = [(self.x_send, 3 * self.parts[0][1] + staged * self.parts[-1][1]), (self.c_send, CHUNKS * CHUNK // 2)]
        for level, (radix, _) in enumerate(self.stages):
            sent.append((self.sems[2 * level], staged * (radix - 1) * self.parts[level + 1][1]))
        for sem, size in sent:
            where = self.zall.at[0, pl.ds(0, size)]
            remote(where, where, sem.at[0], self.x_recv.at[0], self.x_peer).wait_send()


def forward_kernel(
    stages, p_hbm, xin, cot, cnt, features, coord_row, coord_col, pick, keep,
    wall_out, cdoc_out, total, rounded_out, qkv_out, probs_out, mixed_out, one_out, inverse_one, low_out, hidden_out,
    slope_out, two_out, inverse_two, layer_out,
    flat, wall, xs, cs, cnt_slots, start, up_bias, acc, indices, short, rounded, qkv, probs, mixed, normed, low, hidden,
    slope, layer,
    in_sem, x_send, x_recv, c_send, c_recv, act_send, act_recv, n_send, n_recv, out_sem, probs_sem, feed_sem, *stage_sems,
):
    net = Gather(stages, wall, x_send, x_recv, c_send, c_recv, stage_sems)
    dp, fs, other = net.dp, net.fs, net.other
    half = LEN // 2
    pieces = 8
    span = FLAT // pieces
    loads = [
        pltpu.make_async_copy(
            p_hbm.at[pl.ds(i * span, span)], flat.at[pl.ds(LEAD + i * span, span)], in_sem.at[i]
        )
        for i in range(pieces)
    ]
    for load in loads:
        load.start()
    flat[pl.ds(0, LEAD), :] = jnp.zeros((LEAD, 128), F32)
    flat[pl.ds(LEAD + FLAT, 288), :] = jnp.zeros((288, 128), F32)
    greet_signal(stages)

    def index_rows(a, carry):
        at = pl.ds(pl.multiple_of(a * 8, 8), 8)
        for table in range(3):
            near = jnp.broadcast_to(coord_col[at, table : table + 1], (8, 128))
            for j in range(4):
                far = coord_row[table : table + 1, j * 128 : (j + 1) * 128]
                indices[table, at, j * 128 : (j + 1) * 128] = (
                    bucket_of(jnp.broadcast_to(far, (8, 128)) - near) + 32 * table
                )
        return carry

    lax.fori_loop(0, LEN // 8, index_rows, 0, unroll=4)
    greet_wait(stages)

    def act_copy(number, source, target, receive):
        where = rows_at((other if receive else fs) * half, half)
        return remote(source.at[other], target.at[where], act_send.at[number], act_recv.at[number], net.x_peer)

    rounds = [
        [
            (member(dp, radix, stride, ((dp // stride) % radix + step) % radix), fs)
            for step in range(1, radix)
        ]
        for radix, stride in stages
    ] + [[net.core_peer], [net.x_peer]]

    def count_copies(number):
        base = sum(len(r) for r in rounds[:number])
        return [
            remote(total.at[...], cnt_slots.at[base + i], n_send.at[base + i], n_recv.at[base + i], peer)
            for i, peer in enumerate(rounds[number])
        ]

    def count_round(number):
        if 0 < number <= len(rounds):
            gathered = total[...]
            base = sum(len(r) for r in rounds[: number - 1])
            for i, copy in enumerate(count_copies(number - 1)):
                copy.wait()
                gathered = gathered + cnt_slots[base + i]
            total[...] = gathered
        if number < len(rounds):
            for copy in count_copies(number):
                copy.start()

    total[...] = cnt[...]
    count_round(0)
    for load in loads:
        load.wait()

    for plane, windows in enumerate((((13824, 16), (18440, 32)), ((8728, 32), (27184, 32), (27976, 16)))):

        @pl.when(fs == plane)
        def _(plane=plane, windows=windows):
            dst = 0
            for src, size in windows:
                short[plane, pl.ds(dst, size), :] = flat[pl.ds(LEAD + src, size), :].astype(BF16)
                dst += size
            short[plane, pl.ds(dst, 96 - dst), :] = jnp.zeros((96 - dst, 128), BF16)

    def short_copy(plane):
        return remote(short.at[plane], short.at[plane], act_send.at[2], act_recv.at[2], net.x_peer)

    short_copy(fs).start()
    for group, (low_at, high_at) in enumerate(((0, 1), (1, 7), (7, CHUNKS))):
        for plane in range(2):

            @pl.when(fs == plane)
            def _(plane=plane, group=group):
                relayout(plane, flat, wall, group)

        net.send(low_at, high_at)
        if group == 1:
            act_copy(0, xin, xs, False).start()
    xs[pl.ds(fs * half, half), :] = xin[fs]
    cs[pl.ds(fs * half, half), :] = cot[fs]
    count_round(1)

    count_round(2)
    outs = []

    def put(source, target):
        copy = pltpu.make_async_copy(source, target, out_sem.at[len(outs)])
        copy.start()
        outs.append(copy)

    short_copy(other).wait_recv()

    small0, small1 = short[0].astype(F32), short[1].astype(F32)
    heads_by_lane = jnp.zeros((16, 128), F32)
    for table in range(3):
        flat_row = row_of(small1, 64 + 3 * table, 3)
        spread = (jnp.broadcast_to(flat_row, (16, 384)) * keep[...]).astype(BF16)
        heads_by_lane = heads_by_lane + nn(spread, pick[table])
    rows_by_head = [jnp.broadcast_to(heads_by_lane[h : h + 1, :], (8, 128)) for h in range(HEADS)]

    def bias_rows(a, carry):
        @pl.when(lax.rem(a, 2) == 0)
        def _():
            net.tick(a // 2)

        for b in range(4):
            row = a * 32 + b * 8
            at = pl.ds(pl.multiple_of(row, 8), 8)
            for j in range(4):
                sums = [None] * HEADS
                for table in range(3):
                    index = indices[table, at, j * 128 : (j + 1) * 128]
                    for h in range(HEADS):
                        found = jnp.take_along_axis(rows_by_head[h], index, axis=1)
                        sums[h] = found if sums[h] is None else sums[h] + found
                for h in range(HEADS):
                    flat[pl.ds(pl.multiple_of((4 * h + j) * LEN + row, 8), 8), :] = sums[h]
        return carry

    lax.fori_loop(0, LEN // 32, bias_rows, 0)

    act_copy(1, cot, cs, False).start()
    count_round(3)
    lag = SKEW * (net.levels + 1)

    def drain(number, carry):
        net.tick(number)
        return carry

    lax.fori_loop(LEN // 64, 2 + lag, drain, 0)
    qv_bias = row_of(small0, 0, 12)
    out_bias, gain_one, shift_one = (row_of(small0, 20 + 6 * i, 6) for i in range(3))
    down_bias, gain_two, shift_two = (row_of(small1, 38 + 6 * i, 6) for i in range(3))
    act_copy(0, xin, xs, True).wait_recv()

    w_layout = jnp.concatenate([wall[1, pl.ds(LAY1 + c * FEAT, FEAT), :] for c in range(6)], axis=1)

    def start_rows(r, carry):
        at = pl.ds(pl.multiple_of(r * QROWS, QROWS), QROWS)
        rows = xs[at, :].astype(F32) + nn(features[at, :], w_layout)
        start[at, :] = rows
        rounded[at, :] = rows.astype(BF16)
        return carry

    lax.fori_loop(0, LEN // QROWS, start_rows, 0)
    put(rounded, rounded_out)
    for i in range(18):
        up_bias[:, i * 128 : (i + 1) * 128] = (
            jnp.zeros((1, 128), F32)
            if i % 3 == 1
            else qv_bias[:, (i // 3 + 3 * (i % 3)) * 128 : (i // 3 + 3 * (i % 3) + 1) * 128]
        )
    left = lax.broadcasted_iota(jnp.int32, (LEN, 128), 1) < HDIM

    def probs_copy(pair):
        where = rows_at(pair * 8 * LEN, 8 * LEN)
        return pltpu.make_async_copy(probs.at[where], probs_out.at[where], probs_sem.at[pair])

    def attend(pair, carry):
        net.tick(2 + lag + pair)
        at = pl.multiple_of(3 * pair * D, 16)
        weight = jnp.concatenate([wall[0, rows_at(at + i * D, D), :] for i in range(3)], axis=1)
        part = nn(rounded[...], weight) + up_bias[:, pl.ds(pl.multiple_of(pair * 384, 128), 384)]
        query = part[:, :128].astype(BF16) * HDIM**-0.5
        key = part[:, 128:256].astype(BF16)
        value = part[:, 256:].astype(BF16)
        qkv[3 * pair] = query
        qkv[3 * pair + 1] = key
        qkv[3 * pair + 2] = value
        found = [[], []]
        for side in range(2):
            head = 2 * pair + side
            mine = left if side == 0 else jnp.logical_not(left)
            for r in range(0, LEN, AROWS):
                some = query[r : r + AROWS]
                extra = jnp.concatenate(
                    [flat[rows_at((4 * head + j) * LEN + r, AROWS), :] for j in range(4)], axis=1
                )
                scores = nt(jnp.where(mine[r : r + AROWS], some, jnp.zeros_like(some)), key) + extra
                scores = jnp.exp(scores - jnp.max(scores, axis=1, keepdims=True))
                soft = (scores * (1.0 / jnp.sum(scores, axis=1, keepdims=True))).astype(BF16)
                for j in range(4):
                    probs[rows_at((4 * head + j) * LEN + r, AROWS), :] = soft[:, j * 128 : (j + 1) * 128]
                found[side].append(nn(soft, value))
        mixed[:, pl.ds(pl.multiple_of(pair * 128, 128), 128)] = jnp.where(
            left, jnp.concatenate(found[0], axis=0), jnp.concatenate(found[1], axis=0)
        ).astype(BF16)
        probs_copy(pair).start()
        return carry

    lax.fori_loop(0, PAIRS, attend, 0)
    put(qkv, qkv_out)
    put(mixed, mixed_out)
    count_round(4)
    lax.fori_loop(2 + lag + PAIRS, 10 + lag, drain, 0)

    w_out = jnp.concatenate([wall[0, pl.ds(OUT0 + c * D, D), :] for c in range(6)], axis=1)

    def first_rows(r, carry):
        at = pl.ds(pl.multiple_of(r * QROWS, QROWS), QROWS)
        unit, inverse = stats(start[at, :] + nn(mixed[at, :], w_out) + out_bias)
        normed[at, :] = unit
        inverse_one[at, :] = inverse
        result = unit * gain_one + shift_one
        low[at, :] = result.astype(BF16)
        acc[at, :] = result + down_bias
        return carry

    lax.fori_loop(0, LEN // QROWS, first_rows, 0)
    put(normed, one_out)
    put(low, low_out)
    count_round(5)
    lax.fori_loop(10 + lag, net.ticks(), drain, 0)
    net.finish()
    merge_up(wall)
    put(wall, wall_out)
    for j in range(12):
        up_bias[:, j * 256 : (j + 1) * 256] = row_of(small1, 6 + 2 * j, 2)

    def feed_copies(j):
        lanes = pl.ds(pl.multiple_of(j * 256, 256), 256)
        return [
            pltpu.make_async_copy(hidden.at[:, lanes], hidden_out.at[:, lanes], feed_sem.at[0, j]),
            pltpu.make_async_copy(slope.at[:, lanes], slope_out.at[:, lanes], feed_sem.at[1, j]),
        ]

    def feed_step(j, carry):
        lanes = pl.ds(pl.multiple_of(j * 256, 256), 256)
        up = nn(low[...], up_block(wall, j)) + up_bias[:, lanes]
        half_up = 0.5 + 0.5 * lax.erf(up * math.sqrt(0.5))
        bell = jnp.exp(-0.5 * up * up) * (1.0 / math.sqrt(2.0 * math.pi))
        slope[:, lanes] = (half_up + up * bell).astype(BF16)
        part = (up * half_up).astype(BF16)
        hidden[:, lanes] = part
        acc[...] += nn(part, down_rows(wall, j))
        for copy in feed_copies(j):
            copy.start()
        return carry

    lax.fori_loop(0, 12, feed_step, 0, unroll=3)

    def second_rows(r, carry):
        at = pl.ds(pl.multiple_of(r * QROWS, QROWS), QROWS)
        unit, inverse = stats(acc[at, :])
        acc[at, :] = unit
        inverse_two[at, :] = inverse
        layer[at, :] = (unit * gain_two + shift_two).astype(BF16)
        return carry

    lax.fori_loop(0, LEN // QROWS, second_rows, 0)
    put(acc, two_out)
    put(layer, layer_out)
    act_copy(1, cot, cs, True).wait_recv()
    put(cs, cdoc_out)
    for number in range(2):
        act_copy(number, (xin, cot)[number], (xs, cs)[number], False).wait_send()
    short_copy(fs).wait_send()
    for pair in range(PAIRS):
        probs_copy(pair).wait()
    for copy in outs:
        copy.wait()

    def feed_wait(j, carry):
        for copy in feed_copies(j):
            copy.wait()
        return carry

    lax.fori_loop(0, 12, feed_wait, 0)


def forward_pass(stages, p2, xin, cot, cnt, features, coord_row, coord_col):
    pick, keep = table_constants()
    sds = jax.ShapeDtypeStruct
    dma = pltpu.SemaphoreType.DMA
    count_peers = 2 + sum(radix - 1 for radix, _ in stages)
    sems = []
    for radix, _ in stages:
        sems += [dma((1,)), dma((CHUNKS,))]
    return pl.pallas_call(
        functools.partial(forward_kernel, stages),
        name="gather_forward",
        out_shape=(
            sds((2, ROWS, 128), BF16),
            sds((LEN, D), BF16),
            sds((8, 128), F32),
            sds((LEN, D), BF16),
            sds((18, LEN, 128), BF16),
            sds((HEADS * 4 * LEN, 128), BF16),
            sds((LEN, D), BF16),
            sds((LEN, D), F32),
            sds((LEN, 1), F32),
            sds((LEN, D), BF16),
            sds((LEN, FF), BF16),
            sds((LEN, FF), BF16),
            sds((LEN, D), F32),
            sds((LEN, 1), F32),
            sds((LEN, D), BF16),
        ),
        in_specs=[ANY] + [VMEM] * 8,
        out_specs=(ANY, ANY, VMEM, ANY, ANY, ANY, ANY, ANY, VMEM, ANY, ANY, ANY, ANY, VMEM, ANY),
        scratch_shapes=[
            pltpu.VMEM((LEAD + FLAT + 288, 128), F32),
            pltpu.VMEM((2, ROWS, 128), BF16),
            pltpu.VMEM((LEN, D), BF16),
            pltpu.VMEM((LEN, D), BF16),
            pltpu.VMEM((count_peers, 8, 128), F32),
            pltpu.VMEM((LEN, D), F32),
            pltpu.VMEM((1, FF), F32),
            pltpu.VMEM((LEN, D), F32),
            pltpu.VMEM((3, LEN, LEN), jnp.int32),
            pltpu.VMEM((2, 96, 128), BF16),
            pltpu.VMEM((LEN, D), BF16),
            pltpu.VMEM((18, LEN, 128), BF16),
            pltpu.VMEM((HEADS * 4 * LEN, 128), BF16),
            pltpu.VMEM((LEN, D), BF16),
            pltpu.VMEM((LEN, D), F32),
            pltpu.VMEM((LEN, D), BF16),
            pltpu.VMEM((LEN, FF), BF16),
            pltpu.VMEM((LEN, FF), BF16),
            pltpu.VMEM((LEN, D), BF16),
            dma((8,)), dma((1,)), dma((CHUNKS,)), dma((1,)), dma((CHUNKS,)), dma((3,)), dma((3,)),
            dma((count_peers,)), dma((count_peers,)), dma((16,)), dma((PAIRS,)), dma((2, 12)),
        ]
        + sems,
        compiler_params=pltpu.CompilerParams(
            collective_id=1, has_side_effects=True, vmem_limit_bytes=64 * 2**20 - 2**16
        ),
    )(p2, xin, cot, cnt, features, coord_row, coord_col, jnp.asarray(pick), jnp.asarray(keep))


G_SMALL = (("qv_bias", 0, 0, 12), ("out_bias", 0, 12, 6), ("gain_one", 0, 18, 6), ("shift_one", 0, 24, 6),
           ("up_bias", 1, 0, 24), ("down_bias", 1, 24, 6), ("gain_two", 1, 30, 6), ("shift_two", 1, 36, 6))


def spread_norm(normed, inverse, gain, grad):
    scaled = grad * gain
    return inverse * (
        scaled
        - jnp.mean(scaled, axis=1, keepdims=True)
        - normed * jnp.mean(scaled * normed, axis=1, keepdims=True)
    )


def total_rows(values):
    return jnp.sum(values.astype(F32), axis=0, keepdims=True)


def reduce_chunk(stages):
    replicas = 2
    for radix, _ in stages:
        replicas *= radix
    return max(1024, 16 * replicas)


class Reduction:
    def __init__(self, stages, gstack, out, core_slots, x_slots, pieces, slots, sems):
        self.stages, self.gstack, self.out = stages, gstack, out
        self.core_slots, self.x_slots, self.pieces, self.slots = core_slots, x_slots, pieces, slots
        (self.c_send, self.c_recv, self.x_send, self.x_recv, self.b_send, self.b_recv, self.own_sem) = sems[:7]
        self.sems = sems[7:]
        self.dp, self.fs = place()
        self.other = 1 - self.fs
        self.size = reduce_chunk(stages)
        self.count = ROWS // self.size
        self.levels = len(stages)
        self.parts = offsets(self.dp, stages, self.size)
        self.half = self.size // 2
        self.x_peer = (self.dp, self.other)
        self.core_peer = (self.dp + 1 - 2 * (self.dp % 2), self.fs)

    def base(self, position):
        return lax.rem(2 * self.count - 2 - position, self.count) * self.size

    def ready(self, row):
        return jnp.maximum(self.count - 1 - (row + self.size - 1) // self.size, 0)

    def core_copy(self, position, plane):
        where = rows_at(self.base(position) + (1 - self.dp % 2) * self.half, self.half)
        return remote(
            self.gstack.at[plane, where], self.core_slots.at[plane, position],
            self.c_send.at[0], self.c_recv.at[plane, position], self.core_peer,
        )

    def x_copy(self, position):
        where = rows_at(self.base(position) + self.parts[0][0], self.half)
        return remote(
            self.gstack.at[self.other, where], self.x_slots.at[position],
            self.x_send.at[0], self.x_recv.at[position], self.x_peer,
        )

    def scatter_copies(self, level, position):
        radix, stride = self.stages[level]
        start, size = self.parts[level]
        size = size // radix
        mine = (self.dp // stride) % radix
        copies = []
        for step in range(1, radix):
            target = (mine + step) % radix
            where = rows_at(self.base(position) + start + target * size, size)
            copies.append(
                remote(
                    self.gstack.at[self.fs, where], self.slots[level].at[position, step - 1],
                    self.sems[4 * level].at[0], self.sems[4 * level + 1].at[position],
                    (member(self.dp, radix, stride, target), self.fs),
                )
            )
        return copies

    def scatter_wait(self, level, position):
        where = self.slots[level].at[position]
        remote(where, where, self.sems[4 * level].at[0], self.sems[4 * level + 1].at[position], self.x_peer).wait_recv()

    def spread_wait(self, level, position):
        size = (self.stages[level][0] - 1) * self.parts[level + 1][1]
        where = self.out.at[rows_at(self.base(position) + self.parts[level][0], size)]
        remote(
            where, where, self.sems[4 * level + 2].at[0], self.sems[4 * level + 3].at[position], self.x_peer
        ).wait_recv()

    def spread_copies(self, level, position):
        radix, stride = self.stages[level]
        start, size = self.parts[level + 1]
        mine = (self.dp // stride) % radix
        copies = []
        for step in range(1, radix):
            where = self.out.at[rows_at(self.base(position) + start, size)]
            source = self.pieces.at[position] if level == self.levels - 1 else where
            copies.append(
                remote(
                    source, where,
                    self.sems[4 * level + 2].at[0], self.sems[4 * level + 3].at[position],
                    (member(self.dp, radix, stride, (mine + step) % radix), self.fs),
                )
            )
        return copies

    def own_copy(self, position):
        start, size = self.parts[-1]
        return pltpu.make_async_copy(
            self.pieces.at[position], self.out.at[rows_at(self.base(position) + start, size)],
            self.own_sem.at[position],
        )

    def back_copy(self, position, receive):
        start = (1 - self.dp % 2 if receive else self.dp % 2) * self.half
        where = self.out.at[rows_at(self.base(position) + start, self.half)]
        return remote(where, where, self.b_send.at[0], self.b_recv.at[position], self.core_peer)

    def feed(self, plane, low, high):
        def one(position, carry):
            self.core_copy(position, plane).start()
            return carry

        lax.fori_loop(low, high, one, 0)

    def push(self, low, high):
        def one(position, carry):
            self.core_copy(position, self.other).wait_recv()
            where = rows_at(self.base(position) + self.parts[0][0], self.half)
            value = self.gstack[self.other, where, :].astype(F32) + self.core_slots[self.other, position].astype(F32)
            self.gstack[self.other, where, :] = value.astype(BF16)
            self.x_copy(position).start()
            return carry

        lax.fori_loop(low, high, one, 0)

    def work(self, position, step):
        levels = self.levels
        base = self.base(position)
        if step <= levels:
            start, size = self.parts[step]
            where = rows_at(base + start, size)
            if step == 0:
                self.core_copy(position, self.fs).wait_recv()
                self.x_copy(position).wait_recv()
                terms = [self.core_slots[self.fs, position], self.x_slots[position]]
            else:
                self.scatter_wait(step - 1, position)
                terms = [self.slots[step - 1][position, i] for i in range(self.stages[step - 1][0] - 1)]
            value = self.gstack[self.fs, where, :].astype(F32)
            for term in terms:
                value = value + term.astype(F32)
            if step < levels:
                self.gstack[self.fs, where, :] = value.astype(BF16)
                for copy in self.scatter_copies(step, position):
                    copy.start()
            else:
                self.pieces[position] = value.astype(BF16)
                self.own_copy(position).start()
                for copy in self.spread_copies(levels - 1, position):
                    copy.start()
        else:
            level = 2 * levels - step
            self.spread_wait(level, position)
            if level == levels - 1:
                self.own_copy(position).wait()
            if level > 0:
                for copy in self.spread_copies(level - 1, position):
                    copy.start()
            else:
                self.back_copy(position, False).start()

    def tick(self, number):
        for step in range(2 * self.levels, -1, -1):
            position = number - SKEW * step

            @pl.when((position >= 0) & (position < self.count))
            def _(position=position, step=step):
                self.work(position, step)

    def ticks(self):
        return self.count + 2 * SKEW * self.levels

    def finish(self):
        def one(position, carry):
            self.back_copy(position, True).wait_recv()
            return carry

        lax.fori_loop(0, self.count, one, 0)
        sent = [(self.c_send, 2 * self.half), (self.x_send, self.half), (self.b_send, self.half)]
        for level, (radix, _) in enumerate(self.stages):
            size = (radix - 1) * self.parts[level + 1][1]
            sent += [(self.sems[4 * level], size), (self.sems[4 * level + 2], size)]
        for sem, size in sent:
            where = self.gstack.at[0, pl.ds(0, self.count * size)]
            remote(where, where, sem.at[0], self.x_recv.at[0], self.x_peer).wait_send()


def reduction_scratch(stages):
    size = reduce_chunk(stages)
    count, half = ROWS // size, size // 2
    dma = pltpu.SemaphoreType.DMA
    slots, sems = [], []
    for radix, _ in stages:
        half = half // radix
        slots.append(pltpu.VMEM((count, radix - 1, half, 128), BF16))
        sems += [dma((1,)), dma((count,))] * 2
    return (
        [
            pltpu.VMEM((2, count, size // 2, 128), BF16),
            pltpu.VMEM((count, size // 2, 128), BF16),
            pltpu.VMEM((count, half, 128), BF16),
        ]
        + slots,
        [dma((1,)), dma((2, count)), dma((1,)), dma((count,)), dma((1,)), dma((count,)), dma((count,))] + sems,
    )


def backward_kernel(
    stages,
    wall_hbm, cdoc_hbm, total, layer_hbm, rounded_hbm, qkv_hbm, probs_hbm, mixed_hbm, one_hbm, inverse_one, low_hbm, hidden_hbm,
    slope_hbm, two_hbm, inverse_two, features, coord_row, coord_col, pick, keep,
    layer_out, input_grad, reduced, tables, norm,
    wall, gstack, acc, branch, hidden, d_up, low, rounded, qkv, mixed, normed_one, places, lut, ranks, layer, small,
    square_slots, load_sem, step_sem, probs_sem, act_send, act_recv, act_sem, n_send, n_recv, *rest,
):
    levels = len(stages)
    parts_vmem, sems = rest[: 3 + levels], rest[3 + levels :]
    red = Reduction(stages, gstack, reduced, parts_vmem[0], parts_vmem[1], parts_vmem[2], parts_vmem[3:], sems)
    dp, fs, other = red.dp, red.fs, red.other
    half = LEN // 2

    early = [
        pltpu.make_async_copy(wall_hbm.at[:, pl.ds(SM0, 256)], wall.at[:, pl.ds(SM0, 256)], load_sem.at[0]),
        pltpu.make_async_copy(cdoc_hbm, branch, load_sem.at[1]),
        pltpu.make_async_copy(two_hbm, acc, load_sem.at[2]),
    ]
    early.append(pltpu.make_async_copy(layer_hbm, layer, load_sem.at[9]))
    lows = [pltpu.make_async_copy(low_hbm, low, load_sem.at[3])]
    rest_loads = [
        pltpu.make_async_copy(one_hbm, normed_one, load_sem.at[4]),
        pltpu.make_async_copy(wall_hbm.at[0, pl.ds(0, UP0)], wall.at[0, pl.ds(0, UP0)], load_sem.at[5]),
        pltpu.make_async_copy(mixed_hbm, mixed, load_sem.at[6]),
        pltpu.make_async_copy(qkv_hbm, qkv, load_sem.at[7]),
        pltpu.make_async_copy(rounded_hbm, rounded, load_sem.at[8]),
    ]

    def step_loads(j):
        lanes = pl.ds(pl.multiple_of(j * 256, 256), 256)
        areas = [(1, DOWN1 + 1536 * j, 1536), (0, UP0 + 2 * UP_A * j, 2 * UP_A), (1, UP1 + 2 * UP_B * j, 2 * UP_B)]
        copies = [
            pltpu.make_async_copy(
                wall_hbm.at[plane, rows_at(start, size)], wall.at[plane, rows_at(start, size)], step_sem.at[i, j]
            )
            for i, (plane, start, size) in enumerate(areas)
        ]
        copies.append(pltpu.make_async_copy(hidden_hbm.at[:, lanes], hidden.at[:, lanes], step_sem.at[3, j]))
        copies.append(pltpu.make_async_copy(slope_hbm.at[:, lanes], d_up.at[:, lanes], step_sem.at[4, j]))
        return copies

    for load in early + lows:
        load.start()

    def start_loads(it, carry):
        for load in step_loads(11 - it):
            load.start()
        return carry

    lax.fori_loop(0, 12, start_loads, 0)
    for load in rest_loads:
        load.start()
    greet_signal(stages)
    find_places(coord_col, lut, ranks, places)
    for table in (1, 2):
        key_row = jnp.broadcast_to(coord_row[table : table + 1, :], (256, LEN))
        for r in (0, 256):
            near = jnp.broadcast_to(coord_col[r : r + 256, table : table + 1], (256, LEN))
            lower = jnp.where(key_row < near, 1.0, 0.0).astype(BF16)
            ranks[table - 1, r : r + 256, :] = nn(lower, jnp.ones((LEN, 128), BF16))
    greet_wait(stages)

    def layer_copy(receive):
        return remote(
            layer.at[rows_at(other * half, half)], layer_out.at[other if receive else fs],
            act_send.at[1], act_recv.at[1], red.x_peer,
        )

    layer_own = pltpu.make_async_copy(layer.at[rows_at(fs * half, half)], layer_out.at[fs], act_sem.at[1])
    small[...] = jnp.zeros_like(small)
    gstack[1, pl.ds(DOWN_END, LAY1 - DOWN_END), :] = jnp.zeros((LAY1 - DOWN_END, 128), BF16)
    for load in early:
        load.wait()

    layer_copy(False).start()
    layer_own.start()
    small0 = wall[0, pl.ds(SM0, 48), :].astype(F32)
    small1 = wall[1, pl.ds(SM1, 80), :].astype(F32)
    gain_one = row_of(small0, 26, 6)
    gain_two = row_of(small1, 44, 6)
    spots = {name: (plane, first_row) for name, plane, first_row, _ in G_SMALL}

    def keep_small(name, vector):
        plane, at = spots[name]
        for i in range(vector.shape[1] // 128):
            small[plane, at + i : at + i + 1, :] = vector[:, i * 128 : (i + 1) * 128]

    count = total[0:1, 0:1]
    none = jnp.zeros((1, D), F32)

    def second_rows(r, sums):
        at = pl.ds(pl.multiple_of(r * QROWS, QROWS), QROWS)
        grad_out = branch[at, :].astype(F32) / count
        normed = acc[at, :]
        result = spread_norm(normed, inverse_two[at, :], gain_two, grad_out)
        acc[at, :] = result
        lower = result.astype(BF16)
        branch[at, :] = lower
        return sums[0] + total_rows(grad_out * normed), sums[1] + total_rows(grad_out), sums[2] + total_rows(lower)

    sums = lax.fori_loop(0, LEN // QROWS, second_rows, (none, none, none))
    for name, vector in zip(("gain_two", "shift_two", "down_bias"), sums):
        keep_small(name, vector)
    plane_up, at_up = spots["up_bias"]
    lows[0].wait()

    def fed(plane, it):
        row = UP0 + 2 * UP_A * (11 - it) if plane == 0 else DOWN1 + 1536 * (11 - it)
        return red.ready(row)

    def of_other(values):
        return jnp.where(other == 0, values[0], values[1])

    fine = red.count >= 28
    tile_row = lax.broadcasted_iota(jnp.int32, (16, 128), 0)

    def feed_step(it, carry):
        j = 11 - it
        for load in step_loads(j):
            load.wait()
        for plane in range(2):
            red.feed(plane, fed(plane, it - 2), fed(plane, it - 1))
        red.push(of_other([fed(p, it - 3) for p in range(2)]), of_other([fed(p, it - 2) for p in range(2)]))
        lanes = pl.ds(pl.multiple_of(j * 256, 256), 256)
        grad = nt(branch[...], down_rows(wall, j))
        part = (grad * d_up[:, lanes].astype(F32)).astype(BF16)
        d_up[:, lanes] = part
        sums = total_rows(part)
        small[plane_up, pl.ds(at_up + 2 * j, 1), :] = sums[:, :128]
        small[plane_up, pl.ds(at_up + 2 * j + 1, 1), :] = sums[:, 128:]
        down = tn(hidden[:, lanes], branch[...]).astype(BF16)
        for c in range(6):
            gstack[1, rows_at(DOWN1 + j * 1536 + c * 256, 256), :] = down[:, c * 128 : (c + 1) * 128]
        up = tn(low[...], part)
        for i in range(2):
            c = 2 * j + i
            cut = jnp.where(c < 2, CUT + 1 - 400, CUT - 400)
            columns = up[:, i * 128 : (i + 1) * 128]
            tile = columns[400:416]
            gstack[0, rows_at(UP0 + c * UP_A, 400), :] = columns[:400].astype(BF16)
            gstack[0, rows_at(UP0 + c * UP_A + 400, 16), :] = jnp.where(tile_row < cut, tile, 0.0).astype(BF16)
            gstack[1, rows_at(UP1 + c * UP_B, 16), :] = jnp.where(tile_row < cut, 0.0, tile).astype(BF16)
            gstack[1, rows_at(UP1 + c * UP_B + 16, UP_B - 16), :] = columns[416:].astype(BF16)
        acc[...] += nt(part, up_block(wall, j))
        return carry

    lax.fori_loop(0, 12, feed_step, 0)

    def probs_copy(pair, slot):
        size = 8 * LEN
        return pltpu.make_async_copy(
            probs_hbm.at[rows_at(pair * size, size)], wall.at[0, rows_at(UP0 + slot * size, size)], probs_sem.at[slot]
        )

    probs_copy(PAIRS - 1, 0).start()
    last = red.count - 1
    red.feed(0, fed(0, 10), fed(0, 11))
    red.feed(1, fed(1, 10), last)
    red.push(of_other([fed(p, 9) for p in range(2)]), of_other([fed(p, 10) for p in range(2)]))
    for load in rest_loads:
        load.wait()

    w_out = jnp.concatenate([wall[0, pl.ds(OUT0 + c * D, D), :] for c in range(6)], axis=1)

    def first_rows(r, sums):
        at = pl.ds(pl.multiple_of(r * QROWS, QROWS), QROWS)
        grad, normed = acc[at, :], normed_one[at, :]
        result = spread_norm(normed, inverse_one[at, :], gain_one, grad)
        acc[at, :] = result
        lower = result.astype(BF16)
        branch[at, :] = lower
        low[at, :] = nt(lower, w_out).astype(BF16)
        return sums[0] + total_rows(grad * normed), sums[1] + total_rows(grad), sums[2] + total_rows(lower)

    sums = lax.fori_loop(0, LEN // QROWS, first_rows, (none, none, none))
    for name, vector in zip(("gain_one", "shift_one", "out_bias"), sums):
        keep_small(name, vector)
    red.push(of_other([fed(p, 10) for p in range(2)]), jnp.where(other == 0, fed(0, 11), last))

    def drain(number, carry):
        red.tick(number)
        return carry

    per_pair = 2 if fine else 1

    def out_step(j, carry):
        lanes = pl.ds(pl.multiple_of(j * 256, 256), 256)
        part = tn(mixed[...], branch[:, lanes]).astype(BF16)
        for i in range(2):
            gstack[0, rows_at(OUT0 + (2 * j + i) * D, D), :] = part[:, i * 128 : (i + 1) * 128]
        return carry

    lax.fori_loop(0, 3, out_step, 0)
    drain(0, 0)
    drain(1, 0)

    left = lax.broadcasted_iota(jnp.int32, (LEN, 128), 1) < HDIM

    def sent(it):
        return red.ready(jnp.where(it <= -2, UP0, 2304 * (5 - it)))

    def score_rows(head, j, start, size):
        return rows_at((4 * head + j) * LEN + start, size)

    def attend(it, carry):
        pair = PAIRS - 1 - it
        slot = lax.rem(it, 2)

        @pl.when(it + 1 < PAIRS)
        def _():
            probs_copy(pair - 1, 1 - slot).start()

        red.feed(0, sent(it - 2), sent(it - 1))

        @pl.when(other == 0)
        def _():
            red.push(sent(it - 3), sent(it - 2))

        lax.fori_loop(2 + per_pair * it, 2 + per_pair * (it + 1), drain, 0)
        probs_copy(pair, slot).wait()
        query, key, value = qkv[3 * pair], qkv[3 * pair + 1], qkv[3 * pair + 2]
        grad = low[:, pl.ds(pl.multiple_of(pair * 128, 128), 128)]
        found = []
        for side in range(2):
            head = 2 * pair + side
            mine = left if side == 0 else jnp.logical_not(left)
            base = UP0 + slot * 8 * LEN + side * 4 * LEN
            for r in range(0, LEN, BROWS):
                part = grad[r : r + BROWS]
                d_probs = nt(jnp.where(mine[r : r + BROWS], part, jnp.zeros_like(part)), value)
                soft = jnp.concatenate(
                    [wall[0, rows_at(base + j * LEN + r, BROWS), :] for j in range(4)], axis=1
                ).astype(F32)
                inner = jnp.sum(soft * d_probs, axis=1, keepdims=True)
                scores = (soft * (d_probs - inner)).astype(BF16)
                for j in range(4):
                    wall[1, score_rows(head, j, r, BROWS), :] = scores[:, j * 128 : (j + 1) * 128]
            scores = jnp.concatenate([wall[1, score_rows(head, j, 0, LEN), :] for j in range(4)], axis=1)
            chances = jnp.concatenate([wall[0, rows_at(base + j * LEN, LEN), :] for j in range(4)], axis=1)
            found.append((nn(scores, key), tn(scores, query), tn(chances, grad)))
        d_query = (jnp.where(left, found[0][0], found[1][0]) * HDIM**-0.5).astype(BF16)
        d_key = jnp.where(left, found[0][1], found[1][1]).astype(BF16)
        d_value = jnp.where(left, found[0][2], found[1][2]).astype(BF16)
        both = jnp.concatenate([d_query, d_key, d_value], axis=1)
        plane, spot = spots["qv_bias"]
        small[plane, pl.ds(spot + pair, 1), :] = total_rows(d_query)
        small[plane, pl.ds(spot + 6 + pair, 1), :] = total_rows(d_value)
        at = pl.multiple_of(3 * pair * D, 16)
        weight = jnp.concatenate([wall[0, rows_at(at + i * D, D), :] for i in range(3)], axis=1)
        acc[...] += nt(both, weight)
        part = tn(rounded[...], both).astype(BF16)
        for i in range(3):
            gstack[0, rows_at(at + i * D, D), :] = part[:, i * 128 : (i + 1) * 128]
        return carry

    lax.fori_loop(0, PAIRS, attend, 0)
    red.feed(0, sent(4), sent(5))

    @pl.when(other == 0)
    def _():
        red.push(sent(3), sent(4))

    branch[...] = acc[...].astype(BF16)
    act_out = remote(branch.at[rows_at(other * half, half)], input_grad.at[fs], act_send.at[0], act_recv.at[0], red.x_peer)
    act_in = remote(branch.at[rows_at(other * half, half)], input_grad.at[other], act_send.at[0], act_recv.at[0], red.x_peer)
    act_own = pltpu.make_async_copy(branch.at[rows_at(fs * half, half)], input_grad.at[fs], act_sem.at[0])
    act_out.start()
    act_own.start()
    layout = tn(features[...], branch[...]).astype(BF16)
    for c in range(6):
        gstack[1, pl.ds(LAY1 + c * FEAT, FEAT), :] = layout[:, c * 128 : (c + 1) * 128]

    @pl.when(other == 0)
    def _():
        red.push(sent(4), sent(5))

    late = 2 + per_pair * PAIRS
    for plane in range(2):
        gstack[plane, pl.ds(SM0, 64), :] = small[plane].astype(BF16)
        gstack[plane, pl.ds(SM0 + 64, ROWS - SM0 - 64), :] = jnp.zeros((ROWS - SM0 - 64, 128), BF16)
        red.feed(plane, last, last + 1)
    drain(late, 0)
    red.push(last, last + 1)
    late += 1
    pace = 2 if fine else 4
    table_grads(wall, coord_col, pick, keep, hidden, places, ranks, normed_one, tables, red, late, pace)
    late += 24 // pace

    summed = red.count + SKEW * levels
    assert late <= summed
    lax.fori_loop(late, summed, drain, 0)

    def squares(position, carry):
        piece = red.pieces[position].astype(F32)
        return carry + jnp.sum((piece * piece).reshape(-1, 8, 128), axis=0)

    value = lax.fori_loop(0, red.count, squares, jnp.zeros((8, 128), F32))
    value = jnp.sum(jnp.sum(value, axis=0, keepdims=True), axis=1, keepdims=True)
    tables[9:10, :] = jnp.broadcast_to(value, (1, 128))
    rounds = [
        [
            (member(dp, radix, stride, ((dp // stride) % radix + step) % radix), fs)
            for step in range(1, radix)
        ]
        for radix, stride in stages
    ] + [[red.core_peer], [red.x_peer]]

    def square_copies(number):
        base = sum(len(r) for r in rounds[:number])
        return [
            remote(tables.at[...], square_slots.at[base + i], n_send.at[base + i], n_recv.at[base + i], peer)
            for i, peer in enumerate(rounds[number])
        ]

    for number in range(max(red.ticks() - summed, len(rounds)) + 1):
        if number < len(rounds):
            for copy in square_copies(number):
                copy.start()
        if summed + number < red.ticks():
            red.tick(summed + number)
        if number < len(rounds):
            gathered = tables[...]
            base = sum(len(r) for r in rounds[:number])
            for i, copy in enumerate(square_copies(number)):
                copy.wait()
                gathered = gathered + square_slots[base + i]
            tables[...] = gathered
    gathered = tables[0:9, :]
    gathered = jnp.sum(jnp.sum(gathered * gathered, axis=0, keepdims=True), axis=1, keepdims=True)
    norm[...] = jnp.broadcast_to(jnp.sqrt(tables[9:10, :] + gathered), (8, 128))

    red.finish()
    act_own.wait()
    act_out.wait_send()
    act_in.wait_recv()
    layer_own.wait()
    layer_copy(False).wait_send()
    layer_copy(True).wait_recv()


def table_grads(wall, coord_col, pick, keep, less, places, ranks, prefix, tables, red, late, pace):
    tables[...] = jnp.zeros_like(tables)
    block = 64
    for table in range(3):
        order = lax.broadcasted_iota(jnp.int32, (16, LEN), 1)

        def less_rows(a, carry):
            at = pl.ds(pl.multiple_of(a * 16, 16), 16)
            if table == 0:
                near = jnp.broadcast_to(coord_col[at, 0:1], (16, LEN))
            else:
                near = jnp.concatenate([ranks[table - 1, at, :].astype(jnp.int32)] * 4, axis=1)
            less[at, 0:LEN] = jnp.where(near <= order, 1.0, 0.0).astype(BF16)
            return carry

        lax.fori_loop(0, LEN // 16, less_rows, 0, unroll=4)

        def query_rows(b, sums):
            @pl.when(lax.rem(table * 8 + b, pace) == 0)
            def _():
                red.tick(late + (table * 8 + b) // pace)

            start = b * block
            scores = jnp.concatenate(
                [
                    jnp.concatenate(
                        [wall[1, rows_at((4 * h + j) * LEN + start, block), :] for j in range(4)], axis=1
                    )
                    for h in range(HEADS)
                ],
                axis=0,
            )
            summed = nn(scores, less[:, 0:LEN])
            for h in range(HEADS):
                for j in range(4):
                    r, c = (4 * h + j) // 6 * 64, (4 * h + j) % 6 * 128
                    prefix[r : r + 64, c : c + 128] = summed[h * block : (h + 1) * block, j * 128 : (j + 1) * 128]

            def pick_up(a, carry):
                place_of = places[table, pl.ds(pl.multiple_of(start + a * 8, 8), 8), :]
                low, high = place_of & 127, place_of >> 7
                result = []
                for h in range(HEADS):
                    value = jnp.zeros((8, 128), F32)
                    for j in range(4):
                        r, c = (4 * h + j) // 6 * 64, (4 * h + j) % 6 * 128
                        rows = pl.ds(pl.multiple_of(r + a * 8, 8), 8)
                        part = jnp.take_along_axis(prefix[rows, c : c + 128], low, axis=1)
                        value = jnp.where(high == j, part, value)
                    result.append(carry[h] + value)
                return tuple(result)

            return lax.fori_loop(0, block // 8, pick_up, sums, unroll=8)

        sums = lax.fori_loop(
            0, LEN // block, query_rows, tuple(jnp.zeros((8, 128), F32) for _ in range(HEADS))
        )
        heads = jnp.concatenate(
            [jnp.sum(s, axis=0, keepdims=True) for s in sums] + [jnp.zeros((4, 128), F32)], axis=0
        )
        after = pltpu.roll(heads, 127, 1)
        whole = pltpu.roll(heads, 15, 1)
        lanes = lax.broadcasted_iota(jnp.int32, (16, 128), 1)
        buckets = jnp.where(lanes < 16, heads - after, after - heads)
        buckets = jnp.where(lanes == 15, heads, buckets)
        buckets = jnp.where(lanes == 16, 0.0, buckets)
        buckets = jnp.where(lanes == 31, whole - heads, buckets)
        buckets = jnp.where(lanes < 32, buckets, 0.0)
        placed = buckets if table == 0 else pltpu.roll(buckets, 32 * table, 1)
        parts, left_over = [], placed
        for _ in range(2):
            parts.append(left_over.astype(BF16))
            left_over = left_over - parts[-1].astype(F32)
        spread = sum(nt(part, pick[table]) for part in parts)
        flat_row = jnp.sum(spread * keep[...], axis=0, keepdims=True)
        for i in range(3):
            tables[3 * table + i : 3 * table + i + 1, :] = flat_row[:, i * 128 : (i + 1) * 128]


def backward_pass(stages, wall, cdoc, total, out_doc, saved, features, coord_row, coord_col):
    pick, keep = table_constants()
    sds = jax.ShapeDtypeStruct
    count_peers = 2 + sum(radix - 1 for radix, _ in stages)
    dma = pltpu.SemaphoreType.DMA
    buffers, sems = reduction_scratch(stages)
    return pl.pallas_call(
        functools.partial(backward_kernel, stages),
        name="backward_reduce",
        out_shape=(sds((2, LEN // 2, D), BF16), sds((2, LEN // 2, D), BF16), sds((ROWS, 128), BF16), sds((16, 128), F32), sds((8, 128), F32)),
        in_specs=[ANY, ANY, VMEM, ANY, ANY, ANY, ANY, ANY, ANY, VMEM, ANY, ANY, ANY, ANY, VMEM] + [VMEM] * 5,
        out_specs=(ANY, ANY, ANY, VMEM, VMEM),
        scratch_shapes=[
            pltpu.VMEM((2, ROWS, 128), BF16),
            pltpu.VMEM((2, ROWS, 128), BF16),
            pltpu.VMEM((LEN, D), F32),
            pltpu.VMEM((LEN, D), BF16),
            pltpu.VMEM((LEN, FF), BF16),
            pltpu.VMEM((LEN, FF), BF16),
            pltpu.VMEM((LEN, D), BF16),
            pltpu.VMEM((LEN, D), BF16),
            pltpu.VMEM((18, LEN, 128), BF16),
            pltpu.VMEM((LEN, D), BF16),
            pltpu.VMEM((LEN, D), F32),
            pltpu.VMEM((3, LEN, 128), jnp.int32),
            pltpu.VMEM((16, 128), jnp.int32),
            pltpu.VMEM((2, LEN, 128), F32),
            pltpu.VMEM((LEN, D), BF16),
            pltpu.VMEM((2, 64, 128), F32),
            pltpu.VMEM((count_peers, 16, 128), F32),
            dma((10,)), dma((5, 12)), dma((2,)), dma((2,)), dma((2,)), dma((2,)), dma((count_peers,)), dma((count_peers,)),
        ]
        + buffers
        + sems,
        compiler_params=pltpu.CompilerParams(
            collective_id=2, has_side_effects=True, vmem_limit_bytes=64 * 2**20 - 2**16
        ),
    )(wall, cdoc, total, out_doc, *saved, features, coord_row, coord_col, jnp.asarray(pick), jnp.asarray(keep))


BLOCK = 3520


DOWN_STEPS = (0, 0, 2, 4, 6, 9, 11, 12, 12)


def flatten_rows(plane, step, source, tables, flat):
    def blocks(low, high, src, dst, rows, stride):
        def one(i, carry):
            flat[pl.ds(LEAD + dst(i), rows, stride=stride), :] = source[rows_at(src(i), rows), :].astype(F32)
            return carry

        lax.fori_loop(low, high, one, 0)

    if plane == 0:
        if step == 0:
            blocks(0, 18, lambda pos: pos * D, lambda pos: lax.rem(pos, 3) * 6 + pos // 3, D, 18)
            small = source[pl.ds(SM0, 64), :].astype(F32)
            flat[pl.ds(LEAD + 13824, 12), :] = small[0:12]
            flat[pl.ds(LEAD + 18444, 18), :] = small[12:30]
        elif step == 2:
            blocks(0, 6, lambda c: OUT0 + c * D, lambda c: F_OUT + c, D, 6)
        elif step == 4:
            blocks(0, 24, lambda c: UP0 + c * UP_A, lambda c: F_UP + c, UP_A, 24)
    else:
        if step == 0:
            blocks(0, 24, lambda c: UP1 + c * UP_B, lambda c: c - 98, UP_B, 24)
            small = source[pl.ds(SM1, 64), :].astype(F32)
            flat[pl.ds(LEAD + F_UPB1, 24), :] = small[0:24]
            flat[pl.ds(LEAD + F_SM1, 18), :] = small[24:42]
            flat[pl.ds(LEAD + F_TAB1, 9), :] = tables[0:9, :]
            rest = FLAT - F_TAB1 - 9
            flat[pl.ds(LEAD + F_TAB1 + 9, rest), :] = jnp.zeros((rest, 128), F32)
        elif step == 6:
            blocks(0, 6, lambda c: LAY1 + c * FEAT, lambda c: F_LAY1 + c, FEAT, 6)
        low, high = DOWN_STEPS[step], DOWN_STEPS[step + 1]
        if low < high:
            for c in range(6):
                blocks(
                    low, high, lambda j: DOWN1 + j * 1536 + c * 256, lambda j: F_DOWN1 + j * 1536 + c, 256, 6
                )


def adam_kernel(
    source_hbm, tables, weights, first, second, grad_out, update_out, first_out, source, flat, sem,
):
    step = pl.program_id(0)
    fs = lax.axis_index("fsdp")
    spans = ((0, OUT0), (SM0, ROWS - SM0), (OUT0, SM0 - OUT0))
    loads = [
        pltpu.make_async_copy(source_hbm.at[pl.ds(a, n)], source.at[pl.ds(a, n)], sem.at[i])
        for i, (a, n) in enumerate(spans)
    ]

    @pl.when(step == 0)
    def _():
        for load in loads:
            load.start()
        for load in loads[:2]:
            load.wait()

    @pl.when(step == 1)
    def _():
        loads[2].wait()

    for number in range(FLAT // BLOCK):
        for plane in range(2):

            @pl.when((step == number) & (fs == plane))
            def _(plane=plane, number=number):
                flatten_rows(plane, number, source, tables, flat)

    part = 160
    row = lax.broadcasted_iota(jnp.int32, (part, 128), 0)

    def some(i, carry):
        at = pl.ds(pl.multiple_of(i * part, 8), part)
        begin = pl.multiple_of(step * BLOCK + i * part, 8)
        grad = flat[pl.ds(LEAD + begin, part), :]
        grad_out[at, :] = grad
        new_first = adam_one * first[at, :] + (1.0 - adam_one) * grad
        new_second = adam_two * second[at, :] + (1.0 - adam_two) * grad * grad
        spread = jnp.sqrt(new_second * (1.0 / (1.0 - adam_two**adam_steps))) + adam_eps
        corrected = new_first * (1.0 / (1.0 - adam_one**adam_steps)) / spread
        rate = jnp.where((fs == 1) & (row + begin >= F_LAY1), table_factor, 1.0)
        update_out[at, :] = rate * (corrected + decay_rate * weights[at, :])
        first_out[at, :] = new_first
        return carry

    lax.fori_loop(0, BLOCK // part, some, 0)


def adam(source, tables, weights, first, second):
    block = pl.BlockSpec((BLOCK, 128), lambda i: (i, 0))
    vector = jax.ShapeDtypeStruct((FLAT, 128), F32)
    return pl.pallas_call(
        adam_kernel,
        name="adamw",
        grid=(FLAT // BLOCK,),
        out_shape=(vector, vector, vector),
        in_specs=[ANY, pl.BlockSpec((16, 128), lambda i: (0, 0)), block, block, block],
        out_specs=(block, block, block),
        scratch_shapes=[
            pltpu.VMEM((ROWS, 128), BF16),
            pltpu.VMEM((LEAD + FLAT + 288, 128), F32),
            pltpu.SemaphoreType.DMA((3,)),
        ],
        compiler_params=pltpu.CompilerParams(vmem_limit_bytes=60 * 2**20),
    )(source, tables, weights, first, second)


def layout_features(coords):
    freq_count = FEAT // 8
    factors = (jnp.arange(freq_count, dtype=jnp.int32) + 1) ** 2
    phases = coords[..., :, None] * factors % 4096
    angles = phases.astype(F32) * (2.0 * math.pi / 4096.0)
    wave_parts = jnp.concatenate([jnp.sin(angles), jnp.cos(angles)], axis=-1)
    return wave_parts.reshape(coords.shape[:-1] + (FEAT,))


def local(stages, inputs, box_coords, mlm_mask, cotangent, params, first_moment, second_moment):
    fs = lax.axis_index("fsdp")
    masked = cotangent * mlm_mask.astype(BF16)[..., None]
    count = jnp.full((8, 128), jnp.sum(mlm_mask.astype(F32)))
    boxes = lax.dynamic_index_in_dim(box_coords, fs, 0, keepdims=False)
    features = layout_features(boxes).astype(BF16)
    coord_col = jnp.stack(
        [jnp.arange(LEN, dtype=jnp.int32), boxes[:, 0] + boxes[:, 2], boxes[:, 1] + boxes[:, 3]], axis=1
    )
    coord_row = coord_col.T
    flat = [v.reshape(FLAT, 128) for v in (params, first_moment, second_moment)]
    wall, cdoc, total, *saved, out_doc = forward_pass(
        stages, flat[0], inputs, masked, count, features, coord_row, coord_col
    )
    layer_out, input_grad, reduced, tables, norm = backward_pass(
        stages, wall, cdoc, total, out_doc, saved, features, coord_row, coord_col
    )
    grad, update, new_first = adam(reduced, tables, *flat)
    return (layer_out, input_grad, grad.reshape(-1), norm[0, 0], update.reshape(-1), new_first.reshape(-1))


def solution(mesh):
    in_specs = (
        P("dp", "fsdp", None),
        P("dp", None, None),
        P("dp", "fsdp"),
        P("dp", "fsdp", None),
        P("fsdp"),
        P("fsdp"),
        P("fsdp"),
    )
    out_specs = (P("dp", "fsdp", None), P("dp", "fsdp", None), P("fsdp"), P(), P("fsdp"), P("fsdp"))
    stages = radices(mesh.shape["dp"])
    return jax.shard_map(
        functools.partial(local, stages), mesh=mesh, in_specs=in_specs, out_specs=out_specs, check_vma=False
    )
```

```python
import functools
import math

import jax
import jax.numpy as jnp
import numpy as np
from jax import lax
from jax.experimental import pallas as pl
from jax.experimental.pallas import tpu as pltpu
from jax.sharding import PartitionSpec as P

D = 768
HEADS = 12
HDIM = 64
FF = 3072
BUCKETS = 32
FEAT = 128
LEN = 512
PADDED = 7208960
SHARD = PADDED // 2
FLAT = SHARD // 128
PAIRS = HEADS // 2
QROWS = 256
AROWS = 512
BROWS = 256
SKEW = 2

norm_eps = 1e-05
adam_one = 0.9
adam_two = 0.999
adam_eps = 1e-08
adam_steps = 100.0
decay_rate = 0.01
table_factor = 5.0

MESH = pl.DeviceIdType.MESH
F32 = jnp.float32
BF16 = jnp.bfloat16
VMEM = pl.BlockSpec(memory_space=pltpu.VMEM)
ANY = pl.BlockSpec(memory_space=pl.ANY)

ROWS = 28672
CHUNK = 2048
CHUNKS = ROWS // CHUNK
CUT = 404
UP_A, UP_B = 416, 368
OUT0 = 18 * D
UP0 = OUT0 + 6 * D
SM0 = UP0 + 24 * UP_A
UP1 = 0
DOWN1 = 24 * UP_B
DOWN_END = DOWN1 + 6 * FF
LAY1 = 27648
SM1 = LAY1 + 6 * FEAT
F_OUT = 13836
F_UP = 18462
F_UPB1 = 8734
F_DOWN1 = 8758
F_SM1 = 27190
F_LAY1 = 27208
F_TAB1 = 27976
LEAD = 104


def nt(a, b):
    return lax.dot_general(a, b, (((1,), (1,)), ((), ())), preferred_element_type=F32)


def nn(a, b):
    return lax.dot_general(a, b, (((1,), (0,)), ((), ())), preferred_element_type=F32)


def tn(a, b):
    return lax.dot_general(a, b, (((0,), (0,)), ((), ())), preferred_element_type=F32)


def radices(replicas):
    stages, stride, left = [], 2, replicas // 2
    if left % 2 == 0:
        stages.append((2, stride))
        stride, left = stride * 2, left // 2
    while left > 1:
        radix = left if left <= 8 else 4
        stages.append((radix, stride))
        stride, left = stride * radix, left // radix
    return stages


def place():
    return lax.axis_index("dp"), lax.axis_index("fsdp")


def member(dp, radix, stride, digit):
    return dp + (digit - (dp // stride) % radix) * stride


def peers(stages):
    dp, fs = place()
    found = [(dp + 1 - 2 * (dp % 2), fs), (dp, 1 - fs)]
    for radix, stride in stages:
        mine = (dp // stride) % radix
        for step in range(1, radix):
            found.append((member(dp, radix, stride, (mine + step) % radix), fs))
    return found


def greet_signal(stages):
    barrier = pltpu.get_barrier_semaphore()
    for peer in peers(stages):
        pl.semaphore_signal(barrier, inc=1, device_id=peer, device_id_type=MESH)


def greet_wait(stages):
    pl.semaphore_wait(pltpu.get_barrier_semaphore(), len(peers(stages)))


def remote(src, dst, send, recv, peer):
    return pltpu.make_async_remote_copy(
        src_ref=src, dst_ref=dst, send_sem=send, recv_sem=recv, device_id=peer, device_id_type=MESH
    )


def rows_at(start, size):
    return pl.ds(pl.multiple_of(start, 16), size)


def offsets(dp, stages, extent):
    size = extent // 2
    start = (dp % 2) * size
    found = [(start, size)]
    for radix, stride in stages:
        size = size // radix
        start = start + ((dp // stride) % radix) * size
        found.append((start, size))
    return found


def row_of(ref_rows, start, count):
    return jnp.concatenate([ref_rows[start + i : start + i + 1, :] for i in range(count)], axis=1)


def table_constants():
    width = BUCKETS * HEADS
    lane = np.arange(width)
    pick = np.zeros((3, width, 128), np.float32)
    for table in range(3):
        pick[table, lane, 32 * table + lane // HEADS] = 1.0
    keep = (lane[None, :] % HEADS == np.arange(16)[:, None]).astype(np.float32)
    return pick.astype(jnp.bfloat16), keep


def bucket_of(offset):
    spread = jnp.abs(offset)
    result = jnp.minimum(spread, 8) + jnp.where(offset > 0, 16, 0)
    for level in range(9, 16):
        result = result + jnp.where(spread >= 8 * 2 ** (level - 8), 1, 0)
    return result


def up_block(wall, j):
    columns = []
    for c in (2 * j, 2 * j + 1):
        first = wall[0, rows_at(UP0 + c * UP_A, UP_A), :]
        second = wall[1, rows_at(UP1 + c * UP_B + 16, UP_B - 16), :]
        columns.append(jnp.concatenate([first, second], axis=0))
    return jnp.concatenate(columns, axis=1)


def down_rows(wall, j):
    return jnp.concatenate(
        [wall[1, rows_at(DOWN1 + j * 1536 + c * 256, 256), :] for c in range(6)], axis=1
    )


def merge_up(wall):
    row = lax.broadcasted_iota(jnp.int32, (16, 128), 0)

    def one(c, carry):
        low_at = rows_at(UP0 + c * UP_A + UP_A - 16, 16)
        low = wall[0, low_at, :].astype(F32)
        high = wall[1, rows_at(UP1 + c * UP_B, 16), :].astype(F32)
        cut = jnp.where(c < 2, CUT + 1 - 400, CUT - 400)
        wall[0, low_at, :] = jnp.where(row < cut, low, high).astype(BF16)
        return carry

    lax.fori_loop(0, 24, one, 0)


def stats(values):
    mean = jnp.mean(values, axis=1, keepdims=True)
    centered = values - mean
    inverse = lax.rsqrt(jnp.mean(centered * centered, axis=1, keepdims=True) + norm_eps)
    return centered * inverse, inverse


def find_places(coord_col, lut, ranks, places, tick):
    lane = lax.broadcasted_iota(jnp.int32, (8, 128), 1)
    step = lane % 16
    level = jnp.where(step <= 8, step, lax.shift_left(jnp.full_like(step, 8), jnp.maximum(step - 8, 0)))
    edge = jnp.where(lane < 16, 1 - level, jnp.where(lane == 16, 1 << 12, level))

    def line_rows(a, carry):
        at = pl.ds(pl.multiple_of(a * 8, 8), 8)
        value = coord_col[at, 0:1] + edge
        places[0, at, :] = jnp.where(value <= 0, LEN, jnp.minimum(value, LEN) - 1)
        return carry

    lax.fori_loop(0, LEN // 8, line_rows, 0, unroll=4)
    lanes = lax.broadcasted_iota(jnp.int32, (LEN, 128), 1)
    ones = jnp.ones((LEN, 128), BF16)

    def flags(condition):
        return jnp.where(condition, 1.0, 0.0).astype(BF16)

    for table in (1, 2):
        near = jnp.broadcast_to(coord_col[:, table : table + 1], (LEN, 128))
        group = near >> 7
        below = tn(flags(group == lanes), flags((near & 127) < lanes)) + tn(flags(group < lanes), ones)
        lut[...] = below[:16].astype(jnp.int32)
        luts = [jnp.broadcast_to(lut[g : g + 1, :], (8, 128)) for g in range(16)]

        def find(a, carry):
            at = pl.ds(pl.multiple_of(a * 8, 8), 8)
            value = jnp.clip(coord_col[at, table : table + 1] + edge, 0, 2047)
            low, high = value & 127, value >> 7
            found = jnp.zeros((8, 128), jnp.int32)
            for g in range(16):
                found = jnp.where(high == g, jnp.take_along_axis(luts[g], low, axis=1), found)
            places[table, at, :] = jnp.where(found == 0, LEN, found - 1)
            return carry

        for part in range(2):
            tick()
            lax.fori_loop(part * 32, part * 32 + 32, find, 0, unroll=8)


def relayout(plane, flat, out, group):
    def blocks(count, dst, src, rows, stride):
        def one(i, carry):
            out[plane, rows_at(dst(i), rows), :] = flat[pl.ds(LEAD + src(i), rows, stride=stride), :].astype(BF16)
            return carry

        lax.fori_loop(0, count, one, 0)

    def window(dst, src, count):
        out[plane, pl.ds(dst, count), :] = flat[pl.ds(LEAD + src, count), :].astype(BF16)

    def clear(low, high):
        out[plane, pl.ds(low, high - low), :] = jnp.zeros((high - low, 128), BF16)

    if plane == 0 and group == 0:
        blocks(24, lambda c: UP0 + c * UP_A, lambda c: F_UP + c, UP_A, 24)
        window(SM0, 13824, 16)
        window(SM0 + 16, 18440, 32)
        clear(SM0 + 48, ROWS)
    elif plane == 0 and group == 1:
        blocks(18, lambda pos: pos * D, lambda pos: lax.rem(pos, 3) * 6 + pos // 3, D, 18)
    elif plane == 0:
        blocks(6, lambda c: OUT0 + c * D, lambda c: F_OUT + c, D, 6)
    elif group == 0:
        for c in range(6):
            blocks(12, lambda j: DOWN1 + j * 1536 + c * 256, lambda j: F_DOWN1 + j * 1536 + c, 256, 6)
        clear(DOWN_END, LAY1)
        blocks(6, lambda c: LAY1 + c * FEAT, lambda c: F_LAY1 + c, FEAT, 6)
        window(SM1, 8728, 32)
        window(SM1 + 32, 27184, 32)
        window(SM1 + 64, 27976, 16)
        clear(SM1 + 80, ROWS)
    elif group == 1:
        blocks(24, lambda c: UP1 + c * UP_B, lambda c: c - 98, UP_B, 24)


class Gather:
    def __init__(self, stages, zall, x_send, x_recv, c_send, c_recv, sems):
        self.stages, self.zall, self.sems = stages, zall, sems
        self.x_send, self.x_recv, self.c_send, self.c_recv = x_send, x_recv, c_send, c_recv
        self.dp, self.fs = place()
        self.other = 1 - self.fs
        self.levels = len(stages)
        self.parts = offsets(self.dp, stages, CHUNK)
        self.x_peer = (self.dp, self.other)
        self.core_peer = (self.dp + 1 - 2 * (self.dp % 2), self.fs)

    def base(self, position):
        return lax.rem(CHUNKS - 1 + position, CHUNKS) * CHUNK

    def direct(self, position):
        return position >= CHUNKS - 3

    def x_copy(self, position, plane, direct):
        start, size = self.parts[0] if direct else self.parts[-1]
        where = self.zall.at[plane, rows_at(self.base(position) + start, size)]
        return remote(where, where, self.x_send.at[0], self.x_recv.at[position], self.x_peer)

    def send(self, low, high):
        def one(position, carry):
            direct = self.direct(position)

            @pl.when(direct)
            def _():
                self.x_copy(position, self.fs, True).start()

            @pl.when(jnp.logical_not(direct))
            def _():
                self.x_copy(position, self.fs, False).start()

            return carry

        lax.fori_loop(low, high, one, 0)

    def stage_copies(self, level, position):
        radix, stride = self.stages[level]
        start, size = self.parts[level + 1]
        mine = (self.dp // stride) % radix
        copies = []
        for step in range(1, radix):
            peer = (member(self.dp, radix, stride, (mine + step) % radix), self.fs)
            where = self.zall.at[self.other, rows_at(self.base(position) + start, size)]
            copies.append(
                remote(where, where, self.sems[2 * level].at[0], self.sems[2 * level + 1].at[position], peer)
            )
        return copies

    def stage_wait(self, level, position):
        size = (self.stages[level][0] - 1) * self.parts[level + 1][1]
        where = self.zall.at[self.other, rows_at(self.base(position) + self.parts[level][0], size)]
        remote(
            where, where, self.sems[2 * level].at[0], self.sems[2 * level + 1].at[position], self.x_peer
        ).wait_recv()

    def core_copy(self, position, receive):
        size = CHUNK // 2
        start = (1 - self.dp % 2 if receive else self.dp % 2) * size
        where = self.zall.at[self.other, rows_at(self.base(position) + start, size)]
        return remote(where, where, self.c_send.at[0], self.c_recv.at[position], self.core_peer)

    def work(self, position, step):
        direct = self.direct(position)
        levels = self.levels
        if step == levels + 1:
            self.core_copy(position, True).wait_recv()
            return
        if step == 0:

            @pl.when(direct)
            def _():
                self.x_copy(position, self.other, True).wait_recv()
                self.core_copy(position, False).start()

        @pl.when(jnp.logical_not(direct))
        def _():
            if step == 0:
                self.x_copy(position, self.other, False).wait_recv()
            else:
                self.stage_wait(levels - step, position)
            if step < levels:
                for copy in self.stage_copies(levels - 1 - step, position):
                    copy.start()
            else:
                self.core_copy(position, False).start()

    def tick(self, number):
        for step in range(self.levels + 1, -1, -1):
            position = number - SKEW * step

            @pl.when((position >= 0) & (position < CHUNKS))
            def _(position=position, step=step):
                self.work(position, step)

    def ticks(self):
        return CHUNKS + SKEW * (self.levels + 1)

    def finish(self):
        staged = CHUNKS - 3
        sent = [(self.x_send, 3 * self.parts[0][1] + staged * self.parts[-1][1]), (self.c_send, CHUNKS * CHUNK // 2)]
        for level, (radix, _) in enumerate(self.stages):
            sent.append((self.sems[2 * level], staged * (radix - 1) * self.parts[level + 1][1]))
        for sem, size in sent:
            where = self.zall.at[0, pl.ds(0, size)]
            remote(where, where, sem.at[0], self.x_recv.at[0], self.x_peer).wait_send()


def forward_kernel(
    stages, p_hbm, xin, cot, cnt, features, coord_row, coord_col, pick, keep,
    wall_out, cdoc_out, total, rounded_out, qkv_out, probs_out, mixed_out, one_out, inverse_one, low_out, hidden_out,
    slope_out, two_out, inverse_two, layer_out,
    flat, wall, xs, cs, cnt_slots, start, up_bias, acc, indices, short, rounded, qkv, probs, mixed, normed, low, hidden,
    slope, layer,
    in_sem, x_send, x_recv, c_send, c_recv, act_send, act_recv, n_send, n_recv, out_sem, probs_sem, feed_sem, *stage_sems,
):
    net = Gather(stages, wall, x_send, x_recv, c_send, c_recv, stage_sems)
    dp, fs, other = net.dp, net.fs, net.other
    half = LEN // 2
    pieces = 8
    span = FLAT // pieces
    loads = [
        pltpu.make_async_copy(
            p_hbm.at[pl.ds(i * span, span)], flat.at[pl.ds(LEAD + i * span, span)], in_sem.at[i]
        )
        for i in range(pieces)
    ]
    for load in loads:
        load.start()
    flat[pl.ds(0, LEAD), :] = jnp.zeros((LEAD, 128), F32)
    flat[pl.ds(LEAD + FLAT, 288), :] = jnp.zeros((288, 128), F32)
    greet_signal(stages)

    def index_rows(a, carry):
        at = pl.ds(pl.multiple_of(a * 8, 8), 8)
        for table in range(3):
            near = jnp.broadcast_to(coord_col[at, table : table + 1], (8, 128))
            for j in range(4):
                far = coord_row[table : table + 1, j * 128 : (j + 1) * 128]
                indices[table, at, j * 128 : (j + 1) * 128] = (
                    bucket_of(jnp.broadcast_to(far, (8, 128)) - near) + 32 * table
                )
        return carry

    lax.fori_loop(0, LEN // 8, index_rows, 0, unroll=4)
    greet_wait(stages)

    def act_copy(number, source, target, receive):
        where = rows_at((other if receive else fs) * half, half)
        return remote(source.at[other], target.at[where], act_send.at[number], act_recv.at[number], net.x_peer)

    rounds = [
        [
            (member(dp, radix, stride, ((dp // stride) % radix + step) % radix), fs)
            for step in range(1, radix)
        ]
        for radix, stride in stages
    ] + [[net.core_peer], [net.x_peer]]

    def count_copies(number):
        base = sum(len(r) for r in rounds[:number])
        return [
            remote(total.at[...], cnt_slots.at[base + i], n_send.at[base + i], n_recv.at[base + i], peer)
            for i, peer in enumerate(rounds[number])
        ]

    def count_round(number):
        if 0 < number <= len(rounds):
            gathered = total[...]
            base = sum(len(r) for r in rounds[: number - 1])
            for i, copy in enumerate(count_copies(number - 1)):
                copy.wait()
                gathered = gathered + cnt_slots[base + i]
            total[...] = gathered
        if number < len(rounds):
            for copy in count_copies(number):
                copy.start()

    total[...] = cnt[...]
    count_round(0)
    for load in loads:
        load.wait()

    for plane, windows in enumerate((((13824, 16), (18440, 32)), ((8728, 32), (27184, 32), (27976, 16)))):

        @pl.when(fs == plane)
        def _(plane=plane, windows=windows):
            dst = 0
            for src, size in windows:
                short[plane, pl.ds(dst, size), :] = flat[pl.ds(LEAD + src, size), :].astype(BF16)
                dst += size
            short[plane, pl.ds(dst, 96 - dst), :] = jnp.zeros((96 - dst, 128), BF16)

    def short_copy(plane):
        return remote(short.at[plane], short.at[plane], act_send.at[2], act_recv.at[2], net.x_peer)

    short_copy(fs).start()
    for group, (low_at, high_at) in enumerate(((0, 1), (1, 7), (7, CHUNKS - 3))):
        for plane in range(2):

            @pl.when(fs == plane)
            def _(plane=plane, group=group):
                relayout(plane, flat, wall, group)

        net.send(low_at, high_at)
    act_copy(0, xin, xs, False).start()
    net.send(CHUNKS - 3, CHUNKS)
    xs[pl.ds(fs * half, half), :] = xin[fs]
    cs[pl.ds(fs * half, half), :] = cot[fs]
    count_round(1)

    count_round(2)
    outs = []

    def put(source, target):
        copy = pltpu.make_async_copy(source, target, out_sem.at[len(outs)])
        copy.start()
        outs.append(copy)

    short_copy(other).wait_recv()

    small0, small1 = short[0].astype(F32), short[1].astype(F32)
    heads_by_lane = jnp.zeros((16, 128), F32)
    for table in range(3):
        flat_row = row_of(small1, 64 + 3 * table, 3)
        spread = (jnp.broadcast_to(flat_row, (16, 384)) * keep[...]).astype(BF16)
        heads_by_lane = heads_by_lane + nn(spread, pick[table])
    rows_by_head = [jnp.broadcast_to(heads_by_lane[h : h + 1, :], (8, 128)) for h in range(HEADS)]

    def bias_rows(a, carry):
        @pl.when(lax.rem(a, 2) == 0)
        def _():
            net.tick(a // 2)

        for b in range(4):
            row = a * 32 + b * 8
            at = pl.ds(pl.multiple_of(row, 8), 8)
            for j in range(4):
                sums = [None] * HEADS
                for table in range(3):
                    index = indices[table, at, j * 128 : (j + 1) * 128]
                    for h in range(HEADS):
                        found = jnp.take_along_axis(rows_by_head[h], index, axis=1)
                        sums[h] = found if sums[h] is None else sums[h] + found
                for h in range(HEADS):
                    flat[pl.ds(pl.multiple_of((4 * h + j) * LEN + row, 8), 8), :] = sums[h]
        return carry

    lax.fori_loop(0, LEN // 32, bias_rows, 0)

    act_copy(1, cot, cs, False).start()
    count_round(3)
    lag = SKEW * (net.levels + 1)

    def drain(number, carry):
        net.tick(number)
        return carry

    lax.fori_loop(LEN // 64, 2 + lag, drain, 0)
    qv_bias = row_of(small0, 0, 12)
    out_bias, gain_one, shift_one = (row_of(small0, 20 + 6 * i, 6) for i in range(3))
    down_bias, gain_two, shift_two = (row_of(small1, 38 + 6 * i, 6) for i in range(3))
    act_copy(0, xin, xs, True).wait_recv()

    w_layout = jnp.concatenate([wall[1, pl.ds(LAY1 + c * FEAT, FEAT), :] for c in range(6)], axis=1)

    def start_rows(r, carry):
        at = pl.ds(pl.multiple_of(r * QROWS, QROWS), QROWS)
        rows = xs[at, :].astype(F32) + nn(features[at, :], w_layout)
        start[at, :] = rows
        rounded[at, :] = rows.astype(BF16)
        return carry

    lax.fori_loop(0, LEN // QROWS, start_rows, 0)
    put(rounded, rounded_out)
    for i in range(18):
        up_bias[:, i * 128 : (i + 1) * 128] = (
            jnp.zeros((1, 128), F32)
            if i % 3 == 1
            else qv_bias[:, (i // 3 + 3 * (i % 3)) * 128 : (i // 3 + 3 * (i % 3) + 1) * 128]
        )
    left = lax.broadcasted_iota(jnp.int32, (LEN, 128), 1) < HDIM

    def probs_copy(pair):
        where = rows_at(pair * 8 * LEN, 8 * LEN)
        return pltpu.make_async_copy(probs.at[where], probs_out.at[where], probs_sem.at[pair])

    def attend(pair, carry):
        net.tick(2 + lag + pair)
        at = pl.multiple_of(3 * pair * D, 16)
        weight = jnp.concatenate([wall[0, rows_at(at + i * D, D), :] for i in range(3)], axis=1)
        part = nn(rounded[...], weight) + up_bias[:, pl.ds(pl.multiple_of(pair * 384, 128), 384)]
        query = part[:, :128].astype(BF16) * HDIM**-0.5
        key = part[:, 128:256].astype(BF16)
        value = part[:, 256:].astype(BF16)
        qkv[3 * pair] = query
        qkv[3 * pair + 1] = key
        qkv[3 * pair + 2] = value
        found = [[], []]
        for side in range(2):
            head = 2 * pair + side
            mine = left if side == 0 else jnp.logical_not(left)
            for r in range(0, LEN, AROWS):
                some = query[r : r + AROWS]
                extra = jnp.concatenate(
                    [flat[rows_at((4 * head + j) * LEN + r, AROWS), :] for j in range(4)], axis=1
                )
                scores = nt(jnp.where(mine[r : r + AROWS], some, jnp.zeros_like(some)), key) + extra
                scores = jnp.exp(scores - jnp.max(scores, axis=1, keepdims=True))
                soft = (scores * (1.0 / jnp.sum(scores, axis=1, keepdims=True))).astype(BF16)
                for j in range(4):
                    probs[rows_at((4 * head + j) * LEN + r, AROWS), :] = soft[:, j * 128 : (j + 1) * 128]
                found[side].append(nn(soft, value))
        mixed[:, pl.ds(pl.multiple_of(pair * 128, 128), 128)] = jnp.where(
            left, jnp.concatenate(found[0], axis=0), jnp.concatenate(found[1], axis=0)
        ).astype(BF16)
        probs_copy(pair).start()
        return carry

    lax.fori_loop(0, PAIRS, attend, 0)
    put(qkv, qkv_out)
    put(mixed, mixed_out)
    count_round(4)
    lax.fori_loop(2 + lag + PAIRS, 10 + lag, drain, 0)

    w_out = jnp.concatenate([wall[0, pl.ds(OUT0 + c * D, D), :] for c in range(6)], axis=1)

    def first_rows(r, carry):
        at = pl.ds(pl.multiple_of(r * QROWS, QROWS), QROWS)
        unit, inverse = stats(start[at, :] + nn(mixed[at, :], w_out) + out_bias)
        normed[at, :] = unit
        inverse_one[at, :] = inverse
        result = unit * gain_one + shift_one
        low[at, :] = result.astype(BF16)
        acc[at, :] = result + down_bias
        return carry

    lax.fori_loop(0, LEN // QROWS, first_rows, 0)
    put(normed, one_out)
    put(low, low_out)
    count_round(5)
    lax.fori_loop(10 + lag, net.ticks(), drain, 0)
    net.finish()
    merge_up(wall)
    put(wall, wall_out)
    for j in range(12):
        up_bias[:, j * 256 : (j + 1) * 256] = row_of(small1, 6 + 2 * j, 2)

    def feed_copies(j):
        lanes = pl.ds(pl.multiple_of(j * 256, 256), 256)
        return [
            pltpu.make_async_copy(hidden.at[:, lanes], hidden_out.at[:, lanes], feed_sem.at[0, j]),
            pltpu.make_async_copy(slope.at[:, lanes], slope_out.at[:, lanes], feed_sem.at[1, j]),
        ]

    def feed_step(j, carry):
        lanes = pl.ds(pl.multiple_of(j * 256, 256), 256)
        up = nn(low[...], up_block(wall, j)) + up_bias[:, lanes]
        half_up = 0.5 + 0.5 * lax.erf(up * math.sqrt(0.5))
        bell = jnp.exp(-0.5 * up * up) * (1.0 / math.sqrt(2.0 * math.pi))
        slope[:, lanes] = (half_up + up * bell).astype(BF16)
        part = (up * half_up).astype(BF16)
        hidden[:, lanes] = part
        acc[...] += nn(part, down_rows(wall, j))
        for copy in feed_copies(j):
            copy.start()
        return carry

    lax.fori_loop(0, 12, feed_step, 0, unroll=3)

    def second_rows(r, carry):
        at = pl.ds(pl.multiple_of(r * QROWS, QROWS), QROWS)
        unit, inverse = stats(acc[at, :])
        acc[at, :] = unit
        inverse_two[at, :] = inverse
        layer[at, :] = (unit * gain_two + shift_two).astype(BF16)
        return carry

    lax.fori_loop(0, LEN // QROWS, second_rows, 0)
    put(acc, two_out)
    put(layer, layer_out)
    act_copy(1, cot, cs, True).wait_recv()
    put(cs, cdoc_out)
    for number in range(2):
        act_copy(number, (xin, cot)[number], (xs, cs)[number], False).wait_send()
    short_copy(fs).wait_send()
    for pair in range(PAIRS):
        probs_copy(pair).wait()
    for copy in outs:
        copy.wait()

    def feed_wait(j, carry):
        for copy in feed_copies(j):
            copy.wait()
        return carry

    lax.fori_loop(0, 12, feed_wait, 0)


def forward_pass(stages, p2, xin, cot, cnt, features, coord_row, coord_col):
    pick, keep = table_constants()
    sds = jax.ShapeDtypeStruct
    dma = pltpu.SemaphoreType.DMA
    count_peers = 2 + sum(radix - 1 for radix, _ in stages)
    sems = []
    for radix, _ in stages:
        sems += [dma((1,)), dma((CHUNKS,))]
    return pl.pallas_call(
        functools.partial(forward_kernel, stages),
        name="gather_forward",
        out_shape=(
            sds((2, ROWS, 128), BF16),
            sds((LEN, D), BF16),
            sds((8, 128), F32),
            sds((LEN, D), BF16),
            sds((18, LEN, 128), BF16),
            sds((HEADS * 4 * LEN, 128), BF16),
            sds((LEN, D), BF16),
            sds((LEN, D), F32),
            sds((LEN, 1), F32),
            sds((LEN, D), BF16),
            sds((LEN, FF), BF16),
            sds((LEN, FF), BF16),
            sds((LEN, D), F32),
            sds((LEN, 1), F32),
            sds((LEN, D), BF16),
        ),
        in_specs=[ANY] + [VMEM] * 8,
        out_specs=(ANY, ANY, VMEM, ANY, ANY, ANY, ANY, ANY, VMEM, ANY, ANY, ANY, ANY, VMEM, ANY),
        scratch_shapes=[
            pltpu.VMEM((LEAD + FLAT + 288, 128), F32),
            pltpu.VMEM((2, ROWS, 128), BF16),
            pltpu.VMEM((LEN, D), BF16),
            pltpu.VMEM((LEN, D), BF16),
            pltpu.VMEM((count_peers, 8, 128), F32),
            pltpu.VMEM((LEN, D), F32),
            pltpu.VMEM((1, FF), F32),
            pltpu.VMEM((LEN, D), F32),
            pltpu.VMEM((3, LEN, LEN), jnp.int32),
            pltpu.VMEM((2, 96, 128), BF16),
            pltpu.VMEM((LEN, D), BF16),
            pltpu.VMEM((18, LEN, 128), BF16),
            pltpu.VMEM((HEADS * 4 * LEN, 128), BF16),
            pltpu.VMEM((LEN, D), BF16),
            pltpu.VMEM((LEN, D), F32),
            pltpu.VMEM((LEN, D), BF16),
            pltpu.VMEM((LEN, FF), BF16),
            pltpu.VMEM((LEN, FF), BF16),
            pltpu.VMEM((LEN, D), BF16),
            dma((8,)), dma((1,)), dma((CHUNKS,)), dma((1,)), dma((CHUNKS,)), dma((3,)), dma((3,)),
            dma((count_peers,)), dma((count_peers,)), dma((16,)), dma((PAIRS,)), dma((2, 12)),
        ]
        + sems,
        compiler_params=pltpu.CompilerParams(
            collective_id=1, has_side_effects=True, vmem_limit_bytes=64 * 2**20 - 2**16
        ),
    )(p2, xin, cot, cnt, features, coord_row, coord_col, jnp.asarray(pick), jnp.asarray(keep))


G_SMALL = (("qv_bias", 0, 0, 12), ("out_bias", 0, 12, 6), ("gain_one", 0, 18, 6), ("shift_one", 0, 24, 6),
           ("up_bias", 1, 0, 24), ("down_bias", 1, 24, 6), ("gain_two", 1, 30, 6), ("shift_two", 1, 36, 6))


def spread_norm(normed, inverse, gain, grad):
    scaled = grad * gain
    return inverse * (
        scaled
        - jnp.mean(scaled, axis=1, keepdims=True)
        - normed * jnp.mean(scaled * normed, axis=1, keepdims=True)
    )


def total_rows(values):
    return jnp.sum(values.astype(F32), axis=0, keepdims=True)


def reduce_chunk(stages):
    replicas = 2
    for radix, _ in stages:
        replicas *= radix
    return max(1024, 16 * replicas)


class Reduction:
    def __init__(self, stages, gstack, out, core_slots, x_slots, pieces, slots, sems):
        self.stages, self.gstack, self.out = stages, gstack, out
        self.core_slots, self.x_slots, self.pieces, self.slots = core_slots, x_slots, pieces, slots
        (self.c_send, self.c_recv, self.x_send, self.x_recv, self.b_send, self.b_recv, self.own_sem) = sems[:7]
        self.sems = sems[7:]
        self.dp, self.fs = place()
        self.other = 1 - self.fs
        self.size = reduce_chunk(stages)
        self.count = ROWS // self.size
        self.levels = len(stages)
        self.parts = offsets(self.dp, stages, self.size)
        self.half = self.size // 2
        self.x_peer = (self.dp, self.other)
        self.core_peer = (self.dp + 1 - 2 * (self.dp % 2), self.fs)

    def base(self, position):
        return lax.rem(2 * self.count - 2 - position, self.count) * self.size

    def ready(self, row):
        return jnp.maximum(self.count - 1 - (row + self.size - 1) // self.size, 0)

    def core_copy(self, position, plane):
        where = rows_at(self.base(position) + (1 - self.dp % 2) * self.half, self.half)
        return remote(
            self.gstack.at[plane, where], self.core_slots.at[plane, position],
            self.c_send.at[0], self.c_recv.at[plane, position], self.core_peer,
        )

    def x_copy(self, position):
        where = rows_at(self.base(position) + self.parts[0][0], self.half)
        return remote(
            self.gstack.at[self.other, where], self.x_slots.at[position],
            self.x_send.at[0], self.x_recv.at[position], self.x_peer,
        )

    def scatter_copies(self, level, position):
        radix, stride = self.stages[level]
        start, size = self.parts[level]
        size = size // radix
        mine = (self.dp // stride) % radix
        copies = []
        for step in range(1, radix):
            target = (mine + step) % radix
            where = rows_at(self.base(position) + start + target * size, size)
            copies.append(
                remote(
                    self.gstack.at[self.fs, where], self.slots[level].at[position, step - 1],
                    self.sems[4 * level].at[0], self.sems[4 * level + 1].at[position],
                    (member(self.dp, radix, stride, target), self.fs),
                )
            )
        return copies

    def scatter_wait(self, level, position):
        where = self.slots[level].at[position]
        remote(where, where, self.sems[4 * level].at[0], self.sems[4 * level + 1].at[position], self.x_peer).wait_recv()

    def spread_wait(self, level, position):
        size = (self.stages[level][0] - 1) * self.parts[level + 1][1]
        where = self.out.at[rows_at(self.base(position) + self.parts[level][0], size)]
        remote(
            where, where, self.sems[4 * level + 2].at[0], self.sems[4 * level + 3].at[position], self.x_peer
        ).wait_recv()

    def spread_copies(self, level, position):
        radix, stride = self.stages[level]
        start, size = self.parts[level + 1]
        mine = (self.dp // stride) % radix
        copies = []
        for step in range(1, radix):
            where = self.out.at[rows_at(self.base(position) + start, size)]
            source = self.pieces.at[position] if level == self.levels - 1 else where
            copies.append(
                remote(
                    source, where,
                    self.sems[4 * level + 2].at[0], self.sems[4 * level + 3].at[position],
                    (member(self.dp, radix, stride, (mine + step) % radix), self.fs),
                )
            )
        return copies

    def own_copy(self, position):
        start, size = self.parts[-1]
        return pltpu.make_async_copy(
            self.pieces.at[position], self.out.at[rows_at(self.base(position) + start, size)],
            self.own_sem.at[position],
        )

    def back_copy(self, position, receive):
        start = (1 - self.dp % 2 if receive else self.dp % 2) * self.half
        where = self.out.at[rows_at(self.base(position) + start, self.half)]
        return remote(where, where, self.b_send.at[0], self.b_recv.at[position], self.core_peer)

    def feed(self, plane, low, high):
        def one(position, carry):
            self.core_copy(position, plane).start()
            return carry

        lax.fori_loop(low, high, one, 0)

    def push(self, low, high):
        def one(position, carry):
            self.core_copy(position, self.other).wait_recv()
            where = rows_at(self.base(position) + self.parts[0][0], self.half)
            value = self.gstack[self.other, where, :].astype(F32) + self.core_slots[self.other, position].astype(F32)
            self.gstack[self.other, where, :] = value.astype(BF16)
            self.x_copy(position).start()
            return carry

        lax.fori_loop(low, high, one, 0)

    def work(self, position, step):
        levels = self.levels
        base = self.base(position)
        if step <= levels:
            start, size = self.parts[step]
            where = rows_at(base + start, size)
            if step == 0:
                self.core_copy(position, self.fs).wait_recv()
                self.x_copy(position).wait_recv()
                terms = [self.core_slots[self.fs, position], self.x_slots[position]]
            else:
                self.scatter_wait(step - 1, position)
                terms = [self.slots[step - 1][position, i] for i in range(self.stages[step - 1][0] - 1)]
            value = self.gstack[self.fs, where, :].astype(F32)
            for term in terms:
                value = value + term.astype(F32)
            if step < levels:
                self.gstack[self.fs, where, :] = value.astype(BF16)
                for copy in self.scatter_copies(step, position):
                    copy.start()
            else:
                self.pieces[position] = value.astype(BF16)
                self.own_copy(position).start()
                for copy in self.spread_copies(levels - 1, position):
                    copy.start()
        else:
            level = 2 * levels - step
            self.spread_wait(level, position)
            if level == levels - 1:
                self.own_copy(position).wait()
            if level > 0:
                for copy in self.spread_copies(level - 1, position):
                    copy.start()
            else:
                self.back_copy(position, False).start()

    def tick(self, number):
        for step in range(2 * self.levels, -1, -1):
            position = number - SKEW * step

            @pl.when((position >= 0) & (position < self.count))
            def _(position=position, step=step):
                self.work(position, step)

    def ticks(self):
        return self.count + 2 * SKEW * self.levels

    def finish(self):
        def one(position, carry):
            self.back_copy(position, True).wait_recv()
            return carry

        lax.fori_loop(0, self.count, one, 0)
        sent = [(self.c_send, 2 * self.half), (self.x_send, self.half), (self.b_send, self.half)]
        for level, (radix, _) in enumerate(self.stages):
            size = (radix - 1) * self.parts[level + 1][1]
            sent += [(self.sems[4 * level], size), (self.sems[4 * level + 2], size)]
        for sem, size in sent:
            where = self.gstack.at[0, pl.ds(0, self.count * size)]
            remote(where, where, sem.at[0], self.x_recv.at[0], self.x_peer).wait_send()


def reduction_scratch(stages):
    size = reduce_chunk(stages)
    count, half = ROWS // size, size // 2
    dma = pltpu.SemaphoreType.DMA
    slots, sems = [], []
    for radix, _ in stages:
        half = half // radix
        slots.append(pltpu.VMEM((count, radix - 1, half, 128), BF16))
        sems += [dma((1,)), dma((count,))] * 2
    return (
        [
            pltpu.VMEM((2, count, size // 2, 128), BF16),
            pltpu.VMEM((count, size // 2, 128), BF16),
            pltpu.VMEM((count, half, 128), BF16),
        ]
        + slots,
        [dma((1,)), dma((2, count)), dma((1,)), dma((count,)), dma((1,)), dma((count,)), dma((count,))] + sems,
    )


def backward_kernel(
    stages,
    wall_hbm, cdoc_hbm, total, rounded_hbm, qkv_hbm, probs_hbm, mixed_hbm, one_hbm, inverse_one, low_hbm, hidden_hbm,
    slope_hbm, two_hbm, inverse_two, features, coord_row, coord_col, pick, keep,
    input_grad, reduced, tables, norm,
    wall, gstack, acc, branch, hidden, d_up, low, rounded, qkv, mixed, normed_one, places, lut, ranks, small,
    square_slots, load_sem, step_sem, probs_sem, act_sem, n_send, n_recv, *rest,
):
    levels = len(stages)
    parts_vmem, sems = rest[: 3 + levels], rest[3 + levels :]
    red = Reduction(stages, gstack, reduced, parts_vmem[0], parts_vmem[1], parts_vmem[2], parts_vmem[3:], sems)
    dp, fs, other = red.dp, red.fs, red.other

    early = [
        pltpu.make_async_copy(wall_hbm.at[:, pl.ds(SM0, 256)], wall.at[:, pl.ds(SM0, 256)], load_sem.at[0]),
        pltpu.make_async_copy(cdoc_hbm, branch, load_sem.at[1]),
        pltpu.make_async_copy(two_hbm, acc, load_sem.at[2]),
    ]
    lows = [pltpu.make_async_copy(low_hbm, low, load_sem.at[3])]
    rest_loads = [
        pltpu.make_async_copy(one_hbm, normed_one, load_sem.at[4]),
        pltpu.make_async_copy(wall_hbm.at[0, pl.ds(0, UP0)], wall.at[0, pl.ds(0, UP0)], load_sem.at[5]),
        pltpu.make_async_copy(mixed_hbm, mixed, load_sem.at[6]),
        pltpu.make_async_copy(qkv_hbm, qkv, load_sem.at[7]),
        pltpu.make_async_copy(rounded_hbm, rounded, load_sem.at[8]),
    ]

    def step_loads(j):
        lanes = pl.ds(pl.multiple_of(j * 256, 256), 256)
        areas = [(1, DOWN1 + 1536 * j, 1536), (0, UP0 + 2 * UP_A * j, 2 * UP_A), (1, UP1 + 2 * UP_B * j, 2 * UP_B)]
        copies = [
            pltpu.make_async_copy(
                wall_hbm.at[plane, rows_at(start, size)], wall.at[plane, rows_at(start, size)], step_sem.at[i, j]
            )
            for i, (plane, start, size) in enumerate(areas)
        ]
        copies.append(pltpu.make_async_copy(hidden_hbm.at[:, lanes], hidden.at[:, lanes], step_sem.at[3, j]))
        copies.append(pltpu.make_async_copy(slope_hbm.at[:, lanes], d_up.at[:, lanes], step_sem.at[4, j]))
        return copies

    for load in early + lows:
        load.start()

    def start_loads(it, carry):
        for load in step_loads(11 - it):
            load.start()
        return carry

    lax.fori_loop(0, 12, start_loads, 0)
    for load in rest_loads:
        load.start()
    greet_signal(stages)
    greet_wait(stages)
    small[...] = jnp.zeros_like(small)
    gstack[1, pl.ds(DOWN_END, LAY1 - DOWN_END), :] = jnp.zeros((LAY1 - DOWN_END, 128), BF16)
    for load in early:
        load.wait()

    small0 = wall[0, pl.ds(SM0, 48), :].astype(F32)
    small1 = wall[1, pl.ds(SM1, 80), :].astype(F32)
    gain_one = row_of(small0, 26, 6)
    gain_two = row_of(small1, 44, 6)
    spots = {name: (plane, first_row) for name, plane, first_row, _ in G_SMALL}

    def keep_small(name, vector):
        plane, at = spots[name]
        for i in range(vector.shape[1] // 128):
            small[plane, at + i : at + i + 1, :] = vector[:, i * 128 : (i + 1) * 128]

    count = total[0:1, 0:1]
    none = jnp.zeros((1, D), F32)

    def second_rows(r, sums):
        at = pl.ds(pl.multiple_of(r * QROWS, QROWS), QROWS)
        grad_out = branch[at, :].astype(F32) / count
        normed = acc[at, :]
        result = spread_norm(normed, inverse_two[at, :], gain_two, grad_out)
        acc[at, :] = result
        lower = result.astype(BF16)
        branch[at, :] = lower
        return sums[0] + total_rows(grad_out * normed), sums[1] + total_rows(grad_out), sums[2] + total_rows(lower)

    sums = lax.fori_loop(0, LEN // QROWS, second_rows, (none, none, none))
    for name, vector in zip(("gain_two", "shift_two", "down_bias"), sums):
        keep_small(name, vector)
    plane_up, at_up = spots["up_bias"]
    lows[0].wait()

    def fed(plane, it):
        row = UP0 + 2 * UP_A * (11 - it) if plane == 0 else DOWN1 + 1536 * (11 - it)
        return red.ready(row)

    def of_other(values):
        return jnp.where(other == 0, values[0], values[1])

    fine = red.count >= 28
    tile_row = lax.broadcasted_iota(jnp.int32, (16, 128), 0)

    def feed_step(it, carry):
        j = 11 - it
        for load in step_loads(j):
            load.wait()
        for plane in range(2):
            red.feed(plane, fed(plane, it - 2), fed(plane, it - 1))
        red.push(of_other([fed(p, it - 3) for p in range(2)]), of_other([fed(p, it - 2) for p in range(2)]))
        @pl.when(it == 10)
        def _():
            red.tick(0)

        lanes = pl.ds(pl.multiple_of(j * 256, 256), 256)
        grad = nt(branch[...], down_rows(wall, j))
        part = (grad * d_up[:, lanes].astype(F32)).astype(BF16)
        d_up[:, lanes] = part
        sums = total_rows(part)
        small[plane_up, pl.ds(at_up + 2 * j, 1), :] = sums[:, :128]
        small[plane_up, pl.ds(at_up + 2 * j + 1, 1), :] = sums[:, 128:]
        down = tn(hidden[:, lanes], branch[...]).astype(BF16)
        for c in range(6):
            gstack[1, rows_at(DOWN1 + j * 1536 + c * 256, 256), :] = down[:, c * 128 : (c + 1) * 128]
        up = tn(low[...], part)
        for i in range(2):
            c = 2 * j + i
            cut = jnp.where(c < 2, CUT + 1 - 400, CUT - 400)
            columns = up[:, i * 128 : (i + 1) * 128]
            tile = columns[400:416]
            gstack[0, rows_at(UP0 + c * UP_A, 400), :] = columns[:400].astype(BF16)
            gstack[0, rows_at(UP0 + c * UP_A + 400, 16), :] = jnp.where(tile_row < cut, tile, 0.0).astype(BF16)
            gstack[1, rows_at(UP1 + c * UP_B, 16), :] = jnp.where(tile_row < cut, 0.0, tile).astype(BF16)
            gstack[1, rows_at(UP1 + c * UP_B + 16, UP_B - 16), :] = columns[416:].astype(BF16)
        acc[...] += nt(part, up_block(wall, j))
        return carry

    lax.fori_loop(0, 12, feed_step, 0)

    def probs_copy(pair, slot):
        size = 8 * LEN
        return pltpu.make_async_copy(
            probs_hbm.at[rows_at(pair * size, size)], wall.at[0, rows_at(UP0 + slot * size, size)], probs_sem.at[slot]
        )

    probs_copy(PAIRS - 1, 0).start()
    last = red.count - 1
    red.feed(0, fed(0, 10), fed(0, 11))
    red.feed(1, fed(1, 10), last)
    red.push(of_other([fed(p, 9) for p in range(2)]), of_other([fed(p, 10) for p in range(2)]))
    red.tick(1)
    for load in rest_loads:
        load.wait()

    w_out = jnp.concatenate([wall[0, pl.ds(OUT0 + c * D, D), :] for c in range(6)], axis=1)

    def first_rows(r, sums):
        at = pl.ds(pl.multiple_of(r * QROWS, QROWS), QROWS)
        grad, normed = acc[at, :], normed_one[at, :]
        result = spread_norm(normed, inverse_one[at, :], gain_one, grad)
        acc[at, :] = result
        lower = result.astype(BF16)
        branch[at, :] = lower
        low[at, :] = nt(lower, w_out).astype(BF16)
        return sums[0] + total_rows(grad * normed), sums[1] + total_rows(grad), sums[2] + total_rows(lower)

    sums = lax.fori_loop(0, LEN // QROWS, first_rows, (none, none, none))
    for name, vector in zip(("gain_one", "shift_one", "out_bias"), sums):
        keep_small(name, vector)
    red.push(of_other([fed(p, 10) for p in range(2)]), jnp.where(other == 0, fed(0, 11), last))

    red.tick(2)

    def drain(number, carry):
        red.tick(number)
        return carry

    per_pair = 2 if fine else 1

    def out_step(j, carry):
        lanes = pl.ds(pl.multiple_of(j * 256, 256), 256)
        part = tn(mixed[...], branch[:, lanes]).astype(BF16)
        for i in range(2):
            gstack[0, rows_at(OUT0 + (2 * j + i) * D, D), :] = part[:, i * 128 : (i + 1) * 128]
        return carry

    lax.fori_loop(0, 3, out_step, 0)
    begun = 3
    if fine:
        red.tick(3)
        begun = 4

    left = lax.broadcasted_iota(jnp.int32, (LEN, 128), 1) < HDIM

    def sent(it):
        return red.ready(jnp.where(it <= -2, UP0, 2304 * (5 - it)))

    def score_rows(head, j, start, size):
        return rows_at((4 * head + j) * LEN + start, size)

    def attend(it, carry):
        pair = PAIRS - 1 - it
        slot = lax.rem(it, 2)

        @pl.when(it + 1 < PAIRS)
        def _():
            probs_copy(pair - 1, 1 - slot).start()

        red.feed(0, sent(it - 2), sent(it - 1))

        @pl.when(other == 0)
        def _():
            red.push(sent(it - 3), sent(it - 2))

        red.tick(begun + per_pair * it)
        probs_copy(pair, slot).wait()
        query, key, value = qkv[3 * pair], qkv[3 * pair + 1], qkv[3 * pair + 2]
        grad = low[:, pl.ds(pl.multiple_of(pair * 128, 128), 128)]
        found = []
        for side in range(2):
            if side == 1 and per_pair == 2:
                red.tick(begun + per_pair * it + 1)
            head = 2 * pair + side
            mine = left if side == 0 else jnp.logical_not(left)
            base = UP0 + slot * 8 * LEN + side * 4 * LEN
            for r in range(0, LEN, BROWS):
                part = grad[r : r + BROWS]
                d_probs = nt(jnp.where(mine[r : r + BROWS], part, jnp.zeros_like(part)), value)
                soft = jnp.concatenate(
                    [wall[0, rows_at(base + j * LEN + r, BROWS), :] for j in range(4)], axis=1
                ).astype(F32)
                inner = jnp.sum(soft * d_probs, axis=1, keepdims=True)
                scores = (soft * (d_probs - inner)).astype(BF16)
                for j in range(4):
                    wall[1, score_rows(head, j, r, BROWS), :] = scores[:, j * 128 : (j + 1) * 128]
            scores = jnp.concatenate([wall[1, score_rows(head, j, 0, LEN), :] for j in range(4)], axis=1)
            chances = jnp.concatenate([wall[0, rows_at(base + j * LEN, LEN), :] for j in range(4)], axis=1)
            found.append((nn(scores, key), tn(scores, query), tn(chances, grad)))
        d_query = (jnp.where(left, found[0][0], found[1][0]) * HDIM**-0.5).astype(BF16)
        d_key = jnp.where(left, found[0][1], found[1][1]).astype(BF16)
        d_value = jnp.where(left, found[0][2], found[1][2]).astype(BF16)
        both = jnp.concatenate([d_query, d_key, d_value], axis=1)
        plane, spot = spots["qv_bias"]
        small[plane, pl.ds(spot + pair, 1), :] = total_rows(d_query)
        small[plane, pl.ds(spot + 6 + pair, 1), :] = total_rows(d_value)
        at = pl.multiple_of(3 * pair * D, 16)
        weight = jnp.concatenate([wall[0, rows_at(at + i * D, D), :] for i in range(3)], axis=1)
        acc[...] += nt(both, weight)
        part = tn(rounded[...], both).astype(BF16)
        for i in range(3):
            gstack[0, rows_at(at + i * D, D), :] = part[:, i * 128 : (i + 1) * 128]
        return carry

    lax.fori_loop(0, PAIRS, attend, 0)
    red.feed(0, sent(4), sent(5))

    @pl.when(other == 0)
    def _():
        red.push(sent(3), sent(4))

    branch[...] = acc[...].astype(BF16)
    act_out = pltpu.make_async_copy(branch, input_grad, act_sem.at[0])
    act_out.start()
    layout = tn(features[...], branch[...]).astype(BF16)
    for c in range(6):
        gstack[1, pl.ds(LAY1 + c * FEAT, FEAT), :] = layout[:, c * 128 : (c + 1) * 128]

    @pl.when(other == 0)
    def _():
        red.push(sent(4), sent(5))

    late = begun + per_pair * PAIRS
    for plane in range(2):
        gstack[plane, pl.ds(SM0, 64), :] = small[plane].astype(BF16)
        gstack[plane, pl.ds(SM0 + 64, ROWS - SM0 - 64), :] = jnp.zeros((ROWS - SM0 - 64, 128), BF16)
        red.feed(plane, last, last + 1)
    drain(late, 0)
    red.push(last, last + 1)
    late += 1
    summed = red.count + SKEW * levels
    passed = [late]

    def tick():
        red.tick(passed[0])
        passed[0] += 1

    find_places(coord_col, lut, ranks, places, tick if fine else lambda: None)
    for table in (1, 2):
        key_row = jnp.broadcast_to(coord_row[table : table + 1, :], (256, LEN))
        for r in (0, 256):
            near = jnp.broadcast_to(coord_col[r : r + 256, table : table + 1], (256, LEN))
            lower = jnp.where(key_row < near, 1.0, 0.0).astype(BF16)
            ranks[table - 1, r : r + 256, :] = nn(lower, jnp.ones((LEN, 128), BF16))
    late = passed[0]
    pace = 2 if fine else 4
    table_grads(wall, coord_col, pick, keep, hidden, places, ranks, normed_one, tables, red, late, pace, summed)
    late = min(late + 24 // pace, summed)
    lax.fori_loop(late, summed, drain, 0)

    def squares(position, carry):
        piece = red.pieces[position].astype(F32)
        return carry + jnp.sum((piece * piece).reshape(-1, 8, 128), axis=0)

    value = lax.fori_loop(0, red.count, squares, jnp.zeros((8, 128), F32))
    value = jnp.sum(jnp.sum(value, axis=0, keepdims=True), axis=1, keepdims=True)
    tables[9:10, :] = jnp.broadcast_to(value, (1, 128))
    rounds = [
        [
            (member(dp, radix, stride, ((dp // stride) % radix + step) % radix), fs)
            for step in range(1, radix)
        ]
        for radix, stride in stages
    ] + [[red.core_peer], [red.x_peer]]

    def square_copies(number):
        base = sum(len(r) for r in rounds[:number])
        return [
            remote(tables.at[...], square_slots.at[base + i], n_send.at[base + i], n_recv.at[base + i], peer)
            for i, peer in enumerate(rounds[number])
        ]

    for number in range(max(red.ticks() - summed, len(rounds)) + 1):
        if number < len(rounds):
            for copy in square_copies(number):
                copy.start()
        if summed + number < red.ticks():
            red.tick(summed + number)
        if number < len(rounds):
            gathered = tables[...]
            base = sum(len(r) for r in rounds[:number])
            for i, copy in enumerate(square_copies(number)):
                copy.wait()
                gathered = gathered + square_slots[base + i]
            tables[...] = gathered
    gathered = tables[0:9, :]
    gathered = jnp.sum(jnp.sum(gathered * gathered, axis=0, keepdims=True), axis=1, keepdims=True)
    norm[...] = jnp.broadcast_to(jnp.sqrt(tables[9:10, :] + gathered), (8, 128))

    red.finish()
    act_out.wait()


def table_grads(wall, coord_col, pick, keep, less, places, ranks, prefix, tables, red, late, pace, summed):
    tables[...] = jnp.zeros_like(tables)
    block = 64
    for table in range(3):
        order = lax.broadcasted_iota(jnp.int32, (16, LEN), 1)

        def less_rows(a, carry):
            at = pl.ds(pl.multiple_of(a * 16, 16), 16)
            if table == 0:
                near = jnp.broadcast_to(coord_col[at, 0:1], (16, LEN))
            else:
                near = jnp.concatenate([ranks[table - 1, at, :].astype(jnp.int32)] * 4, axis=1)
            less[at, 0:LEN] = jnp.where(near <= order, 1.0, 0.0).astype(BF16)
            return carry

        lax.fori_loop(0, LEN // 16, less_rows, 0, unroll=4)

        def query_rows(b, sums):
            number = late + (table * 8 + b) // pace

            @pl.when((lax.rem(table * 8 + b, pace) == 0) & (number < summed))
            def _():
                red.tick(number)

            start = b * block
            scores = jnp.concatenate(
                [
                    jnp.concatenate(
                        [wall[1, rows_at((4 * h + j) * LEN + start, block), :] for j in range(4)], axis=1
                    )
                    for h in range(HEADS)
                ],
                axis=0,
            )
            running = nn(scores, less[:, 0:LEN])
            for h in range(HEADS):
                for j in range(4):
                    r, c = (4 * h + j) // 6 * 64, (4 * h + j) % 6 * 128
                    prefix[r : r + 64, c : c + 128] = running[h * block : (h + 1) * block, j * 128 : (j + 1) * 128]

            def pick_up(a, carry):
                place_of = places[table, pl.ds(pl.multiple_of(start + a * 8, 8), 8), :]
                low, high = place_of & 127, place_of >> 7
                result = []
                for h in range(HEADS):
                    value = jnp.zeros((8, 128), F32)
                    for j in range(4):
                        r, c = (4 * h + j) // 6 * 64, (4 * h + j) % 6 * 128
                        rows = pl.ds(pl.multiple_of(r + a * 8, 8), 8)
                        part = jnp.take_along_axis(prefix[rows, c : c + 128], low, axis=1)
                        value = jnp.where(high == j, part, value)
                    result.append(carry[h] + value)
                return tuple(result)

            return lax.fori_loop(0, block // 8, pick_up, sums, unroll=8)

        sums = lax.fori_loop(
            0, LEN // block, query_rows, tuple(jnp.zeros((8, 128), F32) for _ in range(HEADS))
        )
        heads = jnp.concatenate(
            [jnp.sum(s, axis=0, keepdims=True) for s in sums] + [jnp.zeros((4, 128), F32)], axis=0
        )
        after = pltpu.roll(heads, 127, 1)
        whole = pltpu.roll(heads, 15, 1)
        lanes = lax.broadcasted_iota(jnp.int32, (16, 128), 1)
        buckets = jnp.where(lanes < 16, heads - after, after - heads)
        buckets = jnp.where(lanes == 15, heads, buckets)
        buckets = jnp.where(lanes == 16, 0.0, buckets)
        buckets = jnp.where(lanes == 31, whole - heads, buckets)
        buckets = jnp.where(lanes < 32, buckets, 0.0)
        placed = buckets if table == 0 else pltpu.roll(buckets, 32 * table, 1)
        parts, left_over = [], placed
        for _ in range(2):
            parts.append(left_over.astype(BF16))
            left_over = left_over - parts[-1].astype(F32)
        spread = sum(nt(part, pick[table]) for part in parts)
        flat_row = jnp.sum(spread * keep[...], axis=0, keepdims=True)
        for i in range(3):
            tables[3 * table + i : 3 * table + i + 1, :] = flat_row[:, i * 128 : (i + 1) * 128]


def backward_pass(stages, wall, cdoc, total, saved, features, coord_row, coord_col):
    pick, keep = table_constants()
    sds = jax.ShapeDtypeStruct
    count_peers = 2 + sum(radix - 1 for radix, _ in stages)
    dma = pltpu.SemaphoreType.DMA
    buffers, sems = reduction_scratch(stages)
    return pl.pallas_call(
        functools.partial(backward_kernel, stages),
        name="backward_reduce",
        out_shape=(sds((LEN, D), BF16), sds((ROWS, 128), BF16), sds((16, 128), F32), sds((8, 128), F32)),
        in_specs=[ANY, ANY, VMEM, ANY, ANY, ANY, ANY, ANY, VMEM, ANY, ANY, ANY, ANY, VMEM] + [VMEM] * 5,
        out_specs=(ANY, ANY, VMEM, VMEM),
        scratch_shapes=[
            pltpu.VMEM((2, ROWS, 128), BF16),
            pltpu.VMEM((2, ROWS, 128), BF16),
            pltpu.VMEM((LEN, D), F32),
            pltpu.VMEM((LEN, D), BF16),
            pltpu.VMEM((LEN, FF), BF16),
            pltpu.VMEM((LEN, FF), BF16),
            pltpu.VMEM((LEN, D), BF16),
            pltpu.VMEM((LEN, D), BF16),
            pltpu.VMEM((18, LEN, 128), BF16),
            pltpu.VMEM((LEN, D), BF16),
            pltpu.VMEM((LEN, D), F32),
            pltpu.VMEM((3, LEN, 128), jnp.int32),
            pltpu.VMEM((16, 128), jnp.int32),
            pltpu.VMEM((2, LEN, 128), F32),
            pltpu.VMEM((2, 64, 128), F32),
            pltpu.VMEM((count_peers, 16, 128), F32),
            dma((10,)), dma((5, 12)), dma((2,)), dma((1,)), dma((count_peers,)), dma((count_peers,)),
        ]
        + buffers
        + sems,
        compiler_params=pltpu.CompilerParams(
            collective_id=2, has_side_effects=True, vmem_limit_bytes=64 * 2**20 - 2**16
        ),
    )(wall, cdoc, total, *saved, features, coord_row, coord_col, jnp.asarray(pick), jnp.asarray(keep))


BLOCK = 1408
DEEP_IN, DEEP_OUT = 4, 3


def flatten_rows(plane, step, source, tables, flat):
    def blocks(low, high, src, dst, rows, stride):
        def one(i, carry):
            flat[pl.ds(LEAD + dst(i), rows, stride=stride), :] = source[rows_at(src(i), rows), :].astype(F32)
            return carry

        lax.fori_loop(low, high, one, 0)

    if plane == 0:
        for part in (0, 1) if step == 0 else (step + 1,) if step < 7 else ():
            blocks(
                0, 18, lambda pos: pos * D + 96 * part,
                lambda pos: lax.rem(pos, 3) * 6 + pos // 3 + 96 * 18 * part, 96, 18,
            )
        if step == 4:
            small = source[pl.ds(SM0, 64), :].astype(F32)
            flat[pl.ds(LEAD + 13824, 12), :] = small[0:12]
            flat[pl.ds(LEAD + 18444, 18), :] = small[12:30]
        elif step == 7:
            blocks(0, 6, lambda c: OUT0 + c * D, lambda c: F_OUT + c, D, 6)
        elif step in (10, 11):
            first = 208 * (step - 10)
            blocks(0, 24, lambda c: UP0 + c * UP_A + first, lambda c: F_UP + c + 24 * first, 208, 24)
    else:
        if step < 4:
            first, rows = 96 * step, min(96, UP_B - 96 * step)
            blocks(0, 24, lambda c: UP1 + c * UP_B + first, lambda c: c - 98 + 24 * first, rows, 24)
        elif step < 16:
            j = step - 4
            blocks(
                0, 6, lambda c: DOWN1 + j * 1536 + c * 256, lambda c: F_DOWN1 + j * 1536 + c, 256, 6
            )
        if step == 4:
            small = source[pl.ds(SM1, 64), :].astype(F32)
            flat[pl.ds(LEAD + F_UPB1, 24), :] = small[0:24]
            flat[pl.ds(LEAD + F_SM1, 18), :] = small[24:42]
            flat[pl.ds(LEAD + F_TAB1, 9), :] = tables[0:9, :]
            rest = FLAT - F_TAB1 - 9
            flat[pl.ds(LEAD + F_TAB1 + 9, rest), :] = jnp.zeros((rest, 128), F32)
        elif step == 16:
            blocks(0, 6, lambda c: LAY1 + c * FEAT, lambda c: F_LAY1 + c, FEAT, 6)


def adam_kernel(
    source_hbm, tables, weights_hbm, first_hbm, second_hbm, grad_hbm, update_hbm, new_hbm,
    source, flat, weights, first, second, update, new, sem, in_sem, out_sem,
):
    fs = lax.axis_index("fsdp")
    steps = FLAT // BLOCK
    loads = [
        pltpu.make_async_copy(source_hbm.at[pl.ds(a, n)], source.at[pl.ds(a, n)], sem.at[i])
        for i, (a, n) in enumerate(((0, OUT0), (OUT0, ROWS - OUT0)))
    ]

    def fetch(step):
        where, slot = pl.ds(step * BLOCK, BLOCK), step % DEEP_IN
        return [
            pltpu.make_async_copy(ref.at[where], buffer.at[slot], in_sem.at[i, slot])
            for i, (ref, buffer) in enumerate(((weights_hbm, weights), (first_hbm, first), (second_hbm, second)))
        ]

    def store(step):
        where, slot = pl.ds(step * BLOCK, BLOCK), step % DEEP_OUT
        return [
            pltpu.make_async_copy(flat.at[pl.ds(LEAD + step * BLOCK, BLOCK)], grad_hbm.at[where], out_sem.at[0, slot]),
            pltpu.make_async_copy(update.at[slot], update_hbm.at[where], out_sem.at[1, slot]),
            pltpu.make_async_copy(new.at[slot], new_hbm.at[where], out_sem.at[2, slot]),
        ]

    loads[0].start()
    for step in range(DEEP_IN):
        for copy in fetch(step):
            copy.start()
        if step == 0:
            loads[1].start()
    part = 176
    row = lax.broadcasted_iota(jnp.int32, (part, 128), 0)
    for step in range(steps):
        if step == 0:
            loads[0].wait()
        if step == 3:
            loads[1].wait()
        for plane in range(2):

            @pl.when(fs == plane)
            def _(plane=plane, step=step):
                flatten_rows(plane, step, source, tables, flat)

        if step >= DEEP_OUT:
            for copy in store(step - DEEP_OUT):
                copy.wait()
        for copy in fetch(step):
            copy.wait()
        slot_in, slot_out = step % DEEP_IN, step % DEEP_OUT

        def some(i, carry):
            at = pl.ds(pl.multiple_of(i * part, 8), part)
            begin = pl.multiple_of(step * BLOCK + i * part, 8)
            grad = flat[pl.ds(LEAD + begin, part), :]
            new_first = adam_one * first[slot_in, at, :] + (1.0 - adam_one) * grad
            new_second = adam_two * second[slot_in, at, :] + (1.0 - adam_two) * grad * grad
            spread = jnp.sqrt(new_second * (1.0 / (1.0 - adam_two**adam_steps))) + adam_eps
            corrected = new_first * (1.0 / (1.0 - adam_one**adam_steps)) / spread
            rate = jnp.where((fs == 1) & (row + begin >= F_LAY1), table_factor, 1.0)
            update[slot_out, at, :] = rate * (corrected + decay_rate * weights[slot_in, at, :])
            new[slot_out, at, :] = new_first
            return carry

        lax.fori_loop(0, BLOCK // part, some, 0)
        for copy in store(step):
            copy.start()
        if step + DEEP_IN < steps:
            for copy in fetch(step + DEEP_IN):
                copy.start()
    for step in range(steps - DEEP_OUT, steps):
        for copy in store(step):
            copy.wait()


def adam(source, tables, weights, first, second):
    vector = jax.ShapeDtypeStruct((FLAT, 128), F32)
    dma = pltpu.SemaphoreType.DMA
    return pl.pallas_call(
        adam_kernel,
        name="adamw",
        out_shape=(vector, vector, vector),
        in_specs=[ANY, VMEM, ANY, ANY, ANY],
        out_specs=(ANY, ANY, ANY),
        scratch_shapes=[
            pltpu.VMEM((ROWS, 128), BF16),
            pltpu.VMEM((LEAD + FLAT + 288, 128), F32),
        ]
        + [pltpu.VMEM((DEEP_IN, BLOCK, 128), F32)] * 3
        + [pltpu.VMEM((DEEP_OUT, BLOCK, 128), F32)] * 2
        + [dma((2,)), dma((3, DEEP_IN)), dma((3, DEEP_OUT))],
        compiler_params=pltpu.CompilerParams(vmem_limit_bytes=60 * 2**20),
    )(source, tables, weights, first, second)


def layout_features(coords):
    freq_count = FEAT // 8
    factors = (jnp.arange(freq_count, dtype=jnp.int32) + 1) ** 2
    phases = coords[..., :, None] * factors % 4096
    angles = phases.astype(F32) * (2.0 * math.pi / 4096.0)
    wave_parts = jnp.concatenate([jnp.sin(angles), jnp.cos(angles)], axis=-1)
    return wave_parts.reshape(coords.shape[:-1] + (FEAT,))


def local(stages, inputs, box_coords, mlm_mask, cotangent, params, first_moment, second_moment):
    fs = lax.axis_index("fsdp")
    masked = cotangent * mlm_mask.astype(BF16)[..., None]
    count = jnp.full((8, 128), jnp.sum(mlm_mask.astype(F32)))
    boxes = lax.dynamic_index_in_dim(box_coords, fs, 0, keepdims=False)
    features = layout_features(boxes).astype(BF16)
    coord_col = jnp.stack(
        [jnp.arange(LEN, dtype=jnp.int32), boxes[:, 0] + boxes[:, 2], boxes[:, 1] + boxes[:, 3]], axis=1
    )
    coord_row = coord_col.T
    flat = [v.reshape(FLAT, 128) for v in (params, first_moment, second_moment)]
    wall, cdoc, total, *saved, out_doc = forward_pass(
        stages, flat[0], inputs, masked, count, features, coord_row, coord_col
    )
    grad_doc, reduced, tables, norm = backward_pass(
        stages, wall, cdoc, total, saved, features, coord_row, coord_col
    )
    half = LEN // 2

    def moved(doc):
        return lax.ppermute(lax.dynamic_slice_in_dim(doc, (1 - fs) * half, half, 0), "fsdp", [(0, 1), (1, 0)])

    def owned(doc, other):
        mine = lax.dynamic_slice_in_dim(doc, fs * half, half, 0)
        return jnp.where(fs == 0, jnp.stack([mine, other]), jnp.stack([other, mine]))

    out_other, grad_other = moved(out_doc), moved(grad_doc)
    grad, update, new_first = adam(reduced, tables, *flat)
    return (
        owned(out_doc, out_other),
        owned(grad_doc, grad_other),
        grad.reshape(-1),
        norm[0, 0],
        update.reshape(-1),
        new_first.reshape(-1),
    )


def solution(mesh):
    in_specs = (
        P("dp", "fsdp", None),
        P("dp", None, None),
        P("dp", "fsdp"),
        P("dp", "fsdp", None),
        P("fsdp"),
        P("fsdp"),
        P("fsdp"),
    )
    out_specs = (P("dp", "fsdp", None), P("dp", "fsdp", None), P("fsdp"), P(), P("fsdp"), P("fsdp"))
    stages = radices(mesh.shape["dp"])
    return jax.shard_map(
        functools.partial(local, stages), mesh=mesh, in_specs=in_specs, out_specs=out_specs, check_vma=False
    )
```

```python
import functools
import math

import jax
import jax.numpy as jnp
import numpy as np
from jax import lax
from jax.experimental import pallas as pl
from jax.experimental.pallas import tpu as pltpu
from jax.sharding import PartitionSpec as P

D = 768
HEADS = 12
HDIM = 64
FF = 3072
BUCKETS = 32
FEAT = 128
LEN = 512
PADDED = 7208960
SHARD = PADDED // 2
FLAT = SHARD // 128
PAIRS = HEADS // 2
QROWS = 256
AROWS = 512
BROWS = 256
SKEW = 2

norm_eps = 1e-05
adam_one = 0.9
adam_two = 0.999
adam_eps = 1e-08
adam_steps = 100.0
decay_rate = 0.01
table_factor = 5.0

MESH = pl.DeviceIdType.MESH
F32 = jnp.float32
BF16 = jnp.bfloat16
VMEM = pl.BlockSpec(memory_space=pltpu.VMEM)
ANY = pl.BlockSpec(memory_space=pl.ANY)

ROWS = 28672
CHUNK = 2048
CHUNKS = ROWS // CHUNK
CUT = 404
UP_A, UP_B = 416, 368
OUT0 = 18 * D
UP0 = OUT0 + 6 * D
SM0 = UP0 + 24 * UP_A
UP1 = 0
DOWN1 = 24 * UP_B
DOWN_END = DOWN1 + 6 * FF
LAY1 = 27648
SM1 = LAY1 + 6 * FEAT
F_OUT = 13836
F_UP = 18462
F_UPB1 = 8734
F_DOWN1 = 8758
F_SM1 = 27190
F_LAY1 = 27208
F_TAB1 = 27976
LEAD = 104


def nt(a, b):
    return lax.dot_general(a, b, (((1,), (1,)), ((), ())), preferred_element_type=F32)


def nn(a, b):
    return lax.dot_general(a, b, (((1,), (0,)), ((), ())), preferred_element_type=F32)


def tn(a, b):
    return lax.dot_general(a, b, (((0,), (0,)), ((), ())), preferred_element_type=F32)


def radices(replicas):
    stages, stride, left = [], 2, replicas // 2
    if left % 2 == 0:
        stages.append((2, stride))
        stride, left = stride * 2, left // 2
    while left > 1:
        radix = left if left <= 8 else 4
        stages.append((radix, stride))
        stride, left = stride * radix, left // radix
    return stages


def place():
    return lax.axis_index("dp"), lax.axis_index("fsdp")


def member(dp, radix, stride, digit):
    return dp + (digit - (dp // stride) % radix) * stride


def peers(stages):
    dp, fs = place()
    found = [(dp + 1 - 2 * (dp % 2), fs), (dp, 1 - fs)]
    for radix, stride in stages:
        mine = (dp // stride) % radix
        for step in range(1, radix):
            found.append((member(dp, radix, stride, (mine + step) % radix), fs))
    return found


def greet_signal(stages):
    barrier = pltpu.get_barrier_semaphore()
    for peer in peers(stages):
        pl.semaphore_signal(barrier, inc=1, device_id=peer, device_id_type=MESH)


def greet_wait(stages):
    pl.semaphore_wait(pltpu.get_barrier_semaphore(), len(peers(stages)))


def remote(src, dst, send, recv, peer):
    return pltpu.make_async_remote_copy(
        src_ref=src, dst_ref=dst, send_sem=send, recv_sem=recv, device_id=peer, device_id_type=MESH
    )


def rows_at(start, size):
    return pl.ds(pl.multiple_of(start, 16), size)


def offsets(dp, stages, extent):
    size = extent // 2
    start = (dp % 2) * size
    found = [(start, size)]
    for radix, stride in stages:
        size = size // radix
        start = start + ((dp // stride) % radix) * size
        found.append((start, size))
    return found


def row_of(ref_rows, start, count):
    return jnp.concatenate([ref_rows[start + i : start + i + 1, :] for i in range(count)], axis=1)


def table_constants():
    width = BUCKETS * HEADS
    lane = np.arange(width)
    pick = np.zeros((3, width, 128), np.float32)
    for table in range(3):
        pick[table, lane, 32 * table + lane // HEADS] = 1.0
    keep = (lane[None, :] % HEADS == np.arange(16)[:, None]).astype(np.float32)
    return pick.astype(jnp.bfloat16), keep


def bucket_of(offset):
    spread = jnp.abs(offset)
    result = jnp.minimum(spread, 8) + jnp.where(offset > 0, 16, 0)
    for level in range(9, 16):
        result = result + jnp.where(spread >= 8 * 2 ** (level - 8), 1, 0)
    return result


def up_block(wall, j):
    columns = []
    for c in (2 * j, 2 * j + 1):
        first = wall[0, rows_at(UP0 + c * UP_A, UP_A), :]
        second = wall[1, rows_at(UP1 + c * UP_B + 16, UP_B - 16), :]
        columns.append(jnp.concatenate([first, second], axis=0))
    return jnp.concatenate(columns, axis=1)


def down_rows(wall, j):
    return jnp.concatenate(
        [wall[1, rows_at(DOWN1 + j * 1536 + c * 256, 256), :] for c in range(6)], axis=1
    )


def merge_up(wall):
    row = lax.broadcasted_iota(jnp.int32, (16, 128), 0)

    def one(c, carry):
        low_at = rows_at(UP0 + c * UP_A + UP_A - 16, 16)
        low = wall[0, low_at, :].astype(F32)
        high = wall[1, rows_at(UP1 + c * UP_B, 16), :].astype(F32)
        cut = jnp.where(c < 2, CUT + 1 - 400, CUT - 400)
        wall[0, low_at, :] = jnp.where(row < cut, low, high).astype(BF16)
        return carry

    lax.fori_loop(0, 24, one, 0)


def stats(values):
    mean = jnp.mean(values, axis=1, keepdims=True)
    centered = values - mean
    inverse = lax.rsqrt(jnp.mean(centered * centered, axis=1, keepdims=True) + norm_eps)
    return centered * inverse, inverse


def find_places(coord_col, lut, ranks, places, tick):
    lane = lax.broadcasted_iota(jnp.int32, (8, 128), 1)
    step = lane % 16
    level = jnp.where(step <= 8, step, lax.shift_left(jnp.full_like(step, 8), jnp.maximum(step - 8, 0)))
    edge = jnp.where(lane < 16, 1 - level, jnp.where(lane == 16, 1 << 12, level))

    def line_rows(a, carry):
        at = pl.ds(pl.multiple_of(a * 8, 8), 8)
        value = coord_col[at, 0:1] + edge
        places[0, at, :] = jnp.where(value <= 0, LEN, jnp.minimum(value, LEN) - 1)
        return carry

    lax.fori_loop(0, LEN // 8, line_rows, 0, unroll=4)
    lanes = lax.broadcasted_iota(jnp.int32, (LEN, 128), 1)
    ones = jnp.ones((LEN, 128), BF16)

    def flags(condition):
        return jnp.where(condition, 1.0, 0.0).astype(BF16)

    for table in (1, 2):
        near = jnp.broadcast_to(coord_col[:, table : table + 1], (LEN, 128))
        group = near >> 7
        below = tn(flags(group == lanes), flags((near & 127) < lanes)) + tn(flags(group < lanes), ones)
        lut[...] = below[:16].astype(jnp.int32)
        luts = [jnp.broadcast_to(lut[g : g + 1, :], (8, 128)) for g in range(16)]

        def find(a, carry):
            at = pl.ds(pl.multiple_of(a * 8, 8), 8)
            value = jnp.clip(coord_col[at, table : table + 1] + edge, 0, 2047)
            low, high = value & 127, value >> 7
            found = jnp.zeros((8, 128), jnp.int32)
            for g in range(16):
                found = jnp.where(high == g, jnp.take_along_axis(luts[g], low, axis=1), found)
            places[table, at, :] = jnp.where(found == 0, LEN, found - 1)
            return carry

        for part in range(2):
            tick()
            lax.fori_loop(part * 32, part * 32 + 32, find, 0, unroll=8)


def relayout(plane, flat, out, group):
    def blocks(count, dst, src, rows, stride):
        def one(i, carry):
            out[plane, rows_at(dst(i), rows), :] = flat[pl.ds(LEAD + src(i), rows, stride=stride), :].astype(BF16)
            return carry

        lax.fori_loop(0, count, one, 0)

    def window(dst, src, count):
        out[plane, pl.ds(dst, count), :] = flat[pl.ds(LEAD + src, count), :].astype(BF16)

    def clear(low, high):
        out[plane, pl.ds(low, high - low), :] = jnp.zeros((high - low, 128), BF16)

    if plane == 0 and group == 0:
        blocks(24, lambda c: UP0 + c * UP_A, lambda c: F_UP + c, UP_A, 24)
        window(SM0, 13824, 16)
        window(SM0 + 16, 18440, 32)
        clear(SM0 + 48, ROWS)
    elif plane == 0 and group == 1:
        blocks(18, lambda pos: pos * D, lambda pos: lax.rem(pos, 3) * 6 + pos // 3, D, 18)
    elif plane == 0:
        blocks(6, lambda c: OUT0 + c * D, lambda c: F_OUT + c, D, 6)
    elif group == 0:
        for c in range(6):
            blocks(12, lambda j: DOWN1 + j * 1536 + c * 256, lambda j: F_DOWN1 + j * 1536 + c, 256, 6)
        clear(DOWN_END, LAY1)
        blocks(6, lambda c: LAY1 + c * FEAT, lambda c: F_LAY1 + c, FEAT, 6)
        window(SM1, 8728, 32)
        window(SM1 + 32, 27184, 32)
        window(SM1 + 64, 27976, 16)
        clear(SM1 + 80, ROWS)
    elif group == 1:
        blocks(24, lambda c: UP1 + c * UP_B, lambda c: c - 98, UP_B, 24)


class Gather:
    def __init__(self, stages, zall, x_send, x_recv, c_send, c_recv, sems):
        self.stages, self.zall, self.sems = stages, zall, sems
        self.x_send, self.x_recv, self.c_send, self.c_recv = x_send, x_recv, c_send, c_recv
        self.dp, self.fs = place()
        self.other = 1 - self.fs
        self.levels = len(stages)
        self.parts = offsets(self.dp, stages, CHUNK)
        self.x_peer = (self.dp, self.other)
        self.core_peer = (self.dp + 1 - 2 * (self.dp % 2), self.fs)

    def base(self, position):
        return lax.rem(CHUNKS - 1 + position, CHUNKS) * CHUNK

    def direct(self, position):
        return position >= CHUNKS - 3

    def x_copy(self, position, plane, direct):
        start, size = self.parts[0] if direct else self.parts[-1]
        where = self.zall.at[plane, rows_at(self.base(position) + start, size)]
        return remote(where, where, self.x_send.at[0], self.x_recv.at[position], self.x_peer)

    def send(self, low, high):
        def one(position, carry):
            direct = self.direct(position)

            @pl.when(direct)
            def _():
                self.x_copy(position, self.fs, True).start()

            @pl.when(jnp.logical_not(direct))
            def _():
                self.x_copy(position, self.fs, False).start()

            return carry

        lax.fori_loop(low, high, one, 0)

    def stage_copies(self, level, position):
        radix, stride = self.stages[level]
        start, size = self.parts[level + 1]
        mine = (self.dp // stride) % radix
        copies = []
        for step in range(1, radix):
            peer = (member(self.dp, radix, stride, (mine + step) % radix), self.fs)
            where = self.zall.at[self.other, rows_at(self.base(position) + start, size)]
            copies.append(
                remote(where, where, self.sems[2 * level].at[0], self.sems[2 * level + 1].at[position], peer)
            )
        return copies

    def stage_wait(self, level, position):
        size = (self.stages[level][0] - 1) * self.parts[level + 1][1]
        where = self.zall.at[self.other, rows_at(self.base(position) + self.parts[level][0], size)]
        remote(
            where, where, self.sems[2 * level].at[0], self.sems[2 * level + 1].at[position], self.x_peer
        ).wait_recv()

    def core_copy(self, position, receive):
        size = CHUNK // 2
        start = (1 - self.dp % 2 if receive else self.dp % 2) * size
        where = self.zall.at[self.other, rows_at(self.base(position) + start, size)]
        return remote(where, where, self.c_send.at[0], self.c_recv.at[position], self.core_peer)

    def work(self, position, step):
        direct = self.direct(position)
        levels = self.levels
        if step == levels + 1:
            self.core_copy(position, True).wait_recv()
            return
        if step == 0:

            @pl.when(direct)
            def _():
                self.x_copy(position, self.other, True).wait_recv()
                self.core_copy(position, False).start()

        @pl.when(jnp.logical_not(direct))
        def _():
            if step == 0:
                self.x_copy(position, self.other, False).wait_recv()
            else:
                self.stage_wait(levels - step, position)
            if step < levels:
                for copy in self.stage_copies(levels - 1 - step, position):
                    copy.start()
            else:
                self.core_copy(position, False).start()

    def tick(self, number):
        for step in range(self.levels + 1, -1, -1):
            position = number - SKEW * step

            @pl.when((position >= 0) & (position < CHUNKS))
            def _(position=position, step=step):
                self.work(position, step)

    def ticks(self):
        return CHUNKS + SKEW * (self.levels + 1)

    def finish(self):
        staged = CHUNKS - 3
        sent = [(self.x_send, 3 * self.parts[0][1] + staged * self.parts[-1][1]), (self.c_send, CHUNKS * CHUNK // 2)]
        for level, (radix, _) in enumerate(self.stages):
            sent.append((self.sems[2 * level], staged * (radix - 1) * self.parts[level + 1][1]))
        for sem, size in sent:
            where = self.zall.at[0, pl.ds(0, size)]
            remote(where, where, sem.at[0], self.x_recv.at[0], self.x_peer).wait_send()


def forward_kernel(
    stages, p_hbm, xin, cot, mask, features, coord_row, coord_col, pick, keep,
    wall_out, cdoc_out, total, rounded_out, qkv_out, probs_out, mixed_out, one_out, inverse_one, low_out, hidden_out,
    slope_out, two_out, inverse_two, layer_out,
    flat, wall, xs, cs, masked, cnt_slots, start, up_bias, acc, indices, short, rounded, qkv, probs, mixed, normed, low, hidden,
    slope, layer,
    in_sem, x_send, x_recv, c_send, c_recv, act_send, act_recv, n_send, n_recv, out_sem, probs_sem, feed_sem, *stage_sems,
):
    net = Gather(stages, wall, x_send, x_recv, c_send, c_recv, stage_sems)
    dp, fs, other = net.dp, net.fs, net.other
    pieces = 8
    span = FLAT // pieces
    loads = [
        pltpu.make_async_copy(
            p_hbm.at[pl.ds(i * span, span)], flat.at[pl.ds(LEAD + i * span, span)], in_sem.at[i]
        )
        for i in range(pieces)
    ]
    for load in loads:
        load.start()
    flat[pl.ds(0, LEAD), :] = jnp.zeros((LEAD, 128), F32)
    flat[pl.ds(LEAD + FLAT, 288), :] = jnp.zeros((288, 128), F32)
    greet_signal(stages)

    def index_rows(a, carry):
        at = pl.ds(pl.multiple_of(a * 8, 8), 8)
        for table in range(3):
            near = jnp.broadcast_to(coord_col[at, table : table + 1], (8, 128))
            for j in range(4):
                far = coord_row[table : table + 1, j * 128 : (j + 1) * 128]
                indices[table, at, j * 128 : (j + 1) * 128] = (
                    bucket_of(jnp.broadcast_to(far, (8, 128)) - near) + 32 * table
                )
        return carry

    lax.fori_loop(0, LEN // 8, index_rows, 0, unroll=4)

    half = LEN // 2
    square = [lax.broadcasted_iota(jnp.int32, (half, half), axis) for axis in range(2)]

    def masked_rows(which):
        row = jnp.broadcast_to(mask[pl.ds(which, 1), :], (half, half))
        column = nn(
            jnp.where((square[0] == square[1]) & (row > 0), 1.0, 0.0).astype(BF16), jnp.ones((half, 128), BF16)
        )
        return (cot[which].astype(F32) * jnp.concatenate([column] * 6, axis=1)).astype(BF16)

    masked[...] = masked_rows(other)
    cs[pl.ds(fs * half, half), :] = masked_rows(fs)
    xs[pl.ds(fs * half, half), :] = xin[fs]
    marks = jnp.sum(mask[...].astype(F32), axis=0, keepdims=True)
    total[...] = jnp.broadcast_to(jnp.sum(marks, axis=1, keepdims=True), (8, 128))
    greet_wait(stages)

    def act_copy(number, receive):
        where = rows_at((other if receive else fs) * half, half)
        source, target = ((xin.at[other], xs), (masked, cs))[number]
        return remote(source, target.at[where], act_send.at[number], act_recv.at[number], net.x_peer)

    rounds = [
        [
            (member(dp, radix, stride, ((dp // stride) % radix + step) % radix), fs)
            for step in range(1, radix)
        ]
        for radix, stride in stages
    ] + [[net.core_peer], [net.x_peer]]

    def count_copies(number):
        base = sum(len(r) for r in rounds[:number])
        return [
            remote(total.at[...], cnt_slots.at[base + i], n_send.at[base + i], n_recv.at[base + i], peer)
            for i, peer in enumerate(rounds[number])
        ]

    def count_round(number):
        if 0 < number <= len(rounds):
            gathered = total[...]
            base = sum(len(r) for r in rounds[: number - 1])
            for i, copy in enumerate(count_copies(number - 1)):
                copy.wait()
                gathered = gathered + cnt_slots[base + i]
            total[...] = gathered
        if number < len(rounds):
            for copy in count_copies(number):
                copy.start()

    count_round(0)
    for load in loads:
        load.wait()

    for plane, windows in enumerate((((13824, 16), (18440, 32)), ((8728, 32), (27184, 32), (27976, 16)))):

        @pl.when(fs == plane)
        def _(plane=plane, windows=windows):
            dst = 0
            for src, size in windows:
                short[plane, pl.ds(dst, size), :] = flat[pl.ds(LEAD + src, size), :].astype(BF16)
                dst += size
            short[plane, pl.ds(dst, 96 - dst), :] = jnp.zeros((96 - dst, 128), BF16)

    def short_copy(plane):
        return remote(short.at[plane], short.at[plane], act_send.at[2], act_recv.at[2], net.x_peer)

    short_copy(fs).start()
    for group, (low_at, high_at) in enumerate(((0, 1), (1, 7), (7, CHUNKS - 3))):
        for plane in range(2):

            @pl.when(fs == plane)
            def _(plane=plane, group=group):
                relayout(plane, flat, wall, group)

        net.send(low_at, high_at)
    act_copy(0, False).start()
    net.send(CHUNKS - 3, CHUNKS)
    count_round(1)

    count_round(2)
    outs = []

    def put(source, target):
        copy = pltpu.make_async_copy(source, target, out_sem.at[len(outs)])
        copy.start()
        outs.append(copy)

    short_copy(other).wait_recv()

    small0, small1 = short[0].astype(F32), short[1].astype(F32)
    heads_by_lane = jnp.zeros((16, 128), F32)
    for table in range(3):
        flat_row = row_of(small1, 64 + 3 * table, 3)
        spread = (jnp.broadcast_to(flat_row, (16, 384)) * keep[...]).astype(BF16)
        heads_by_lane = heads_by_lane + nn(spread, pick[table])
    rows_by_head = [jnp.broadcast_to(heads_by_lane[h : h + 1, :], (8, 128)) for h in range(HEADS)]

    def bias_rows(a, carry):
        @pl.when(lax.rem(a, 2) == 0)
        def _():
            net.tick(a // 2)

        for b in range(4):
            row = a * 32 + b * 8
            at = pl.ds(pl.multiple_of(row, 8), 8)
            for j in range(4):
                sums = [None] * HEADS
                for table in range(3):
                    index = indices[table, at, j * 128 : (j + 1) * 128]
                    for h in range(HEADS):
                        found = jnp.take_along_axis(rows_by_head[h], index, axis=1)
                        sums[h] = found if sums[h] is None else sums[h] + found
                for h in range(HEADS):
                    flat[pl.ds(pl.multiple_of((4 * h + j) * LEN + row, 8), 8), :] = sums[h]
        return carry

    lax.fori_loop(0, LEN // 32, bias_rows, 0)

    act_copy(1, False).start()
    count_round(3)
    lag = SKEW * (net.levels + 1)

    def drain(number, carry):
        net.tick(number)
        return carry

    lax.fori_loop(LEN // 64, 2 + lag, drain, 0)
    qv_bias = row_of(small0, 0, 12)
    out_bias, gain_one, shift_one = (row_of(small0, 20 + 6 * i, 6) for i in range(3))
    down_bias, gain_two, shift_two = (row_of(small1, 38 + 6 * i, 6) for i in range(3))
    act_copy(0, True).wait_recv()

    w_layout = jnp.concatenate([wall[1, pl.ds(LAY1 + c * FEAT, FEAT), :] for c in range(6)], axis=1)

    def start_rows(r, carry):
        at = pl.ds(pl.multiple_of(r * QROWS, QROWS), QROWS)
        rows = xs[at, :].astype(F32) + nn(features[at, :], w_layout)
        start[at, :] = rows
        rounded[at, :] = rows.astype(BF16)
        return carry

    lax.fori_loop(0, LEN // QROWS, start_rows, 0)
    put(rounded, rounded_out)
    for i in range(18):
        up_bias[:, i * 128 : (i + 1) * 128] = (
            jnp.zeros((1, 128), F32)
            if i % 3 == 1
            else qv_bias[:, (i // 3 + 3 * (i % 3)) * 128 : (i // 3 + 3 * (i % 3) + 1) * 128]
        )
    left = lax.broadcasted_iota(jnp.int32, (LEN, 128), 1) < HDIM

    def probs_copy(pair):
        where = rows_at(pair * 8 * LEN, 8 * LEN)
        return pltpu.make_async_copy(probs.at[where], probs_out.at[where], probs_sem.at[pair])

    def attend(pair, carry):
        net.tick(2 + lag + pair)
        at = pl.multiple_of(3 * pair * D, 16)
        weight = jnp.concatenate([wall[0, rows_at(at + i * D, D), :] for i in range(3)], axis=1)
        part = nn(rounded[...], weight) + up_bias[:, pl.ds(pl.multiple_of(pair * 384, 128), 384)]
        query = part[:, :128].astype(BF16) * HDIM**-0.5
        key = part[:, 128:256].astype(BF16)
        value = part[:, 256:].astype(BF16)
        qkv[3 * pair] = query
        qkv[3 * pair + 1] = key
        qkv[3 * pair + 2] = value
        found = [[], []]
        for side in range(2):
            head = 2 * pair + side
            mine = left if side == 0 else jnp.logical_not(left)
            for r in range(0, LEN, AROWS):
                some = query[r : r + AROWS]
                extra = jnp.concatenate(
                    [flat[rows_at((4 * head + j) * LEN + r, AROWS), :] for j in range(4)], axis=1
                )
                scores = nt(jnp.where(mine[r : r + AROWS], some, jnp.zeros_like(some)), key) + extra
                scores = jnp.exp(scores - jnp.max(scores, axis=1, keepdims=True))
                soft = (scores * (1.0 / jnp.sum(scores, axis=1, keepdims=True))).astype(BF16)
                for j in range(4):
                    probs[rows_at((4 * head + j) * LEN + r, AROWS), :] = soft[:, j * 128 : (j + 1) * 128]
                found[side].append(nn(soft, value))
        mixed[:, pl.ds(pl.multiple_of(pair * 128, 128), 128)] = jnp.where(
            left, jnp.concatenate(found[0], axis=0), jnp.concatenate(found[1], axis=0)
        ).astype(BF16)
        probs_copy(pair).start()
        return carry

    lax.fori_loop(0, PAIRS, attend, 0)
    put(qkv, qkv_out)
    put(mixed, mixed_out)
    count_round(4)
    lax.fori_loop(2 + lag + PAIRS, 10 + lag, drain, 0)

    w_out = jnp.concatenate([wall[0, pl.ds(OUT0 + c * D, D), :] for c in range(6)], axis=1)

    def first_rows(r, carry):
        at = pl.ds(pl.multiple_of(r * QROWS, QROWS), QROWS)
        unit, inverse = stats(start[at, :] + nn(mixed[at, :], w_out) + out_bias)
        normed[at, :] = unit
        inverse_one[at, :] = inverse
        result = unit * gain_one + shift_one
        low[at, :] = result.astype(BF16)
        acc[at, :] = result + down_bias
        return carry

    lax.fori_loop(0, LEN // QROWS, first_rows, 0)
    put(normed, one_out)
    put(low, low_out)
    count_round(5)
    lax.fori_loop(10 + lag, net.ticks(), drain, 0)
    net.finish()
    merge_up(wall)
    put(wall, wall_out)
    for j in range(12):
        up_bias[:, j * 256 : (j + 1) * 256] = row_of(small1, 6 + 2 * j, 2)

    def feed_copies(j):
        lanes = pl.ds(pl.multiple_of(j * 256, 256), 256)
        return [
            pltpu.make_async_copy(hidden.at[:, lanes], hidden_out.at[:, lanes], feed_sem.at[0, j]),
            pltpu.make_async_copy(slope.at[:, lanes], slope_out.at[:, lanes], feed_sem.at[1, j]),
        ]

    def feed_step(j, carry):
        lanes = pl.ds(pl.multiple_of(j * 256, 256), 256)
        up = nn(low[...], up_block(wall, j)) + up_bias[:, lanes]
        half_up = 0.5 + 0.5 * lax.erf(up * math.sqrt(0.5))
        bell = jnp.exp(-0.5 * up * up) * (1.0 / math.sqrt(2.0 * math.pi))
        slope[:, lanes] = (half_up + up * bell).astype(BF16)
        part = (up * half_up).astype(BF16)
        hidden[:, lanes] = part
        acc[...] += nn(part, down_rows(wall, j))
        for copy in feed_copies(j):
            copy.start()
        return carry

    lax.fori_loop(0, 12, feed_step, 0, unroll=3)

    def second_rows(r, carry):
        at = pl.ds(pl.multiple_of(r * QROWS, QROWS), QROWS)
        unit, inverse = stats(acc[at, :])
        acc[at, :] = unit
        inverse_two[at, :] = inverse
        layer[at, :] = (unit * gain_two + shift_two).astype(BF16)
        return carry

    lax.fori_loop(0, LEN // QROWS, second_rows, 0)
    put(acc, two_out)
    put(layer, layer_out)
    act_copy(1, True).wait_recv()
    put(cs, cdoc_out)
    for number in range(2):
        act_copy(number, False).wait_send()
    short_copy(fs).wait_send()
    for pair in range(PAIRS):
        probs_copy(pair).wait()
    for copy in outs:
        copy.wait()

    def feed_wait(j, carry):
        for copy in feed_copies(j):
            copy.wait()
        return carry

    lax.fori_loop(0, 12, feed_wait, 0)


def forward_pass(stages, p2, xin, cot, mask, features, coord_row, coord_col):
    pick, keep = table_constants()
    sds = jax.ShapeDtypeStruct
    dma = pltpu.SemaphoreType.DMA
    count_peers = 2 + sum(radix - 1 for radix, _ in stages)
    sems = []
    for radix, _ in stages:
        sems += [dma((1,)), dma((CHUNKS,))]
    return pl.pallas_call(
        functools.partial(forward_kernel, stages),
        name="gather_forward",
        out_shape=(
            sds((2, ROWS, 128), BF16),
            sds((LEN, D), BF16),
            sds((8, 128), F32),
            sds((LEN, D), BF16),
            sds((18, LEN, 128), BF16),
            sds((HEADS * 4 * LEN, 128), BF16),
            sds((LEN, D), BF16),
            sds((LEN, D), F32),
            sds((LEN, 1), F32),
            sds((LEN, D), BF16),
            sds((LEN, FF), BF16),
            sds((LEN, FF), BF16),
            sds((LEN, D), F32),
            sds((LEN, 1), F32),
            sds((LEN, D), BF16),
        ),
        in_specs=[ANY] + [VMEM] * 8,
        out_specs=(ANY, ANY, VMEM, ANY, ANY, ANY, ANY, ANY, VMEM, ANY, ANY, ANY, ANY, VMEM, ANY),
        scratch_shapes=[
            pltpu.VMEM((LEAD + FLAT + 288, 128), F32),
            pltpu.VMEM((2, ROWS, 128), BF16),
            pltpu.VMEM((LEN, D), BF16),
            pltpu.VMEM((LEN, D), BF16),
            pltpu.VMEM((LEN // 2, D), BF16),
            pltpu.VMEM((count_peers, 8, 128), F32),
            pltpu.VMEM((LEN, D), F32),
            pltpu.VMEM((1, FF), F32),
            pltpu.VMEM((LEN, D), F32),
            pltpu.VMEM((3, LEN, LEN), jnp.int32),
            pltpu.VMEM((2, 96, 128), BF16),
            pltpu.VMEM((LEN, D), BF16),
            pltpu.VMEM((18, LEN, 128), BF16),
            pltpu.VMEM((HEADS * 4 * LEN, 128), BF16),
            pltpu.VMEM((LEN, D), BF16),
            pltpu.VMEM((LEN, D), F32),
            pltpu.VMEM((LEN, D), BF16),
            pltpu.VMEM((LEN, FF), BF16),
            pltpu.VMEM((LEN, FF), BF16),
            pltpu.VMEM((LEN, D), BF16),
            dma((8,)), dma((1,)), dma((CHUNKS,)), dma((1,)), dma((CHUNKS,)), dma((3,)), dma((3,)),
            dma((count_peers,)), dma((count_peers,)), dma((16,)), dma((PAIRS,)), dma((2, 12)),
        ]
        + sems,
        compiler_params=pltpu.CompilerParams(
            collective_id=1, has_side_effects=True, vmem_limit_bytes=64 * 2**20 - 2**16
        ),
    )(p2, xin, cot, mask, features, coord_row, coord_col, jnp.asarray(pick), jnp.asarray(keep))


G_SMALL = (("qv_bias", 0, 0, 12), ("out_bias", 0, 12, 6), ("gain_one", 0, 18, 6), ("shift_one", 0, 24, 6),
           ("up_bias", 1, 0, 24), ("down_bias", 1, 24, 6), ("gain_two", 1, 30, 6), ("shift_two", 1, 36, 6))


def spread_norm(normed, inverse, gain, grad):
    scaled = grad * gain
    return inverse * (
        scaled
        - jnp.mean(scaled, axis=1, keepdims=True)
        - normed * jnp.mean(scaled * normed, axis=1, keepdims=True)
    )


def total_rows(values):
    return jnp.sum(values.astype(F32), axis=0, keepdims=True)


def reduce_chunk(stages):
    replicas = 2
    for radix, _ in stages:
        replicas *= radix
    return max(1024, 16 * replicas)


class Reduction:
    def __init__(self, stages, gstack, out, core_slots, x_slots, pieces, slots, sems):
        self.stages, self.gstack, self.out = stages, gstack, out
        self.core_slots, self.x_slots, self.pieces, self.slots = core_slots, x_slots, pieces, slots
        (self.c_send, self.c_recv, self.x_send, self.x_recv, self.b_send, self.b_recv, self.own_sem) = sems[:7]
        self.sems = sems[7:]
        self.dp, self.fs = place()
        self.other = 1 - self.fs
        self.size = reduce_chunk(stages)
        self.count = ROWS // self.size
        self.levels = len(stages)
        self.parts = offsets(self.dp, stages, self.size)
        self.half = self.size // 2
        self.x_peer = (self.dp, self.other)
        self.core_peer = (self.dp + 1 - 2 * (self.dp % 2), self.fs)

    def base(self, position):
        return lax.rem(2 * self.count - 2 - position, self.count) * self.size

    def ready(self, row):
        return jnp.maximum(self.count - 1 - (row + self.size - 1) // self.size, 0)

    def core_copy(self, position, plane):
        where = rows_at(self.base(position) + (1 - self.dp % 2) * self.half, self.half)
        return remote(
            self.gstack.at[plane, where], self.core_slots.at[plane, position],
            self.c_send.at[0], self.c_recv.at[plane, position], self.core_peer,
        )

    def x_copy(self, position):
        where = rows_at(self.base(position) + self.parts[0][0], self.half)
        return remote(
            self.gstack.at[self.other, where], self.x_slots.at[position],
            self.x_send.at[0], self.x_recv.at[position], self.x_peer,
        )

    def scatter_copies(self, level, position):
        radix, stride = self.stages[level]
        start, size = self.parts[level]
        size = size // radix
        mine = (self.dp // stride) % radix
        copies = []
        for step in range(1, radix):
            target = (mine + step) % radix
            where = rows_at(self.base(position) + start + target * size, size)
            copies.append(
                remote(
                    self.gstack.at[self.fs, where], self.slots[level].at[position, step - 1],
                    self.sems[4 * level].at[0], self.sems[4 * level + 1].at[position],
                    (member(self.dp, radix, stride, target), self.fs),
                )
            )
        return copies

    def scatter_wait(self, level, position):
        where = self.slots[level].at[position]
        remote(where, where, self.sems[4 * level].at[0], self.sems[4 * level + 1].at[position], self.x_peer).wait_recv()

    def spread_wait(self, level, position):
        size = (self.stages[level][0] - 1) * self.parts[level + 1][1]
        where = self.out.at[rows_at(self.base(position) + self.parts[level][0], size)]
        remote(
            where, where, self.sems[4 * level + 2].at[0], self.sems[4 * level + 3].at[position], self.x_peer
        ).wait_recv()

    def spread_copies(self, level, position):
        radix, stride = self.stages[level]
        start, size = self.parts[level + 1]
        mine = (self.dp // stride) % radix
        copies = []
        for step in range(1, radix):
            where = self.out.at[rows_at(self.base(position) + start, size)]
            source = self.pieces.at[position] if level == self.levels - 1 else where
            copies.append(
                remote(
                    source, where,
                    self.sems[4 * level + 2].at[0], self.sems[4 * level + 3].at[position],
                    (member(self.dp, radix, stride, (mine + step) % radix), self.fs),
                )
            )
        return copies

    def own_copy(self, position):
        start, size = self.parts[-1]
        return pltpu.make_async_copy(
            self.pieces.at[position], self.out.at[rows_at(self.base(position) + start, size)],
            self.own_sem.at[position],
        )

    def back_copy(self, position, receive):
        start = (1 - self.dp % 2 if receive else self.dp % 2) * self.half
        where = self.out.at[rows_at(self.base(position) + start, self.half)]
        return remote(where, where, self.b_send.at[0], self.b_recv.at[position], self.core_peer)

    def feed(self, plane, low, high):
        def one(position, carry):
            self.core_copy(position, plane).start()
            return carry

        lax.fori_loop(low, high, one, 0)

    def push(self, low, high):
        def one(position, carry):
            self.core_copy(position, self.other).wait_recv()
            where = rows_at(self.base(position) + self.parts[0][0], self.half)
            value = self.gstack[self.other, where, :].astype(F32) + self.core_slots[self.other, position].astype(F32)
            self.gstack[self.other, where, :] = value.astype(BF16)
            self.x_copy(position).start()
            return carry

        lax.fori_loop(low, high, one, 0)

    def work(self, position, step):
        levels = self.levels
        base = self.base(position)
        if step <= levels:
            start, size = self.parts[step]
            where = rows_at(base + start, size)
            if step == 0:
                self.core_copy(position, self.fs).wait_recv()
                self.x_copy(position).wait_recv()
                terms = [self.core_slots[self.fs, position], self.x_slots[position]]
            else:
                self.scatter_wait(step - 1, position)
                terms = [self.slots[step - 1][position, i] for i in range(self.stages[step - 1][0] - 1)]
            value = self.gstack[self.fs, where, :].astype(F32)
            for term in terms:
                value = value + term.astype(F32)
            if step < levels:
                self.gstack[self.fs, where, :] = value.astype(BF16)
                for copy in self.scatter_copies(step, position):
                    copy.start()
            else:
                self.pieces[position] = value.astype(BF16)
                self.own_copy(position).start()
                for copy in self.spread_copies(levels - 1, position):
                    copy.start()
        else:
            level = 2 * levels - step
            self.spread_wait(level, position)
            if level == levels - 1:
                self.own_copy(position).wait()
            if level > 0:
                for copy in self.spread_copies(level - 1, position):
                    copy.start()
            else:
                self.back_copy(position, False).start()

    def tick(self, number):
        for step in range(2 * self.levels, -1, -1):
            position = number - SKEW * step

            @pl.when((position >= 0) & (position < self.count))
            def _(position=position, step=step):
                self.work(position, step)

    def ticks(self):
        return self.count + 2 * SKEW * self.levels

    def finish(self):
        def one(position, carry):
            self.back_copy(position, True).wait_recv()
            return carry

        lax.fori_loop(0, self.count, one, 0)
        sent = [(self.c_send, 2 * self.half), (self.x_send, self.half), (self.b_send, self.half)]
        for level, (radix, _) in enumerate(self.stages):
            size = (radix - 1) * self.parts[level + 1][1]
            sent += [(self.sems[4 * level], size), (self.sems[4 * level + 2], size)]
        for sem, size in sent:
            where = self.gstack.at[0, pl.ds(0, self.count * size)]
            remote(where, where, sem.at[0], self.x_recv.at[0], self.x_peer).wait_send()


def reduction_scratch(stages):
    size = reduce_chunk(stages)
    count, half = ROWS // size, size // 2
    dma = pltpu.SemaphoreType.DMA
    slots, sems = [], []
    for radix, _ in stages:
        half = half // radix
        slots.append(pltpu.VMEM((count, radix - 1, half, 128), BF16))
        sems += [dma((1,)), dma((count,))] * 2
    return (
        [
            pltpu.VMEM((2, count, size // 2, 128), BF16),
            pltpu.VMEM((count, size // 2, 128), BF16),
            pltpu.VMEM((count, half, 128), BF16),
        ]
        + slots,
        [dma((1,)), dma((2, count)), dma((1,)), dma((count,)), dma((1,)), dma((count,)), dma((count,))] + sems,
    )


def backward_kernel(
    stages,
    wall_hbm, cdoc_hbm, total, layer_hbm, rounded_hbm, qkv_hbm, probs_hbm, mixed_hbm, one_hbm, inverse_one, low_hbm, hidden_hbm,
    slope_hbm, two_hbm, inverse_two, features, coord_row, coord_col, pick, keep,
    layer_out, input_grad, reduced, tables, norm,
    wall, gstack, acc, branch, hidden, d_up, low, rounded, qkv, mixed, normed_one, places, lut, ranks, small,
    square_slots, load_sem, step_sem, probs_sem, act_send, act_recv, act_sem, n_send, n_recv, *rest,
):
    levels = len(stages)
    parts_vmem, sems = rest[: 3 + levels], rest[3 + levels :]
    red = Reduction(stages, gstack, reduced, parts_vmem[0], parts_vmem[1], parts_vmem[2], parts_vmem[3:], sems)
    dp, fs, other = red.dp, red.fs, red.other

    early = [
        pltpu.make_async_copy(wall_hbm.at[:, pl.ds(SM0, 256)], wall.at[:, pl.ds(SM0, 256)], load_sem.at[0]),
        pltpu.make_async_copy(cdoc_hbm, branch, load_sem.at[1]),
        pltpu.make_async_copy(two_hbm, acc, load_sem.at[2]),
    ]
    early.append(pltpu.make_async_copy(layer_hbm, rounded, load_sem.at[9]))
    lows = [pltpu.make_async_copy(low_hbm, low, load_sem.at[3])]
    rounded_load = pltpu.make_async_copy(rounded_hbm, rounded, load_sem.at[8])

    half = LEN // 2

    def out_copies(number, source, target, receive):
        moved = remote(
            source.at[rows_at(other * half, half)], target.at[other if receive else fs],
            act_send.at[number], act_recv.at[number], red.x_peer,
        )
        own = pltpu.make_async_copy(source.at[rows_at(fs * half, half)], target.at[fs], act_sem.at[number])
        return moved, own
    rest_loads = [
        pltpu.make_async_copy(one_hbm, normed_one, load_sem.at[4]),
        pltpu.make_async_copy(wall_hbm.at[0, pl.ds(0, UP0)], wall.at[0, pl.ds(0, UP0)], load_sem.at[5]),
        pltpu.make_async_copy(mixed_hbm, mixed, load_sem.at[6]),
        pltpu.make_async_copy(qkv_hbm, qkv, load_sem.at[7]),
    ]

    def step_loads(j):
        lanes = pl.ds(pl.multiple_of(j * 256, 256), 256)
        areas = [(1, DOWN1 + 1536 * j, 1536), (0, UP0 + 2 * UP_A * j, 2 * UP_A), (1, UP1 + 2 * UP_B * j, 2 * UP_B)]
        copies = [
            pltpu.make_async_copy(
                wall_hbm.at[plane, rows_at(start, size)], wall.at[plane, rows_at(start, size)], step_sem.at[i, j]
            )
            for i, (plane, start, size) in enumerate(areas)
        ]
        copies.append(pltpu.make_async_copy(hidden_hbm.at[:, lanes], hidden.at[:, lanes], step_sem.at[3, j]))
        copies.append(pltpu.make_async_copy(slope_hbm.at[:, lanes], d_up.at[:, lanes], step_sem.at[4, j]))
        return copies

    for load in early + lows:
        load.start()

    def start_loads(it, carry):
        for load in step_loads(11 - it):
            load.start()
        return carry

    lax.fori_loop(0, 12, start_loads, 0)
    for load in rest_loads:
        load.start()
    greet_signal(stages)
    greet_wait(stages)
    small[...] = jnp.zeros_like(small)
    gstack[1, pl.ds(DOWN_END, LAY1 - DOWN_END), :] = jnp.zeros((LAY1 - DOWN_END, 128), BF16)
    for load in early:
        load.wait()

    for copy in out_copies(0, rounded, layer_out, False):
        copy.start()
    small0 = wall[0, pl.ds(SM0, 48), :].astype(F32)
    small1 = wall[1, pl.ds(SM1, 80), :].astype(F32)
    gain_one = row_of(small0, 26, 6)
    gain_two = row_of(small1, 44, 6)
    spots = {name: (plane, first_row) for name, plane, first_row, _ in G_SMALL}

    def keep_small(name, vector):
        plane, at = spots[name]
        for i in range(vector.shape[1] // 128):
            small[plane, at + i : at + i + 1, :] = vector[:, i * 128 : (i + 1) * 128]

    count = total[0:1, 0:1]
    none = jnp.zeros((1, D), F32)

    def second_rows(r, sums):
        at = pl.ds(pl.multiple_of(r * QROWS, QROWS), QROWS)
        grad_out = branch[at, :].astype(F32) / count
        normed = acc[at, :]
        result = spread_norm(normed, inverse_two[at, :], gain_two, grad_out)
        acc[at, :] = result
        lower = result.astype(BF16)
        branch[at, :] = lower
        return sums[0] + total_rows(grad_out * normed), sums[1] + total_rows(grad_out), sums[2] + total_rows(lower)

    sums = lax.fori_loop(0, LEN // QROWS, second_rows, (none, none, none))
    for name, vector in zip(("gain_two", "shift_two", "down_bias"), sums):
        keep_small(name, vector)
    plane_up, at_up = spots["up_bias"]
    lows[0].wait()

    def fed(plane, it):
        row = UP0 + 2 * UP_A * (11 - it) if plane == 0 else DOWN1 + 1536 * (11 - it)
        return red.ready(row)

    def of_other(values):
        return jnp.where(other == 0, values[0], values[1])

    fine = red.count >= 28
    tile_row = lax.broadcasted_iota(jnp.int32, (16, 128), 0)

    def feed_step(it, carry):
        j = 11 - it
        for load in step_loads(j):
            load.wait()
        for plane in range(2):
            red.feed(plane, fed(plane, it - 2), fed(plane, it - 1))
        red.push(of_other([fed(p, it - 3) for p in range(2)]), of_other([fed(p, it - 2) for p in range(2)]))
        @pl.when(it == 10)
        def _():
            red.tick(0)

        lanes = pl.ds(pl.multiple_of(j * 256, 256), 256)
        grad = nt(branch[...], down_rows(wall, j))
        part = (grad * d_up[:, lanes].astype(F32)).astype(BF16)
        d_up[:, lanes] = part
        sums = total_rows(part)
        small[plane_up, pl.ds(at_up + 2 * j, 1), :] = sums[:, :128]
        small[plane_up, pl.ds(at_up + 2 * j + 1, 1), :] = sums[:, 128:]
        down = tn(hidden[:, lanes], branch[...]).astype(BF16)
        for c in range(6):
            gstack[1, rows_at(DOWN1 + j * 1536 + c * 256, 256), :] = down[:, c * 128 : (c + 1) * 128]
        up = tn(low[...], part)
        for i in range(2):
            c = 2 * j + i
            cut = jnp.where(c < 2, CUT + 1 - 400, CUT - 400)
            columns = up[:, i * 128 : (i + 1) * 128]
            tile = columns[400:416]
            gstack[0, rows_at(UP0 + c * UP_A, 400), :] = columns[:400].astype(BF16)
            gstack[0, rows_at(UP0 + c * UP_A + 400, 16), :] = jnp.where(tile_row < cut, tile, 0.0).astype(BF16)
            gstack[1, rows_at(UP1 + c * UP_B, 16), :] = jnp.where(tile_row < cut, 0.0, tile).astype(BF16)
            gstack[1, rows_at(UP1 + c * UP_B + 16, UP_B - 16), :] = columns[416:].astype(BF16)
        acc[...] += nt(part, up_block(wall, j))
        return carry

    lax.fori_loop(0, 12, feed_step, 0)

    def probs_copy(pair, slot):
        size = 8 * LEN
        return pltpu.make_async_copy(
            probs_hbm.at[rows_at(pair * size, size)], wall.at[0, rows_at(UP0 + slot * size, size)], probs_sem.at[slot]
        )

    probs_copy(PAIRS - 1, 0).start()
    last = red.count - 1
    red.feed(0, fed(0, 10), fed(0, 11))
    red.feed(1, fed(1, 10), last)
    red.push(of_other([fed(p, 9) for p in range(2)]), of_other([fed(p, 10) for p in range(2)]))
    red.tick(1)
    for load in rest_loads:
        load.wait()
    layer_moved, layer_own = out_copies(0, rounded, layer_out, False)
    layer_moved.wait_send()
    layer_own.wait()
    rounded_load.start()

    w_out = jnp.concatenate([wall[0, pl.ds(OUT0 + c * D, D), :] for c in range(6)], axis=1)

    def first_rows(r, sums):
        at = pl.ds(pl.multiple_of(r * QROWS, QROWS), QROWS)
        grad, normed = acc[at, :], normed_one[at, :]
        result = spread_norm(normed, inverse_one[at, :], gain_one, grad)
        acc[at, :] = result
        lower = result.astype(BF16)
        branch[at, :] = lower
        low[at, :] = nt(lower, w_out).astype(BF16)
        return sums[0] + total_rows(grad * normed), sums[1] + total_rows(grad), sums[2] + total_rows(lower)

    sums = lax.fori_loop(0, LEN // QROWS, first_rows, (none, none, none))
    for name, vector in zip(("gain_one", "shift_one", "out_bias"), sums):
        keep_small(name, vector)
    red.push(of_other([fed(p, 10) for p in range(2)]), jnp.where(other == 0, fed(0, 11), last))

    red.tick(2)

    def drain(number, carry):
        red.tick(number)
        return carry

    per_pair = 2 if fine else 1

    def out_step(j, carry):
        lanes = pl.ds(pl.multiple_of(j * 256, 256), 256)
        part = tn(mixed[...], branch[:, lanes]).astype(BF16)
        for i in range(2):
            gstack[0, rows_at(OUT0 + (2 * j + i) * D, D), :] = part[:, i * 128 : (i + 1) * 128]
        return carry

    lax.fori_loop(0, 3, out_step, 0)
    begun = 3
    if fine:
        red.tick(3)
        begun = 4

    rounded_load.wait()
    left = lax.broadcasted_iota(jnp.int32, (LEN, 128), 1) < HDIM

    def sent(it):
        return red.ready(jnp.where(it <= -2, UP0, 2304 * (5 - it)))

    def score_rows(head, j, start, size):
        return rows_at((4 * head + j) * LEN + start, size)

    def attend(it, carry):
        pair = PAIRS - 1 - it
        slot = lax.rem(it, 2)

        @pl.when(it + 1 < PAIRS)
        def _():
            probs_copy(pair - 1, 1 - slot).start()

        red.feed(0, sent(it - 2), sent(it - 1))

        @pl.when(other == 0)
        def _():
            red.push(sent(it - 3), sent(it - 2))

        red.tick(begun + per_pair * it)
        probs_copy(pair, slot).wait()
        query, key, value = qkv[3 * pair], qkv[3 * pair + 1], qkv[3 * pair + 2]
        grad = low[:, pl.ds(pl.multiple_of(pair * 128, 128), 128)]
        found = []
        for side in range(2):
            if side == 1 and per_pair == 2:
                red.tick(begun + per_pair * it + 1)
            head = 2 * pair + side
            mine = left if side == 0 else jnp.logical_not(left)
            base = UP0 + slot * 8 * LEN + side * 4 * LEN
            for r in range(0, LEN, BROWS):
                part = grad[r : r + BROWS]
                d_probs = nt(jnp.where(mine[r : r + BROWS], part, jnp.zeros_like(part)), value)
                soft = jnp.concatenate(
                    [wall[0, rows_at(base + j * LEN + r, BROWS), :] for j in range(4)], axis=1
                ).astype(F32)
                inner = jnp.sum(soft * d_probs, axis=1, keepdims=True)
                scores = (soft * (d_probs - inner)).astype(BF16)
                for j in range(4):
                    wall[1, score_rows(head, j, r, BROWS), :] = scores[:, j * 128 : (j + 1) * 128]
            scores = jnp.concatenate([wall[1, score_rows(head, j, 0, LEN), :] for j in range(4)], axis=1)
            chances = jnp.concatenate([wall[0, rows_at(base + j * LEN, LEN), :] for j in range(4)], axis=1)
            found.append((nn(scores, key), tn(scores, query), tn(chances, grad)))
        d_query = (jnp.where(left, found[0][0], found[1][0]) * HDIM**-0.5).astype(BF16)
        d_key = jnp.where(left, found[0][1], found[1][1]).astype(BF16)
        d_value = jnp.where(left, found[0][2], found[1][2]).astype(BF16)
        both = jnp.concatenate([d_query, d_key, d_value], axis=1)
        plane, spot = spots["qv_bias"]
        small[plane, pl.ds(spot + pair, 1), :] = total_rows(d_query)
        small[plane, pl.ds(spot + 6 + pair, 1), :] = total_rows(d_value)
        at = pl.multiple_of(3 * pair * D, 16)
        weight = jnp.concatenate([wall[0, rows_at(at + i * D, D), :] for i in range(3)], axis=1)
        acc[...] += nt(both, weight)
        part = tn(rounded[...], both).astype(BF16)
        for i in range(3):
            gstack[0, rows_at(at + i * D, D), :] = part[:, i * 128 : (i + 1) * 128]
        return carry

    lax.fori_loop(0, PAIRS, attend, 0)
    red.feed(0, sent(4), sent(5))

    @pl.when(other == 0)
    def _():
        red.push(sent(3), sent(4))

    branch[...] = acc[...].astype(BF16)
    layout = tn(features[...], branch[...]).astype(BF16)
    for c in range(6):
        gstack[1, pl.ds(LAY1 + c * FEAT, FEAT), :] = layout[:, c * 128 : (c + 1) * 128]

    @pl.when(other == 0)
    def _():
        red.push(sent(4), sent(5))

    late = begun + per_pair * PAIRS
    for plane in range(2):
        gstack[plane, pl.ds(SM0, 64), :] = small[plane].astype(BF16)
        gstack[plane, pl.ds(SM0 + 64, ROWS - SM0 - 64), :] = jnp.zeros((ROWS - SM0 - 64, 128), BF16)
        red.feed(plane, last, last + 1)
    drain(late, 0)
    red.push(last, last + 1)
    for copy in out_copies(1, branch, input_grad, False):
        copy.start()
    late += 1
    summed = red.count + SKEW * levels
    passed = [late]

    def tick():
        red.tick(passed[0])
        passed[0] += 1

    find_places(coord_col, lut, ranks, places, tick if fine else lambda: None)
    for table in (1, 2):
        key_row = jnp.broadcast_to(coord_row[table : table + 1, :], (256, LEN))
        for r in (0, 256):
            near = jnp.broadcast_to(coord_col[r : r + 256, table : table + 1], (256, LEN))
            lower = jnp.where(key_row < near, 1.0, 0.0).astype(BF16)
            ranks[table - 1, r : r + 256, :] = nn(lower, jnp.ones((LEN, 128), BF16))
    late = passed[0]
    pace = 2 if fine else 4
    table_grads(wall, coord_col, pick, keep, hidden, places, ranks, normed_one, tables, red, late, pace, summed)
    late = min(late + 24 // pace, summed)
    lax.fori_loop(late, summed, drain, 0)

    def squares(position, carry):
        piece = red.pieces[position].astype(F32)
        return carry + jnp.sum((piece * piece).reshape(-1, 8, 128), axis=0)

    value = lax.fori_loop(0, red.count, squares, jnp.zeros((8, 128), F32))
    value = jnp.sum(jnp.sum(value, axis=0, keepdims=True), axis=1, keepdims=True)
    tables[9:10, :] = jnp.broadcast_to(value, (1, 128))
    rounds = [
        [
            (member(dp, radix, stride, ((dp // stride) % radix + step) % radix), fs)
            for step in range(1, radix)
        ]
        for radix, stride in stages
    ] + [[red.core_peer], [red.x_peer]]

    def square_copies(number):
        base = sum(len(r) for r in rounds[:number])
        return [
            remote(tables.at[...], square_slots.at[base + i], n_send.at[base + i], n_recv.at[base + i], peer)
            for i, peer in enumerate(rounds[number])
        ]

    for number in range(max(red.ticks() - summed, len(rounds)) + 1):
        if number < len(rounds):
            for copy in square_copies(number):
                copy.start()
        if summed + number < red.ticks():
            red.tick(summed + number)
        if number < len(rounds):
            gathered = tables[...]
            base = sum(len(r) for r in rounds[:number])
            for i, copy in enumerate(square_copies(number)):
                copy.wait()
                gathered = gathered + square_slots[base + i]
            tables[...] = gathered
    gathered = tables[0:9, :]
    gathered = jnp.sum(jnp.sum(gathered * gathered, axis=0, keepdims=True), axis=1, keepdims=True)
    norm[...] = jnp.sqrt(tables[9:10, 0:1] + gathered)

    red.finish()
    grad_moved, grad_own = out_copies(1, branch, input_grad, False)
    grad_moved.wait_send()
    grad_own.wait()
    out_copies(0, rounded, layer_out, True)[0].wait_recv()
    out_copies(1, branch, input_grad, True)[0].wait_recv()


def table_grads(wall, coord_col, pick, keep, less, places, ranks, prefix, tables, red, late, pace, summed):
    tables[...] = jnp.zeros_like(tables)
    block = 64
    for table in range(3):
        order = lax.broadcasted_iota(jnp.int32, (16, LEN), 1)

        def less_rows(a, carry):
            at = pl.ds(pl.multiple_of(a * 16, 16), 16)
            if table == 0:
                near = jnp.broadcast_to(coord_col[at, 0:1], (16, LEN))
            else:
                near = jnp.concatenate([ranks[table - 1, at, :].astype(jnp.int32)] * 4, axis=1)
            less[at, 0:LEN] = jnp.where(near <= order, 1.0, 0.0).astype(BF16)
            return carry

        lax.fori_loop(0, LEN // 16, less_rows, 0, unroll=4)

        def query_rows(b, sums):
            number = late + (table * 8 + b) // pace

            @pl.when((lax.rem(table * 8 + b, pace) == 0) & (number < summed))
            def _():
                red.tick(number)

            start = b * block
            scores = jnp.concatenate(
                [
                    jnp.concatenate(
                        [wall[1, rows_at((4 * h + j) * LEN + start, block), :] for j in range(4)], axis=1
                    )
                    for h in range(HEADS)
                ],
                axis=0,
            )
            running = nn(scores, less[:, 0:LEN])
            for h in range(HEADS):
                for j in range(4):
                    r, c = (4 * h + j) // 6 * 64, (4 * h + j) % 6 * 128
                    prefix[r : r + 64, c : c + 128] = running[h * block : (h + 1) * block, j * 128 : (j + 1) * 128]

            def pick_up(a, carry):
                place_of = places[table, pl.ds(pl.multiple_of(start + a * 8, 8), 8), :]
                low, high = place_of & 127, place_of >> 7
                result = []
                for h in range(HEADS):
                    value = jnp.zeros((8, 128), F32)
                    for j in range(4):
                        r, c = (4 * h + j) // 6 * 64, (4 * h + j) % 6 * 128
                        rows = pl.ds(pl.multiple_of(r + a * 8, 8), 8)
                        part = jnp.take_along_axis(prefix[rows, c : c + 128], low, axis=1)
                        value = jnp.where(high == j, part, value)
                    result.append(carry[h] + value)
                return tuple(result)

            return lax.fori_loop(0, block // 8, pick_up, sums, unroll=8)

        sums = lax.fori_loop(
            0, LEN // block, query_rows, tuple(jnp.zeros((8, 128), F32) for _ in range(HEADS))
        )
        heads = jnp.concatenate(
            [jnp.sum(s, axis=0, keepdims=True) for s in sums] + [jnp.zeros((4, 128), F32)], axis=0
        )
        after = pltpu.roll(heads, 127, 1)
        whole = pltpu.roll(heads, 15, 1)
        lanes = lax.broadcasted_iota(jnp.int32, (16, 128), 1)
        buckets = jnp.where(lanes < 16, heads - after, after - heads)
        buckets = jnp.where(lanes == 15, heads, buckets)
        buckets = jnp.where(lanes == 16, 0.0, buckets)
        buckets = jnp.where(lanes == 31, whole - heads, buckets)
        buckets = jnp.where(lanes < 32, buckets, 0.0)
        placed = buckets if table == 0 else pltpu.roll(buckets, 32 * table, 1)
        parts, left_over = [], placed
        for _ in range(2):
            parts.append(left_over.astype(BF16))
            left_over = left_over - parts[-1].astype(F32)
        spread = sum(nt(part, pick[table]) for part in parts)
        flat_row = jnp.sum(spread * keep[...], axis=0, keepdims=True)
        for i in range(3):
            tables[3 * table + i : 3 * table + i + 1, :] = flat_row[:, i * 128 : (i + 1) * 128]


def backward_pass(stages, wall, cdoc, total, out_doc, saved, features, coord_row, coord_col):
    pick, keep = table_constants()
    sds = jax.ShapeDtypeStruct
    count_peers = 2 + sum(radix - 1 for radix, _ in stages)
    dma = pltpu.SemaphoreType.DMA
    buffers, sems = reduction_scratch(stages)
    return pl.pallas_call(
        functools.partial(backward_kernel, stages),
        name="backward_reduce",
        out_shape=(sds((2, LEN // 2, D), BF16), sds((2, LEN // 2, D), BF16), sds((ROWS, 128), BF16), sds((16, 128), F32), sds((1, 1), F32)),
        in_specs=[ANY, ANY, VMEM, ANY, ANY, ANY, ANY, ANY, ANY, VMEM, ANY, ANY, ANY, ANY, VMEM] + [VMEM] * 5,
        out_specs=(ANY, ANY, ANY, VMEM, VMEM),
        scratch_shapes=[
            pltpu.VMEM((2, ROWS, 128), BF16),
            pltpu.VMEM((2, ROWS, 128), BF16),
            pltpu.VMEM((LEN, D), F32),
            pltpu.VMEM((LEN, D), BF16),
            pltpu.VMEM((LEN, FF), BF16),
            pltpu.VMEM((LEN, FF), BF16),
            pltpu.VMEM((LEN, D), BF16),
            pltpu.VMEM((LEN, D), BF16),
            pltpu.VMEM((18, LEN, 128), BF16),
            pltpu.VMEM((LEN, D), BF16),
            pltpu.VMEM((LEN, D), F32),
            pltpu.VMEM((3, LEN, 128), jnp.int32),
            pltpu.VMEM((16, 128), jnp.int32),
            pltpu.VMEM((2, LEN, 128), F32),
            pltpu.VMEM((2, 64, 128), F32),
            pltpu.VMEM((count_peers, 16, 128), F32),
            dma((10,)), dma((5, 12)), dma((2,)), dma((2,)), dma((2,)), dma((2,)), dma((count_peers,)), dma((count_peers,)),
        ]
        + buffers
        + sems,
        compiler_params=pltpu.CompilerParams(
            collective_id=2, has_side_effects=True, vmem_limit_bytes=64 * 2**20 - 2**16
        ),
    )(wall, cdoc, total, out_doc, *saved, features, coord_row, coord_col, jnp.asarray(pick), jnp.asarray(keep))


BLOCK = 1408
DEEP_IN, DEEP_OUT = 4, 3


def flatten_rows(plane, step, source, tables, flat):
    def blocks(low, high, src, dst, rows, stride):
        def one(i, carry):
            flat[pl.ds(LEAD + dst(i), rows, stride=stride), :] = source[rows_at(src(i), rows), :].astype(F32)
            return carry

        lax.fori_loop(low, high, one, 0)

    if plane == 0:
        for part in (0, 1) if step == 0 else (step + 1,) if step < 7 else ():
            blocks(
                0, 18, lambda pos: pos * D + 96 * part,
                lambda pos: lax.rem(pos, 3) * 6 + pos // 3 + 96 * 18 * part, 96, 18,
            )
        if step == 4:
            small = source[pl.ds(SM0, 64), :].astype(F32)
            flat[pl.ds(LEAD + 13824, 12), :] = small[0:12]
            flat[pl.ds(LEAD + 18444, 18), :] = small[12:30]
        elif step == 7:
            blocks(0, 6, lambda c: OUT0 + c * D, lambda c: F_OUT + c, D, 6)
        elif step in (10, 11):
            first = 208 * (step - 10)
            blocks(0, 24, lambda c: UP0 + c * UP_A + first, lambda c: F_UP + c + 24 * first, 208, 24)
    else:
        if step < 4:
            first, rows = 96 * step, min(96, UP_B - 96 * step)
            blocks(0, 24, lambda c: UP1 + c * UP_B + first, lambda c: c - 98 + 24 * first, rows, 24)
        elif step < 16:
            j = step - 4
            blocks(
                0, 6, lambda c: DOWN1 + j * 1536 + c * 256, lambda c: F_DOWN1 + j * 1536 + c, 256, 6
            )
        if step == 4:
            small = source[pl.ds(SM1, 64), :].astype(F32)
            flat[pl.ds(LEAD + F_UPB1, 24), :] = small[0:24]
            flat[pl.ds(LEAD + F_SM1, 18), :] = small[24:42]
            flat[pl.ds(LEAD + F_TAB1, 9), :] = tables[0:9, :]
            rest = FLAT - F_TAB1 - 9
            flat[pl.ds(LEAD + F_TAB1 + 9, rest), :] = jnp.zeros((rest, 128), F32)
        elif step == 16:
            blocks(0, 6, lambda c: LAY1 + c * FEAT, lambda c: F_LAY1 + c, FEAT, 6)


def adam_kernel(
    source_hbm, tables, weights_hbm, first_hbm, second_hbm, grad_hbm, update_hbm, new_hbm,
    source, flat, weights, first, second, update, new, sem, in_sem, out_sem,
):
    fs = lax.axis_index("fsdp")
    steps = FLAT // BLOCK
    loads = [
        pltpu.make_async_copy(source_hbm.at[pl.ds(a, n)], source.at[pl.ds(a, n)], sem.at[i])
        for i, (a, n) in enumerate(((0, OUT0), (OUT0, ROWS - OUT0)))
    ]

    def fetch(step):
        where, slot = pl.ds(step * BLOCK, BLOCK), step % DEEP_IN
        return [
            pltpu.make_async_copy(ref.at[where], buffer.at[slot], in_sem.at[i, slot])
            for i, (ref, buffer) in enumerate(((weights_hbm, weights), (first_hbm, first), (second_hbm, second)))
        ]

    def store(step):
        where, slot = pl.ds(step * BLOCK, BLOCK), step % DEEP_OUT
        return [
            pltpu.make_async_copy(flat.at[pl.ds(LEAD + step * BLOCK, BLOCK)], grad_hbm.at[where], out_sem.at[0, slot]),
            pltpu.make_async_copy(update.at[slot], update_hbm.at[where], out_sem.at[1, slot]),
            pltpu.make_async_copy(new.at[slot], new_hbm.at[where], out_sem.at[2, slot]),
        ]

    loads[0].start()
    for step in range(DEEP_IN):
        for copy in fetch(step):
            copy.start()
        if step == 0:
            loads[1].start()
    part = 176
    row = lax.broadcasted_iota(jnp.int32, (part, 128), 0)
    for step in range(steps):
        if step == 0:
            loads[0].wait()
        if step == 3:
            loads[1].wait()
        for plane in range(2):

            @pl.when(fs == plane)
            def _(plane=plane, step=step):
                flatten_rows(plane, step, source, tables, flat)

        if step >= DEEP_OUT:
            for copy in store(step - DEEP_OUT):
                copy.wait()
        for copy in fetch(step):
            copy.wait()
        slot_in, slot_out = step % DEEP_IN, step % DEEP_OUT

        def some(i, carry):
            at = pl.ds(pl.multiple_of(i * part, 8), part)
            begin = pl.multiple_of(step * BLOCK + i * part, 8)
            grad = flat[pl.ds(LEAD + begin, part), :]
            new_first = adam_one * first[slot_in, at, :] + (1.0 - adam_one) * grad
            new_second = adam_two * second[slot_in, at, :] + (1.0 - adam_two) * grad * grad
            spread = jnp.sqrt(new_second * (1.0 / (1.0 - adam_two**adam_steps))) + adam_eps
            corrected = new_first * (1.0 / (1.0 - adam_one**adam_steps)) / spread
            rate = jnp.where((fs == 1) & (row + begin >= F_LAY1), table_factor, 1.0)
            update[slot_out, at, :] = rate * (corrected + decay_rate * weights[slot_in, at, :])
            new[slot_out, at, :] = new_first
            return carry

        lax.fori_loop(0, BLOCK // part, some, 0)
        for copy in store(step):
            copy.start()
        if step + DEEP_IN < steps:
            for copy in fetch(step + DEEP_IN):
                copy.start()
    for step in range(steps - DEEP_OUT, steps):
        for copy in store(step):
            copy.wait()


def adam(source, tables, weights, first, second):
    vector = jax.ShapeDtypeStruct((FLAT, 128), F32)
    dma = pltpu.SemaphoreType.DMA
    return pl.pallas_call(
        adam_kernel,
        name="adamw",
        out_shape=(vector, vector, vector),
        in_specs=[ANY, VMEM, ANY, ANY, ANY],
        out_specs=(ANY, ANY, ANY),
        scratch_shapes=[
            pltpu.VMEM((ROWS, 128), BF16),
            pltpu.VMEM((LEAD + FLAT + 288, 128), F32),
        ]
        + [pltpu.VMEM((DEEP_IN, BLOCK, 128), F32)] * 3
        + [pltpu.VMEM((DEEP_OUT, BLOCK, 128), F32)] * 2
        + [dma((2,)), dma((3, DEEP_IN)), dma((3, DEEP_OUT))],
        compiler_params=pltpu.CompilerParams(vmem_limit_bytes=60 * 2**20),
    )(source, tables, weights, first, second)


def layout_features(coords):
    freq_count = FEAT // 8
    factors = (jnp.arange(freq_count, dtype=jnp.int32) + 1) ** 2
    phases = coords[..., :, None] * factors % 4096
    angles = phases.astype(F32) * (2.0 * math.pi / 4096.0)
    wave_parts = jnp.concatenate([jnp.sin(angles), jnp.cos(angles)], axis=-1)
    return wave_parts.reshape(coords.shape[:-1] + (FEAT,))


def local(stages, inputs, box_coords, mlm_mask, cotangent, params, first_moment, second_moment):
    fs = lax.axis_index("fsdp")
    boxes = lax.dynamic_index_in_dim(box_coords, fs, 0, keepdims=False)
    features = layout_features(boxes).astype(BF16)
    coord_col = jnp.stack(
        [jnp.arange(LEN, dtype=jnp.int32), boxes[:, 0] + boxes[:, 2], boxes[:, 1] + boxes[:, 3]], axis=1
    )
    coord_row = coord_col.T
    flat = [v.reshape(FLAT, 128) for v in (params, first_moment, second_moment)]
    wall, cdoc, total, *saved, out_doc = forward_pass(
        stages, flat[0], inputs, cotangent, mlm_mask, features, coord_row, coord_col
    )
    layer_out, input_grad, reduced, tables, norm = backward_pass(
        stages, wall, cdoc, total, out_doc, saved, features, coord_row, coord_col
    )
    grad, update, new_first = adam(reduced, tables, *flat)
    return (layer_out, input_grad, grad.reshape(-1), norm.reshape(()), update.reshape(-1), new_first.reshape(-1))


def solution(mesh):
    in_specs = (
        P("dp", "fsdp", None),
        P("dp", None, None),
        P("dp", "fsdp"),
        P("dp", "fsdp", None),
        P("fsdp"),
        P("fsdp"),
        P("fsdp"),
    )
    out_specs = (P("dp", "fsdp", None), P("dp", "fsdp", None), P("fsdp"), P(), P("fsdp"), P("fsdp"))
    stages = radices(mesh.shape["dp"])
    return jax.shard_map(
        functools.partial(local, stages), mesh=mesh, in_specs=in_specs, out_specs=out_specs, check_vma=False
    )
```

```python
import functools
import math

import jax
import jax.numpy as jnp
import numpy as np
from jax import lax
from jax.experimental import pallas as pl
from jax.experimental.pallas import tpu as pltpu
from jax.sharding import PartitionSpec as P

D = 768
HEADS = 12
HDIM = 64
FF = 3072
BUCKETS = 32
FEAT = 128
LEN = 512
PADDED = 7208960
SHARD = PADDED // 2
FLAT = SHARD // 128
PAIRS = HEADS // 2
QROWS = 256
AROWS = 512
BROWS = 256
SKEW = 2

norm_eps = 1e-05
adam_one = 0.9
adam_two = 0.999
adam_eps = 1e-08
adam_steps = 100.0
decay_rate = 0.01
table_factor = 5.0

MESH = pl.DeviceIdType.MESH
F32 = jnp.float32
BF16 = jnp.bfloat16
VMEM = pl.BlockSpec(memory_space=pltpu.VMEM)
ANY = pl.BlockSpec(memory_space=pl.ANY)

ROWS = 28672
CHUNK = 2048
CHUNKS = ROWS // CHUNK
CUT = 404
UP_A, UP_B = 416, 368
OUT0 = 18 * D
UP0 = OUT0 + 6 * D
SM0 = UP0 + 24 * UP_A
UP1 = 0
DOWN1 = 24 * UP_B
DOWN_END = DOWN1 + 6 * FF
LAY1 = 27648
SM1 = LAY1 + 6 * FEAT
F_OUT = 13836
F_UP = 18462
F_UPB1 = 8734
F_DOWN1 = 8758
F_SM1 = 27190
F_LAY1 = 27208
F_TAB1 = 27976
LEAD = 104


def nt(a, b):
    return lax.dot_general(a, b, (((1,), (1,)), ((), ())), preferred_element_type=F32)


def nn(a, b):
    return lax.dot_general(a, b, (((1,), (0,)), ((), ())), preferred_element_type=F32)


def tn(a, b):
    return lax.dot_general(a, b, (((0,), (0,)), ((), ())), preferred_element_type=F32)


def radices(replicas):
    stages, stride, left = [], 2, replicas // 2
    if left % 2 == 0:
        stages.append((2, stride))
        stride, left = stride * 2, left // 2
    while left > 1:
        radix = left if left <= 8 else 4
        stages.append((radix, stride))
        stride, left = stride * radix, left // radix
    return stages


def place():
    return lax.axis_index("dp"), lax.axis_index("fsdp")


def member(dp, radix, stride, digit):
    return dp + (digit - (dp // stride) % radix) * stride


def peers(stages):
    dp, fs = place()
    found = [(dp + 1 - 2 * (dp % 2), fs), (dp, 1 - fs)]
    for radix, stride in stages:
        mine = (dp // stride) % radix
        for step in range(1, radix):
            found.append((member(dp, radix, stride, (mine + step) % radix), fs))
    return found


def greet_signal(stages):
    barrier = pltpu.get_barrier_semaphore()
    for peer in peers(stages):
        pl.semaphore_signal(barrier, inc=1, device_id=peer, device_id_type=MESH)


def greet_wait(stages):
    pl.semaphore_wait(pltpu.get_barrier_semaphore(), len(peers(stages)))


def remote(src, dst, send, recv, peer):
    return pltpu.make_async_remote_copy(
        src_ref=src, dst_ref=dst, send_sem=send, recv_sem=recv, device_id=peer, device_id_type=MESH
    )


def rows_at(start, size):
    return pl.ds(pl.multiple_of(start, 16), size)


def offsets(dp, stages, extent):
    size = extent // 2
    start = (dp % 2) * size
    found = [(start, size)]
    for radix, stride in stages:
        size = size // radix
        start = start + ((dp // stride) % radix) * size
        found.append((start, size))
    return found


def row_of(ref_rows, start, count):
    return jnp.concatenate([ref_rows[start + i : start + i + 1, :] for i in range(count)], axis=1)


def table_constants():
    width = BUCKETS * HEADS
    lane = np.arange(width)
    pick = np.zeros((3, width, 128), np.float32)
    for table in range(3):
        pick[table, lane, 32 * table + lane // HEADS] = 1.0
    keep = (lane[None, :] % HEADS == np.arange(16)[:, None]).astype(np.float32)
    return pick.astype(jnp.bfloat16), keep


def bucket_of(offset):
    spread = jnp.abs(offset)
    result = jnp.minimum(spread, 8) + jnp.where(offset > 0, 16, 0)
    for level in range(9, 16):
        result = result + jnp.where(spread >= 8 * 2 ** (level - 8), 1, 0)
    return result


def up_block(wall, j):
    row = lax.broadcasted_iota(jnp.int32, (16, 128), 0)
    columns = []
    for c in (2 * j, 2 * j + 1):
        first = wall[0, rows_at(UP0 + c * UP_A, UP_A - 16), :]
        low = wall[0, rows_at(UP0 + c * UP_A + UP_A - 16, 16), :].astype(F32)
        high = wall[1, rows_at(UP1 + c * UP_B, 16), :].astype(F32)
        second = wall[1, rows_at(UP1 + c * UP_B + 16, UP_B - 16), :]
        cut = jnp.where(c < 2, CUT + 1 - 400, CUT - 400)
        columns.append(jnp.concatenate([first, jnp.where(row < cut, low, high).astype(BF16), second], axis=0))
    return jnp.concatenate(columns, axis=1)


def down_rows(wall, j):
    return jnp.concatenate(
        [wall[1, rows_at(DOWN1 + j * 1536 + c * 256, 256), :] for c in range(6)], axis=1
    )


def stats(values):
    mean = jnp.mean(values, axis=1, keepdims=True)
    centered = values - mean
    inverse = lax.rsqrt(jnp.mean(centered * centered, axis=1, keepdims=True) + norm_eps)
    return centered * inverse, inverse


def find_places(coord_col, lut, ranks, places, tick):
    lane = lax.broadcasted_iota(jnp.int32, (8, 128), 1)
    step = lane % 16
    level = jnp.where(step <= 8, step, lax.shift_left(jnp.full_like(step, 8), jnp.maximum(step - 8, 0)))
    edge = jnp.where(lane < 16, 1 - level, jnp.where(lane == 16, 1 << 12, level))

    def line_rows(a, carry):
        at = pl.ds(pl.multiple_of(a * 8, 8), 8)
        value = coord_col[at, 0:1] + edge
        places[0, at, :] = jnp.where(value <= 0, LEN, jnp.minimum(value, LEN) - 1)
        return carry

    lax.fori_loop(0, LEN // 8, line_rows, 0, unroll=4)
    lanes = lax.broadcasted_iota(jnp.int32, (LEN, 128), 1)
    ones = jnp.ones((LEN, 128), BF16)

    def flags(condition):
        return jnp.where(condition, 1.0, 0.0).astype(BF16)

    for table in (1, 2):
        near = jnp.broadcast_to(coord_col[:, table : table + 1], (LEN, 128))
        group = near >> 7
        below = tn(flags(group == lanes), flags((near & 127) < lanes)) + tn(flags(group < lanes), ones)
        lut[...] = below[:16].astype(jnp.int32)
        luts = [jnp.broadcast_to(lut[g : g + 1, :], (8, 128)) for g in range(16)]

        def find(a, carry):
            at = pl.ds(pl.multiple_of(a * 8, 8), 8)
            value = jnp.clip(coord_col[at, table : table + 1] + edge, 0, 2047)
            low, high = value & 127, value >> 7
            found = jnp.zeros((8, 128), jnp.int32)
            for g in range(16):
                found = jnp.where(high == g, jnp.take_along_axis(luts[g], low, axis=1), found)
            places[table, at, :] = jnp.where(found == 0, LEN, found - 1)
            return carry

        for part in range(2):
            tick()
            lax.fori_loop(part * 32, part * 32 + 32, find, 0, unroll=8)


def relayout(plane, flat, out, group):
    def blocks(count, dst, src, rows, stride):
        def one(i, carry):
            out[plane, rows_at(dst(i), rows), :] = flat[pl.ds(LEAD + src(i), rows, stride=stride), :].astype(BF16)
            return carry

        lax.fori_loop(0, count, one, 0)

    def window(dst, src, count):
        out[plane, pl.ds(dst, count), :] = flat[pl.ds(LEAD + src, count), :].astype(BF16)

    def clear(low, high):
        out[plane, pl.ds(low, high - low), :] = jnp.zeros((high - low, 128), BF16)

    if plane == 0 and group == 0:
        blocks(24, lambda c: UP0 + c * UP_A, lambda c: F_UP + c, UP_A, 24)
        window(SM0, 13824, 16)
        window(SM0 + 16, 18440, 32)
        clear(SM0 + 48, ROWS)
    elif plane == 0 and group == 1:
        blocks(18, lambda pos: pos * D, lambda pos: lax.rem(pos, 3) * 6 + pos // 3, D, 18)
    elif plane == 0:
        blocks(6, lambda c: OUT0 + c * D, lambda c: F_OUT + c, D, 6)
    elif group == 0:
        for c in range(6):
            blocks(12, lambda j: DOWN1 + j * 1536 + c * 256, lambda j: F_DOWN1 + j * 1536 + c, 256, 6)
        clear(DOWN_END, LAY1)
        blocks(6, lambda c: LAY1 + c * FEAT, lambda c: F_LAY1 + c, FEAT, 6)
        window(SM1, 8728, 32)
        window(SM1 + 32, 27184, 32)
        window(SM1 + 64, 27976, 16)
        clear(SM1 + 80, ROWS)
    elif group == 1:
        blocks(24, lambda c: UP1 + c * UP_B, lambda c: c - 98, UP_B, 24)


class Gather:
    def __init__(self, stages, zall, x_send, x_recv, c_send, c_recv, sems):
        self.stages, self.zall, self.sems = stages, zall, sems
        self.x_send, self.x_recv, self.c_send, self.c_recv = x_send, x_recv, c_send, c_recv
        self.dp, self.fs = place()
        self.other = 1 - self.fs
        self.levels = len(stages)
        self.parts = offsets(self.dp, stages, CHUNK)
        self.x_peer = (self.dp, self.other)
        self.core_peer = (self.dp + 1 - 2 * (self.dp % 2), self.fs)
        self.partners = [
            [
                (member(self.dp, radix, stride, ((self.dp // stride) % radix + step) % radix), self.fs)
                for step in range(1, radix)
            ]
            for radix, stride in stages
        ]

    def base(self, position):
        return jnp.where(position == 0, CHUNKS - 1, position - 1) * CHUNK

    def direct(self, position):
        return position >= CHUNKS - 3

    def x_copy(self, position, plane, direct):
        start, size = self.parts[0] if direct else self.parts[-1]
        where = self.zall.at[plane, rows_at(self.base(position) + start, size)]
        return remote(where, where, self.x_send.at[0], self.x_recv.at[position], self.x_peer)

    def send(self, low, high):
        def one(position, carry):
            direct = self.direct(position)

            @pl.when(direct)
            def _():
                self.x_copy(position, self.fs, True).start()

            @pl.when(jnp.logical_not(direct))
            def _():
                self.x_copy(position, self.fs, False).start()

            return carry

        lax.fori_loop(low, high, one, 0)

    def stage_copies(self, level, position):
        start, size = self.parts[level + 1]
        where = self.zall.at[self.other, rows_at(self.base(position) + start, size)]
        return [
            remote(where, where, self.sems[2 * level].at[0], self.sems[2 * level + 1].at[position], peer)
            for peer in self.partners[level]
        ]

    def stage_wait(self, level, position):
        size = (self.stages[level][0] - 1) * self.parts[level + 1][1]
        where = self.zall.at[self.other, rows_at(self.base(position) + self.parts[level][0], size)]
        remote(
            where, where, self.sems[2 * level].at[0], self.sems[2 * level + 1].at[position], self.x_peer
        ).wait_recv()

    def core_copy(self, position, receive):
        size = CHUNK // 2
        start = size - self.parts[0][0] if receive else self.parts[0][0]
        where = self.zall.at[self.other, rows_at(self.base(position) + start, size)]
        return remote(where, where, self.c_send.at[0], self.c_recv.at[position], self.core_peer)

    def work(self, position, step):
        direct = self.direct(position)
        levels = self.levels
        if step == levels + 1:
            self.core_copy(position, True).wait_recv()
            return
        if step == levels:

            @pl.when(direct)
            def _():
                self.x_copy(position, self.other, True).wait_recv()
                self.core_copy(position, False).start()

        @pl.when(jnp.logical_not(direct))
        def _():
            if step == 0:
                self.x_copy(position, self.other, False).wait_recv()
            else:
                self.stage_wait(levels - step, position)
            if step < levels:
                for copy in self.stage_copies(levels - 1 - step, position):
                    copy.start()
            else:
                self.core_copy(position, False).start()

    def tick(self, number):
        for step in range(self.levels + 1, -1, -1):
            position = number - SKEW * step

            @pl.when((position >= 0) & (position < CHUNKS))
            def _(position=position, step=step):
                self.work(position, step)

    def ticks(self):
        return CHUNKS + SKEW * (self.levels + 1)

    def finish(self):
        staged = CHUNKS - 3
        sent = [(self.x_send, 3 * self.parts[0][1] + staged * self.parts[-1][1]), (self.c_send, CHUNKS * CHUNK // 2)]
        for level, (radix, _) in enumerate(self.stages):
            sent.append((self.sems[2 * level], staged * (radix - 1) * self.parts[level + 1][1]))
        for sem, size in sent:
            where = self.zall.at[0, pl.ds(0, size)]
            remote(where, where, sem.at[0], self.x_recv.at[0], self.x_peer).wait_send()


def forward_kernel(
    stages, p_hbm, xin, cot, mask, features, coord_row, coord_col, pick, keep,
    wall_out, cdoc_out, total, rounded_out, qkv_out, probs_out, mixed_out, one_out, inverse_one, low_out, hidden_out,
    slope_out, two_out, inverse_two, layer_out,
    flat, wall, xs, cs, masked, cnt_slots, start, up_bias, acc, indices, short, rounded, qkv, probs, mixed, normed, low, hidden,
    slope, layer,
    in_sem, x_send, x_recv, c_send, c_recv, act_send, act_recv, n_send, n_recv, out_sem, probs_sem, feed_sem, *stage_sems,
):
    net = Gather(stages, wall, x_send, x_recv, c_send, c_recv, stage_sems)
    dp, fs, other = net.dp, net.fs, net.other
    pieces = 8
    span = FLAT // pieces
    loads = [
        pltpu.make_async_copy(
            p_hbm.at[pl.ds(i * span, span)], flat.at[pl.ds(LEAD + i * span, span)], in_sem.at[i]
        )
        for i in range(pieces)
    ]
    for load in loads:
        load.start()
    flat[pl.ds(0, LEAD), :] = jnp.zeros((LEAD, 128), F32)
    flat[pl.ds(LEAD + FLAT, 288), :] = jnp.zeros((288, 128), F32)
    greet_signal(stages)

    def index_rows(a, carry):
        at = pl.ds(pl.multiple_of(a * 8, 8), 8)
        for table in range(3):
            near = jnp.broadcast_to(coord_col[at, table : table + 1], (8, 128))
            for j in range(4):
                far = coord_row[table : table + 1, j * 128 : (j + 1) * 128]
                indices[table, at, j * 128 : (j + 1) * 128] = (
                    bucket_of(jnp.broadcast_to(far, (8, 128)) - near) + 32 * table
                )
        return carry

    lax.fori_loop(0, LEN // 8, index_rows, 0, unroll=4)

    half = LEN // 2
    square = [lax.broadcasted_iota(jnp.int32, (half, half), axis) for axis in range(2)]

    def masked_rows(which):
        row = jnp.broadcast_to(mask[pl.ds(which, 1), :], (half, half))
        column = nn(
            jnp.where((square[0] == square[1]) & (row > 0), 1.0, 0.0).astype(BF16), jnp.ones((half, 128), BF16)
        )
        return (cot[which].astype(F32) * jnp.concatenate([column] * 6, axis=1)).astype(BF16)

    masked[...] = masked_rows(other)
    cs[pl.ds(fs * half, half), :] = masked_rows(fs)
    xs[pl.ds(fs * half, half), :] = xin[fs]
    marks = jnp.sum(mask[...].astype(F32), axis=0, keepdims=True)
    total[...] = jnp.broadcast_to(jnp.sum(marks, axis=1, keepdims=True), (8, 128))
    greet_wait(stages)

    def act_copy(number, receive):
        where = rows_at((other if receive else fs) * half, half)
        source, target = ((xin.at[other], xs), (masked, cs))[number]
        return remote(source, target.at[where], act_send.at[number], act_recv.at[number], net.x_peer)

    rounds = [
        [
            (member(dp, radix, stride, ((dp // stride) % radix + step) % radix), fs)
            for step in range(1, radix)
        ]
        for radix, stride in stages
    ] + [[net.core_peer], [net.x_peer]]

    def count_copies(number):
        base = sum(len(r) for r in rounds[:number])
        return [
            remote(total.at[...], cnt_slots.at[base + i], n_send.at[base + i], n_recv.at[base + i], peer)
            for i, peer in enumerate(rounds[number])
        ]

    def count_round(number):
        if 0 < number <= len(rounds):
            gathered = total[...]
            base = sum(len(r) for r in rounds[: number - 1])
            for i, copy in enumerate(count_copies(number - 1)):
                copy.wait()
                gathered = gathered + cnt_slots[base + i]
            total[...] = gathered
        if number < len(rounds):
            for copy in count_copies(number):
                copy.start()

    count_round(0)
    for load in loads:
        load.wait()

    for plane, windows in enumerate((((13824, 16), (18440, 32)), ((8728, 32), (27184, 32), (27976, 16)))):

        @pl.when(fs == plane)
        def _(plane=plane, windows=windows):
            dst = 0
            for src, size in windows:
                short[plane, pl.ds(dst, size), :] = flat[pl.ds(LEAD + src, size), :].astype(BF16)
                dst += size
            short[plane, pl.ds(dst, 96 - dst), :] = jnp.zeros((96 - dst, 128), BF16)

    def short_copy(plane):
        return remote(short.at[plane], short.at[plane], act_send.at[2], act_recv.at[2], net.x_peer)

    short_copy(fs).start()
    for group, (low_at, high_at) in enumerate(((0, 1), (1, 7), (7, CHUNKS - 3))):
        for plane in range(2):

            @pl.when(fs == plane)
            def _(plane=plane, group=group):
                relayout(plane, flat, wall, group)

        net.send(low_at, high_at)
    act_copy(0, False).start()
    net.send(CHUNKS - 3, CHUNKS)
    count_round(1)

    count_round(2)
    outs = []

    def put(source, target):
        copy = pltpu.make_async_copy(source, target, out_sem.at[len(outs)])
        copy.start()
        outs.append(copy)

    put(wall.at[fs], wall_out.at[fs])
    short_copy(other).wait_recv()

    small0, small1 = short[0].astype(F32), short[1].astype(F32)
    heads_by_lane = jnp.zeros((16, 128), F32)
    for table in range(3):
        flat_row = row_of(small1, 64 + 3 * table, 3)
        spread = (jnp.broadcast_to(flat_row, (16, 384)) * keep[...]).astype(BF16)
        heads_by_lane = heads_by_lane + nn(spread, pick[table])
    rows_by_head = [jnp.broadcast_to(heads_by_lane[h : h + 1, :], (8, 128)) for h in range(HEADS)]

    def bias_rows(a, carry):
        @pl.when(lax.rem(a, 2) == 0)
        def _():
            net.tick(a // 2)

        for b in range(4):
            row = a * 32 + b * 8
            at = pl.ds(pl.multiple_of(row, 8), 8)
            for j in range(4):
                sums = [None] * HEADS
                for table in range(3):
                    index = indices[table, at, j * 128 : (j + 1) * 128]
                    for h in range(HEADS):
                        found = jnp.take_along_axis(rows_by_head[h], index, axis=1)
                        sums[h] = found if sums[h] is None else sums[h] + found
                for h in range(HEADS):
                    flat[pl.ds(pl.multiple_of((4 * h + j) * LEN + row, 8), 8), :] = sums[h]
        return carry

    lax.fori_loop(0, LEN // 32, bias_rows, 0)

    act_copy(1, False).start()
    count_round(3)
    lag = SKEW * (net.levels + 1)

    def drain(number, carry):
        net.tick(number)
        return carry

    lax.fori_loop(LEN // 64, 2 + lag, drain, 0)
    qv_bias = row_of(small0, 0, 12)
    out_bias, gain_one, shift_one = (row_of(small0, 20 + 6 * i, 6) for i in range(3))
    down_bias, gain_two, shift_two = (row_of(small1, 38 + 6 * i, 6) for i in range(3))
    act_copy(0, True).wait_recv()

    w_layout = jnp.concatenate([wall[1, pl.ds(LAY1 + c * FEAT, FEAT), :] for c in range(6)], axis=1)

    def start_rows(r, carry):
        at = pl.ds(pl.multiple_of(r * QROWS, QROWS), QROWS)
        rows = xs[at, :].astype(F32) + nn(features[at, :], w_layout)
        start[at, :] = rows
        rounded[at, :] = rows.astype(BF16)
        return carry

    lax.fori_loop(0, LEN // QROWS, start_rows, 0)
    put(rounded, rounded_out)
    for i in range(18):
        up_bias[:, i * 128 : (i + 1) * 128] = (
            jnp.zeros((1, 128), F32)
            if i % 3 == 1
            else qv_bias[:, (i // 3 + 3 * (i % 3)) * 128 : (i // 3 + 3 * (i % 3) + 1) * 128]
        )
    left = lax.broadcasted_iota(jnp.int32, (LEN, 128), 1) < HDIM

    def probs_copy(pair):
        where = rows_at(pair * 8 * LEN, 8 * LEN)
        return pltpu.make_async_copy(probs.at[where], probs_out.at[where], probs_sem.at[pair])

    def attend(pair, carry):
        net.tick(2 + lag + pair)
        at = pl.multiple_of(3 * pair * D, 16)
        weight = jnp.concatenate([wall[0, rows_at(at + i * D, D), :] for i in range(3)], axis=1)
        part = nn(rounded[...], weight) + up_bias[:, pl.ds(pl.multiple_of(pair * 384, 128), 384)]
        query = part[:, :128].astype(BF16) * HDIM**-0.5
        key = part[:, 128:256].astype(BF16)
        value = part[:, 256:].astype(BF16)
        qkv[3 * pair] = query
        qkv[3 * pair + 1] = key
        qkv[3 * pair + 2] = value
        found = [[], []]
        for side in range(2):
            head = 2 * pair + side
            mine = left if side == 0 else jnp.logical_not(left)
            for r in range(0, LEN, AROWS):
                some = query[r : r + AROWS]
                extra = jnp.concatenate(
                    [flat[rows_at((4 * head + j) * LEN + r, AROWS), :] for j in range(4)], axis=1
                )
                scores = nt(jnp.where(mine[r : r + AROWS], some, jnp.zeros_like(some)), key) + extra
                scores = jnp.exp(scores - jnp.max(scores, axis=1, keepdims=True))
                soft = (scores * (1.0 / jnp.sum(scores, axis=1, keepdims=True))).astype(BF16)
                for j in range(4):
                    probs[rows_at((4 * head + j) * LEN + r, AROWS), :] = soft[:, j * 128 : (j + 1) * 128]
                found[side].append(nn(soft, value))
        mixed[:, pl.ds(pl.multiple_of(pair * 128, 128), 128)] = jnp.where(
            left, jnp.concatenate(found[0], axis=0), jnp.concatenate(found[1], axis=0)
        ).astype(BF16)
        probs_copy(pair).start()
        return carry

    lax.fori_loop(0, PAIRS, attend, 0)
    put(qkv, qkv_out)
    put(mixed, mixed_out)
    count_round(4)
    lax.fori_loop(2 + lag + PAIRS, 10 + lag, drain, 0)

    w_out = jnp.concatenate([wall[0, pl.ds(OUT0 + c * D, D), :] for c in range(6)], axis=1)

    def first_rows(r, carry):
        at = pl.ds(pl.multiple_of(r * QROWS, QROWS), QROWS)
        unit, inverse = stats(start[at, :] + nn(mixed[at, :], w_out) + out_bias)
        normed[at, :] = unit
        inverse_one[at, :] = inverse
        result = unit * gain_one + shift_one
        low[at, :] = result.astype(BF16)
        acc[at, :] = result + down_bias
        return carry

    lax.fori_loop(0, LEN // QROWS, first_rows, 0)
    put(normed, one_out)
    put(low, low_out)
    count_round(5)
    lax.fori_loop(10 + lag, 11 + lag, drain, 0)
    put(wall.at[other, pl.ds(0, UP0)], wall_out.at[other, pl.ds(0, UP0)])
    for j in range(12):
        up_bias[:, j * 256 : (j + 1) * 256] = row_of(small1, 6 + 2 * j, 2)

    def feed_copies(j):
        lanes = pl.ds(pl.multiple_of(j * 256, 256), 256)
        return [
            pltpu.make_async_copy(hidden.at[:, lanes], hidden_out.at[:, lanes], feed_sem.at[0, j]),
            pltpu.make_async_copy(slope.at[:, lanes], slope_out.at[:, lanes], feed_sem.at[1, j]),
        ]

    def feed_step(j, carry):
        lanes = pl.ds(pl.multiple_of(j * 256, 256), 256)
        up = nn(low[...], up_block(wall, j)) + up_bias[:, lanes]
        half_up = 0.5 + 0.5 * lax.erf(up * math.sqrt(0.5))
        bell = jnp.exp(-0.5 * up * up) * (1.0 / math.sqrt(2.0 * math.pi))
        slope[:, lanes] = (half_up + up * bell).astype(BF16)
        part = (up * half_up).astype(BF16)
        hidden[:, lanes] = part
        acc[...] += nn(part, down_rows(wall, j))
        for copy in feed_copies(j):
            copy.start()
        return carry

    def feed_group(group, carry):
        @pl.when(group > 0)
        def _():
            net.tick(11 + lag + group)

        for i in range(3):
            feed_step(3 * group + i, carry)
        return carry

    net.tick(11 + lag)
    lax.fori_loop(0, 4, feed_group, 0)
    put(wall.at[other, pl.ds(UP0, ROWS - UP0)], wall_out.at[other, pl.ds(UP0, ROWS - UP0)])

    def second_rows(r, carry):
        at = pl.ds(pl.multiple_of(r * QROWS, QROWS), QROWS)
        unit, inverse = stats(acc[at, :])
        acc[at, :] = unit
        inverse_two[at, :] = inverse
        layer[at, :] = (unit * gain_two + shift_two).astype(BF16)
        return carry

    lax.fori_loop(0, LEN // QROWS, second_rows, 0)
    put(acc, two_out)
    put(layer, layer_out)
    act_copy(1, True).wait_recv()
    put(cs, cdoc_out)
    for number in range(2):
        act_copy(number, False).wait_send()
    short_copy(fs).wait_send()
    net.finish()
    for pair in range(PAIRS):
        probs_copy(pair).wait()
    for copy in outs:
        copy.wait()

    def feed_wait(j, carry):
        for copy in feed_copies(j):
            copy.wait()
        return carry

    lax.fori_loop(0, 12, feed_wait, 0)


def forward_pass(stages, p2, xin, cot, mask, features, coord_row, coord_col):
    pick, keep = table_constants()
    sds = jax.ShapeDtypeStruct
    dma = pltpu.SemaphoreType.DMA
    count_peers = 2 + sum(radix - 1 for radix, _ in stages)
    sems = []
    for radix, _ in stages:
        sems += [dma((1,)), dma((CHUNKS,))]
    return pl.pallas_call(
        functools.partial(forward_kernel, stages),
        name="gather_forward",
        out_shape=(
            sds((2, ROWS, 128), BF16),
            sds((LEN, D), BF16),
            sds((8, 128), F32),
            sds((LEN, D), BF16),
            sds((18, LEN, 128), BF16),
            sds((HEADS * 4 * LEN, 128), BF16),
            sds((LEN, D), BF16),
            sds((LEN, D), F32),
            sds((LEN, 1), F32),
            sds((LEN, D), BF16),
            sds((LEN, FF), BF16),
            sds((LEN, FF), BF16),
            sds((LEN, D), F32),
            sds((LEN, 1), F32),
            sds((LEN, D), BF16),
        ),
        in_specs=[ANY] + [VMEM] * 8,
        out_specs=(ANY, ANY, VMEM, ANY, ANY, ANY, ANY, ANY, VMEM, ANY, ANY, ANY, ANY, VMEM, ANY),
        scratch_shapes=[
            pltpu.VMEM((LEAD + FLAT + 288, 128), F32),
            pltpu.VMEM((2, ROWS, 128), BF16),
            pltpu.VMEM((LEN, D), BF16),
            pltpu.VMEM((LEN, D), BF16),
            pltpu.VMEM((LEN // 2, D), BF16),
            pltpu.VMEM((count_peers, 8, 128), F32),
            pltpu.VMEM((LEN, D), F32),
            pltpu.VMEM((1, FF), F32),
            pltpu.VMEM((LEN, D), F32),
            pltpu.VMEM((3, LEN, LEN), jnp.int32),
            pltpu.VMEM((2, 96, 128), BF16),
            pltpu.VMEM((LEN, D), BF16),
            pltpu.VMEM((18, LEN, 128), BF16),
            pltpu.VMEM((HEADS * 4 * LEN, 128), BF16),
            pltpu.VMEM((LEN, D), BF16),
            pltpu.VMEM((LEN, D), F32),
            pltpu.VMEM((LEN, D), BF16),
            pltpu.VMEM((LEN, FF), BF16),
            pltpu.VMEM((LEN, FF), BF16),
            pltpu.VMEM((LEN, D), BF16),
            dma((8,)), dma((1,)), dma((CHUNKS,)), dma((1,)), dma((CHUNKS,)), dma((3,)), dma((3,)),
            dma((count_peers,)), dma((count_peers,)), dma((16,)), dma((PAIRS,)), dma((2, 12)),
        ]
        + sems,
        compiler_params=pltpu.CompilerParams(
            collective_id=1, has_side_effects=True, vmem_limit_bytes=64 * 2**20 - 2**16
        ),
    )(p2, xin, cot, mask, features, coord_row, coord_col, jnp.asarray(pick), jnp.asarray(keep))


G_SMALL = (("qv_bias", 0, 0, 12), ("out_bias", 0, 12, 6), ("gain_one", 0, 18, 6), ("shift_one", 0, 24, 6),
           ("up_bias", 1, 0, 24), ("down_bias", 1, 24, 6), ("gain_two", 1, 30, 6), ("shift_two", 1, 36, 6))


def spread_norm(normed, inverse, gain, grad):
    scaled = grad * gain
    return inverse * (
        scaled
        - jnp.mean(scaled, axis=1, keepdims=True)
        - normed * jnp.mean(scaled * normed, axis=1, keepdims=True)
    )


def total_rows(values):
    return jnp.sum(values.astype(F32), axis=0, keepdims=True)


def reduce_chunk(stages):
    replicas = 2
    for radix, _ in stages:
        replicas *= radix
    return max(1024, 16 * replicas)


class Reduction:
    def __init__(self, stages, gstack, out, core_slots, x_slots, pieces, slots, sems):
        self.stages, self.gstack, self.out = stages, gstack, out
        self.core_slots, self.x_slots, self.pieces, self.slots = core_slots, x_slots, pieces, slots
        (self.c_send, self.c_recv, self.x_send, self.x_recv, self.b_send, self.b_recv, self.own_sem) = sems[:7]
        self.sems = sems[7:]
        self.dp, self.fs = place()
        self.other = 1 - self.fs
        self.size = reduce_chunk(stages)
        self.count = ROWS // self.size
        self.levels = len(stages)
        self.parts = offsets(self.dp, stages, self.size)
        self.half = self.size // 2
        self.x_peer = (self.dp, self.other)
        self.core_peer = (self.dp + 1 - 2 * (self.dp % 2), self.fs)
        self.core_start = (1 - self.dp % 2) * self.half
        self.partners = []
        for level, (radix, stride) in enumerate(stages):
            mine = (self.dp // stride) % radix
            start, size = self.parts[level][0], self.parts[level + 1][1]
            found = []
            for step in range(1, radix):
                target = (mine + step) % radix
                found.append((step, (member(self.dp, radix, stride, target), self.fs), start + target * size))
            self.partners.append(found)

    def base(self, position):
        last = self.count - 1
        return jnp.where(position == last, last, last - 1 - position) * self.size

    def ready(self, row):
        return jnp.maximum(self.count - 1 - (row + self.size - 1) // self.size, 0)

    def core_copy(self, position, plane):
        where = rows_at(self.base(position) + self.core_start, self.half)
        return remote(
            self.gstack.at[plane, where], self.core_slots.at[plane, position],
            self.c_send.at[0], self.c_recv.at[plane, position], self.core_peer,
        )

    def x_copy(self, position):
        where = rows_at(self.base(position) + self.parts[0][0], self.half)
        return remote(
            self.gstack.at[self.other, where], self.x_slots.at[position],
            self.x_send.at[0], self.x_recv.at[position], self.x_peer,
        )

    def scatter_copies(self, level, position):
        size = self.parts[level + 1][1]
        base = self.base(position)
        return [
            remote(
                self.gstack.at[self.fs, rows_at(base + start, size)], self.slots[level].at[position, step - 1],
                self.sems[4 * level].at[0], self.sems[4 * level + 1].at[position], peer,
            )
            for step, peer, start in self.partners[level]
        ]

    def scatter_wait(self, level, position):
        where = self.slots[level].at[position]
        remote(where, where, self.sems[4 * level].at[0], self.sems[4 * level + 1].at[position], self.x_peer).wait_recv()

    def spread_wait(self, level, position):
        size = (self.stages[level][0] - 1) * self.parts[level + 1][1]
        where = self.out.at[rows_at(self.base(position) + self.parts[level][0], size)]
        remote(
            where, where, self.sems[4 * level + 2].at[0], self.sems[4 * level + 3].at[position], self.x_peer
        ).wait_recv()

    def spread_copies(self, level, position):
        start, size = self.parts[level + 1]
        where = self.out.at[rows_at(self.base(position) + start, size)]
        source = self.pieces.at[position] if level == self.levels - 1 else where
        return [
            remote(source, where, self.sems[4 * level + 2].at[0], self.sems[4 * level + 3].at[position], peer)
            for _, peer, _ in self.partners[level]
        ]

    def own_copy(self, position):
        start, size = self.parts[-1]
        return pltpu.make_async_copy(
            self.pieces.at[position], self.out.at[rows_at(self.base(position) + start, size)],
            self.own_sem.at[position],
        )

    def back_copy(self, position, receive):
        start = self.core_start if receive else self.parts[0][0]
        where = self.out.at[rows_at(self.base(position) + start, self.half)]
        return remote(where, where, self.b_send.at[0], self.b_recv.at[0], self.core_peer)

    def feed(self, plane, low, high):
        def one(position, carry):
            self.core_copy(position, plane).start()
            return carry

        lax.fori_loop(low, high, one, 0)

    def push(self, low, high):
        def one(position, carry):
            self.core_copy(position, self.other).wait_recv()
            where = rows_at(self.base(position) + self.parts[0][0], self.half)
            value = self.gstack[self.other, where, :].astype(F32) + self.core_slots[self.other, position].astype(F32)
            self.gstack[self.other, where, :] = value.astype(BF16)
            self.x_copy(position).start()
            return carry

        lax.fori_loop(low, high, one, 0)

    def work(self, position, step):
        levels = self.levels
        base = self.base(position)
        if step <= levels:
            start, size = self.parts[step]
            where = rows_at(base + start, size)
            if step == 0:
                self.core_copy(position, self.fs).wait_recv()
                self.x_copy(position).wait_recv()
                terms = [self.core_slots[self.fs, position], self.x_slots[position]]
            else:
                self.scatter_wait(step - 1, position)
                terms = [self.slots[step - 1][position, i] for i in range(self.stages[step - 1][0] - 1)]
            value = self.gstack[self.fs, where, :].astype(F32)
            for term in terms:
                value = value + term.astype(F32)
            if step < levels:
                self.gstack[self.fs, where, :] = value.astype(BF16)
                for copy in self.scatter_copies(step, position):
                    copy.start()
            else:
                self.pieces[position] = value.astype(BF16)
                self.own_copy(position).start()
                for copy in self.spread_copies(levels - 1, position):
                    copy.start()
        else:
            level = 2 * levels - step
            self.spread_wait(level, position)
            if level == levels - 1:
                self.own_copy(position).wait()
            if level > 0:
                for copy in self.spread_copies(level - 1, position):
                    copy.start()
            else:
                self.back_copy(position, False).start()

    def tick(self, number):
        for step in range(2 * self.levels, -1, -1):
            position = number - SKEW * step

            @pl.when((position >= 0) & (position < self.count))
            def _(position=position, step=step):
                self.work(position, step)

    def ticks(self):
        return self.count + 2 * SKEW * self.levels

    def finish(self):
        where = self.out.at[pl.ds(0, self.count * self.half)]
        remote(where, where, self.b_send.at[0], self.b_recv.at[0], self.core_peer).wait_recv()
        sent = [(self.c_send, 2 * self.half), (self.x_send, self.half), (self.b_send, self.half)]
        for level, (radix, _) in enumerate(self.stages):
            size = (radix - 1) * self.parts[level + 1][1]
            sent += [(self.sems[4 * level], size), (self.sems[4 * level + 2], size)]
        for sem, size in sent:
            where = self.gstack.at[0, pl.ds(0, self.count * size)]
            remote(where, where, sem.at[0], self.x_recv.at[0], self.x_peer).wait_send()


def reduction_scratch(stages):
    size = reduce_chunk(stages)
    count, half = ROWS // size, size // 2
    dma = pltpu.SemaphoreType.DMA
    slots, sems = [], []
    for radix, _ in stages:
        half = half // radix
        slots.append(pltpu.VMEM((count, radix - 1, half, 128), BF16))
        sems += [dma((1,)), dma((count,))] * 2
    return (
        [
            pltpu.VMEM((2, count, size // 2, 128), BF16),
            pltpu.VMEM((count, size // 2, 128), BF16),
            pltpu.VMEM((count, half, 128), BF16),
        ]
        + slots,
        [dma((1,)), dma((2, count)), dma((1,)), dma((count,)), dma((1,)), dma((1,)), dma((count,))] + sems,
    )


def backward_kernel(
    stages,
    wall_hbm, cdoc_hbm, total, layer_hbm, rounded_hbm, qkv_hbm, probs_hbm, mixed_hbm, one_hbm, inverse_one, low_hbm, hidden_hbm,
    slope_hbm, two_hbm, inverse_two, features, coord_row, coord_col, pick, keep,
    layer_out, input_grad, reduced, tables, norm,
    wall, gstack, acc, branch, hidden, d_up, low, rounded, qkv, mixed, normed_one, places, lut, ranks, small,
    square_slots, load_sem, step_sem, probs_sem, act_send, act_recv, act_sem, n_send, n_recv, *rest,
):
    levels = len(stages)
    parts_vmem, sems = rest[: 3 + levels], rest[3 + levels :]
    red = Reduction(stages, gstack, reduced, parts_vmem[0], parts_vmem[1], parts_vmem[2], parts_vmem[3:], sems)
    dp, fs, other = red.dp, red.fs, red.other

    early = [
        pltpu.make_async_copy(wall_hbm.at[:, pl.ds(SM0, 256)], wall.at[:, pl.ds(SM0, 256)], load_sem.at[0]),
        pltpu.make_async_copy(cdoc_hbm, branch, load_sem.at[1]),
        pltpu.make_async_copy(two_hbm, acc, load_sem.at[2]),
    ]
    early.append(pltpu.make_async_copy(layer_hbm, rounded, load_sem.at[9]))
    lows = [pltpu.make_async_copy(low_hbm, low, load_sem.at[3])]
    rounded_load = pltpu.make_async_copy(rounded_hbm, rounded, load_sem.at[8])

    half = LEN // 2

    def out_copies(number, source, target, receive):
        moved = remote(
            source.at[rows_at(other * half, half)], target.at[other if receive else fs],
            act_send.at[number], act_recv.at[number], red.x_peer,
        )
        own = pltpu.make_async_copy(source.at[rows_at(fs * half, half)], target.at[fs], act_sem.at[number])
        return moved, own
    rest_loads = [
        pltpu.make_async_copy(one_hbm, normed_one, load_sem.at[4]),
        pltpu.make_async_copy(wall_hbm.at[0, pl.ds(0, UP0)], wall.at[0, pl.ds(0, UP0)], load_sem.at[5]),
        pltpu.make_async_copy(mixed_hbm, mixed, load_sem.at[6]),
        pltpu.make_async_copy(qkv_hbm, qkv, load_sem.at[7]),
    ]

    def step_loads(j):
        lanes = pl.ds(pl.multiple_of(j * 256, 256), 256)
        areas = [(1, DOWN1 + 1536 * j, 1536), (0, UP0 + 2 * UP_A * j, 2 * UP_A), (1, UP1 + 2 * UP_B * j, 2 * UP_B)]
        copies = [
            pltpu.make_async_copy(
                wall_hbm.at[plane, rows_at(start, size)], wall.at[plane, rows_at(start, size)], step_sem.at[j]
            )
            for plane, start, size in areas
        ]
        copies.append(pltpu.make_async_copy(hidden_hbm.at[:, lanes], hidden.at[:, lanes], step_sem.at[j]))
        copies.append(pltpu.make_async_copy(slope_hbm.at[:, lanes], d_up.at[:, lanes], step_sem.at[j]))
        return copies

    def step_wait(j):
        where = pl.ds(0, 1536 + 2 * UP_A + 2 * UP_B + 2 * 2 * LEN)
        pltpu.make_async_copy(wall_hbm.at[0, where], wall.at[0, where], step_sem.at[j]).wait()

    for load in early + lows:
        load.start()

    def start_loads(it, carry):
        for load in step_loads(11 - it):
            load.start()
        return carry

    lax.fori_loop(0, 12, start_loads, 0)
    for load in rest_loads:
        load.start()
    greet_signal(stages)
    greet_wait(stages)
    small[...] = jnp.zeros_like(small)
    gstack[1, pl.ds(DOWN_END, LAY1 - DOWN_END), :] = jnp.zeros((LAY1 - DOWN_END, 128), BF16)
    for load in early:
        load.wait()

    for copy in out_copies(0, rounded, layer_out, False):
        copy.start()
    small0 = wall[0, pl.ds(SM0, 48), :].astype(F32)
    small1 = wall[1, pl.ds(SM1, 80), :].astype(F32)
    gain_one = row_of(small0, 26, 6)
    gain_two = row_of(small1, 44, 6)
    spots = {name: (plane, first_row) for name, plane, first_row, _ in G_SMALL}

    def keep_small(name, vector):
        plane, at = spots[name]
        for i in range(vector.shape[1] // 128):
            small[plane, at + i : at + i + 1, :] = vector[:, i * 128 : (i + 1) * 128]

    count = total[0:1, 0:1]
    none = jnp.zeros((1, D), F32)

    def second_rows(r, sums):
        at = pl.ds(pl.multiple_of(r * QROWS, QROWS), QROWS)
        grad_out = branch[at, :].astype(F32) / count
        normed = acc[at, :]
        result = spread_norm(normed, inverse_two[at, :], gain_two, grad_out)
        acc[at, :] = result
        lower = result.astype(BF16)
        branch[at, :] = lower
        return sums[0] + total_rows(grad_out * normed), sums[1] + total_rows(grad_out), sums[2] + total_rows(lower)

    sums = lax.fori_loop(0, LEN // QROWS, second_rows, (none, none, none))
    for name, vector in zip(("gain_two", "shift_two", "down_bias"), sums):
        keep_small(name, vector)
    plane_up, at_up = spots["up_bias"]
    lows[0].wait()

    def fed(plane, it):
        row = UP0 + 2 * UP_A * (11 - it) if plane == 0 else DOWN1 + 1536 * (11 - it)
        return red.ready(row)

    def of_other(values):
        return jnp.where(other == 0, values[0], values[1])

    fine = red.count >= 28
    tile_row = lax.broadcasted_iota(jnp.int32, (16, 128), 0)

    def feed_step(it, carry):
        j = 11 - it
        step_wait(j)
        for plane in range(2):
            red.feed(plane, fed(plane, it - 2), fed(plane, it - 1))
        red.push(of_other([fed(p, it - 3) for p in range(2)]), of_other([fed(p, it - 2) for p in range(2)]))
        @pl.when(it == 10)
        def _():
            red.tick(0)

        lanes = pl.ds(pl.multiple_of(j * 256, 256), 256)
        grad = nt(branch[...], down_rows(wall, j))
        part = (grad * d_up[:, lanes].astype(F32)).astype(BF16)
        d_up[:, lanes] = part
        sums = total_rows(part)
        small[plane_up, pl.ds(at_up + 2 * j, 1), :] = sums[:, :128]
        small[plane_up, pl.ds(at_up + 2 * j + 1, 1), :] = sums[:, 128:]
        down = tn(hidden[:, lanes], branch[...]).astype(BF16)
        for c in range(6):
            gstack[1, rows_at(DOWN1 + j * 1536 + c * 256, 256), :] = down[:, c * 128 : (c + 1) * 128]
        up = tn(low[...], part)
        for i in range(2):
            c = 2 * j + i
            cut = jnp.where(c < 2, CUT + 1 - 400, CUT - 400)
            columns = up[:, i * 128 : (i + 1) * 128]
            tile = columns[400:416]
            gstack[0, rows_at(UP0 + c * UP_A, 400), :] = columns[:400].astype(BF16)
            gstack[0, rows_at(UP0 + c * UP_A + 400, 16), :] = jnp.where(tile_row < cut, tile, 0.0).astype(BF16)
            gstack[1, rows_at(UP1 + c * UP_B, 16), :] = jnp.where(tile_row < cut, 0.0, tile).astype(BF16)
            gstack[1, rows_at(UP1 + c * UP_B + 16, UP_B - 16), :] = columns[416:].astype(BF16)
        acc[...] += nt(part, up_block(wall, j))
        return carry

    lax.fori_loop(0, 12, feed_step, 0)

    def probs_copy(pair, slot):
        size = 8 * LEN
        return pltpu.make_async_copy(
            probs_hbm.at[rows_at(pair * size, size)], wall.at[0, rows_at(UP0 + slot * size, size)], probs_sem.at[slot]
        )

    probs_copy(PAIRS - 1, 0).start()
    last = red.count - 1
    red.feed(0, fed(0, 10), fed(0, 11))
    red.feed(1, fed(1, 10), last)
    red.push(of_other([fed(p, 9) for p in range(2)]), of_other([fed(p, 10) for p in range(2)]))
    red.tick(1)
    for load in rest_loads:
        load.wait()
    layer_moved, layer_own = out_copies(0, rounded, layer_out, False)
    layer_moved.wait_send()
    layer_own.wait()
    rounded_load.start()

    w_out = jnp.concatenate([wall[0, pl.ds(OUT0 + c * D, D), :] for c in range(6)], axis=1)

    def first_rows(r, sums):
        at = pl.ds(pl.multiple_of(r * QROWS, QROWS), QROWS)
        grad, normed = acc[at, :], normed_one[at, :]
        result = spread_norm(normed, inverse_one[at, :], gain_one, grad)
        acc[at, :] = result
        lower = result.astype(BF16)
        branch[at, :] = lower
        low[at, :] = nt(lower, w_out).astype(BF16)
        return sums[0] + total_rows(grad * normed), sums[1] + total_rows(grad), sums[2] + total_rows(lower)

    sums = lax.fori_loop(0, LEN // QROWS, first_rows, (none, none, none))
    for name, vector in zip(("gain_one", "shift_one", "out_bias"), sums):
        keep_small(name, vector)
    red.push(of_other([fed(p, 10) for p in range(2)]), jnp.where(other == 0, fed(0, 11), last))

    red.tick(2)

    def drain(number, carry):
        red.tick(number)
        return carry

    per_pair = 2 if fine else 1

    def out_step(j, carry):
        lanes = pl.ds(pl.multiple_of(j * 256, 256), 256)
        part = tn(mixed[...], branch[:, lanes]).astype(BF16)
        for i in range(2):
            gstack[0, rows_at(OUT0 + (2 * j + i) * D, D), :] = part[:, i * 128 : (i + 1) * 128]
        return carry

    lax.fori_loop(0, 3, out_step, 0)
    begun = 3
    if fine:
        red.tick(3)
        begun = 4

    rounded_load.wait()
    left = lax.broadcasted_iota(jnp.int32, (LEN, 128), 1) < HDIM

    def sent(it):
        return red.ready(jnp.where(it <= -2, UP0, 2304 * (5 - it)))

    def score_rows(head, j, start, size):
        return rows_at((4 * head + j) * LEN + start, size)

    def attend(it, carry):
        pair = PAIRS - 1 - it
        slot = lax.rem(it, 2)

        @pl.when(it + 1 < PAIRS)
        def _():
            probs_copy(pair - 1, 1 - slot).start()

        red.feed(0, sent(it - 2), sent(it - 1))

        @pl.when(other == 0)
        def _():
            red.push(sent(it - 3), sent(it - 2))

        red.tick(begun + per_pair * it)
        probs_copy(pair, slot).wait()
        query, key, value = qkv[3 * pair], qkv[3 * pair + 1], qkv[3 * pair + 2]
        grad = low[:, pl.ds(pl.multiple_of(pair * 128, 128), 128)]
        found = []
        for side in range(2):
            if side == 1 and per_pair == 2:
                red.tick(begun + per_pair * it + 1)
            head = 2 * pair + side
            mine = left if side == 0 else jnp.logical_not(left)
            base = UP0 + slot * 8 * LEN + side * 4 * LEN
            for r in range(0, LEN, BROWS):
                part = grad[r : r + BROWS]
                d_probs = nt(jnp.where(mine[r : r + BROWS], part, jnp.zeros_like(part)), value)
                soft = jnp.concatenate(
                    [wall[0, rows_at(base + j * LEN + r, BROWS), :] for j in range(4)], axis=1
                ).astype(F32)
                inner = jnp.sum(soft * d_probs, axis=1, keepdims=True)
                scores = (soft * (d_probs - inner)).astype(BF16)
                for j in range(4):
                    wall[1, score_rows(head, j, r, BROWS), :] = scores[:, j * 128 : (j + 1) * 128]
            scores = jnp.concatenate([wall[1, score_rows(head, j, 0, LEN), :] for j in range(4)], axis=1)
            chances = jnp.concatenate([wall[0, rows_at(base + j * LEN, LEN), :] for j in range(4)], axis=1)
            found.append((nn(scores, key), tn(scores, query), tn(chances, grad)))
        d_query = (jnp.where(left, found[0][0], found[1][0]) * HDIM**-0.5).astype(BF16)
        d_key = jnp.where(left, found[0][1], found[1][1]).astype(BF16)
        d_value = jnp.where(left, found[0][2], found[1][2]).astype(BF16)
        both = jnp.concatenate([d_query, d_key, d_value], axis=1)
        plane, spot = spots["qv_bias"]
        small[plane, pl.ds(spot + pair, 1), :] = total_rows(d_query)
        small[plane, pl.ds(spot + 6 + pair, 1), :] = total_rows(d_value)
        at = pl.multiple_of(3 * pair * D, 16)
        weight = jnp.concatenate([wall[0, rows_at(at + i * D, D), :] for i in range(3)], axis=1)
        acc[...] += nt(both, weight)
        part = tn(rounded[...], both).astype(BF16)
        for i in range(3):
            gstack[0, rows_at(at + i * D, D), :] = part[:, i * 128 : (i + 1) * 128]
        return carry

    lax.fori_loop(0, PAIRS, attend, 0)
    red.feed(0, sent(4), sent(5))

    @pl.when(other == 0)
    def _():
        red.push(sent(3), sent(4))

    branch[...] = acc[...].astype(BF16)
    layout = tn(features[...], branch[...]).astype(BF16)
    for c in range(6):
        gstack[1, pl.ds(LAY1 + c * FEAT, FEAT), :] = layout[:, c * 128 : (c + 1) * 128]

    @pl.when(other == 0)
    def _():
        red.push(sent(4), sent(5))

    late = begun + per_pair * PAIRS
    for plane in range(2):
        gstack[plane, pl.ds(SM0, 64), :] = small[plane].astype(BF16)
        gstack[plane, pl.ds(SM0 + 64, ROWS - SM0 - 64), :] = jnp.zeros((ROWS - SM0 - 64, 128), BF16)
        red.feed(plane, last, last + 1)
    drain(late, 0)
    red.push(last, last + 1)
    for copy in out_copies(1, branch, input_grad, False):
        copy.start()
    late += 1
    summed = red.count + SKEW * levels
    passed = [late]

    def tick():
        red.tick(passed[0])
        passed[0] += 1

    find_places(coord_col, lut, ranks, places, tick if fine else lambda: None)
    for table in (1, 2):
        key_row = jnp.broadcast_to(coord_row[table : table + 1, :], (256, LEN))
        for r in (0, 256):
            near = jnp.broadcast_to(coord_col[r : r + 256, table : table + 1], (256, LEN))
            lower = jnp.where(key_row < near, 1.0, 0.0).astype(BF16)
            ranks[table - 1, r : r + 256, :] = nn(lower, jnp.ones((LEN, 128), BF16))
    late = passed[0]
    pace = 2 if fine else 4
    table_grads(wall, coord_col, pick, keep, hidden, places, ranks, normed_one, tables, red, late, pace, summed)
    late = min(late + 24 // pace, summed)
    lax.fori_loop(late, summed, drain, 0)

    def squares(position, carry):
        piece = red.pieces[position].astype(F32)
        return carry + jnp.sum((piece * piece).reshape(-1, 8, 128), axis=0)

    value = lax.fori_loop(0, red.count, squares, jnp.zeros((8, 128), F32))
    value = jnp.sum(jnp.sum(value, axis=0, keepdims=True), axis=1, keepdims=True)
    tables[9:10, :] = jnp.broadcast_to(value, (1, 128))
    rounds = [
        [
            (member(dp, radix, stride, ((dp // stride) % radix + step) % radix), fs)
            for step in range(1, radix)
        ]
        for radix, stride in stages
    ] + [[red.core_peer], [red.x_peer]]

    def square_copies(number):
        base = sum(len(r) for r in rounds[:number])
        return [
            remote(tables.at[...], square_slots.at[base + i], n_send.at[base + i], n_recv.at[base + i], peer)
            for i, peer in enumerate(rounds[number])
        ]

    for number in range(max(red.ticks() - summed, len(rounds)) + 1):
        if number < len(rounds):
            for copy in square_copies(number):
                copy.start()
        if summed + number < red.ticks():
            red.tick(summed + number)
        if number < len(rounds):
            gathered = tables[...]
            base = sum(len(r) for r in rounds[:number])
            for i, copy in enumerate(square_copies(number)):
                copy.wait()
                gathered = gathered + square_slots[base + i]
            tables[...] = gathered
    gathered = tables[0:9, :]
    gathered = jnp.sum(jnp.sum(gathered * gathered, axis=0, keepdims=True), axis=1, keepdims=True)
    norm[...] = jnp.sqrt(tables[9:10, 0:1] + gathered)

    red.finish()
    grad_moved, grad_own = out_copies(1, branch, input_grad, False)
    grad_moved.wait_send()
    grad_own.wait()
    out_copies(0, rounded, layer_out, True)[0].wait_recv()
    out_copies(1, branch, input_grad, True)[0].wait_recv()


def table_grads(wall, coord_col, pick, keep, less, places, ranks, prefix, tables, red, late, pace, summed):
    tables[...] = jnp.zeros_like(tables)
    block = 64
    for table in range(3):
        order = lax.broadcasted_iota(jnp.int32, (16, LEN), 1)

        def less_rows(a, carry):
            at = pl.ds(pl.multiple_of(a * 16, 16), 16)
            if table == 0:
                near = jnp.broadcast_to(coord_col[at, 0:1], (16, LEN))
            else:
                near = jnp.concatenate([ranks[table - 1, at, :].astype(jnp.int32)] * 4, axis=1)
            less[at, 0:LEN] = jnp.where(near <= order, 1.0, 0.0).astype(BF16)
            return carry

        lax.fori_loop(0, LEN // 16, less_rows, 0, unroll=4)

        def query_rows(b, sums):
            number = late + (table * 8 + b) // pace

            @pl.when((lax.rem(table * 8 + b, pace) == 0) & (number < summed))
            def _():
                red.tick(number)

            start = b * block
            scores = jnp.concatenate(
                [
                    jnp.concatenate(
                        [wall[1, rows_at((4 * h + j) * LEN + start, block), :] for j in range(4)], axis=1
                    )
                    for h in range(HEADS)
                ],
                axis=0,
            )
            running = nn(scores, less[:, 0:LEN])
            for h in range(HEADS):
                for j in range(4):
                    r, c = (4 * h + j) // 6 * 64, (4 * h + j) % 6 * 128
                    prefix[r : r + 64, c : c + 128] = running[h * block : (h + 1) * block, j * 128 : (j + 1) * 128]

            def pick_up(a, carry):
                place_of = places[table, pl.ds(pl.multiple_of(start + a * 8, 8), 8), :]
                low, high = place_of & 127, place_of >> 7
                result = []
                for h in range(HEADS):
                    value = jnp.zeros((8, 128), F32)
                    for j in range(4):
                        r, c = (4 * h + j) // 6 * 64, (4 * h + j) % 6 * 128
                        rows = pl.ds(pl.multiple_of(r + a * 8, 8), 8)
                        part = jnp.take_along_axis(prefix[rows, c : c + 128], low, axis=1)
                        value = jnp.where(high == j, part, value)
                    result.append(carry[h] + value)
                return tuple(result)

            return lax.fori_loop(0, block // 8, pick_up, sums, unroll=8)

        sums = lax.fori_loop(
            0, LEN // block, query_rows, tuple(jnp.zeros((8, 128), F32) for _ in range(HEADS))
        )
        heads = jnp.concatenate(
            [jnp.sum(s, axis=0, keepdims=True) for s in sums] + [jnp.zeros((4, 128), F32)], axis=0
        )
        after = pltpu.roll(heads, 127, 1)
        whole = pltpu.roll(heads, 15, 1)
        lanes = lax.broadcasted_iota(jnp.int32, (16, 128), 1)
        buckets = jnp.where(lanes < 16, heads - after, after - heads)
        buckets = jnp.where(lanes == 15, heads, buckets)
        buckets = jnp.where(lanes == 16, 0.0, buckets)
        buckets = jnp.where(lanes == 31, whole - heads, buckets)
        buckets = jnp.where(lanes < 32, buckets, 0.0)
        placed = buckets if table == 0 else pltpu.roll(buckets, 32 * table, 1)
        parts, left_over = [], placed
        for _ in range(2):
            parts.append(left_over.astype(BF16))
            left_over = left_over - parts[-1].astype(F32)
        spread = sum(nt(part, pick[table]) for part in parts)
        flat_row = jnp.sum(spread * keep[...], axis=0, keepdims=True)
        for i in range(3):
            tables[3 * table + i : 3 * table + i + 1, :] = flat_row[:, i * 128 : (i + 1) * 128]


def backward_pass(stages, wall, cdoc, total, out_doc, saved, features, coord_row, coord_col):
    pick, keep = table_constants()
    sds = jax.ShapeDtypeStruct
    count_peers = 2 + sum(radix - 1 for radix, _ in stages)
    dma = pltpu.SemaphoreType.DMA
    buffers, sems = reduction_scratch(stages)
    return pl.pallas_call(
        functools.partial(backward_kernel, stages),
        name="backward_reduce",
        out_shape=(sds((2, LEN // 2, D), BF16), sds((2, LEN // 2, D), BF16), sds((ROWS, 128), BF16), sds((16, 128), F32), sds((1, 1), F32)),
        in_specs=[ANY, ANY, VMEM, ANY, ANY, ANY, ANY, ANY, ANY, VMEM, ANY, ANY, ANY, ANY, VMEM] + [VMEM] * 5,
        out_specs=(ANY, ANY, ANY, VMEM, VMEM),
        scratch_shapes=[
            pltpu.VMEM((2, ROWS, 128), BF16),
            pltpu.VMEM((2, ROWS, 128), BF16),
            pltpu.VMEM((LEN, D), F32),
            pltpu.VMEM((LEN, D), BF16),
            pltpu.VMEM((LEN, FF), BF16),
            pltpu.VMEM((LEN, FF), BF16),
            pltpu.VMEM((LEN, D), BF16),
            pltpu.VMEM((LEN, D), BF16),
            pltpu.VMEM((18, LEN, 128), BF16),
            pltpu.VMEM((LEN, D), BF16),
            pltpu.VMEM((LEN, D), F32),
            pltpu.VMEM((3, LEN, 128), jnp.int32),
            pltpu.VMEM((16, 128), jnp.int32),
            pltpu.VMEM((2, LEN, 128), F32),
            pltpu.VMEM((2, 64, 128), F32),
            pltpu.VMEM((count_peers, 16, 128), F32),
            dma((10,)), dma((12,)), dma((2,)), dma((2,)), dma((2,)), dma((2,)), dma((count_peers,)), dma((count_peers,)),
        ]
        + buffers
        + sems,
        compiler_params=pltpu.CompilerParams(
            collective_id=2, has_side_effects=True, vmem_limit_bytes=64 * 2**20 - 2**16
        ),
    )(wall, cdoc, total, out_doc, *saved, features, coord_row, coord_col, jnp.asarray(pick), jnp.asarray(keep))


BLOCK = 1408
DEEP_IN, DEEP_OUT = 4, 3


def flatten_rows(plane, step, source, tables, flat):
    def blocks(low, high, src, dst, rows, stride):
        def one(i, carry):
            flat[pl.ds(LEAD + dst(i), rows, stride=stride), :] = source[rows_at(src(i), rows), :].astype(F32)
            return carry

        lax.fori_loop(low, high, one, 0)

    if plane == 0:
        for part in (0, 1) if step == 0 else (step + 1,) if step < 7 else ():
            blocks(
                0, 18, lambda pos: pos * D + 96 * part,
                lambda pos: lax.rem(pos, 3) * 6 + pos // 3 + 96 * 18 * part, 96, 18,
            )
        if step == 4:
            small = source[pl.ds(SM0, 64), :].astype(F32)
            flat[pl.ds(LEAD + 13824, 12), :] = small[0:12]
            flat[pl.ds(LEAD + 18444, 18), :] = small[12:30]
        elif step == 7:
            blocks(0, 6, lambda c: OUT0 + c * D, lambda c: F_OUT + c, D, 6)
        elif step in (10, 11):
            first = 208 * (step - 10)
            blocks(0, 24, lambda c: UP0 + c * UP_A + first, lambda c: F_UP + c + 24 * first, 208, 24)
    else:
        if step < 4:
            first, rows = 96 * step, min(96, UP_B - 96 * step)
            blocks(0, 24, lambda c: UP1 + c * UP_B + first, lambda c: c - 98 + 24 * first, rows, 24)
        elif step < 16:
            j = step - 4
            blocks(
                0, 6, lambda c: DOWN1 + j * 1536 + c * 256, lambda c: F_DOWN1 + j * 1536 + c, 256, 6
            )
        if step == 4:
            small = source[pl.ds(SM1, 64), :].astype(F32)
            flat[pl.ds(LEAD + F_UPB1, 24), :] = small[0:24]
            flat[pl.ds(LEAD + F_SM1, 18), :] = small[24:42]
            flat[pl.ds(LEAD + F_TAB1, 9), :] = tables[0:9, :]
            rest = FLAT - F_TAB1 - 9
            flat[pl.ds(LEAD + F_TAB1 + 9, rest), :] = jnp.zeros((rest, 128), F32)
        elif step == 16:
            blocks(0, 6, lambda c: LAY1 + c * FEAT, lambda c: F_LAY1 + c, FEAT, 6)


def adam_kernel(
    source_hbm, tables, weights_hbm, first_hbm, second_hbm, grad_hbm, update_hbm, new_hbm,
    source, flat, weights, first, second, update, new, sem, in_sem, out_sem,
):
    fs = lax.axis_index("fsdp")
    steps = FLAT // BLOCK
    loads = [
        pltpu.make_async_copy(source_hbm.at[pl.ds(a, n)], source.at[pl.ds(a, n)], sem.at[i])
        for i, (a, n) in enumerate(((0, OUT0), (OUT0, ROWS - OUT0)))
    ]

    def fetch(step):
        where, slot = pl.ds(step * BLOCK, BLOCK), step % DEEP_IN
        return [
            pltpu.make_async_copy(ref.at[where], buffer.at[slot], in_sem.at[i, slot])
            for i, (ref, buffer) in enumerate(((weights_hbm, weights), (first_hbm, first), (second_hbm, second)))
        ]

    def store(step):
        where, slot = pl.ds(step * BLOCK, BLOCK), step % DEEP_OUT
        return [
            pltpu.make_async_copy(flat.at[pl.ds(LEAD + step * BLOCK, BLOCK)], grad_hbm.at[where], out_sem.at[0, slot]),
            pltpu.make_async_copy(update.at[slot], update_hbm.at[where], out_sem.at[1, slot]),
            pltpu.make_async_copy(new.at[slot], new_hbm.at[where], out_sem.at[2, slot]),
        ]

    loads[0].start()
    for step in range(DEEP_IN):
        for copy in fetch(step):
            copy.start()
        if step == 0:
            loads[1].start()
    part = 176
    row = lax.broadcasted_iota(jnp.int32, (part, 128), 0)
    for step in range(steps):
        if step == 0:
            loads[0].wait()
        if step == 3:
            loads[1].wait()
        for plane in range(2):

            @pl.when(fs == plane)
            def _(plane=plane, step=step):
                flatten_rows(plane, step, source, tables, flat)

        if step >= DEEP_OUT:
            for copy in store(step - DEEP_OUT):
                copy.wait()
        for copy in fetch(step):
            copy.wait()
        slot_in, slot_out = step % DEEP_IN, step % DEEP_OUT

        def some(i, carry):
            at = pl.ds(pl.multiple_of(i * part, 8), part)
            begin = pl.multiple_of(step * BLOCK + i * part, 8)
            grad = flat[pl.ds(LEAD + begin, part), :]
            new_first = adam_one * first[slot_in, at, :] + (1.0 - adam_one) * grad
            new_second = adam_two * second[slot_in, at, :] + (1.0 - adam_two) * grad * grad
            spread = jnp.sqrt(new_second * (1.0 / (1.0 - adam_two**adam_steps))) + adam_eps
            corrected = new_first * (1.0 / (1.0 - adam_one**adam_steps)) / spread
            rate = jnp.where((fs == 1) & (row + begin >= F_LAY1), table_factor, 1.0)
            update[slot_out, at, :] = rate * (corrected + decay_rate * weights[slot_in, at, :])
            new[slot_out, at, :] = new_first
            return carry

        lax.fori_loop(0, BLOCK // part, some, 0)
        for copy in store(step):
            copy.start()
        if step + DEEP_IN < steps:
            for copy in fetch(step + DEEP_IN):
                copy.start()
    for step in range(steps - DEEP_OUT, steps):
        for copy in store(step):
            copy.wait()


def adam(source, tables, weights, first, second):
    vector = jax.ShapeDtypeStruct((FLAT, 128), F32)
    dma = pltpu.SemaphoreType.DMA
    return pl.pallas_call(
        adam_kernel,
        name="adamw",
        out_shape=(vector, vector, vector),
        in_specs=[ANY, VMEM, ANY, ANY, ANY],
        out_specs=(ANY, ANY, ANY),
        scratch_shapes=[
            pltpu.VMEM((ROWS, 128), BF16),
            pltpu.VMEM((LEAD + FLAT + 288, 128), F32),
        ]
        + [pltpu.VMEM((DEEP_IN, BLOCK, 128), F32)] * 3
        + [pltpu.VMEM((DEEP_OUT, BLOCK, 128), F32)] * 2
        + [dma((2,)), dma((3, DEEP_IN)), dma((3, DEEP_OUT))],
        compiler_params=pltpu.CompilerParams(vmem_limit_bytes=60 * 2**20),
    )(source, tables, weights, first, second)


def layout_features(coords):
    freq_count = FEAT // 8
    factors = (jnp.arange(freq_count, dtype=jnp.int32) + 1) ** 2
    phases = coords[..., :, None] * factors % 4096
    angles = phases.astype(F32) * (2.0 * math.pi / 4096.0)
    wave_parts = jnp.concatenate([jnp.sin(angles), jnp.cos(angles)], axis=-1)
    return wave_parts.reshape(coords.shape[:-1] + (FEAT,))


def local(stages, inputs, box_coords, mlm_mask, cotangent, params, first_moment, second_moment):
    fs = lax.axis_index("fsdp")
    boxes = lax.dynamic_index_in_dim(box_coords, fs, 0, keepdims=False)
    features = layout_features(boxes).astype(BF16)
    coord_col = jnp.stack(
        [jnp.arange(LEN, dtype=jnp.int32), boxes[:, 0] + boxes[:, 2], boxes[:, 1] + boxes[:, 3]], axis=1
    )
    coord_row = coord_col.T
    flat = [v.reshape(FLAT, 128) for v in (params, first_moment, second_moment)]
    wall, cdoc, total, *saved, out_doc = forward_pass(
        stages, flat[0], inputs, cotangent, mlm_mask, features, coord_row, coord_col
    )
    layer_out, input_grad, reduced, tables, norm = backward_pass(
        stages, wall, cdoc, total, out_doc, saved, features, coord_row, coord_col
    )
    grad, update, new_first = adam(reduced, tables, *flat)
    return (layer_out, input_grad, grad.reshape(-1), norm.reshape(()), update.reshape(-1), new_first.reshape(-1))


def solution(mesh):
    in_specs = (
        P("dp", "fsdp", None),
        P("dp", None, None),
        P("dp", "fsdp"),
        P("dp", "fsdp", None),
        P("fsdp"),
        P("fsdp"),
        P("fsdp"),
    )
    out_specs = (P("dp", "fsdp", None), P("dp", "fsdp", None), P("fsdp"), P(), P("fsdp"), P("fsdp"))
    stages = radices(mesh.shape["dp"])
    return jax.shard_map(
        functools.partial(local, stages), mesh=mesh, in_specs=in_specs, out_specs=out_specs, check_vma=False
    )
```
